32 devices in a mesh: groups: 1, blk: 8 (over z, y), inner: 4 (over x, core).
Axes of the slice: x: 2, y: 2, z: 4, core: 2. Of those that a mesh axis runs over, the one named last changes fastest.
Arguments:
- alignment_left: float32 [128, 4096], P(('groups', 'blk')), may hold values from -6 to 6
- alignment_right: float32 [512, 4096], P(('groups', 'blk', 'inner')), may hold values from -6 to 6
- projection_matrix: float32 [1024, 128], replicated, may hold values from -0.1875 to 0.1875
- cotangent: float32 [128, 8, 64, 128], P(('groups', 'blk'), None, 'inner'), may hold values from -6 to 6
Outputs:
- pair_update: float32 [128, 8, 64, 128], P(('groups', 'blk'), None, 'inner')
- grad_left: float32 [128, 4096], P(('groups', 'blk'), 'inner')
- grad_right: float32 [512, 4096], P(('groups', 'blk', 'inner'))
- grad_weight: float32 [1024, 128], P('groups')
The draws below stay inside these ranges and needn't reach their ends.
All inputs are finite; a program needn't handle non-finite values.
Results may differ from the reference program's by a relative error of at most 0.0001.
Values sent between devices are 32-bit elements; how exact they have to be, the bound alone decides.
No kernel may reach another device: no remote copies, remote signals or barrier semaphores. Data moves between devices by JAX's collectives and lax.ppermute only.
A program may use at most 128 MiB of HBM per device.

```python
import jax
import jax.numpy as jnp
from jax import lax

ENTRY_CHANNELS = 32
PAIR_CH = 128
SEQUENCE_TOTAL = 128
BLOCK_ROWS = 16
WINDOW_ROWS = 128
COL_BLOCK = 64
RESIDUE_TOTAL = 512
FEATURE_WIDTH = 4096
OUTER = 1024
N_BLK = 8


def spiked(entries, stream_key, source, target, parts, factor):
    owner, partner = [(jnp.arange(entries.shape[position]) // (entries.shape[position] // parts)).reshape([-1 if axis == position else 1 for axis in range(entries.ndim)]) for position in (source, target)]
    chosen = jax.random.permutation(stream_key, parts)[partner]
    strong = (owner == chosen) | (owner == (partner + parts // 2) % parts)
    return jnp.where(strong, factor * entries, entries)


def levels(own_key, shape, cuts, least, top_value):
    def one(position, blocks):
        draws = jax.random.uniform(jax.random.fold_in(jax.random.fold_in(own_key, 6), position), (blocks,), jnp.float32, least / len(cuts), top_value / len(cuts))
        return jnp.repeat(jnp.exp(draws), shape[position] // blocks).reshape((-1,) + (1,) * (len(shape) - position - 1))

    loudness = one(*cuts[0])
    for cut in cuts[1:]:
        loudness = loudness * one(*cut)
    return loudness


def scatter_about(own_key, dims, scale, bound, split=(), held_as=jnp.bfloat16):
    level = levels(own_key, dims, split, -0.22, 0.18) if split else 1.0
    drawn = jax.random.normal(own_key, dims, jnp.float32) * scale * level
    return jnp.minimum(jnp.maximum(drawn, -bound), bound).astype(held_as)


def noise_with(stream_key, dims, width, limit, split, heavy, held_as=jnp.bfloat16):
    drawn = width * jax.random.normal(stream_key, dims, jnp.float32)
    if split:
        drawn = drawn * levels(stream_key, dims, split, -0.22, 0.18)
    return jnp.clip(spiked(drawn, jax.random.fold_in(stream_key, 3), *heavy), -limit, limit).astype(held_as)


def setup_inputs(seed: int = 0, part: int = 0) -> dict:
    splits = jax.random.split(jax.random.key(seed), 5)
    part_keys = jax.random.split(jax.random.fold_in(splits[4], part), 5)
    alignment_left = scatter_about(part_keys[0], (WINDOW_ROWS, FEATURE_WIDTH), 1.0, 6.0, ((0, 8),), jnp.float32)
    alignment_right = scatter_about(part_keys[1], (RESIDUE_TOTAL, FEATURE_WIDTH), 1.0, 6.0, ((0, 32),), jnp.float32)
    projection_matrix = scatter_about(splits[2], (OUTER, PAIR_CH), OUTER ** -0.5, 0.1875, (), jnp.float32)
    cotangent = noise_with(part_keys[3], (WINDOW_ROWS, N_BLK, COL_BLOCK, PAIR_CH), 1.0, 6.0, ((0, 8), (2, 4)), (0, 1, 8, 2.0), jnp.float32)
    return dict(alignment_left=alignment_left, alignment_right=alignment_right, projection_matrix=projection_matrix, cotangent=cotangent)


highest = lax.Precision.HIGHEST


def reference(alignment_left, alignment_right, projection_matrix, cotangent):
    right_sequence = alignment_right.reshape(RESIDUE_TOTAL, SEQUENCE_TOTAL, ENTRY_CHANNELS)
    grad_rows = cotangent.reshape(N_BLK, BLOCK_ROWS, RESIDUE_TOTAL, PAIR_CH)
    left_window_rows = alignment_left.reshape(N_BLK, BLOCK_ROWS, SEQUENCE_TOTAL, ENTRY_CHANNELS)

    def row_step(running, inputs):
        weight_acc, right_acc = running
        left_sequence, grad_block = inputs
        outer = jnp.einsum('isx,jsy->ijxy', left_sequence, right_sequence, precision=highest) / SEQUENCE_TOTAL
        outer_flat = outer.reshape(BLOCK_ROWS, RESIDUE_TOTAL, OUTER)
        pair_block = jnp.einsum('ijk,kp->ijp', outer_flat, projection_matrix, precision=highest)
        outer_grad = jnp.einsum('ijp,kp->ijk', grad_block, projection_matrix, precision=highest)
        outer_grad = outer_grad.reshape(BLOCK_ROWS, RESIDUE_TOTAL, ENTRY_CHANNELS, ENTRY_CHANNELS)
        weight_acc = weight_acc + jnp.einsum('ijk,ijp->kp', outer_flat, grad_block, precision=highest)
        left_block = jnp.einsum('ijxy,jsy->isx', outer_grad, right_sequence, precision=highest) / SEQUENCE_TOTAL
        right_acc = right_acc + jnp.einsum('ijxy,isx->jsy', outer_grad, left_sequence, precision=highest) / SEQUENCE_TOTAL
        return (weight_acc, right_acc), (pair_block, left_block.reshape(BLOCK_ROWS, FEATURE_WIDTH))

    initial = (jnp.zeros((OUTER, PAIR_CH), jnp.float32), jnp.zeros((RESIDUE_TOTAL, SEQUENCE_TOTAL, ENTRY_CHANNELS), jnp.float32))
    finals, blocks = lax.scan(row_step, initial, (left_window_rows, grad_rows))
    grad_weight, right_acc = finals
    pair_blocks, left_blocks = blocks
    pair_update = pair_blocks.reshape(WINDOW_ROWS, N_BLK, COL_BLOCK, PAIR_CH)
    return pair_update, left_blocks.reshape(WINDOW_ROWS, FEATURE_WIDTH), right_acc.reshape(RESIDUE_TOTAL, FEATURE_WIDTH), grad_weight
```

```python
import functools

import jax
import jax.numpy as jnp
from jax import lax
from jax.experimental import pallas as pl
from jax.experimental.pallas import tpu as pltpu
from jax.sharding import PartitionSpec as P

ENTRY_CHANNELS = 32
F32 = jnp.float32
BF16 = jnp.bfloat16
VMEM_LIMIT = 48 * 1024 * 1024


def halves(values):
    high = values.astype(BF16)
    low = (values - high.astype(F32)).astype(BF16)
    return high, low


def dot(left, right):
    return jnp.dot(left, right, preferred_element_type=F32)


def dot_rows(left, right):
    return lax.dot_general(left, right, (((1,), (1,)), ((), ())), preferred_element_type=F32)


def ring_position(block, count):
    return jnp.where(lax.rem(block, 2) == 0, block // 2, count - 1 - block // 2)


def ring_block(position, count):
    return jnp.where(position < count // 2, 2 * position, 2 * count - 1 - 2 * position)


def slot_blocks(count):
    position = ring_position(lax.axis_index("blk"), count)
    return [ring_block(lax.rem(position + slot, count), count) for slot in range(count)]


def pair_rows(block_refs, index):
    return jnp.concatenate([ref[index] for ref in block_refs], axis=0)


def cotangent_rows(cotangent_ref, row, blocks):
    return jnp.concatenate([cotangent_ref[row, block] for block in blocks], axis=0)


def weight_by_y(weight_ref, y, channels):
    return weight_ref[pl.ds(y, channels, stride=channels), :]


def gradient_kernel(count, weight_ref, cotangent_ref, left_ref, *refs):
    right_refs = refs[:count]
    high_ref, low_ref, weight_cat, left_flip = refs[count:]
    rows = cotangent_ref.shape[0]
    channels = ENTRY_CHANNELS
    sequences = left_ref.shape[1]
    blocks = slot_blocks(count)
    columns = count * cotangent_ref.shape[2]
    for y in range(channels):
        high, low = halves(weight_by_y(weight_ref, y, channels))
        weight_cat[y * channels : (y + 1) * channels, :] = jnp.concatenate([high, low, high], 1)
    flip_high, flip_low = halves(left_ref[...].T)
    left_flip[:sequences, :] = flip_high
    left_flip[sequences:, :] = flip_low

    def grad_step(pair, carry):
        grads = [cotangent_rows(cotangent_ref, 2 * pair + part, blocks) for part in range(2)]
        high, low = halves(jnp.concatenate(grads, 0))
        found = dot_rows(weight_cat[...], jnp.concatenate([high, high, low], 1))
        high, low = halves(found)
        high_ref[pair] = high
        low_ref[pair] = low
        return carry

    lax.fori_loop(0, rows // 2, grad_step, 0)

    def right_step(step, carry):
        def stacked(ref):
            return jnp.concatenate(
                [rows_of_y(ref, 2 * step + part, rows, columns) for part in range(2)], 1
            )

        first = dot(left_flip[...], stacked(high_ref))
        second = dot(left_flip[:sequences, :], stacked(low_ref))
        found = first[:sequences] + first[sequences:] + second
        for part in range(2):
            turned = found[:, part * columns : (part + 1) * columns].T
            depth = columns // count
            for slot in range(count):
                right_refs[slot][2 * step + part] = turned[slot * depth : (slot + 1) * depth]
        return carry

    lax.fori_loop(0, channels // 2, right_step, 0)


def rows_of_y(ref, y, rows, columns):
    channels = ENTRY_CHANNELS
    start = pl.multiple_of(y * channels, channels)
    return jnp.concatenate(
        [
            ref[row // 2, pl.ds(start, channels), (row % 2) * columns : (row % 2 + 1) * columns]
            for row in range(rows)
        ],
        0,
    )


def outer_phase(left_ref, block_refs, high_ref, low_ref, rows):
    channels = ENTRY_CHANNELS
    count = len(block_refs)
    columns = count * block_refs[0].shape[1]
    high, low = halves(left_ref[...])
    left_cat = jnp.concatenate([high, low, high], 1)

    def step_of(step, carry):
        right = [pair_rows(block_refs, 2 * step + part) for part in range(2)]
        high, low = halves(jnp.concatenate(right, 0))
        found = dot_rows(left_cat, jnp.concatenate([high, high, low], 1))
        high, low = halves(found)
        for ref, values in ((high_ref, high), (low_ref, low)):
            for part in range(2):
                start = pl.multiple_of((2 * step + part) * channels, channels)
                for row in range(rows):
                    ref[
                        row // 2,
                        pl.ds(start, channels),
                        (row % 2) * columns : (row % 2 + 1) * columns,
                    ] = values[
                        row * channels : (row + 1) * channels,
                        part * columns : (part + 1) * columns,
                    ]
        return carry

    lax.fori_loop(0, channels // 2, step_of, 0)


def weight_kernel(count, inner, left_ref, cotangent_ref, *refs):
    block_refs = refs[:count]
    out_refs = refs[count : count + inner]
    high_ref, low_ref, total = refs[count + inner :]
    rows = cotangent_ref.shape[0]
    pairs = cotangent_ref.shape[3]
    blocks = slot_blocks(count)
    outer_phase(left_ref, block_refs, high_ref, low_ref, rows)
    total[...] = jnp.zeros_like(total)

    def step_of(pair, carry):
        grads = [cotangent_rows(cotangent_ref, 2 * pair + part, blocks) for part in range(2)]
        high, low = halves(jnp.concatenate(grads, 0))
        both = dot(high_ref[pair], jnp.concatenate([high, low], 1))
        total[...] += both[:, :pairs] + both[:, pairs:] + dot(low_ref[pair], high)
        return carry

    lax.fori_loop(0, rows // 2, step_of, 0)
    mine = lax.axis_index("inner")
    here = lax.axis_index("blk")
    size = total.shape[0] // (inner * count)
    for other in range(inner):
        for part in range(count):
            chunk = lax.bitwise_xor(mine, other) * count + lax.bitwise_xor(here, part)
            out_refs[other][part] = total[pl.ds(pl.multiple_of(chunk * size, size), size), :]


def left_kernel(count, inner, high_ref, low_ref, *refs):
    block_refs = refs[:count]
    out_refs = refs[count : count + inner]
    total, flipped = refs[count + inner :]
    rows = 2 * high_ref.shape[0]
    channels = ENTRY_CHANNELS
    columns = high_ref.shape[2] // 2
    sequences = block_refs[0].shape[2]
    total[...] = jnp.zeros_like(total)
    group = 4

    def step_of(step, carry):
        ys = [group * step + part for part in range(group)]
        high, low = halves(jnp.concatenate([pair_rows(block_refs, y) for y in ys], 0))
        grads_high = jnp.concatenate([rows_of_y(high_ref, y, rows, columns) for y in ys], 1)
        grads_low = jnp.concatenate([rows_of_y(low_ref, y, rows, columns) for y in ys], 1)
        both = dot(grads_high, jnp.concatenate([high, low], 1))
        total[...] += both[:, :sequences] + both[:, sequences:] + dot(grads_low, high)
        return carry

    lax.fori_loop(0, channels // group, step_of, 0)
    flipped[...] = total[...].T * (1.0 / sequences)
    mine = lax.axis_index("inner")
    size = sequences // inner
    for other in range(inner):
        start = pl.multiple_of(lax.bitwise_xor(mine, other) * size, size)
        out_refs[other][...] = flipped[pl.ds(start, size), :]


def pair_kernel(count, left_ref, weight_ref, *refs):
    block_refs = refs[:count]
    out_ref, high_ref, low_ref, weight_flip, weight_rows = refs[count:]
    rows = out_ref.shape[0]
    channels = ENTRY_CHANNELS
    depth = out_ref.shape[2]
    pairs = out_ref.shape[3]
    columns = count * depth
    blocks = slot_blocks(count)
    for y in range(channels):
        weight_rows[y * channels : (y + 1) * channels, :] = weight_by_y(weight_ref, y, channels)
    flip_high, flip_low = halves(weight_rows[...].T)
    weight_flip[:pairs, :] = flip_high
    weight_flip[pairs:, :] = flip_low
    outer_phase(left_ref, block_refs, high_ref, low_ref, rows)

    def step_of(pair, carry):
        first = dot(weight_flip[...], high_ref[pair])
        found = first[:pairs] + first[pairs:] + dot(weight_flip[:pairs, :], low_ref[pair])
        for part in range(2):
            turned = found[:, part * columns : (part + 1) * columns].T
            for slot in range(count):
                out_ref[2 * pair + part, blocks[slot]] = turned[slot * depth : (slot + 1) * depth]
        return carry

    lax.fori_loop(0, rows // 2, step_of, 0)


def place_kernel(count, inner, *refs):
    own_refs = refs[:count]
    other_refs = refs[count : count + inner - 1]
    out_ref = refs[-1]
    channels = ENTRY_CHANNELS
    mine = lax.axis_index("inner")
    here = lax.axis_index("blk")
    size = own_refs[0].shape[0]
    for other in range(inner):
        for part in range(count):
            chunk = lax.bitwise_xor(mine, other) * count + lax.bitwise_xor(here, part)
            first = chunk * size
            y = first // channels
            x = lax.rem(first, channels)
            piece = own_refs[part][...] if other == 0 else other_refs[other - 1][part]
            out_ref[pl.ds(x * channels + y, size, stride=channels), :] = piece


def call(kernel, out_shape, scratch, flops):
    return pl.pallas_call(
        kernel,
        out_shape=out_shape,
        scratch_shapes=scratch,
        compiler_params=pltpu.CompilerParams(vmem_limit_bytes=VMEM_LIMIT),
        cost_estimate=pl.CostEstimate(flops=flops, bytes_accessed=8 << 20, transcendentals=0),
    )


def ring_moves(count, inner):
    order = [2 * r if r < count // 2 else 2 * count - 1 - 2 * r for r in range(count)]
    upward = [(order[r], order[(r + 1) % count]) for r in range(count)]
    downward = [(there, here) for here, there in upward]
    across = []
    for q in range(inner):
        for here, there in upward if q % 2 == 0 else downward:
            across.append((here * inner + q, there * inner + q))
    return upward, downward, across


def ring_gather(block, count, inner):
    upward, downward, across = ring_moves(count, inner)
    even = lax.rem(lax.axis_index("inner"), 2) == 0
    slots = [block] * count
    up = down = block
    for step in range(1, count // 2):
        up = lax.ppermute(up, "blk", upward)
        down = lax.ppermute(down, "blk", downward)
        slots[count - step] = up
        slots[step] = down
    slots[count // 2] = lax.ppermute(jnp.where(even, up, down), ("blk", "inner"), across)
    return slots


def ring_scatter(parts, count, inner):
    upward, downward, across = ring_moves(count, inner)
    even = lax.rem(lax.axis_index("inner"), 2) == 0
    half = count // 2
    first = lax.ppermute(parts[half], ("blk", "inner"), across)
    up = parts[half - 1] + jnp.where(even, first, 0.0)
    down = parts[half + 1] + jnp.where(even, 0.0, first)
    for step in range(half - 1, 0, -1):
        up = lax.ppermute(up, "blk", upward)
        down = lax.ppermute(down, "blk", downward)
        if step > 1:
            up = parts[step - 1] + up
            down = parts[count - step + 1] + down
    return parts[0] + up + down


def swap(value, axis, size, distance):
    return lax.ppermute(value, axis, [(here, here ^ distance) for here in range(size)])


def local(alignment_left, alignment_right, projection_matrix, cotangent):
    rows, features = alignment_left.shape
    depth = alignment_right.shape[0]
    count = lax.axis_size("blk")
    inner = lax.axis_size("inner")
    channels = ENTRY_CHANNELS
    sequences = features // channels
    outer, pairs = projection_matrix.shape
    columns = count * depth
    flops = 2 * rows * columns * outer * pairs * 3

    right = alignment_right.reshape(depth, sequences, channels).transpose(2, 0, 1)
    slots = ring_gather(right, count, inner)

    left = alignment_left.reshape(rows, sequences, channels).transpose(0, 2, 1)
    left = left.reshape(rows * channels, sequences) * (1.0 / sequences)

    wide = (rows // 2, outer, 2 * columns)
    block_shape = jax.ShapeDtypeStruct((channels, depth, sequences), F32)
    found = call(
        functools.partial(gradient_kernel, count),
        [block_shape] * count + [jax.ShapeDtypeStruct(wide, BF16)] * 2,
        [pltpu.VMEM((outer, 3 * pairs), BF16), pltpu.VMEM((2 * sequences, rows * channels), BF16)],
        2 * flops,
    )(projection_matrix, cotangent, left)
    grads_high, grads_low = found[count:]
    right_grad = ring_scatter(found[:count], count, inner)
    grad_right = right_grad.transpose(1, 2, 0).reshape(depth, features)

    size = outer // (count * inner)
    wide_scratch = [pltpu.VMEM(wide, BF16), pltpu.VMEM(wide, BF16)]
    weight_parts = call(
        functools.partial(weight_kernel, count, inner),
        [jax.ShapeDtypeStruct((count, size, pairs), F32)] * inner,
        wide_scratch + [pltpu.VMEM((outer, pairs), F32)],
        2 * flops,
    )(left, cotangent, *slots)

    weight_own = weight_parts[0]
    for other in range(1, inner):
        weight_own = weight_own + swap(weight_parts[other], "inner", inner, other)
    weight_sum = weight_own[0]
    for other in range(1, count):
        weight_sum = weight_sum + swap(weight_own[other], "blk", count, other)
    gathered = [weight_sum]
    for other in range(1, count):
        gathered.append(swap(weight_sum, "blk", count, other))
    stacked = jnp.stack(gathered)
    spread = [swap(stacked, "inner", inner, other) for other in range(1, inner)]

    left_parts = call(
        functools.partial(left_kernel, count, inner),
        [jax.ShapeDtypeStruct((sequences // inner, rows * channels), F32)] * inner,
        [
            pltpu.VMEM((rows * channels, sequences), F32),
            pltpu.VMEM((sequences, rows * channels), F32),
        ],
        flops,
    )(grads_high, grads_low, *slots)
    left_sum = left_parts[0]
    for other in range(1, inner):
        left_sum = left_sum + swap(left_parts[other], "inner", inner, other)
    grad_left = left_sum.reshape(sequences // inner, rows, channels).transpose(1, 0, 2)
    grad_left = grad_left.reshape(rows, features // inner)

    pair_update = call(
        functools.partial(pair_kernel, count),
        jax.ShapeDtypeStruct(cotangent.shape, F32),
        wide_scratch
        + [pltpu.VMEM((2 * pairs, outer), BF16), pltpu.VMEM((outer, pairs), F32)],
        2 * flops,
    )(left, projection_matrix, *slots)

    grad_weight = call(
        functools.partial(place_kernel, count, inner),
        jax.ShapeDtypeStruct(projection_matrix.shape, F32),
        [],
        0,
    )(*gathered, *spread)
    return (pair_update, grad_left, grad_right, grad_weight)


def solution(mesh):
    placed = (
        P(("groups", "blk"), None),
        P(("groups", "blk", "inner"), None),
        P(),
        P(("groups", "blk"), None, "inner", None),
    )
    return jax.shard_map(
        local,
        mesh=mesh,
        in_specs=placed,
        out_specs=(
            P(("groups", "blk"), None, "inner", None),
            P(("groups", "blk"), "inner"),
            P(("groups", "blk", "inner"), None),
            P("groups", None),
        ),
        check_vma=False,
    )
```

```python
import functools

import jax
import jax.numpy as jnp
from jax import lax
from jax.experimental import pallas as pl
from jax.experimental.pallas import tpu as pltpu
from jax.sharding import PartitionSpec as P

ENTRY_CHANNELS = 32
F32 = jnp.float32
BF16 = jnp.bfloat16
VMEM_LIMIT = 48 * 1024 * 1024


def halves(values):
    high = values.astype(BF16)
    low = (values - high.astype(F32)).astype(BF16)
    return high, low


def dot(left, right):
    return jnp.dot(left, right, preferred_element_type=F32)


def dot_rows(left, right):
    return lax.dot_general(left, right, (((1,), (1,)), ((), ())), preferred_element_type=F32)


def ring_position(block, count):
    return jnp.where(lax.rem(block, 2) == 0, block // 2, count - 1 - block // 2)


def ring_block(position, count):
    return jnp.where(position < count // 2, 2 * position, 2 * count - 1 - 2 * position)


def slot_blocks(count):
    position = ring_position(lax.axis_index("blk"), count)
    return [ring_block(lax.rem(position + slot, count), count) for slot in range(count)]


def pair_rows(block_refs, index):
    return jnp.concatenate([ref[index] for ref in block_refs], axis=0)


def cotangent_rows(cotangent_ref, row, blocks):
    return jnp.concatenate([cotangent_ref[row, block] for block in blocks], axis=0)


def weight_by_y(weight_ref, y, channels):
    return weight_ref[pl.ds(y, channels, stride=channels), :]


def gradient_kernel(count, weight_ref, cotangent_ref, high_ref, low_ref, weight_cat):
    rows = cotangent_ref.shape[0]
    channels = ENTRY_CHANNELS
    blocks = slot_blocks(count)
    for y in range(channels):
        high, low = halves(weight_by_y(weight_ref, y, channels))
        weight_cat[y * channels : (y + 1) * channels, :] = jnp.concatenate([high, low, high], 1)

    def grad_step(pair, carry):
        grads = [cotangent_rows(cotangent_ref, 2 * pair + part, blocks) for part in range(2)]
        high, low = halves(jnp.concatenate(grads, 0))
        found = dot_rows(weight_cat[...], jnp.concatenate([high, high, low], 1))
        high, low = halves(found)
        high_ref[pair] = high
        low_ref[pair] = low
        return carry

    lax.fori_loop(0, rows // 2, grad_step, 0)


def right_kernel(count, high_ref, low_ref, left_ref, *refs):
    right_refs = refs[:count]
    left_flip = refs[count]
    rows = 2 * high_ref.shape[0]
    columns = high_ref.shape[2] // 2
    channels = ENTRY_CHANNELS
    sequences = left_ref.shape[1]
    flip_high, flip_low = halves(left_ref[...].T)
    left_flip[:sequences, :] = flip_high
    left_flip[sequences:, :] = flip_low

    def right_step(step, carry):
        def stacked(ref):
            return jnp.concatenate(
                [rows_of_y(ref, 2 * step + part, rows, columns) for part in range(2)], 1
            )

        first = dot(left_flip[...], stacked(high_ref))
        second = dot(left_flip[:sequences, :], stacked(low_ref))
        found = first[:sequences] + first[sequences:] + second
        for part in range(2):
            turned = found[:, part * columns : (part + 1) * columns].T
            depth = columns // count
            for slot in range(count):
                right_refs[slot][2 * step + part] = turned[slot * depth : (slot + 1) * depth]
        return carry

    lax.fori_loop(0, channels // 2, right_step, 0)


def rows_of_y(ref, y, rows, columns):
    channels = ENTRY_CHANNELS
    start = pl.multiple_of(y * channels, channels)
    return jnp.concatenate(
        [
            ref[row // 2, pl.ds(start, channels), (row % 2) * columns : (row % 2 + 1) * columns]
            for row in range(rows)
        ],
        0,
    )


def outer_phase(left_ref, block_refs, high_ref, low_ref, rows):
    channels = ENTRY_CHANNELS
    count = len(block_refs)
    columns = count * block_refs[0].shape[1]
    high, low = halves(left_ref[...])
    left_cat = jnp.concatenate([high, low, high], 1)

    def step_of(step, carry):
        right = [pair_rows(block_refs, 2 * step + part) for part in range(2)]
        high, low = halves(jnp.concatenate(right, 0))
        found = dot_rows(left_cat, jnp.concatenate([high, high, low], 1))
        high, low = halves(found)
        for ref, values in ((high_ref, high), (low_ref, low)):
            for part in range(2):
                start = pl.multiple_of((2 * step + part) * channels, channels)
                for row in range(rows):
                    ref[
                        row // 2,
                        pl.ds(start, channels),
                        (row % 2) * columns : (row % 2 + 1) * columns,
                    ] = values[
                        row * channels : (row + 1) * channels,
                        part * columns : (part + 1) * columns,
                    ]
        return carry

    lax.fori_loop(0, channels // 2, step_of, 0)


def weight_kernel(count, left_ref, cotangent_ref, *refs):
    block_refs = refs[:count]
    out_ref, high_ref, low_ref, total = refs[count:]
    rows = cotangent_ref.shape[0]
    pairs = cotangent_ref.shape[3]
    blocks = slot_blocks(count)
    outer_phase(left_ref, block_refs, high_ref, low_ref, rows)
    total[...] = jnp.zeros_like(total)

    def step_of(pair, carry):
        grads = [cotangent_rows(cotangent_ref, 2 * pair + part, blocks) for part in range(2)]
        high, low = halves(jnp.concatenate(grads, 0))
        both = dot(high_ref[pair], jnp.concatenate([high, low], 1))
        total[...] += both[:, :pairs] + both[:, pairs:] + dot(low_ref[pair], high)
        return carry

    lax.fori_loop(0, rows // 2, step_of, 0)
    out_ref[...] = total[...]


def left_kernel(count, inner, high_ref, low_ref, *refs):
    block_refs = refs[:count]
    out_refs = refs[count : count + inner]
    total, flipped = refs[count + inner :]
    rows = 2 * high_ref.shape[0]
    channels = ENTRY_CHANNELS
    columns = high_ref.shape[2] // 2
    sequences = block_refs[0].shape[2]
    total[...] = jnp.zeros_like(total)
    group = 4

    def step_of(step, carry):
        ys = [group * step + part for part in range(group)]
        high, low = halves(jnp.concatenate([pair_rows(block_refs, y) for y in ys], 0))
        grads_high = jnp.concatenate([rows_of_y(high_ref, y, rows, columns) for y in ys], 1)
        grads_low = jnp.concatenate([rows_of_y(low_ref, y, rows, columns) for y in ys], 1)
        both = dot(grads_high, jnp.concatenate([high, low], 1))
        total[...] += both[:, :sequences] + both[:, sequences:] + dot(grads_low, high)
        return carry

    lax.fori_loop(0, channels // group, step_of, 0)
    flipped[...] = total[...].T * (1.0 / sequences)
    mine = lax.axis_index("inner")
    size = sequences // inner
    for other in range(inner):
        start = pl.multiple_of(lax.bitwise_xor(mine, other) * size, size)
        out_refs[other][...] = flipped[pl.ds(start, size), :]


def pair_kernel(count, high_ref, low_ref, weight_ref, out_ref, weight_flip, weight_rows):
    rows = out_ref.shape[0]
    channels = ENTRY_CHANNELS
    depth = out_ref.shape[2]
    pairs = out_ref.shape[3]
    columns = count * depth
    blocks = slot_blocks(count)
    for y in range(channels):
        weight_rows[y * channels : (y + 1) * channels, :] = weight_by_y(weight_ref, y, channels)
    flip_high, flip_low = halves(weight_rows[...].T)
    weight_flip[:pairs, :] = flip_high
    weight_flip[pairs:, :] = flip_low

    def step_of(pair, carry):
        first = dot(weight_flip[...], high_ref[pair])
        found = first[:pairs] + first[pairs:] + dot(weight_flip[:pairs, :], low_ref[pair])
        for part in range(2):
            turned = found[:, part * columns : (part + 1) * columns].T
            for slot in range(count):
                out_ref[2 * pair + part, blocks[slot]] = turned[slot * depth : (slot + 1) * depth]
        return carry

    lax.fori_loop(0, rows // 2, step_of, 0)


def place_kernel(in_ref, out_ref):
    channels = ENTRY_CHANNELS
    for y in range(channels):
        rows = in_ref[y * channels : (y + 1) * channels, :]
        out_ref[pl.ds(y, channels, stride=channels), :] = rows


def call(kernel, out_shape, scratch, flops):
    return pl.pallas_call(
        kernel,
        out_shape=out_shape,
        scratch_shapes=scratch,
        compiler_params=pltpu.CompilerParams(vmem_limit_bytes=VMEM_LIMIT),
        cost_estimate=pl.CostEstimate(flops=flops, bytes_accessed=8 << 20, transcendentals=0),
    )


def ring_moves(count, inner):
    order = [2 * r if r < count // 2 else 2 * count - 1 - 2 * r for r in range(count)]
    upward = [(order[r], order[(r + 1) % count]) for r in range(count)]
    downward = [(there, here) for here, there in upward]
    across = []
    for q in range(inner):
        for here, there in upward if q % 2 == 0 else downward:
            across.append((here * inner + q, there * inner + q))
    return upward, downward, across


def ring_gather(block, count, inner):
    upward, downward, across = ring_moves(count, inner)
    even = lax.rem(lax.axis_index("inner"), 2) == 0
    slots = [block] * count
    up = down = block
    for step in range(1, count // 2):
        up = lax.ppermute(up, "blk", upward)
        down = lax.ppermute(down, "blk", downward)
        slots[count - step] = up
        slots[step] = down
    slots[count // 2] = lax.ppermute(jnp.where(even, up, down), ("blk", "inner"), across)
    return slots


def ring_scatter(parts, count, inner):
    upward, downward, across = ring_moves(count, inner)
    even = lax.rem(lax.axis_index("inner"), 2) == 0
    half = count // 2
    first = lax.ppermute(parts[half], ("blk", "inner"), across)
    up = parts[half - 1] + jnp.where(even, first, 0.0)
    down = parts[half + 1] + jnp.where(even, 0.0, first)
    for step in range(half - 1, 0, -1):
        up = lax.ppermute(up, "blk", upward)
        down = lax.ppermute(down, "blk", downward)
        if step > 1:
            up = parts[step - 1] + up
            down = parts[count - step + 1] + down
    return parts[0] + up + down


def swap(value, axis, size, distance):
    return lax.ppermute(value, axis, [(here, here ^ distance) for here in range(size)])


def local(alignment_left, alignment_right, projection_matrix, cotangent):
    rows, features = alignment_left.shape
    depth = alignment_right.shape[0]
    count = lax.axis_size("blk")
    inner = lax.axis_size("inner")
    channels = ENTRY_CHANNELS
    sequences = features // channels
    outer, pairs = projection_matrix.shape
    columns = count * depth
    flops = 2 * rows * columns * outer * pairs * 3

    right = alignment_right.reshape(depth, sequences, channels).transpose(2, 0, 1)
    slots = ring_gather(right, count, inner)

    left = alignment_left.reshape(rows, sequences, channels).transpose(0, 2, 1)
    left = left.reshape(rows * channels, sequences) * (1.0 / sequences)

    wide = jax.ShapeDtypeStruct((rows // 2, outer, 2 * columns), BF16)
    block_shape = jax.ShapeDtypeStruct((channels, depth, sequences), F32)
    grads_high, grads_low = call(
        functools.partial(gradient_kernel, count),
        [wide] * 2,
        [pltpu.VMEM((outer, 3 * pairs), BF16)],
        flops,
    )(projection_matrix, cotangent)
    right_parts = call(
        functools.partial(right_kernel, count),
        [block_shape] * count,
        [pltpu.VMEM((2 * sequences, rows * channels), BF16)],
        flops,
    )(grads_high, grads_low, left)
    right_grad = ring_scatter(right_parts, count, inner)
    grad_right = right_grad.transpose(1, 2, 0).reshape(depth, features)

    size = outer // (count * inner)
    weight_part, outer_high, outer_low = call(
        functools.partial(weight_kernel, count),
        [jax.ShapeDtypeStruct((outer, pairs), F32)] + [wide] * 2,
        [pltpu.VMEM((outer, pairs), F32)],
        2 * flops,
    )(left, cotangent, *slots)
    everyone = ("blk", "inner")
    pieces = lax.all_to_all(weight_part.reshape(count * inner, size, pairs), everyone, 0, 0)
    weight_sum = jnp.sum(pieces, axis=0)
    weight_full = lax.all_gather(weight_sum, everyone, axis=0, tiled=True)
    grad_weight = call(
        place_kernel, jax.ShapeDtypeStruct(projection_matrix.shape, F32), [], 0
    )(weight_full)

    left_parts = call(
        functools.partial(left_kernel, count, inner),
        [jax.ShapeDtypeStruct((sequences // inner, rows * channels), F32)] * inner,
        [
            pltpu.VMEM((rows * channels, sequences), F32),
            pltpu.VMEM((sequences, rows * channels), F32),
        ],
        flops,
    )(grads_high, grads_low, *slots)
    left_sum = left_parts[0]
    for other in range(1, inner):
        left_sum = left_sum + swap(left_parts[other], "inner", inner, other)
    grad_left = left_sum.reshape(sequences // inner, rows, channels).transpose(1, 0, 2)
    grad_left = grad_left.reshape(rows, features // inner)

    pair_update = call(
        functools.partial(pair_kernel, count),
        jax.ShapeDtypeStruct(cotangent.shape, F32),
        [pltpu.VMEM((2 * pairs, outer), BF16), pltpu.VMEM((outer, pairs), F32)],
        flops,
    )(outer_high, outer_low, projection_matrix)
    return (pair_update, grad_left, grad_right, grad_weight)


def solution(mesh):
    placed = (
        P(("groups", "blk"), None),
        P(("groups", "blk", "inner"), None),
        P(),
        P(("groups", "blk"), None, "inner", None),
    )
    return jax.shard_map(
        local,
        mesh=mesh,
        in_specs=placed,
        out_specs=(
            P(("groups", "blk"), None, "inner", None),
            P(("groups", "blk"), "inner"),
            P(("groups", "blk", "inner"), None),
            P("groups", None),
        ),
        check_vma=False,
    )
```

```python
import functools

import jax
import jax.numpy as jnp
from jax import lax
from jax.experimental import pallas as pl
from jax.experimental.pallas import tpu as pltpu
from jax.sharding import PartitionSpec as P

ENTRY_CHANNELS = 32
LANES = 128
F32 = jnp.float32
BF16 = jnp.bfloat16
MIB = 1024 * 1024


def halves(values):
    high = values.astype(BF16)
    low = (values - high.astype(F32)).astype(BF16)
    return high, low


def dot(left, right):
    return jnp.dot(left, right, preferred_element_type=F32)


def dot_rows(left, right):
    return lax.dot_general(left, right, (((1,), (1,)), ((), ())), preferred_element_type=F32)


def fold_of(columns):
    return max(1, LANES // columns)


def strided_rows(ref, first):
    return ref[pl.ds(first, ENTRY_CHANNELS, stride=ENTRY_CHANNELS), :]


def folded_weight(weight_ref, step, fold):
    return jnp.concatenate(
        [strided_rows(weight_ref, step * fold + part) for part in range(fold)], 1
    )


def gradient_kernel(
    by_parity, weight_ref, cotangent_ref, high_ref, low_ref, spread_high, spread_low, weight_cat
):
    channels = ENTRY_CHANNELS
    depth, pairs = cotangent_ref.shape[2:]
    block_count = cotangent_ref.shape[1]
    blocks = list(range(block_count))
    if by_parity:
        parity = lax.rem(lax.axis_index("blk"), 2)
        blocks = [2 * block + parity for block in range(block_count // 2)]
    fold = fold_of(len(blocks) * depth)
    columns = len(blocks) * depth
    for step in range(channels // fold):
        high, low = halves(folded_weight(weight_ref, step, fold))
        weight_cat[step * channels : (step + 1) * channels, :] = jnp.concatenate(
            [high, low, high], 1
        )
    empty = jnp.zeros((columns, pairs), BF16)

    def step_of(pair, carry):
        spread = ([], [])
        for part in range(2):
            rows = jnp.concatenate([cotangent_ref[2 * pair + part, block] for block in blocks], 0)
            for found, values in zip(spread, halves(rows)):
                for place in range(fold):
                    found.append(
                        jnp.concatenate(
                            [values if place == other else empty for other in range(fold)], 1
                        )
                    )
        high, low = (jnp.concatenate(found, 0) for found in spread)
        spread_high[pair] = high
        spread_low[pair] = low
        found = dot_rows(weight_cat[...], jnp.concatenate([high, high, low], 1))
        high, low = halves(found)
        high_ref[pair] = high
        low_ref[pair] = low
        return carry

    lax.fori_loop(0, high_ref.shape[0], step_of, 0)


def rows_of_step(refs, step, lanes):
    start = pl.multiple_of(step * ENTRY_CHANNELS, ENTRY_CHANNELS)
    return jnp.concatenate(
        [
            ref[pair, pl.ds(start, ENTRY_CHANNELS), part * lanes : (part + 1) * lanes]
            for ref in refs
            for pair in range(ref.shape[0])
            for part in range(2)
        ],
        0,
    )


def right_rows(right_ref, step, fold):
    return jnp.concatenate(
        [
            right_ref[block, step * fold + part]
            for part in range(fold)
            for block in range(right_ref.shape[0])
        ],
        0,
    )


def both_left(left_refs):
    sequences = left_refs[0].shape[1]
    return jnp.concatenate([ref[...] for ref in left_refs], 0) * (1.0 / sequences)


def right_kernel(own_high, own_low, peer_high, peer_low, own_left, peer_left, out_ref, left_flip):
    sequences = own_left.shape[1]
    blocks, channels, depth = out_ref.shape[:3]
    lanes = own_high.shape[2] // 2
    fold = lanes // (blocks * depth)
    flip_high, flip_low = halves(both_left([own_left, peer_left]).T)
    left_flip[:sequences, :] = flip_high
    left_flip[sequences:, :] = flip_low

    def step_of(step, carry):
        def stacked(refs):
            return jnp.concatenate(
                [rows_of_step(refs, 2 * step + part, lanes) for part in range(2)], 1
            )

        first = dot(left_flip[...], stacked([own_high, peer_high]))
        second = dot(left_flip[:sequences, :], stacked([own_low, peer_low]))
        found = first[:sequences] + first[sequences:] + second
        for part in range(2):
            turned = found[:, part * lanes : (part + 1) * lanes].T
            for place in range(fold):
                for block in range(blocks):
                    start = (place * blocks + block) * depth
                    y = (2 * step + part) * fold + place
                    out_ref[block, y] = turned[start : start + depth]
        return carry

    lax.fori_loop(0, channels // (2 * fold), step_of, 0)


def weight_kernel(
    own_left,
    peer_left,
    right_ref,
    own_spread_high,
    own_spread_low,
    peer_spread_high,
    peer_spread_low,
    keep_ref,
    send_ref,
    own_high,
    own_low,
    peer_high,
    peer_low,
    total,
):
    channels = ENTRY_CHANNELS
    blocks, _, depth, _ = right_ref.shape
    fold = fold_of(blocks * depth)
    lanes = fold * blocks * depth
    pairs = total.shape[1] // fold
    high, low = halves(both_left([own_left, peer_left]))
    left_cat = jnp.concatenate([high, low, high], 1)

    def outer_step(step, carry):
        right = [right_rows(right_ref, 2 * step + part, fold) for part in range(2)]
        high, low = halves(jnp.concatenate(right, 0))
        found = dot_rows(left_cat, jnp.concatenate([high, high, low], 1))
        high, low = halves(found)
        for part in range(2):
            start = pl.multiple_of((2 * step + part) * channels, channels)
            row = 0
            for high_ref, low_ref in ((own_high, own_low), (peer_high, peer_low)):
                for index in range(2 * high_ref.shape[0]):
                    place = (
                        index // 2,
                        pl.ds(start, channels),
                        slice((index % 2) * lanes, (index % 2 + 1) * lanes),
                    )
                    source = (
                        slice(row, row + channels),
                        slice(part * lanes, (part + 1) * lanes),
                    )
                    high_ref[place] = high[source]
                    low_ref[place] = low[source]
                    row += channels
        return carry

    lax.fori_loop(0, channels // (2 * fold), outer_step, 0)
    total[...] = jnp.zeros_like(total)

    def weight_step(pair, carry):
        found = None
        for high_ref, low_ref, spread_high, spread_low in (
            (own_high, own_low, own_spread_high, own_spread_low),
            (peer_high, peer_low, peer_spread_high, peer_spread_low),
        ):
            left = jnp.concatenate([high_ref[pair], low_ref[pair], high_ref[pair]], 1)
            high = spread_high[pair]
            term = dot(left, jnp.concatenate([high, high, spread_low[pair]], 0))
            found = term if found is None else found + term
        total[...] += found
        return carry

    lax.fori_loop(0, own_high.shape[0], weight_step, 0)
    core = lax.rem(lax.axis_index("inner"), 2)
    steps = channels // (2 * fold)
    for out_ref, half in ((keep_ref, core), (send_ref, 1 - core)):
        for step in range(steps):
            start = pl.multiple_of((half * steps + step) * channels, channels)
            found = total[pl.ds(start, channels), :]
            for part in range(fold):
                y = step * fold + part
                out_ref[y * channels : (y + 1) * channels, :] = found[
                    :, part * pairs : (part + 1) * pairs
                ]


def left_kernel(own_high, own_low, peer_high, peer_low, right_ref, out_ref, total, flipped):
    lanes = own_high.shape[2] // 2
    blocks, channels, depth, sequences = right_ref.shape
    fold = lanes // (blocks * depth)
    group = 4
    total[...] = jnp.zeros_like(total)

    def step_of(step, carry):
        steps = [group * step + part for part in range(group)]
        high, low = halves(jnp.concatenate([right_rows(right_ref, s, fold) for s in steps], 0))
        grads_high = jnp.concatenate(
            [rows_of_step([own_high, peer_high], s, lanes) for s in steps], 1
        )
        grads_low = jnp.concatenate(
            [rows_of_step([own_low, peer_low], s, lanes) for s in steps], 1
        )
        both = dot(grads_high, jnp.concatenate([high, low], 1))
        total[...] += both[:, :sequences] + both[:, sequences:] + dot(grads_low, high)
        return carry

    lax.fori_loop(0, channels // (fold * group), step_of, 0)
    flipped[...] = total[...].T * (1.0 / sequences)
    parity = lax.rem(lax.axis_index("blk"), 2)
    inner, size, width = out_ref.shape[1:]
    for side, start in ((parity, 0), (1 - parity, width)):
        for part in range(inner):
            out_ref[side, part] = flipped[part * size : (part + 1) * size, start : start + width]


def pair_kernel(final, high_ref, low_ref, weight_ref, *refs):
    if final:
        other_ref, out_ref, weight_flip, weight_rows = refs
    else:
        out_ref, weight_flip, weight_rows = refs
    channels = ENTRY_CHANNELS
    depth, pairs = out_ref.shape[2:]
    blocks = out_ref.shape[1] // 2 if final else out_ref.shape[1]
    lanes = high_ref.shape[2] // 2
    columns = blocks * depth
    fold = lanes // columns
    parity = lax.rem(lax.axis_index("blk"), 2)
    for step in range(channels // fold):
        weight_rows[step * channels : (step + 1) * channels, :] = folded_weight(
            weight_ref, step, fold
        )
    flip_high, flip_low = halves(weight_rows[...].T)
    wide = fold * pairs
    weight_flip[:wide, :] = flip_high
    weight_flip[wide:, :] = flip_low

    def step_of(pair, carry):
        first = dot(weight_flip[...], high_ref[pair])
        found = first[:wide] + first[wide:] + dot(weight_flip[:wide, :], low_ref[pair])
        for part in range(2):
            turned = None
            for place in range(fold):
                start = part * lanes
                piece = found[place * pairs : (place + 1) * pairs, start : start + lanes].T
                piece = piece[place * columns : (place + 1) * columns]
                turned = piece if turned is None else turned + piece
            row = 2 * pair + part
            for block in range(blocks):
                where = 2 * block + parity if final else block
                out_ref[row, where] = turned[block * depth : (block + 1) * depth]
                if final:
                    out_ref[row, 2 * block + 1 - parity] = other_ref[row, block]
        return carry

    lax.fori_loop(0, high_ref.shape[0], step_of, 0)


def place_kernel(mine_ref, other_ref, out_ref):
    channels = ENTRY_CHANNELS
    core = lax.rem(lax.axis_index("inner"), 2)
    steps = mine_ref.shape[0] // channels
    for ref, half in ((mine_ref, core), (other_ref, 1 - core)):
        for step in range(steps):
            rows = ref[step * channels : (step + 1) * channels, :]
            out_ref[pl.ds(half * steps + step, channels, stride=channels), :] = rows


def local(alignment_left, alignment_right, projection_matrix, cotangent):
    rows, features = alignment_left.shape
    depth = alignment_right.shape[0]
    count = lax.axis_size("blk")
    inner = lax.axis_size("inner")
    channels = ENTRY_CHANNELS
    sequences = features // channels
    outer, pairs = projection_matrix.shape
    blocks = count // 2
    columns = blocks * depth
    fold = fold_of(columns)
    lanes = fold * columns
    flops = 2 * rows * 2 * columns * outer * pairs * 3
    limit = (8 + 14 * columns * 2 // LANES) * MIB
    everyone = ("blk", "inner")
    parity = lax.rem(lax.axis_index("blk"), 2)

    def call(kernel, out_shape, scratch, cost):
        return pl.pallas_call(
            kernel,
            out_shape=out_shape,
            scratch_shapes=scratch,
            compiler_params=pltpu.CompilerParams(vmem_limit_bytes=limit),
            cost_estimate=pl.CostEstimate(
                flops=int(cost), bytes_accessed=4 * MIB, transcendentals=0
            ),
        )

    def shape(*sizes, kind=F32):
        return jax.ShapeDtypeStruct(sizes, kind)

    partner = [(here, here ^ 1) for here in range(count)]
    same_parity = [[2 * step + side for step in range(blocks)] for side in range(2)]
    row_groups = [
        [(2 * step + side) * inner + part for side in range(2) for part in range(inner)]
        for step in range(blocks)
    ]
    core_groups = [list(range(core, count * inner, 2)) for core in range(2)]
    cores = [(here, here ^ 1) for here in range(inner)]

    right = alignment_right.reshape(depth, sequences, channels).transpose(2, 0, 1)
    right = jnp.broadcast_to(right[None], (blocks,) + right.shape)
    right = lax.all_to_all(right, "blk", 0, 0, axis_index_groups=same_parity)

    left = alignment_left.reshape(rows, sequences, channels).transpose(0, 2, 1)
    left = left.reshape(rows * channels, sequences)
    left_peer = lax.ppermute(left, "blk", partner)
    by_side = cotangent.reshape(rows, blocks, 2, depth, pairs)
    cotangent_peer = lax.ppermute(
        jnp.where(parity == 0, by_side[:, :, 1], by_side[:, :, 0]), "blk", partner
    )

    tall = shape(rows // 2, outer // fold, 2 * lanes, kind=BF16)
    spread = shape(rows // 2, 2 * lanes, fold * pairs, kind=BF16)
    weight_scratch = [pltpu.VMEM((outer // fold, 3 * fold * pairs), BF16)]
    own = call(
        functools.partial(gradient_kernel, True), [tall] * 2 + [spread] * 2, weight_scratch, flops / 2
    )(projection_matrix, cotangent)
    peer = call(
        functools.partial(gradient_kernel, False),
        [tall] * 2 + [spread] * 2,
        weight_scratch,
        flops / 2,
    )(projection_matrix, cotangent_peer)

    right_parts = call(
        right_kernel,
        shape(blocks, channels, depth, sequences),
        [pltpu.VMEM((2 * sequences, 2 * rows * channels), BF16)],
        flops,
    )(*own[:2], *peer[:2], left, left_peer)
    right_parts = lax.all_to_all(right_parts, "blk", 0, 0, axis_index_groups=same_parity)
    grad_right = jnp.sum(right_parts, 0).transpose(1, 2, 0).reshape(depth, features)

    half = shape(outer // 2, pairs)
    keep, send, *outers = call(
        weight_kernel,
        [half] * 2 + [tall] * 4,
        [pltpu.VMEM((outer // fold, fold * pairs), F32)],
        2 * flops,
    )(left, left_peer, right, *own[2:], *peer[2:])
    keep = keep + lax.ppermute(send, "inner", cores)
    members = count * inner // 2
    pieces = keep.reshape(members, outer // 2 // members, pairs)
    pieces = lax.all_to_all(pieces, everyone, 0, 0, axis_index_groups=core_groups)
    piece = jnp.sum(pieces, 0)
    pieces = jnp.broadcast_to(piece[None], (members,) + piece.shape)
    pieces = lax.all_to_all(pieces, everyone, 0, 0, axis_index_groups=core_groups)
    mine = pieces.reshape(outer // 2, pairs)
    other = lax.ppermute(mine, "inner", cores)
    grad_weight = call(place_kernel, shape(outer, pairs), [], 0)(mine, other)

    pair_scratch = [
        pltpu.VMEM((2 * fold * pairs, outer // fold), BF16),
        pltpu.VMEM((outer // fold, fold * pairs), F32),
    ]
    pair_peer = call(
        functools.partial(pair_kernel, False),
        shape(rows, blocks, depth, pairs),
        pair_scratch,
        flops / 2,
    )(*outers[2:], projection_matrix)
    pair_peer = lax.ppermute(pair_peer, "blk", partner)

    left_parts = call(
        left_kernel,
        shape(2, inner, sequences // inner, rows * channels),
        [
            pltpu.VMEM((2 * rows * channels, sequences), F32),
            pltpu.VMEM((sequences, 2 * rows * channels), F32),
        ],
        flops,
    )(*own[:2], *peer[:2], right)
    left_parts = left_parts.reshape(2 * inner, sequences // inner, rows * channels)
    left_parts = lax.all_to_all(left_parts, everyone, 0, 0, axis_index_groups=row_groups)
    grad_left = jnp.sum(left_parts, 0).reshape(sequences // inner, rows, channels)
    grad_left = grad_left.transpose(1, 0, 2).reshape(rows, features // inner)

    pair_update = call(
        functools.partial(pair_kernel, True), shape(*cotangent.shape), pair_scratch, flops / 2
    )(*outers[:2], projection_matrix, pair_peer)
    return (pair_update, grad_left, grad_right, grad_weight)


def solution(mesh):
    placed = (
        P(("groups", "blk"), None),
        P(("groups", "blk", "inner"), None),
        P(),
        P(("groups", "blk"), None, "inner", None),
    )
    return jax.shard_map(
        local,
        mesh=mesh,
        in_specs=placed,
        out_specs=(
            P(("groups", "blk"), None, "inner", None),
            P(("groups", "blk"), "inner"),
            P(("groups", "blk", "inner"), None),
            P("groups", None),
        ),
        check_vma=False,
    )
```

```python
import functools

import jax
import jax.numpy as jnp
from jax import lax
from jax.experimental import pallas as pl
from jax.experimental.pallas import tpu as pltpu
from jax.sharding import PartitionSpec as P

ENTRY_CHANNELS = 32
LANES = 128
PACK = LANES // ENTRY_CHANNELS
F32 = jnp.float32
BF16 = jnp.bfloat16
MIB = 1024 * 1024
VMEM_LIMIT = 60 * MIB


def halves(values):
    high = values.astype(BF16)
    low = (values - high.astype(F32)).astype(BF16)
    return high, low


def dot(left, right):
    return jnp.dot(left, right, preferred_element_type=F32)


def dot_rows(left, right):
    return lax.dot_general(left, right, (((1,), (1,)), ((), ())), preferred_element_type=F32)


def fold_of(columns):
    return max(1, LANES // columns)


def strided(start, size, stride):
    return pl.ds(start, size, stride=stride)


def folded_weight(weight_ref, step, fold):
    channels = ENTRY_CHANNELS
    return jnp.concatenate(
        [weight_ref[strided(step * fold + part, channels, channels), :] for part in range(fold)], 1
    )


def own_slots(blocks):
    here = lax.axis_index("blk")
    return [lax.bitwise_xor(here, 2 * slot) for slot in range(blocks)]


def peer_slots(blocks):
    here = lax.axis_index("blk") // 2
    return [lax.bitwise_xor(here, slot) for slot in range(blocks)]


def spread_of(cotangent_ref, pair, slots, fold):
    columns = len(slots) * cotangent_ref.shape[2]
    empty = jnp.zeros((columns, cotangent_ref.shape[3]), BF16)
    spread = ([], [])
    for part in range(2):
        rows = jnp.concatenate([cotangent_ref[2 * pair + part, slot] for slot in slots], 0)
        for found, values in zip(spread, halves(rows)):
            for place in range(fold):
                found.append(
                    jnp.concatenate(
                        [values if place == other else empty for other in range(fold)], 1
                    )
                )
    return [jnp.concatenate(found, 0) for found in spread]


def turn_in_kernel(rows_minor, in_ref, out_ref, tiles, square):
    channels = ENTRY_CHANNELS
    rows, features = in_ref.shape
    count = features // LANES
    for tile in range(count):
        tiles[tile * rows : (tile + 1) * rows, :] = in_ref[:, tile * LANES : (tile + 1) * LANES]
    for group in range(rows // PACK):
        found = [tiles[strided(group * PACK + k, count, rows), :] for k in range(PACK)]
        for part in range(PACK):
            lanes = slice(part * channels, (part + 1) * channels)
            square[strided(part, count, PACK), :] = jnp.concatenate([v[:, lanes] for v in found], 1)
        turned = square[...].T
        if rows_minor:
            for k in range(PACK):
                out_ref[strided(group * PACK + k, channels, rows), :] = turned[
                    k * channels : (k + 1) * channels
                ]
        else:
            out_ref[group * LANES : (group + 1) * LANES, :] = turned


def turn_out_kernel(parts, *refs):
    part_refs, (out_ref, total, square, tiles) = refs[:parts], refs[parts:]
    channels = ENTRY_CHANNELS
    rows, features = out_ref.shape
    count = features // LANES
    found = part_refs[0][...]
    for ref in part_refs[1:]:
        found = found + ref[...]
    total[...] = found
    for group in range(rows // PACK):
        stacked = [total[strided(group * PACK + k, channels, rows), :] for k in range(PACK)]
        square[...] = jnp.concatenate(stacked, 0).T
        pieces = [square[strided(part, count, PACK), :] for part in range(PACK)]
        for k in range(PACK):
            lanes = slice(k * channels, (k + 1) * channels)
            tiles[strided(group * PACK + k, count, rows), :] = jnp.concatenate(
                [piece[:, lanes] for piece in pieces], 1
            )
    for tile in range(count):
        out_ref[:, tile * LANES : (tile + 1) * LANES] = tiles[tile * rows : (tile + 1) * rows, :]


def left_sum_kernel(parts_ref, out_ref, total, tiles):
    channels = ENTRY_CHANNELS
    parts, size, width = parts_ref.shape
    rows, features = out_ref.shape
    count = features // LANES
    found = parts_ref[0]
    for part in range(1, parts):
        found = found + parts_ref[part]
    for tile in range(width // LANES):
        total[tile * size : (tile + 1) * size, :] = found[:, tile * LANES : (tile + 1) * LANES]
    for tile in range(width // LANES):
        pieces = [total[strided(tile * size + part, count, PACK), :] for part in range(PACK)]
        for k in range(PACK):
            lanes = slice(k * channels, (k + 1) * channels)
            tiles[strided(tile * PACK + k, count, rows), :] = jnp.concatenate(
                [piece[:, lanes] for piece in pieces], 1
            )
    for tile in range(count):
        out_ref[:, tile * LANES : (tile + 1) * LANES] = tiles[tile * rows : (tile + 1) * rows, :]


def gradient_kernel(own, blocks, weight_ref, cotangent_ref, out_ref, weight_cat):
    channels = ENTRY_CHANNELS
    depth, pairs = cotangent_ref.shape[2:]
    fold = fold_of(blocks * depth)

    @pl.when(pl.program_id(0) == 0)
    def prepare():
        for step in range(channels // fold):
            high, low = halves(folded_weight(weight_ref, step, fold))
            weight_cat[step * channels : (step + 1) * channels, :] = jnp.concatenate(
                [high, low, high], 1
            )

    slots = own_slots(blocks) if own else peer_slots(blocks)
    high, low = spread_of(cotangent_ref, 0, slots, fold)
    found = dot_rows(weight_cat[...], jnp.concatenate([high, high, low], 1))
    out_ref[0] = jnp.concatenate(halves(found), 1)


def rows_of_step(refs, step, half, lanes):
    channels = ENTRY_CHANNELS
    start = 2 * half * lanes
    return jnp.concatenate(
        [
            ref[
                pair,
                step * channels : (step + 1) * channels,
                start + part * lanes : start + (part + 1) * lanes,
            ]
            for ref in refs
            for pair in range(ref.shape[0])
            for part in range(2)
        ],
        0,
    )


def both_left(left_refs):
    sequences = left_refs[0].shape[1]
    return jnp.concatenate([ref[...] for ref in left_refs], 0) * (1.0 / sequences)


def right_kernel(fold, depth, own_ref, peer_ref, own_left, peer_left, *refs):
    out_refs, left_flip = refs[:-1], refs[-1]
    blocks = len(out_refs)
    sequences = own_left.shape[1]
    lanes = fold * blocks * depth

    @pl.when(pl.program_id(0) == 0)
    def prepare():
        flip_high, flip_low = halves(both_left([own_left, peer_left]).T)
        left_flip[:sequences, :] = flip_high
        left_flip[sequences:, :] = flip_low

    def stacked(half):
        return jnp.concatenate(
            [rows_of_step([own_ref, peer_ref], part, half, lanes) for part in range(2)], 1
        )

    first = dot(left_flip[...], stacked(0))
    second = dot(left_flip[:sequences, :], stacked(1))
    found = first[:sequences] + first[sequences:] + second
    for part in range(2):
        turned = found[:, part * lanes : (part + 1) * lanes].T
        for place in range(fold):
            for slot in range(blocks):
                start = (place * blocks + slot) * depth
                y = part * fold + place
                out_refs[slot][y * depth : (y + 1) * depth, :] = turned[start : start + depth]


def right_rows(right_refs, step, fold, depth):
    return jnp.concatenate(
        [
            ref[pl.ds(pl.multiple_of((step * fold + part) * depth, depth), depth), :]
            for part in range(fold)
            for ref in right_refs
        ],
        0,
    )


def weight_kernel(blocks, own_left, peer_left, own_cotangent, peer_cotangent, *refs):
    right_refs = refs[:blocks]
    keep_ref, send_ref, own_out, peer_out, own_ref, peer_ref, total, semaphores = refs[blocks:]
    channels = ENTRY_CHANNELS
    depth, pairs = own_cotangent.shape[2:]
    fold = fold_of(blocks * depth)
    lanes = fold * blocks * depth
    high, low = halves(both_left([own_left, peer_left]))
    left_cat = jnp.concatenate([high, low, high], 1)

    def outer_step(step, carry):
        right = [right_rows(right_refs, 2 * step + part, fold, depth) for part in range(2)]
        high, low = halves(jnp.concatenate(right, 0))
        found = dot_rows(left_cat, jnp.concatenate([high, high, low], 1))
        both = halves(found)
        for part in range(2):
            start = pl.multiple_of((2 * step + part) * channels, channels)
            row = 0
            for ref in (own_ref, peer_ref):
                for index in range(2 * ref.shape[0]):
                    for half in range(2):
                        lane = (2 * half + index % 2) * lanes
                        ref[index // 2, pl.ds(start, channels), lane : lane + lanes] = both[half][
                            row : row + channels, part * lanes : (part + 1) * lanes
                        ]
                    row += channels
        return carry

    lax.fori_loop(0, channels // (2 * fold), outer_step, 0)
    copies = [
        pltpu.make_async_copy(own_ref, own_out, semaphores.at[0]),
        pltpu.make_async_copy(peer_ref, peer_out, semaphores.at[1]),
    ]
    for copy in copies:
        copy.start()
    total[...] = jnp.zeros_like(total)

    def weight_step(pair, carry):
        found = None
        for ref, cotangent_ref, slots in (
            (own_ref, own_cotangent, own_slots(blocks)),
            (peer_ref, peer_cotangent, peer_slots(blocks)),
        ):
            high, low = spread_of(cotangent_ref, pair, slots, fold)
            left = ref[pair]
            left = jnp.concatenate([left, left[:, : 2 * lanes]], 1)
            term = dot(left, jnp.concatenate([high, high, low], 0))
            found = term if found is None else found + term
        total[...] += found
        return carry

    lax.fori_loop(0, own_ref.shape[0], weight_step, 0)
    core = lax.rem(lax.axis_index("inner"), 2)
    steps = channels // (2 * fold)
    for out_ref, half in ((keep_ref, core), (send_ref, 1 - core)):
        for step in range(steps):
            start = pl.multiple_of((half * steps + step) * channels, channels)
            found = total[pl.ds(start, channels), :]
            for part in range(fold):
                y = step * fold + part
                out_ref[y * channels : (y + 1) * channels, :] = found[
                    :, part * pairs : (part + 1) * pairs
                ]
    for copy in copies:
        copy.wait()


def left_kernel(blocks, depth, steps, own_ref, peer_ref, *refs):
    right_refs = refs[:blocks]
    out_ref, total, flipped = refs[blocks:]
    lanes = own_ref.shape[2] // 4
    fold = lanes // (blocks * depth)
    sequences = right_refs[0].shape[1]
    at = pl.program_id(0)

    @pl.when(at == 0)
    def prepare():
        total[...] = jnp.zeros_like(total)

    right = [right_rows(right_refs, at * steps + part, fold, depth) for part in range(steps)]
    high, low = halves(jnp.concatenate(right, 0))
    grads = [
        jnp.concatenate(
            [rows_of_step([own_ref, peer_ref], part, half, lanes) for part in range(steps)], 1
        )
        for half in range(2)
    ]
    both = dot(grads[0], jnp.concatenate([high, low], 1))
    total[...] += both[:, :sequences] + both[:, sequences:] + dot(grads[1], high)

    @pl.when(at == pl.num_programs(0) - 1)
    def finish():
        flipped[...] = total[...].T * (1.0 / sequences)
        parity = lax.rem(lax.axis_index("blk"), 2)
        inner, size, width = out_ref.shape[1:]
        for side, start in ((parity, 0), (1 - parity, width)):
            for part in range(inner):
                out_ref[side, part] = flipped[
                    part * size : (part + 1) * size, start : start + width
                ]


def pair_kernel(final, blocks, outer_ref, weight_ref, *refs):
    if final:
        other_ref, out_ref, weight_flip, weight_rows = refs
    else:
        out_ref, weight_flip, weight_rows = refs
    channels = ENTRY_CHANNELS
    depth, pairs = out_ref.shape[2:]
    lanes = outer_ref.shape[2] // 4
    columns = blocks * depth
    fold = lanes // columns
    wide = fold * pairs

    @pl.when(pl.program_id(0) == 0)
    def prepare():
        for step in range(channels // fold):
            weight_rows[step * channels : (step + 1) * channels, :] = folded_weight(
                weight_ref, step, fold
            )
        flip_high, flip_low = halves(weight_rows[...].T)
        weight_flip[:wide, :] = flip_high
        weight_flip[wide:, :] = flip_low

    first = dot(weight_flip[...], outer_ref[0, :, : 2 * lanes])
    second = dot(weight_flip[:wide, :], outer_ref[0, :, 2 * lanes :])
    found = first[:wide] + first[wide:] + second
    slots = own_slots(blocks) if final else peer_slots(blocks)
    for part in range(2):
        turned = []
        for place in range(fold):
            start = part * lanes
            piece = found[place * pairs : (place + 1) * pairs, start : start + lanes].T
            turned.append(piece[place * columns : (place + 1) * columns])
        turned = functools.reduce(jnp.add, turned)
        for slot in range(blocks):
            out_ref[part, slots[slot]] = turned[slot * depth : (slot + 1) * depth]
            if final:
                other = 2 * slot + 1 - lax.rem(lax.axis_index("blk"), 2)
                out_ref[part, other] = other_ref[part, slot]


def spread_sum_kernel(in_ref, out_ref):
    found = in_ref[0]
    for part in range(1, in_ref.shape[0]):
        found = found + in_ref[part]
    for part in range(in_ref.shape[0]):
        out_ref[part] = found


def place_kernel(mine_ref, other_ref, out_ref):
    channels = ENTRY_CHANNELS
    core = lax.rem(lax.axis_index("inner"), 2)
    steps = mine_ref.shape[0] // channels
    for ref, half in ((mine_ref, core), (other_ref, 1 - core)):
        for step in range(steps):
            rows = ref[step * channels : (step + 1) * channels, :]
            out_ref[strided(half * steps + step, channels, channels), :] = rows


def shape(*sizes, kind=F32):
    return jax.ShapeDtypeStruct(sizes, kind)


def call(kernel, out_shape, scratch=(), cost=0, name=None, **grid):
    return pl.pallas_call(
        kernel,
        out_shape=out_shape,
        scratch_shapes=list(scratch),
        compiler_params=pltpu.CompilerParams(vmem_limit_bytes=VMEM_LIMIT),
        cost_estimate=pl.CostEstimate(flops=int(cost), bytes_accessed=2 * MIB, transcendentals=0),
        name=name,
        **grid,
    )


def whole(*sizes):
    return pl.BlockSpec(sizes, lambda step: (0,) * len(sizes))


def along(axis, *sizes):
    return pl.BlockSpec(
        sizes, lambda step: tuple(step if at == axis else 0 for at in range(len(sizes)))
    )


def local(alignment_left, alignment_right, projection_matrix, cotangent):
    rows, features = alignment_left.shape
    depth = alignment_right.shape[0]
    count = lax.axis_size("blk")
    inner = lax.axis_size("inner")
    channels = ENTRY_CHANNELS
    sequences = features // channels
    outer, pairs = projection_matrix.shape
    blocks = count // 2
    fold = fold_of(blocks * depth)
    lanes = fold * blocks * depth
    tall = outer // fold
    steps = channels // fold
    row_pairs = rows // 2
    flops = 2 * rows * 2 * blocks * depth * outer * pairs * 3
    everyone = ("blk", "inner")

    partner = [(here, here ^ 1) for here in range(count)]
    slot_moves = [[(here, here ^ (2 * slot)) for here in range(count)] for slot in range(blocks)]
    cores = [(here, here ^ 1) for here in range(inner)]
    row_groups = [
        [(2 * step + side) * inner + part for side in range(2) for part in range(inner)]
        for step in range(blocks)
    ]
    core_groups = [list(range(core, count * inner, 2)) for core in range(2)]

    def turn(values, rows_minor, name):
        size = values.shape[0]
        return call(
            functools.partial(turn_in_kernel, rows_minor),
            shape(size * channels, sequences),
            [pltpu.VMEM((size * features // LANES, LANES), F32), pltpu.VMEM((LANES, LANES), F32)],
            name=name,
        )(values)

    right = turn(alignment_right, True, "turn_right")
    rights = [right]
    for slot in range(1, blocks):
        rights.append(lax.ppermute(right, "blk", slot_moves[slot]))

    by_side = cotangent.reshape(rows, blocks, 2, depth, pairs)
    parity = lax.rem(lax.axis_index("blk"), 2)
    cotangent_peer = lax.ppermute(
        jnp.where(parity == 0, by_side[:, :, 1], by_side[:, :, 0]), "blk", partner
    )
    left = turn(alignment_left, False, "turn_left")
    left_peer = lax.ppermute(left, "blk", partner)

    def gradient(values, own, name):
        return call(
            functools.partial(gradient_kernel, own, blocks),
            shape(row_pairs, tall, 4 * lanes, kind=BF16),
            [pltpu.VMEM((tall, 3 * fold * pairs), BF16)],
            flops / 2,
            name,
            grid=(row_pairs,),
            in_specs=[whole(outer, pairs), along(0, 2, values.shape[1], depth, pairs)],
            out_specs=along(0, 1, tall, 4 * lanes),
        )(projection_matrix, values)

    grad_own = gradient(cotangent, True, "gradient_own")
    grad_peer = gradient(cotangent_peer, False, "gradient_peer")

    half_steps = steps // 2
    right_parts = call(
        functools.partial(right_kernel, fold, depth),
        [shape(channels * depth, sequences)] * blocks,
        [pltpu.VMEM((2 * sequences, 2 * rows * channels), BF16)],
        flops,
        "right_parts",
        grid=(half_steps,),
        in_specs=[along(1, row_pairs, 2 * channels, 4 * lanes)] * 2
        + [whole(rows * channels, sequences)] * 2,
        out_specs=[along(0, 2 * fold * depth, sequences)] * blocks,
    )(grad_own, grad_peer, left, left_peer)
    right_found = [right_parts[0]]
    for slot in range(1, blocks):
        right_found.append(lax.ppermute(right_parts[slot], "blk", slot_moves[slot]))

    vmem = pl.BlockSpec(memory_space=pltpu.VMEM)
    hbm = pl.BlockSpec(memory_space=pl.ANY)
    factor = shape(row_pairs, tall, 4 * lanes, kind=BF16)
    factor_scratch = pltpu.VMEM(factor.shape, BF16)
    keep, send, outer_own, outer_peer = call(
        functools.partial(weight_kernel, blocks),
        [shape(outer // 2, pairs)] * 2 + [factor] * 2,
        [
            factor_scratch,
            factor_scratch,
            pltpu.VMEM((tall, fold * pairs), F32),
            pltpu.SemaphoreType.DMA((2,)),
        ],
        2 * flops,
        "weight",
        in_specs=[vmem] * (4 + blocks),
        out_specs=[vmem, vmem, hbm, hbm],
    )(left, left_peer, cotangent, cotangent_peer, *rights)
    keep = keep + lax.ppermute(send, "inner", cores)
    members = count * inner // 2
    pieces = keep.reshape(members, outer // 2 // members, pairs)
    pieces = lax.all_to_all(pieces, everyone, 0, 0, axis_index_groups=core_groups)
    pieces = call(spread_sum_kernel, shape(*pieces.shape), name="weight_sum")(pieces)
    pieces = lax.all_to_all(pieces, everyone, 0, 0, axis_index_groups=core_groups)
    mine = pieces.reshape(outer // 2, pairs)
    other = lax.ppermute(mine, "inner", cores)
    grad_weight = call(place_kernel, shape(outer, pairs), name="place")(mine, other)

    def pair(values, others, name):
        final = bool(others)
        width = count if final else blocks
        return call(
            functools.partial(pair_kernel, final, blocks),
            shape(rows, width, depth, pairs),
            [
                pltpu.VMEM((2 * fold * pairs, tall), BF16),
                pltpu.VMEM((tall, fold * pairs), F32),
            ],
            flops / 2,
            name,
            grid=(row_pairs,),
            in_specs=[along(0, 1, tall, 4 * lanes), whole(outer, pairs)]
            + [along(0, 2, blocks, depth, pairs)] * len(others),
            out_specs=along(0, 2, width, depth, pairs),
        )(values, projection_matrix, *others)

    pair_peer = lax.ppermute(pair(outer_peer, [], "pair_peer"), "blk", partner)

    group = 4
    left_parts = call(
        functools.partial(left_kernel, blocks, depth, group),
        shape(2, inner, sequences // inner, rows * channels),
        [
            pltpu.VMEM((2 * rows * channels, sequences), F32),
            pltpu.VMEM((sequences, 2 * rows * channels), F32),
        ],
        flops,
        "left_parts",
        grid=(steps // group,),
        in_specs=[along(1, row_pairs, group * channels, 4 * lanes)] * 2
        + [whole(channels * depth, sequences)] * blocks,
        out_specs=whole(2, inner, sequences // inner, rows * channels),
    )(grad_own, grad_peer, *rights)
    left_parts = left_parts.reshape(2 * inner, sequences // inner, rows * channels)
    left_parts = lax.all_to_all(left_parts, everyone, 0, 0, axis_index_groups=row_groups)
    size = sequences // inner
    grad_left = call(
        left_sum_kernel,
        shape(rows, features // inner),
        [
            pltpu.VMEM((size * rows * channels // LANES, LANES), F32),
            pltpu.VMEM((rows * features // inner // LANES, LANES), F32),
        ],
        name="left_sum",
    )(left_parts)

    grad_right = call(
        functools.partial(turn_out_kernel, blocks),
        shape(depth, features),
        [
            pltpu.VMEM((channels * depth, sequences), F32),
            pltpu.VMEM((LANES, LANES), F32),
            pltpu.VMEM((depth * features // LANES, LANES), F32),
        ],
        name="turn_right_sum",
    )(*right_found)

    pair_update = pair(outer_own, [pair_peer], "pair_own")
    return (pair_update, grad_left, grad_right, grad_weight)


def solution(mesh):
    placed = (
        P(("groups", "blk"), None),
        P(("groups", "blk", "inner"), None),
        P(),
        P(("groups", "blk"), None, "inner", None),
    )
    return jax.shard_map(
        local,
        mesh=mesh,
        in_specs=placed,
        out_specs=(
            P(("groups", "blk"), None, "inner", None),
            P(("groups", "blk"), "inner"),
            P(("groups", "blk", "inner"), None),
            P("groups", None),
        ),
        check_vma=False,
    )
```

```python
import functools

import jax
import jax.numpy as jnp
from jax import lax
from jax.experimental import pallas as pl
from jax.experimental.pallas import tpu as pltpu
from jax.sharding import PartitionSpec as P

ENTRY_CHANNELS = 32
LANES = 128
PACK = LANES // ENTRY_CHANNELS
F32 = jnp.float32
BF16 = jnp.bfloat16
MIB = 1024 * 1024


def halves(values):
    high = values.astype(BF16)
    low = (values - high.astype(F32)).astype(BF16)
    return high, low


def dot(left, right):
    return jnp.dot(left, right, preferred_element_type=F32)


def dot_rows(left, right):
    return lax.dot_general(left, right, (((1,), (1,)), ((), ())), preferred_element_type=F32)


def fold_of(columns):
    return max(1, LANES // columns)


def strided(start, size, stride):
    return pl.ds(start, size, stride=stride)


def folded_weight(weight_ref, step, fold):
    channels = ENTRY_CHANNELS
    return jnp.concatenate(
        [weight_ref[strided(step * fold + part, channels, channels), :] for part in range(fold)], 1
    )


def own_slots(blocks):
    here = lax.axis_index("blk")
    return [lax.bitwise_xor(here, 2 * slot) for slot in range(blocks)]


def peer_slots(blocks):
    here = lax.axis_index("blk") // 2
    return [lax.bitwise_xor(here, slot) for slot in range(blocks)]


def spread_of(cotangent_ref, pair, slots, fold):
    columns = len(slots) * cotangent_ref.shape[2]
    empty = jnp.zeros((columns, cotangent_ref.shape[3]), BF16)
    spread = ([], [])
    for part in range(2):
        rows = jnp.concatenate([cotangent_ref[2 * pair + part, slot] for slot in slots], 0)
        for found, values in zip(spread, halves(rows)):
            for place in range(fold):
                found.append(
                    jnp.concatenate(
                        [values if place == other else empty for other in range(fold)], 1
                    )
                )
    return [jnp.concatenate(found, 0) for found in spread]


def turn_out_kernel(parts, *refs):
    part_refs, (out_ref, total, square, tiles) = refs[:parts], refs[parts:]
    channels = ENTRY_CHANNELS
    rows, features = out_ref.shape
    count = features // LANES
    found = part_refs[0][...]
    for ref in part_refs[1:]:
        found = found + ref[...]
    total[...] = found
    for group in range(rows // PACK):
        stacked = [total[strided(group * PACK + k, channels, rows), :] for k in range(PACK)]
        square[...] = jnp.concatenate(stacked, 0).T
        pieces = [square[strided(part, count, PACK), :] for part in range(PACK)]
        for k in range(PACK):
            lanes = slice(k * channels, (k + 1) * channels)
            tiles[strided(group * PACK + k, count, rows), :] = jnp.concatenate(
                [piece[:, lanes] for piece in pieces], 1
            )
    for tile in range(count):
        out_ref[:, tile * LANES : (tile + 1) * LANES] = tiles[tile * rows : (tile + 1) * rows, :]


def left_sum_kernel(parts_ref, out_ref, total, tiles):
    channels = ENTRY_CHANNELS
    parts, size, width = parts_ref.shape
    rows, features = out_ref.shape
    count = features // LANES
    found = parts_ref[0]
    for part in range(1, parts):
        found = found + parts_ref[part]
    for tile in range(width // LANES):
        total[tile * size : (tile + 1) * size, :] = found[:, tile * LANES : (tile + 1) * LANES]
    for tile in range(width // LANES):
        pieces = [total[strided(tile * size + part, count, PACK), :] for part in range(PACK)]
        for k in range(PACK):
            lanes = slice(k * channels, (k + 1) * channels)
            tiles[strided(tile * PACK + k, count, rows), :] = jnp.concatenate(
                [piece[:, lanes] for piece in pieces], 1
            )
    for tile in range(count):
        out_ref[:, tile * LANES : (tile + 1) * LANES] = tiles[tile * rows : (tile + 1) * rows, :]


def prepare_weight(weight_ref, weight_cat, fold):
    channels = ENTRY_CHANNELS
    for step in range(channels // fold):
        high, low = halves(folded_weight(weight_ref, step, fold))
        weight_cat[step * channels : (step + 1) * channels, :] = jnp.concatenate(
            [high, low, high], 1
        )


def gradient_phase(slots, fold, cotangent_ref, out_ref, weight_cat):
    def step_of(pair, carry):
        high, low = spread_of(cotangent_ref, pair, slots, fold)
        found = dot_rows(weight_cat[...], jnp.concatenate([high, high, low], 1))
        out_ref[pair] = jnp.concatenate(halves(found), 1)
        return carry

    lax.fori_loop(0, out_ref.shape[0], step_of, 0)


def gradient_kernel(blocks, weight_ref, cotangent_ref, out_ref, weight_cat):
    fold = fold_of(blocks * cotangent_ref.shape[2])
    prepare_weight(weight_ref, weight_cat, fold)
    gradient_phase(own_slots(blocks), fold, cotangent_ref, out_ref, weight_cat)


def rows_of_step(refs, step, half, lanes):
    channels = ENTRY_CHANNELS
    rows = pl.ds(pl.multiple_of(step * channels, channels), channels)
    start = 2 * half * lanes
    return jnp.concatenate(
        [
            ref[pair, rows, start + part * lanes : start + (part + 1) * lanes]
            for ref in refs
            for pair in range(ref.shape[0])
            for part in range(2)
        ],
        0,
    )


def both_left(left_refs):
    sequences = left_refs[0].shape[1]
    return jnp.concatenate([ref[...] for ref in left_refs], 0) * (1.0 / sequences)


def right_kernel(
    blocks, weight_ref, cotangent_ref, own_ref, own_left, peer_left, peer_ref, *refs
):
    out_refs, (weight_cat, left_flip) = refs[:blocks], refs[blocks:]
    sequences = own_left.shape[1]
    depth = cotangent_ref.shape[2]
    fold = fold_of(blocks * depth)
    lanes = fold * blocks * depth
    prepare_weight(weight_ref, weight_cat, fold)
    gradient_phase(peer_slots(blocks), fold, cotangent_ref, peer_ref, weight_cat)
    flip_high, flip_low = halves(both_left([own_left, peer_left]).T)
    left_flip[:sequences, :] = flip_high
    left_flip[sequences:, :] = flip_low

    def step_of(step, carry):
        def stacked(half):
            return jnp.concatenate(
                [
                    rows_of_step([own_ref, peer_ref], 2 * step + part, half, lanes)
                    for part in range(2)
                ],
                1,
            )

        first = dot(left_flip[...], stacked(0))
        second = dot(left_flip[:sequences, :], stacked(1))
        found = first[:sequences] + first[sequences:] + second
        for part in range(2):
            turned = found[:, part * lanes : (part + 1) * lanes].T
            for place in range(fold):
                for slot in range(blocks):
                    start = (place * blocks + slot) * depth
                    row = pl.multiple_of(((2 * step + part) * fold + place) * depth, depth)
                    out_refs[slot][pl.ds(row, depth), :] = turned[start : start + depth]
        return carry

    lax.fori_loop(0, ENTRY_CHANNELS // (2 * fold), step_of, 0)


def right_rows(right_refs, step, fold, depth):
    return jnp.concatenate(
        [
            ref[pl.ds(pl.multiple_of((step * fold + part) * depth, depth), depth), :]
            for part in range(fold)
            for ref in right_refs
        ],
        0,
    )


def weight_kernel(blocks, own_left, peer_left, own_cotangent, peer_cotangent, *refs):
    right_refs, refs = refs[:blocks], refs[blocks + 1 :]
    keep_ref, send_ref, own_out, peer_out, own_ref, peer_ref, total, semaphores = refs
    channels = ENTRY_CHANNELS
    depth, pairs = own_cotangent.shape[2:]
    fold = fold_of(blocks * depth)
    lanes = fold * blocks * depth
    high, low = halves(both_left([own_left, peer_left]))
    left_cat = jnp.concatenate([high, low, high], 1)

    def copies(step):
        size = 2 * channels
        rows = pl.ds(pl.multiple_of(step * size, size), size)
        return [
            pltpu.make_async_copy(ref.at[:, rows], out.at[:, rows], semaphores.at[step, side])
            for side, (ref, out) in enumerate(((own_ref, own_out), (peer_ref, peer_out)))
        ]

    def outer_step(step, carry):
        right = [right_rows(right_refs, 2 * step + part, fold, depth) for part in range(2)]
        high, low = halves(jnp.concatenate(right, 0))
        found = dot_rows(left_cat, jnp.concatenate([high, high, low], 1))
        both = halves(found)
        for part in range(2):
            start = pl.multiple_of((2 * step + part) * channels, channels)
            row = 0
            for ref in (own_ref, peer_ref):
                for index in range(2 * ref.shape[0]):
                    for half in range(2):
                        lane = (2 * half + index % 2) * lanes
                        ref[index // 2, pl.ds(start, channels), lane : lane + lanes] = both[half][
                            row : row + channels, part * lanes : (part + 1) * lanes
                        ]
                    row += channels
        for copy in copies(step):
            copy.start()
        return carry

    lax.fori_loop(0, channels // (2 * fold), outer_step, 0)
    total[...] = jnp.zeros_like(total)

    def weight_step(pair, carry):
        found = None
        for ref, cotangent_ref, slots in (
            (own_ref, own_cotangent, own_slots(blocks)),
            (peer_ref, peer_cotangent, peer_slots(blocks)),
        ):
            high, low = spread_of(cotangent_ref, pair, slots, fold)
            left = ref[pair]
            left = jnp.concatenate([left, left[:, : 2 * lanes]], 1)
            term = dot(left, jnp.concatenate([high, high, low], 0))
            found = term if found is None else found + term
        total[...] += found
        return carry

    lax.fori_loop(0, own_ref.shape[0], weight_step, 0)
    core = lax.rem(lax.axis_index("inner"), 2)
    steps = channels // (2 * fold)
    for out_ref, half in ((keep_ref, core), (send_ref, 1 - core)):
        for step in range(steps):
            start = pl.multiple_of((half * steps + step) * channels, channels)
            found = total[pl.ds(start, channels), :]
            for part in range(fold):
                y = step * fold + part
                out_ref[y * channels : (y + 1) * channels, :] = found[
                    :, part * pairs : (part + 1) * pairs
                ]

    def finish(step, carry):
        for copy in copies(step):
            copy.wait()
        return carry

    lax.fori_loop(0, channels // (2 * fold), finish, 0)


def left_kernel(blocks, depth, own_ref, peer_ref, *refs):
    right_refs = refs[:blocks]
    out_ref, total, flipped = refs[blocks:]
    lanes = own_ref.shape[2] // 4
    fold = lanes // (blocks * depth)
    sequences = right_refs[0].shape[1]
    group = 4
    total[...] = jnp.zeros_like(total)

    def step_of(step, carry):
        steps = [group * step + part for part in range(group)]
        right = [right_rows(right_refs, at, fold, depth) for at in steps]
        high, low = halves(jnp.concatenate(right, 0))
        grads = [
            jnp.concatenate([rows_of_step([own_ref, peer_ref], at, half, lanes) for at in steps], 1)
            for half in range(2)
        ]
        both = dot(grads[0], jnp.concatenate([high, low], 1))
        total[...] += both[:, :sequences] + both[:, sequences:] + dot(grads[1], high)
        return carry

    lax.fori_loop(0, ENTRY_CHANNELS // (fold * group), step_of, 0)
    flipped[...] = total[...].T * (1.0 / sequences)
    parity = lax.rem(lax.axis_index("blk"), 2)
    inner, size, width = out_ref.shape[1:]
    for side, start in ((parity, 0), (1 - parity, width)):
        for part in range(inner):
            out_ref[side, part] = flipped[part * size : (part + 1) * size, start : start + width]


def pair_kernel(final, blocks, outer_hbm, weight_ref, *refs):
    if final:
        other_ref, out_ref, outer_ref, weight_flip, weight_rows, semaphores = refs
    else:
        out_ref, outer_ref, weight_flip, weight_rows, semaphores = refs
    channels = ENTRY_CHANNELS
    depth, pairs = out_ref.shape[2:]
    count = outer_ref.shape[0]
    lanes = outer_ref.shape[2] // 4
    columns = blocks * depth
    fold = lanes // columns
    wide = fold * pairs

    def copy_of(pair):
        return pltpu.make_async_copy(outer_hbm.at[pair], outer_ref.at[pair], semaphores.at[pair])

    for pair in range(count):
        copy_of(pair).start()
    for step in range(channels // fold):
        weight_rows[step * channels : (step + 1) * channels, :] = folded_weight(
            weight_ref, step, fold
        )
    flip_high, flip_low = halves(weight_rows[...].T)
    weight_flip[:wide, :] = flip_high
    weight_flip[wide:, :] = flip_low
    slots = own_slots(blocks) if final else peer_slots(blocks)

    def step_of(pair, carry):
        copy_of(pair).wait()
        first = dot(weight_flip[...], outer_ref[pair, :, : 2 * lanes])
        second = dot(weight_flip[:wide, :], outer_ref[pair, :, 2 * lanes :])
        found = first[:wide] + first[wide:] + second
        for part in range(2):
            turned = []
            for place in range(fold):
                start = part * lanes
                piece = found[place * pairs : (place + 1) * pairs, start : start + lanes].T
                turned.append(piece[place * columns : (place + 1) * columns])
            turned = functools.reduce(jnp.add, turned)
            row = 2 * pair + part
            for slot in range(blocks):
                out_ref[row, slots[slot]] = turned[slot * depth : (slot + 1) * depth]
                if final:
                    other = 2 * slot + 1 - lax.rem(lax.axis_index("blk"), 2)
                    out_ref[row, other] = other_ref[row, slot]
        return carry

    lax.fori_loop(0, count, step_of, 0)


def spread_sum_kernel(in_ref, out_ref):
    found = in_ref[0]
    for part in range(1, in_ref.shape[0]):
        found = found + in_ref[part]
    for part in range(in_ref.shape[0]):
        out_ref[part] = found


def place_kernel(mine_ref, other_ref, out_ref):
    channels = ENTRY_CHANNELS
    core = lax.rem(lax.axis_index("inner"), 2)
    steps = mine_ref.shape[0] // channels
    for ref, half in ((mine_ref, core), (other_ref, 1 - core)):
        for step in range(steps):
            rows = ref[step * channels : (step + 1) * channels, :]
            out_ref[strided(half * steps + step, channels, channels), :] = rows


def shape(*sizes, kind=F32):
    return jax.ShapeDtypeStruct(sizes, kind)


def call(kernel, out_shape, scratch=(), cost=0, name=None, limit=16 * MIB, **specs):
    return pl.pallas_call(
        kernel,
        out_shape=out_shape,
        scratch_shapes=list(scratch),
        compiler_params=pltpu.CompilerParams(vmem_limit_bytes=limit),
        cost_estimate=pl.CostEstimate(flops=int(cost), bytes_accessed=2 * MIB, transcendentals=0),
        name=name,
        **specs,
    )


def local(alignment_left, alignment_right, projection_matrix, cotangent):
    rows, features = alignment_left.shape
    depth = alignment_right.shape[0]
    count = lax.axis_size("blk")
    inner = lax.axis_size("inner")
    channels = ENTRY_CHANNELS
    sequences = features // channels
    outer, pairs = projection_matrix.shape
    blocks = count // 2
    fold = fold_of(blocks * depth)
    lanes = fold * blocks * depth
    tall = outer // fold
    steps = channels // fold
    row_pairs = rows // 2
    flops = 2 * rows * 2 * blocks * depth * outer * pairs * 3
    everyone = ("blk", "inner")

    partner = [(here, here ^ 1) for here in range(count)]
    slot_moves = [[(here, here ^ (2 * slot)) for here in range(count)] for slot in range(blocks)]
    cores = [(here, here ^ 1) for here in range(inner)]
    row_groups = [
        [(2 * step + side) * inner + part for side in range(2) for part in range(inner)]
        for step in range(blocks)
    ]
    core_groups = [list(range(core, count * inner, 2)) for core in range(2)]

    limit = 20 * MIB * max(1, blocks * depth * fold // LANES * 2 // fold)
    large = functools.partial(call, limit=limit)

    right = alignment_right.reshape(depth, sequences, channels).transpose(2, 0, 1)
    right = right.reshape(channels * depth, sequences)
    rights = [right]
    for slot in range(1, blocks):
        rights.append(lax.ppermute(right, "blk", slot_moves[slot]))

    cotangent, alignment_left, _ = lax.optimization_barrier((cotangent, alignment_left, right))
    by_side = cotangent.reshape(rows, blocks, 2, depth, pairs)
    parity = lax.rem(lax.axis_index("blk"), 2)
    cotangent_peer = lax.ppermute(
        jnp.where(parity == 0, by_side[:, :, 1], by_side[:, :, 0]), "blk", partner
    )
    left = alignment_left.reshape(rows, sequences, channels).transpose(0, 2, 1)
    left = left.reshape(rows * channels, sequences)
    left_peer = lax.ppermute(left, "blk", partner)

    factor = shape(row_pairs, tall, 4 * lanes, kind=BF16)
    factor_scratch = pltpu.VMEM(factor.shape, BF16)
    weight_scratch = pltpu.VMEM((tall, 3 * fold * pairs), BF16)
    grad_own = large(
        functools.partial(gradient_kernel, blocks), factor, [weight_scratch], flops, "gradient_own"
    )(projection_matrix, cotangent)
    grad_peer, *right_parts = large(
        functools.partial(right_kernel, blocks),
        [factor] + [shape(channels * depth, sequences)] * blocks,
        [weight_scratch, pltpu.VMEM((2 * sequences, 2 * rows * channels), BF16)],
        2 * flops,
        "right_parts",
    )(projection_matrix, cotangent_peer, grad_own, left, left_peer)

    vmem = pl.BlockSpec(memory_space=pltpu.VMEM)
    hbm = pl.BlockSpec(memory_space=pl.ANY)
    keep, send, outer_own, outer_peer = large(
        functools.partial(weight_kernel, blocks),
        [shape(outer // 2, pairs)] * 2 + [factor] * 2,
        [
            factor_scratch,
            factor_scratch,
            pltpu.VMEM((tall, fold * pairs), F32),
            pltpu.SemaphoreType.DMA((steps // 2, 2)),
        ],
        2 * flops,
        "weight",
        in_specs=[vmem] * (4 + blocks) + [hbm],
        out_specs=[vmem, vmem, hbm, hbm],
    )(left, left_peer, cotangent, cotangent_peer, *rights, right_parts[0])
    sent = lax.ppermute(send, "inner", cores)

    left_parts = large(
        functools.partial(left_kernel, blocks, depth),
        shape(2, inner, sequences // inner, rows * channels),
        [
            pltpu.VMEM((2 * rows * channels, sequences), F32),
            pltpu.VMEM((sequences, 2 * rows * channels), F32),
        ],
        flops,
        "left_parts",
    )(grad_own, grad_peer, *rights)

    keep, left_parts = lax.optimization_barrier((keep, left_parts))
    members = count * inner // 2
    pieces = (keep + sent).reshape(members, outer // 2 // members, pairs)
    pieces, left_parts, outer_own, outer_peer, *right_parts = lax.optimization_barrier(
        (pieces, left_parts, outer_own, outer_peer, *right_parts)
    )
    pieces = lax.all_to_all(pieces, everyone, 0, 0, axis_index_groups=core_groups)
    pieces = call(spread_sum_kernel, shape(*pieces.shape), name="weight_sum")(pieces)
    pieces = lax.all_to_all(pieces, everyone, 0, 0, axis_index_groups=core_groups)
    mine = pieces.reshape(outer // 2, pairs)
    other = lax.ppermute(mine, "inner", cores)
    grad_weight = call(place_kernel, shape(outer, pairs), name="place")(mine, other)

    right_found = [right_parts[0]]
    for slot in range(1, blocks):
        right_found.append(lax.ppermute(right_parts[slot], "blk", slot_moves[slot]))

    def pair(values, others, name):
        final = bool(others)
        return large(
            functools.partial(pair_kernel, final, blocks),
            shape(rows, count if final else blocks, depth, pairs),
            [
                factor_scratch,
                pltpu.VMEM((2 * fold * pairs, tall), BF16),
                pltpu.VMEM((tall, fold * pairs), F32),
                pltpu.SemaphoreType.DMA((row_pairs,)),
            ],
            flops,
            name,
            in_specs=[hbm] + [vmem] * (1 + len(others)),
        )(values, projection_matrix, *others)

    pair_peer = lax.ppermute(pair(outer_peer, [], "pair_peer"), "blk", partner)

    left_parts = left_parts.reshape(2 * inner, sequences // inner, rows * channels)
    left_parts = lax.all_to_all(left_parts, everyone, 0, 0, axis_index_groups=row_groups)
    size = sequences // inner
    grad_left = call(
        left_sum_kernel,
        shape(rows, features // inner),
        [
            pltpu.VMEM((size * rows * channels // LANES, LANES), F32),
            pltpu.VMEM((rows * features // inner // LANES, LANES), F32),
        ],
        name="left_sum",
    )(left_parts)

    grad_right = call(
        functools.partial(turn_out_kernel, blocks),
        shape(depth, features),
        [
            pltpu.VMEM((channels * depth, sequences), F32),
            pltpu.VMEM((LANES, LANES), F32),
            pltpu.VMEM((depth * features // LANES, LANES), F32),
        ],
        name="turn_right_sum",
    )(*right_found)

    pair_update = pair(outer_own, [pair_peer], "pair_own")
    return (pair_update, grad_left, grad_right, grad_weight)


def solution(mesh):
    placed = (
        P(("groups", "blk"), None),
        P(("groups", "blk", "inner"), None),
        P(),
        P(("groups", "blk"), None, "inner", None),
    )
    return jax.shard_map(
        local,
        mesh=mesh,
        in_specs=placed,
        out_specs=(
            P(("groups", "blk"), None, "inner", None),
            P(("groups", "blk"), "inner"),
            P(("groups", "blk", "inner"), None),
            P("groups", None),
        ),
        check_vma=False,
    )
```

```python
import functools

import jax
import jax.numpy as jnp
from jax import lax
from jax.experimental import pallas as pl
from jax.experimental.pallas import tpu as pltpu
from jax.sharding import PartitionSpec as P

ENTRY_CHANNELS = 32
LANES = 128
PACK = LANES // ENTRY_CHANNELS
F32 = jnp.float32
BF16 = jnp.bfloat16
MIB = 1024 * 1024


def halves(values):
    high = values.astype(BF16)
    low = (values - high.astype(F32)).astype(BF16)
    return high, low


def dot(left, right):
    return jnp.dot(left, right, preferred_element_type=F32)


def dot_rows(left, right):
    return lax.dot_general(left, right, (((1,), (1,)), ((), ())), preferred_element_type=F32)


def fold_of(columns):
    return max(1, LANES // columns)


def strided(start, size, stride):
    return pl.ds(start, size, stride=stride)


def folded_weight(weight_ref, step, fold):
    channels = ENTRY_CHANNELS
    return jnp.concatenate(
        [weight_ref[strided(step * fold + part, channels, channels), :] for part in range(fold)], 1
    )


def own_slots(blocks):
    here = lax.axis_index("blk")
    return [lax.bitwise_xor(here, 2 * slot) for slot in range(blocks)]


def peer_slots(blocks):
    here = lax.axis_index("blk") // 2
    return [lax.bitwise_xor(here, slot) for slot in range(blocks)]


def spread_of(cotangent_ref, pair, slots, fold):
    columns = len(slots) * cotangent_ref.shape[2]
    empty = jnp.zeros((columns, cotangent_ref.shape[3]), BF16)
    spread = ([], [])
    for part in range(2):
        rows = jnp.concatenate([cotangent_ref[2 * pair + part, slot] for slot in slots], 0)
        for found, values in zip(spread, halves(rows)):
            for place in range(fold):
                found.append(
                    jnp.concatenate(
                        [values if place == other else empty for other in range(fold)], 1
                    )
                )
    return [jnp.concatenate(found, 0) for found in spread]


def turn_out_kernel(parts, *refs):
    part_refs, (out_ref, total, square, tiles) = refs[:parts], refs[parts:]
    channels = ENTRY_CHANNELS
    rows, features = out_ref.shape
    count = features // LANES
    found = part_refs[0][...]
    for ref in part_refs[1:]:
        found = found + ref[...]
    total[...] = found
    for group in range(rows // PACK):
        stacked = [total[strided(group * PACK + k, channels, rows), :] for k in range(PACK)]
        square[...] = jnp.concatenate(stacked, 0).T
        pieces = [square[strided(part, count, PACK), :] for part in range(PACK)]
        for k in range(PACK):
            lanes = slice(k * channels, (k + 1) * channels)
            tiles[strided(group * PACK + k, count, rows), :] = jnp.concatenate(
                [piece[:, lanes] for piece in pieces], 1
            )
    for tile in range(count):
        out_ref[:, tile * LANES : (tile + 1) * LANES] = tiles[tile * rows : (tile + 1) * rows, :]


def left_sum_kernel(parts_ref, out_ref, total, tiles):
    channels = ENTRY_CHANNELS
    parts, size, width = parts_ref.shape
    rows, features = out_ref.shape
    count = features // LANES
    found = parts_ref[0]
    for part in range(1, parts):
        found = found + parts_ref[part]
    for tile in range(width // LANES):
        total[tile * size : (tile + 1) * size, :] = found[:, tile * LANES : (tile + 1) * LANES]
    for tile in range(width // LANES):
        pieces = [total[strided(tile * size + part, count, PACK), :] for part in range(PACK)]
        for k in range(PACK):
            lanes = slice(k * channels, (k + 1) * channels)
            tiles[strided(tile * PACK + k, count, rows), :] = jnp.concatenate(
                [piece[:, lanes] for piece in pieces], 1
            )
    for tile in range(count):
        out_ref[:, tile * LANES : (tile + 1) * LANES] = tiles[tile * rows : (tile + 1) * rows, :]


def prepare_weight(weight_ref, weight_cat, fold):
    channels = ENTRY_CHANNELS
    for step in range(channels // fold):
        high, low = halves(folded_weight(weight_ref, step, fold))
        weight_cat[step * channels : (step + 1) * channels, :] = jnp.concatenate(
            [high, low, high], 1
        )


def gradient_phase(slots, fold, cotangent_ref, out_ref, weight_cat):
    def step_of(pair, carry):
        high, low = spread_of(cotangent_ref, pair, slots, fold)
        found = dot_rows(weight_cat[...], jnp.concatenate([high, high, low], 1))
        out_ref[pair] = jnp.concatenate(halves(found), 1)
        return carry

    lax.fori_loop(0, out_ref.shape[0], step_of, 0)


def gradient_kernel(blocks, weight_ref, cotangent_ref, out_ref, weight_cat):
    fold = fold_of(blocks * cotangent_ref.shape[2])
    prepare_weight(weight_ref, weight_cat, fold)
    gradient_phase(own_slots(blocks), fold, cotangent_ref, out_ref, weight_cat)


def rows_of_step(refs, step, half, lanes):
    channels = ENTRY_CHANNELS
    rows = pl.ds(pl.multiple_of(step * channels, channels), channels)
    start = 2 * half * lanes
    return jnp.concatenate(
        [
            ref[pair, rows, start + part * lanes : start + (part + 1) * lanes]
            for ref in refs
            for pair in range(ref.shape[0])
            for part in range(2)
        ],
        0,
    )


def both_left(left_refs):
    sequences = left_refs[0].shape[1]
    return jnp.concatenate([ref[...] for ref in left_refs], 0) * (1.0 / sequences)


def right_kernel(
    blocks, weight_ref, cotangent_ref, own_ref, own_left, peer_left, peer_ref, *refs
):
    out_refs, (weight_cat, left_flip) = refs[:blocks], refs[blocks:]
    sequences = own_left.shape[1]
    depth = cotangent_ref.shape[2]
    fold = fold_of(blocks * depth)
    lanes = fold * blocks * depth
    prepare_weight(weight_ref, weight_cat, fold)
    gradient_phase(peer_slots(blocks), fold, cotangent_ref, peer_ref, weight_cat)
    flip_high, flip_low = halves(both_left([own_left, peer_left]).T)
    left_flip[:sequences, :] = flip_high
    left_flip[sequences:, :] = flip_low

    def step_of(step, carry):
        def stacked(half):
            return jnp.concatenate(
                [
                    rows_of_step([own_ref, peer_ref], 2 * step + part, half, lanes)
                    for part in range(2)
                ],
                1,
            )

        first = dot(left_flip[...], stacked(0))
        second = dot(left_flip[:sequences, :], stacked(1))
        found = first[:sequences] + first[sequences:] + second
        for part in range(2):
            turned = found[:, part * lanes : (part + 1) * lanes].T
            for place in range(fold):
                for slot in range(blocks):
                    start = (place * blocks + slot) * depth
                    row = pl.multiple_of(((2 * step + part) * fold + place) * depth, depth)
                    out_refs[slot][pl.ds(row, depth), :] = turned[start : start + depth]
        return carry

    lax.fori_loop(0, ENTRY_CHANNELS // (2 * fold), step_of, 0)


def right_rows(right_refs, step, fold, depth):
    return jnp.concatenate(
        [
            ref[pl.ds(pl.multiple_of((step * fold + part) * depth, depth), depth), :]
            for part in range(fold)
            for ref in right_refs
        ],
        0,
    )


def weight_kernel(blocks, own_left, peer_left, own_cotangent, peer_cotangent, *refs):
    right_refs = refs[:blocks]
    keep_ref, send_ref, own_out, peer_out, own_ref, peer_ref, total, semaphores = refs[blocks:]
    channels = ENTRY_CHANNELS
    depth, pairs = own_cotangent.shape[2:]
    fold = fold_of(blocks * depth)
    lanes = fold * blocks * depth
    high, low = halves(both_left([own_left, peer_left]))
    left_cat = jnp.concatenate([high, low, high], 1)

    def copies(step):
        size = 2 * channels
        rows = pl.ds(pl.multiple_of(step * size, size), size)
        return [
            pltpu.make_async_copy(ref.at[:, rows], out.at[:, rows], semaphores.at[step, side])
            for side, (ref, out) in enumerate(((own_ref, own_out), (peer_ref, peer_out)))
        ]

    def outer_step(step, carry):
        right = [right_rows(right_refs, 2 * step + part, fold, depth) for part in range(2)]
        high, low = halves(jnp.concatenate(right, 0))
        found = dot_rows(left_cat, jnp.concatenate([high, high, low], 1))
        both = halves(found)
        for part in range(2):
            start = pl.multiple_of((2 * step + part) * channels, channels)
            row = 0
            for ref in (own_ref, peer_ref):
                for index in range(2 * ref.shape[0]):
                    for half in range(2):
                        lane = (2 * half + index % 2) * lanes
                        ref[index // 2, pl.ds(start, channels), lane : lane + lanes] = both[half][
                            row : row + channels, part * lanes : (part + 1) * lanes
                        ]
                    row += channels
        for copy in copies(step):
            copy.start()
        return carry

    lax.fori_loop(0, channels // (2 * fold), outer_step, 0)
    total[...] = jnp.zeros_like(total)

    def weight_step(pair, carry):
        found = None
        for ref, cotangent_ref, slots in (
            (own_ref, own_cotangent, own_slots(blocks)),
            (peer_ref, peer_cotangent, peer_slots(blocks)),
        ):
            high, low = spread_of(cotangent_ref, pair, slots, fold)
            left = ref[pair]
            left = jnp.concatenate([left, left[:, : 2 * lanes]], 1)
            term = dot(left, jnp.concatenate([high, high, low], 0))
            found = term if found is None else found + term
        total[...] += found
        return carry

    lax.fori_loop(0, own_ref.shape[0], weight_step, 0)
    core = lax.rem(lax.axis_index("inner"), 2)
    steps = channels // (2 * fold)
    for out_ref, half in ((keep_ref, core), (send_ref, 1 - core)):
        for step in range(steps):
            start = pl.multiple_of((half * steps + step) * channels, channels)
            found = total[pl.ds(start, channels), :]
            for part in range(fold):
                y = step * fold + part
                out_ref[y * channels : (y + 1) * channels, :] = found[
                    :, part * pairs : (part + 1) * pairs
                ]

    def finish(step, carry):
        for copy in copies(step):
            copy.wait()
        return carry

    lax.fori_loop(0, channels // (2 * fold), finish, 0)


def left_kernel(blocks, depth, own_ref, peer_ref, *refs):
    right_refs = refs[:blocks]
    out_ref, total, flipped = refs[blocks:]
    lanes = own_ref.shape[2] // 4
    fold = lanes // (blocks * depth)
    sequences = right_refs[0].shape[1]
    group = 4
    total[...] = jnp.zeros_like(total)

    def step_of(step, carry):
        steps = [group * step + part for part in range(group)]
        right = [right_rows(right_refs, at, fold, depth) for at in steps]
        high, low = halves(jnp.concatenate(right, 0))
        grads = [
            jnp.concatenate([rows_of_step([own_ref, peer_ref], at, half, lanes) for at in steps], 1)
            for half in range(2)
        ]
        both = dot(grads[0], jnp.concatenate([high, low], 1))
        total[...] += both[:, :sequences] + both[:, sequences:] + dot(grads[1], high)
        return carry

    lax.fori_loop(0, ENTRY_CHANNELS // (fold * group), step_of, 0)
    flipped[...] = total[...].T * (1.0 / sequences)
    parity = lax.rem(lax.axis_index("blk"), 2)
    inner, size, width = out_ref.shape[1:]
    for side, start in ((parity, 0), (1 - parity, width)):
        for part in range(inner):
            out_ref[side, part] = flipped[part * size : (part + 1) * size, start : start + width]


def pair_kernel(final, blocks, outer_hbm, weight_ref, *refs):
    if final:
        other_ref, out_ref, outer_ref, weight_flip, weight_rows, semaphores = refs
    else:
        out_ref, outer_ref, weight_flip, weight_rows, semaphores = refs
    channels = ENTRY_CHANNELS
    depth, pairs = out_ref.shape[2:]
    count = outer_ref.shape[0]
    lanes = outer_ref.shape[2] // 4
    columns = blocks * depth
    fold = lanes // columns
    wide = fold * pairs

    def copy_of(pair):
        return pltpu.make_async_copy(outer_hbm.at[pair], outer_ref.at[pair], semaphores.at[pair])

    for pair in range(count):
        copy_of(pair).start()
    for step in range(channels // fold):
        weight_rows[step * channels : (step + 1) * channels, :] = folded_weight(
            weight_ref, step, fold
        )
    flip_high, flip_low = halves(weight_rows[...].T)
    weight_flip[:wide, :] = flip_high
    weight_flip[wide:, :] = flip_low
    slots = own_slots(blocks) if final else peer_slots(blocks)

    def step_of(pair, carry):
        copy_of(pair).wait()
        first = dot(weight_flip[...], outer_ref[pair, :, : 2 * lanes])
        second = dot(weight_flip[:wide, :], outer_ref[pair, :, 2 * lanes :])
        found = first[:wide] + first[wide:] + second
        for part in range(2):
            turned = []
            for place in range(fold):
                start = part * lanes
                piece = found[place * pairs : (place + 1) * pairs, start : start + lanes].T
                turned.append(piece[place * columns : (place + 1) * columns])
            turned = functools.reduce(jnp.add, turned)
            row = 2 * pair + part
            for slot in range(blocks):
                out_ref[row, slots[slot]] = turned[slot * depth : (slot + 1) * depth]
                if final:
                    other = 2 * slot + 1 - lax.rem(lax.axis_index("blk"), 2)
                    out_ref[row, other] = other_ref[row, slot]
        return carry

    lax.fori_loop(0, count, step_of, 0)


def spread_sum_kernel(in_ref, out_ref):
    found = in_ref[0]
    for part in range(1, in_ref.shape[0]):
        found = found + in_ref[part]
    for part in range(in_ref.shape[0]):
        out_ref[part] = found


def place_kernel(mine_ref, other_ref, out_ref):
    channels = ENTRY_CHANNELS
    core = lax.rem(lax.axis_index("inner"), 2)
    steps = mine_ref.shape[0] // channels
    for ref, half in ((mine_ref, core), (other_ref, 1 - core)):
        for step in range(steps):
            rows = ref[step * channels : (step + 1) * channels, :]
            out_ref[strided(half * steps + step, channels, channels), :] = rows


def shape(*sizes, kind=F32):
    return jax.ShapeDtypeStruct(sizes, kind)


def call(kernel, out_shape, scratch=(), name=None, limit=16 * MIB, far=(), after=(), out_specs=None):
    def run(*operands):
        vmem = pl.BlockSpec(memory_space=pltpu.VMEM)
        hbm = pl.BlockSpec(memory_space=pltpu.HBM)
        in_specs = [pl.BlockSpec(memory_space=pl.ANY)] * len(after)
        in_specs += [hbm if at in far else vmem for at in range(len(operands))]
        operands = [
            pltpu.with_memory_space_constraint(operand, pltpu.HBM) if at in far else operand
            for at, operand in enumerate(operands)
        ]
        extra = {} if out_specs is None else {"out_specs": out_specs}
        return pl.pallas_call(
            lambda *refs: kernel(*refs[len(after) :]),
            out_shape=out_shape,
            in_specs=in_specs,
            scratch_shapes=list(scratch),
            compiler_params=pltpu.CompilerParams(vmem_limit_bytes=limit),
            cost_estimate=pl.CostEstimate(flops=1, bytes_accessed=1, transcendentals=0),
            name=name,
            **extra,
        )(*after, *operands)

    return run


def local(alignment_left, alignment_right, projection_matrix, cotangent):
    rows, features = alignment_left.shape
    depth = alignment_right.shape[0]
    count = lax.axis_size("blk")
    inner = lax.axis_size("inner")
    channels = ENTRY_CHANNELS
    sequences = features // channels
    outer, pairs = projection_matrix.shape
    blocks = count // 2
    fold = fold_of(blocks * depth)
    lanes = fold * blocks * depth
    tall = outer // fold
    steps = channels // fold
    row_pairs = rows // 2
    everyone = ("blk", "inner")

    partner = [(here, here ^ 1) for here in range(count)]
    slot_moves = [[(here, here ^ (2 * slot)) for here in range(count)] for slot in range(blocks)]
    cores = [(here, here ^ 1) for here in range(inner)]
    row_groups = [
        [(2 * step + side) * inner + part for side in range(2) for part in range(inner)]
        for step in range(blocks)
    ]
    core_groups = [list(range(core, count * inner, 2)) for core in range(2)]

    limit = 20 * MIB * max(1, blocks * depth * fold // LANES * 2 // fold)
    large = functools.partial(call, limit=limit)

    right = alignment_right.reshape(depth, sequences, channels).transpose(2, 0, 1)
    right = right.reshape(channels * depth, sequences)
    rights = [right]
    for slot in range(1, blocks):
        rights.append(lax.ppermute(right, "blk", slot_moves[slot]))

    cotangent, _ = lax.optimization_barrier((cotangent, right))
    by_side = cotangent.reshape(rows, blocks, 2, depth, pairs)
    parity = lax.rem(lax.axis_index("blk"), 2)
    cotangent_peer = lax.ppermute(
        jnp.where(parity == 0, by_side[:, :, 1], by_side[:, :, 0]), "blk", partner
    )
    left = alignment_left.reshape(rows, sequences, channels).transpose(0, 2, 1)
    left = left.reshape(rows * channels, sequences)
    left_peer = lax.ppermute(left, "blk", partner)

    factor = shape(row_pairs, tall, 4 * lanes, kind=BF16)
    factor_scratch = pltpu.VMEM(factor.shape, BF16)
    weight_scratch = pltpu.VMEM((tall, 3 * fold * pairs), BF16)
    grad_own = large(
        functools.partial(gradient_kernel, blocks), factor, [weight_scratch], "gradient_own"
    )(projection_matrix, cotangent)
    grad_peer, *right_parts = large(
        functools.partial(right_kernel, blocks),
        [factor] + [shape(channels * depth, sequences)] * blocks,
        [weight_scratch, pltpu.VMEM((2 * sequences, 2 * rows * channels), BF16)],
        "right_parts",
    )(projection_matrix, cotangent_peer, grad_own, left, left_peer)
    right_found = [right_parts[0]]
    for slot in range(1, blocks):
        right_found.append(lax.ppermute(right_parts[slot], "blk", slot_moves[slot]))

    vmem = pl.BlockSpec(memory_space=pltpu.VMEM)
    hbm = pl.BlockSpec(memory_space=pltpu.HBM)
    keep, send, outer_own, outer_peer = large(
        functools.partial(weight_kernel, blocks),
        [shape(outer // 2, pairs)] * 2 + [pltpu.HBM(factor.shape, BF16)] * 2,
        [
            factor_scratch,
            factor_scratch,
            pltpu.VMEM((tall, fold * pairs), F32),
            pltpu.SemaphoreType.DMA((steps // 2, 2)),
        ],
        "weight",
        after=[right_parts[0]],
        out_specs=[vmem, vmem, hbm, hbm],
    )(left, left_peer, cotangent, cotangent_peer, *rights)
    sent = lax.ppermute(send, "inner", cores)

    left_parts = large(
        functools.partial(left_kernel, blocks, depth),
        shape(2, inner, sequences // inner, rows * channels),
        [
            pltpu.VMEM((2 * rows * channels, sequences), F32),
            pltpu.VMEM((sequences, 2 * rows * channels), F32),
        ],
        "left_parts",
        after=[keep],
    )(grad_own, grad_peer, *rights)

    members = count * inner // 2
    keep, left_parts = lax.optimization_barrier((keep, left_parts))
    pieces = (keep + sent).reshape(members, outer // 2 // members, pairs)
    pieces, left_parts = lax.optimization_barrier((pieces, left_parts))

    def pair(values, others, after, name):
        final = bool(others)
        return large(
            functools.partial(pair_kernel, final, blocks),
            shape(rows, count if final else blocks, depth, pairs),
            [
                factor_scratch,
                pltpu.VMEM((2 * fold * pairs, tall), BF16),
                pltpu.VMEM((tall, fold * pairs), F32),
                pltpu.SemaphoreType.DMA((row_pairs,)),
            ],
            name,
            far=[0],
            after=after,
        )(values, projection_matrix, *others)

    pair_own_rows = pair(outer_peer, [], [pieces, *right_found[1:]], "pair_peer")
    pair_peer = lax.ppermute(pair_own_rows, "blk", partner)

    pieces = lax.all_to_all(pieces, everyone, 0, 0, axis_index_groups=core_groups)
    pieces = call(
        spread_sum_kernel, shape(*pieces.shape), name="weight_sum", after=[pair_own_rows]
    )(pieces)
    pieces = lax.all_to_all(pieces, everyone, 0, 0, axis_index_groups=core_groups)

    left_parts = left_parts.reshape(2 * inner, sequences // inner, rows * channels)
    left_parts = lax.all_to_all(left_parts, everyone, 0, 0, axis_index_groups=row_groups)
    size = sequences // inner
    grad_left = call(
        left_sum_kernel,
        shape(rows, features // inner),
        [
            pltpu.VMEM((size * rows * channels // LANES, LANES), F32),
            pltpu.VMEM((rows * features // inner // LANES, LANES), F32),
        ],
        name="left_sum",
    )(left_parts)

    grad_right = call(
        functools.partial(turn_out_kernel, blocks),
        shape(depth, features),
        [
            pltpu.VMEM((channels * depth, sequences), F32),
            pltpu.VMEM((LANES, LANES), F32),
            pltpu.VMEM((depth * features // LANES, LANES), F32),
        ],
        name="turn_right_sum",
    )(*right_found)

    pair_update = pair(outer_own, [pair_peer], [], "pair_own")

    pieces, pair_update, grad_left, grad_right = lax.optimization_barrier(
        (pieces, pair_update, grad_left, grad_right)
    )
    mine = pieces.reshape(outer // 2, pairs)
    other = lax.ppermute(mine, "inner", cores)
    grad_weight = call(place_kernel, shape(outer, pairs), name="place")(mine, other)
    return (pair_update, grad_left, grad_right, grad_weight)


def solution(mesh):
    placed = (
        P(("groups", "blk"), None),
        P(("groups", "blk", "inner"), None),
        P(),
        P(("groups", "blk"), None, "inner", None),
    )
    return jax.shard_map(
        local,
        mesh=mesh,
        in_specs=placed,
        out_specs=(
            P(("groups", "blk"), None, "inner", None),
            P(("groups", "blk"), "inner"),
            P(("groups", "blk", "inner"), None),
            P("groups", None),
        ),
        check_vma=False,
    )
```

```python
import functools

import jax
import jax.numpy as jnp
from jax import lax
from jax.experimental import pallas as pl
from jax.experimental.pallas import tpu as pltpu
from jax.sharding import PartitionSpec as P

ENTRY_CHANNELS = 32
LANES = 128
PACK = LANES // ENTRY_CHANNELS
F32 = jnp.float32
BF16 = jnp.bfloat16
MIB = 1024 * 1024


def halves(values):
    high = values.astype(BF16)
    low = (values - high.astype(F32)).astype(BF16)
    return high, low


def dot(left, right):
    return jnp.dot(left, right, preferred_element_type=F32)


def dot_rows(left, right):
    return lax.dot_general(left, right, (((1,), (1,)), ((), ())), preferred_element_type=F32)


def fold_of(columns):
    return max(1, LANES // columns)


def strided(start, size, stride):
    return pl.ds(start, size, stride=stride)


def folded_weight(weight_ref, step, fold):
    channels = ENTRY_CHANNELS
    return jnp.concatenate(
        [weight_ref[strided(step * fold + part, channels, channels), :] for part in range(fold)], 1
    )


def own_slots(blocks):
    parity = lax.rem(lax.axis_index("blk"), 2)
    return [2 * block + parity for block in range(blocks)]


def peer_slots(blocks):
    return list(range(blocks))


def spread_of(cotangent_ref, pair, slots, fold):
    columns = len(slots) * cotangent_ref.shape[2]
    empty = jnp.zeros((columns, cotangent_ref.shape[3]), BF16)
    spread = ([], [])
    for part in range(2):
        rows = jnp.concatenate([cotangent_ref[2 * pair + part, slot] for slot in slots], 0)
        for found, values in zip(spread, halves(rows)):
            for place in range(fold):
                found.append(
                    jnp.concatenate(
                        [values if place == other else empty for other in range(fold)], 1
                    )
                )
    return [jnp.concatenate(found, 0) for found in spread]


def turn_out_kernel(in_ref, out_ref, square, tiles):
    channels = ENTRY_CHANNELS
    rows, features = out_ref.shape
    count = features // LANES
    for group in range(rows // PACK):
        stacked = [in_ref[strided(group * PACK + k, channels, rows), :] for k in range(PACK)]
        square[...] = jnp.concatenate(stacked, 0).T
        pieces = [square[strided(part, count, PACK), :] for part in range(PACK)]
        for k in range(PACK):
            lanes = slice(k * channels, (k + 1) * channels)
            tiles[strided(group * PACK + k, count, rows), :] = jnp.concatenate(
                [piece[:, lanes] for piece in pieces], 1
            )
    for tile in range(count):
        out_ref[:, tile * LANES : (tile + 1) * LANES] = tiles[tile * rows : (tile + 1) * rows, :]


def turn_left_kernel(in_ref, out_ref, total, tiles):
    channels = ENTRY_CHANNELS
    size, width = in_ref.shape
    rows, features = out_ref.shape
    count = features // LANES
    found = in_ref[...]
    for tile in range(width // LANES):
        total[tile * size : (tile + 1) * size, :] = found[:, tile * LANES : (tile + 1) * LANES]
    for tile in range(width // LANES):
        pieces = [total[strided(tile * size + part, count, PACK), :] for part in range(PACK)]
        for k in range(PACK):
            lanes = slice(k * channels, (k + 1) * channels)
            tiles[strided(tile * PACK + k, count, rows), :] = jnp.concatenate(
                [piece[:, lanes] for piece in pieces], 1
            )
    for tile in range(count):
        out_ref[:, tile * LANES : (tile + 1) * LANES] = tiles[tile * rows : (tile + 1) * rows, :]


def prepare_weight(weight_ref, weight_cat, fold):
    channels = ENTRY_CHANNELS
    for step in range(channels // fold):
        high, low = halves(folded_weight(weight_ref, step, fold))
        weight_cat[step * channels : (step + 1) * channels, :] = jnp.concatenate(
            [high, low, high], 1
        )


def gradient_phase(slots, fold, cotangent_ref, out_ref, weight_cat):
    def step_of(pair, carry):
        high, low = spread_of(cotangent_ref, pair, slots, fold)
        found = dot_rows(weight_cat[...], jnp.concatenate([high, high, low], 1))
        out_ref[pair] = jnp.concatenate(halves(found), 1)
        return carry

    lax.fori_loop(0, out_ref.shape[0], step_of, 0)


def gradient_kernel(blocks, weight_ref, cotangent_ref, out_ref, weight_cat):
    fold = fold_of(blocks * cotangent_ref.shape[2])
    prepare_weight(weight_ref, weight_cat, fold)
    gradient_phase(own_slots(blocks), fold, cotangent_ref, out_ref, weight_cat)


def rows_of_step(refs, step, half, lanes):
    channels = ENTRY_CHANNELS
    rows = pl.ds(pl.multiple_of(step * channels, channels), channels)
    start = 2 * half * lanes
    return jnp.concatenate(
        [
            ref[pair, rows, start + part * lanes : start + (part + 1) * lanes]
            for ref in refs
            for pair in range(ref.shape[0])
            for part in range(2)
        ],
        0,
    )


def both_left(left_refs):
    sequences = left_refs[0].shape[1]
    return jnp.concatenate([ref[...] for ref in left_refs], 0) * (1.0 / sequences)


def right_kernel(
    blocks, weight_ref, cotangent_ref, own_ref, own_left, peer_left, peer_ref, *refs
):
    out_ref, weight_cat, left_flip = refs
    sequences = own_left.shape[1]
    depth = cotangent_ref.shape[2]
    fold = fold_of(blocks * depth)
    lanes = fold * blocks * depth
    prepare_weight(weight_ref, weight_cat, fold)
    gradient_phase(peer_slots(blocks), fold, cotangent_ref, peer_ref, weight_cat)
    flip_high, flip_low = halves(both_left([own_left, peer_left]).T)
    left_flip[:sequences, :] = flip_high
    left_flip[sequences:, :] = flip_low

    def step_of(step, carry):
        def stacked(half):
            return jnp.concatenate(
                [
                    rows_of_step([own_ref, peer_ref], 2 * step + part, half, lanes)
                    for part in range(2)
                ],
                1,
            )

        first = dot(left_flip[...], stacked(0))
        second = dot(left_flip[:sequences, :], stacked(1))
        found = first[:sequences] + first[sequences:] + second
        for part in range(2):
            turned = found[:, part * lanes : (part + 1) * lanes].T
            for place in range(fold):
                for slot in range(blocks):
                    start = (place * blocks + slot) * depth
                    row = pl.multiple_of(((2 * step + part) * fold + place) * depth, depth)
                    out_ref[slot, pl.ds(row, depth), :] = turned[start : start + depth]
        return carry

    lax.fori_loop(0, ENTRY_CHANNELS // (2 * fold), step_of, 0)


def right_rows(right_ref, step, fold, depth):
    return jnp.concatenate(
        [
            right_ref[block, pl.ds(pl.multiple_of((step * fold + part) * depth, depth), depth), :]
            for part in range(fold)
            for block in range(right_ref.shape[0])
        ],
        0,
    )


def weight_kernel(blocks, own_left, peer_left, own_cotangent, peer_cotangent, *refs):
    right_ref, keep_ref, send_ref, own_out, peer_out, own_ref, peer_ref, total, semaphores = refs
    channels = ENTRY_CHANNELS
    depth, pairs = own_cotangent.shape[2:]
    fold = fold_of(blocks * depth)
    lanes = fold * blocks * depth
    high, low = halves(both_left([own_left, peer_left]))
    left_cat = jnp.concatenate([high, low, high], 1)

    def copies(step):
        size = 2 * channels
        rows = pl.ds(pl.multiple_of(step * size, size), size)
        return [
            pltpu.make_async_copy(ref.at[:, rows], out.at[:, rows], semaphores.at[step, side])
            for side, (ref, out) in enumerate(((own_ref, own_out), (peer_ref, peer_out)))
        ]

    def outer_step(step, carry):
        right = [right_rows(right_ref, 2 * step + part, fold, depth) for part in range(2)]
        high, low = halves(jnp.concatenate(right, 0))
        found = dot_rows(left_cat, jnp.concatenate([high, high, low], 1))
        both = halves(found)
        for part in range(2):
            start = pl.multiple_of((2 * step + part) * channels, channels)
            row = 0
            for ref in (own_ref, peer_ref):
                for index in range(2 * ref.shape[0]):
                    for half in range(2):
                        lane = (2 * half + index % 2) * lanes
                        ref[index // 2, pl.ds(start, channels), lane : lane + lanes] = both[half][
                            row : row + channels, part * lanes : (part + 1) * lanes
                        ]
                    row += channels
        for copy in copies(step):
            copy.start()
        return carry

    lax.fori_loop(0, channels // (2 * fold), outer_step, 0)
    total[...] = jnp.zeros_like(total)

    def weight_step(pair, carry):
        found = None
        for ref, cotangent_ref, slots in (
            (own_ref, own_cotangent, own_slots(blocks)),
            (peer_ref, peer_cotangent, peer_slots(blocks)),
        ):
            high, low = spread_of(cotangent_ref, pair, slots, fold)
            left = ref[pair]
            left = jnp.concatenate([left, left[:, : 2 * lanes]], 1)
            term = dot(left, jnp.concatenate([high, high, low], 0))
            found = term if found is None else found + term
        total[...] += found
        return carry

    lax.fori_loop(0, own_ref.shape[0], weight_step, 0)
    core = lax.rem(lax.axis_index("inner"), 2)
    steps = channels // (2 * fold)
    for out_ref, half in ((keep_ref, core), (send_ref, 1 - core)):
        for step in range(steps):
            start = pl.multiple_of((half * steps + step) * channels, channels)
            found = total[pl.ds(start, channels), :]
            for part in range(fold):
                y = step * fold + part
                out_ref[y * channels : (y + 1) * channels, :] = found[
                    :, part * pairs : (part + 1) * pairs
                ]

    def finish(step, carry):
        for copy in copies(step):
            copy.wait()
        return carry

    lax.fori_loop(0, channels // (2 * fold), finish, 0)


def left_kernel(own_ref, peer_ref, right_ref, own_out, peer_out, total):
    blocks, rows, sequences = right_ref.shape
    lanes = own_ref.shape[2] // 4
    depth = rows // ENTRY_CHANNELS
    fold = lanes // (blocks * depth)
    group = 4
    total[...] = jnp.zeros_like(total)

    def step_of(step, carry):
        steps = [group * step + part for part in range(group)]
        right = [right_rows(right_ref, at, fold, depth) for at in steps]
        high, low = halves(jnp.concatenate(right, 0))
        grads = [
            jnp.concatenate([rows_of_step([own_ref, peer_ref], at, half, lanes) for at in steps], 1)
            for half in range(2)
        ]
        both = dot(grads[0], jnp.concatenate([high, low], 1))
        total[...] += both[:, :sequences] + both[:, sequences:] + dot(grads[1], high)
        return carry

    lax.fori_loop(0, ENTRY_CHANNELS // (fold * group), step_of, 0)
    flipped = total[...].T * (1.0 / sequences)
    width = own_out.shape[1]
    own_out[...] = flipped[:, :width]
    peer_out[...] = flipped[:, width:]


def pair_kernel(final, blocks, outer_hbm, weight_ref, *refs):
    if final:
        other_ref, out_ref, outer_ref, weight_flip, weight_rows, semaphores = refs
    else:
        out_ref, outer_ref, weight_flip, weight_rows, semaphores = refs
    channels = ENTRY_CHANNELS
    depth, pairs = out_ref.shape[2:]
    count = outer_ref.shape[0]
    lanes = outer_ref.shape[2] // 4
    columns = blocks * depth
    fold = lanes // columns
    wide = fold * pairs

    def copy_of(pair):
        return pltpu.make_async_copy(outer_hbm.at[pair], outer_ref.at[pair], semaphores.at[pair])

    for pair in range(count):
        copy_of(pair).start()
    for step in range(channels // fold):
        weight_rows[step * channels : (step + 1) * channels, :] = folded_weight(
            weight_ref, step, fold
        )
    flip_high, flip_low = halves(weight_rows[...].T)
    weight_flip[:wide, :] = flip_high
    weight_flip[wide:, :] = flip_low
    slots = own_slots(blocks) if final else peer_slots(blocks)

    def step_of(pair, carry):
        copy_of(pair).wait()
        first = dot(weight_flip[...], outer_ref[pair, :, : 2 * lanes])
        second = dot(weight_flip[:wide, :], outer_ref[pair, :, 2 * lanes :])
        found = first[:wide] + first[wide:] + second
        for part in range(2):
            turned = []
            for place in range(fold):
                start = part * lanes
                piece = found[place * pairs : (place + 1) * pairs, start : start + lanes].T
                turned.append(piece[place * columns : (place + 1) * columns])
            turned = functools.reduce(jnp.add, turned)
            row = 2 * pair + part
            for slot in range(blocks):
                out_ref[row, slots[slot]] = turned[slot * depth : (slot + 1) * depth]
                if final:
                    other = 2 * slot + 1 - lax.rem(lax.axis_index("blk"), 2)
                    out_ref[row, other] = other_ref[row, slot]
        return carry

    lax.fori_loop(0, count, step_of, 0)


def spread_sum_kernel(in_ref, out_ref):
    found = in_ref[0]
    for part in range(1, in_ref.shape[0]):
        found = found + in_ref[part]
    for part in range(in_ref.shape[0]):
        out_ref[part] = found


def place_kernel(mine_ref, other_ref, out_ref):
    channels = ENTRY_CHANNELS
    core = lax.rem(lax.axis_index("inner"), 2)
    steps = mine_ref.shape[0] // channels
    for ref, half in ((mine_ref, core), (other_ref, 1 - core)):
        for step in range(steps):
            rows = ref[step * channels : (step + 1) * channels, :]
            out_ref[strided(half * steps + step, channels, channels), :] = rows


def shape(*sizes, kind=F32):
    return jax.ShapeDtypeStruct(sizes, kind)


def call(kernel, out_shape, scratch=(), name=None, limit=16 * MIB, far=(), after=(), out_specs=None):
    def run(*operands):
        vmem = pl.BlockSpec(memory_space=pltpu.VMEM)
        hbm = pl.BlockSpec(memory_space=pltpu.HBM)
        in_specs = [pl.BlockSpec(memory_space=pl.ANY)] * len(after)
        in_specs += [hbm if at in far else vmem for at in range(len(operands))]
        operands = [
            pltpu.with_memory_space_constraint(operand, pltpu.HBM) if at in far else operand
            for at, operand in enumerate(operands)
        ]
        extra = {} if out_specs is None else {"out_specs": out_specs}
        return pl.pallas_call(
            lambda *refs: kernel(*refs[len(after) :]),
            out_shape=out_shape,
            in_specs=in_specs,
            scratch_shapes=list(scratch),
            compiler_params=pltpu.CompilerParams(vmem_limit_bytes=limit),
            cost_estimate=pl.CostEstimate(flops=1, bytes_accessed=1, transcendentals=0),
            name=name,
            **extra,
        )(*after, *operands)

    return run


def local(alignment_left, alignment_right, projection_matrix, cotangent):
    rows, features = alignment_left.shape
    depth = alignment_right.shape[0]
    count = lax.axis_size("blk")
    inner = lax.axis_size("inner")
    channels = ENTRY_CHANNELS
    sequences = features // channels
    outer, pairs = projection_matrix.shape
    blocks = count // 2
    fold = fold_of(blocks * depth)
    lanes = fold * blocks * depth
    tall = outer // fold
    steps = channels // fold
    row_pairs = rows // 2
    everyone = ("blk", "inner")

    partner = [(here, here ^ 1) for here in range(count)]
    same_parity = [[2 * block + side for block in range(blocks)] for side in range(2)]
    cores = [(here, here ^ 1) for here in range(inner)]
    core_groups = [list(range(core, count * inner, 2)) for core in range(2)]

    limit = 20 * MIB * max(1, blocks * depth * fold // LANES * 2 // fold)
    large = functools.partial(call, limit=limit)

    right = alignment_right.reshape(depth, sequences, channels).transpose(2, 0, 1)
    right = right.reshape(channels * depth, sequences)
    right = lax.all_gather(right, "blk", axis_index_groups=same_parity)

    by_side = cotangent.reshape(rows, blocks, 2, depth, pairs)
    parity = lax.rem(lax.axis_index("blk"), 2)
    cotangent_peer = lax.ppermute(
        jnp.where(parity == 0, by_side[:, :, 1], by_side[:, :, 0]), "blk", partner
    )
    left = alignment_left.reshape(rows, sequences, channels).transpose(0, 2, 1)
    left = left.reshape(rows * channels, sequences)
    left_peer = lax.ppermute(left, "blk", partner)

    factor = shape(row_pairs, tall, 4 * lanes, kind=BF16)
    factor_scratch = pltpu.VMEM(factor.shape, BF16)
    weight_scratch = pltpu.VMEM((tall, 3 * fold * pairs), BF16)
    grad_own = large(
        functools.partial(gradient_kernel, blocks), factor, [weight_scratch], "gradient_own"
    )(projection_matrix, cotangent)
    grad_peer, right_parts = large(
        functools.partial(right_kernel, blocks),
        [factor, shape(blocks, channels * depth, sequences)],
        [weight_scratch, pltpu.VMEM((2 * sequences, 2 * rows * channels), BF16)],
        "right_parts",
    )(projection_matrix, cotangent_peer, grad_own, left, left_peer)
    right_sum = lax.psum_scatter(
        right_parts, "blk", scatter_dimension=0, axis_index_groups=same_parity
    )

    vmem = pl.BlockSpec(memory_space=pltpu.VMEM)
    hbm = pl.BlockSpec(memory_space=pltpu.HBM)
    keep, send, outer_own, outer_peer = large(
        functools.partial(weight_kernel, blocks),
        [shape(outer // 2, pairs)] * 2 + [pltpu.HBM(factor.shape, BF16)] * 2,
        [
            factor_scratch,
            factor_scratch,
            pltpu.VMEM((tall, fold * pairs), F32),
            pltpu.SemaphoreType.DMA((steps // 2, 2)),
        ],
        "weight",
        after=[right_parts],
        out_specs=[vmem, vmem, hbm, hbm],
    )(left, left_peer, cotangent, cotangent_peer, right)
    sent = lax.ppermute(send, "inner", cores)

    left_own, left_other = large(
        left_kernel,
        [shape(sequences, rows * channels)] * 2,
        [pltpu.VMEM((2 * rows * channels, sequences), F32)],
        "left_parts",
        after=[keep],
    )(grad_own, grad_peer, right)
    left_other = lax.ppermute(left_other, "blk", partner)
    keep, left_own = lax.optimization_barrier((keep, left_own))
    members = count * inner // 2
    pieces = (keep + sent).reshape(members, outer // 2 // members, pairs)

    def pair(values, others, after, name):
        final = bool(others)
        return large(
            functools.partial(pair_kernel, final, blocks),
            shape(rows, count if final else blocks, depth, pairs),
            [
                factor_scratch,
                pltpu.VMEM((2 * fold * pairs, tall), BF16),
                pltpu.VMEM((tall, fold * pairs), F32),
                pltpu.SemaphoreType.DMA((row_pairs,)),
            ],
            name,
            far=[0],
            after=after,
        )(values, projection_matrix, *others)

    pair_own_rows = pair(outer_peer, [], [pieces], "pair_peer")
    pair_peer = lax.ppermute(pair_own_rows, "blk", partner)

    pieces = lax.all_to_all(pieces, everyone, 0, 0, axis_index_groups=core_groups)
    pieces = call(
        spread_sum_kernel, shape(*pieces.shape), name="weight_sum", after=[pair_own_rows]
    )(pieces)
    pieces = lax.all_to_all(pieces, everyone, 0, 0, axis_index_groups=core_groups)

    left_sum = lax.psum_scatter(
        left_own + left_other, "inner", scatter_dimension=0, tiled=True
    )
    size = sequences // inner
    grad_left = call(
        turn_left_kernel,
        shape(rows, features // inner),
        [
            pltpu.VMEM((size * rows * channels // LANES, LANES), F32),
            pltpu.VMEM((rows * features // inner // LANES, LANES), F32),
        ],
        name="turn_left",
    )(left_sum)

    grad_right = call(
        turn_out_kernel,
        shape(depth, features),
        [pltpu.VMEM((LANES, LANES), F32), pltpu.VMEM((depth * features // LANES, LANES), F32)],
        name="turn_right",
    )(right_sum)

    pair_update = pair(outer_own, [pair_peer], [], "pair_own")

    pieces, pair_update, grad_right = lax.optimization_barrier((pieces, pair_update, grad_right))
    mine = pieces.reshape(outer // 2, pairs)
    other = lax.ppermute(mine, "inner", cores)
    grad_weight = call(place_kernel, shape(outer, pairs), name="place")(mine, other)
    return (pair_update, grad_left, grad_right, grad_weight)


def solution(mesh):
    placed = (
        P(("groups", "blk"), None),
        P(("groups", "blk", "inner"), None),
        P(),
        P(("groups", "blk"), None, "inner", None),
    )
    return jax.shard_map(
        local,
        mesh=mesh,
        in_specs=placed,
        out_specs=(
            P(("groups", "blk"), None, "inner", None),
            P(("groups", "blk"), "inner"),
            P(("groups", "blk", "inner"), None),
            P("groups", None),
        ),
        check_vma=False,
    )
```

```python
import functools

import jax
import jax.numpy as jnp
from jax import lax
from jax.experimental import pallas as pl
from jax.experimental.pallas import tpu as pltpu
from jax.sharding import PartitionSpec as P

ENTRY_CHANNELS = 32
LANES = 128
PACK = LANES // ENTRY_CHANNELS
F32 = jnp.float32
BF16 = jnp.bfloat16
MIB = 1024 * 1024


def halves(values):
    high = values.astype(BF16)
    low = (values - high.astype(F32)).astype(BF16)
    return high, low


def dot(left, right):
    return jnp.dot(left, right, preferred_element_type=F32)


def dot_rows(left, right):
    return lax.dot_general(left, right, (((1,), (1,)), ((), ())), preferred_element_type=F32)


def fold_of(columns):
    return max(1, LANES // columns)


def strided(start, size, stride):
    return pl.ds(start, size, stride=stride)


def folded_weight(weight_ref, step, fold):
    channels = ENTRY_CHANNELS
    return jnp.concatenate(
        [weight_ref[strided(step * fold + part, channels, channels), :] for part in range(fold)], 1
    )


def own_slots(blocks):
    here = lax.axis_index("blk")
    return [lax.bitwise_xor(here, 2 * slot) for slot in range(blocks)]


def peer_slots(blocks):
    here = lax.axis_index("blk") // 2
    return [lax.bitwise_xor(here, slot) for slot in range(blocks)]


def spread_of(cotangent_ref, pair, slots, fold):
    columns = len(slots) * cotangent_ref.shape[2]
    empty = jnp.zeros((columns, cotangent_ref.shape[3]), BF16)
    spread = ([], [])
    for part in range(2):
        rows = jnp.concatenate([cotangent_ref[2 * pair + part, slot] for slot in slots], 0)
        for found, values in zip(spread, halves(rows)):
            for place in range(fold):
                found.append(
                    jnp.concatenate(
                        [values if place == other else empty for other in range(fold)], 1
                    )
                )
    return [jnp.concatenate(found, 0) for found in spread]


def turn_right_kernel(parts, *refs):
    part_refs, (out_ref, total, square, tiles) = refs[:parts], refs[parts:]
    channels = ENTRY_CHANNELS
    rows, features = out_ref.shape
    count = features // LANES
    total[...] = functools.reduce(jnp.add, [ref[...] for ref in part_refs])
    for group in range(rows // PACK):
        stacked = [total[strided(group * PACK + k, channels, rows), :] for k in range(PACK)]
        square[...] = jnp.concatenate(stacked, 0).T
        pieces = [square[strided(part, count, PACK), :] for part in range(PACK)]
        for k in range(PACK):
            lanes = slice(k * channels, (k + 1) * channels)
            tiles[strided(group * PACK + k, count, rows), :] = jnp.concatenate(
                [piece[:, lanes] for piece in pieces], 1
            )
    for tile in range(count):
        out_ref[:, tile * LANES : (tile + 1) * LANES] = tiles[tile * rows : (tile + 1) * rows, :]


def turn_left_kernel(parts, *refs):
    part_refs, (out_ref, total, tiles) = refs[:parts], refs[parts:]
    channels = ENTRY_CHANNELS
    size, width = part_refs[0].shape
    rows, features = out_ref.shape
    count = features // LANES
    found = functools.reduce(jnp.add, [ref[...] for ref in part_refs])
    for tile in range(width // LANES):
        total[tile * size : (tile + 1) * size, :] = found[:, tile * LANES : (tile + 1) * LANES]
    for tile in range(width // LANES):
        pieces = [total[strided(tile * size + part, count, PACK), :] for part in range(PACK)]
        for k in range(PACK):
            lanes = slice(k * channels, (k + 1) * channels)
            tiles[strided(tile * PACK + k, count, rows), :] = jnp.concatenate(
                [piece[:, lanes] for piece in pieces], 1
            )
    for tile in range(count):
        out_ref[:, tile * LANES : (tile + 1) * LANES] = tiles[tile * rows : (tile + 1) * rows, :]


def prepare_weight(weight_ref, weight_cat, fold):
    channels = ENTRY_CHANNELS
    for step in range(channels // fold):
        high, low = halves(folded_weight(weight_ref, step, fold))
        weight_cat[step * channels : (step + 1) * channels, :] = jnp.concatenate(
            [high, low, high], 1
        )


def gradient_phase(slots, fold, cotangent_ref, out_ref, weight_cat):
    def step_of(pair, carry):
        high, low = spread_of(cotangent_ref, pair, slots, fold)
        found = dot_rows(weight_cat[...], jnp.concatenate([high, high, low], 1))
        out_ref[pair] = jnp.concatenate(halves(found), 1)
        return carry

    lax.fori_loop(0, out_ref.shape[0], step_of, 0)


def gradient_kernel(blocks, weight_ref, cotangent_ref, left_ref, out_ref, partial_ref, weight_cat, left_flip):
    fold = fold_of(blocks * cotangent_ref.shape[2])
    prepare_weight(weight_ref, weight_cat, fold)
    gradient_phase(own_slots(blocks), fold, cotangent_ref, out_ref, weight_cat)

    def store(step, found):
        partial_ref[step] = found

    right_phase(left_ref, out_ref, left_flip, store)


def right_phase(left_ref, factor_ref, left_flip, store):
    sequences = left_ref.shape[1]
    lanes = factor_ref.shape[2] // 4
    flip_high, flip_low = halves((left_ref[...] * (1.0 / sequences)).T)
    left_flip[:sequences, :] = flip_high
    left_flip[sequences:, :] = flip_low

    def step_of(step, carry):
        high, low = (
            jnp.concatenate(
                [rows_of_step([factor_ref], 2 * step + part, half, lanes) for part in range(2)], 1
            )
            for half in range(2)
        )
        first = dot(left_flip[...], high)
        second = dot(left_flip[:sequences, :], low)
        store(step, first[:sequences] + first[sequences:] + second)
        return carry

    lax.fori_loop(0, factor_ref.shape[1] // (2 * ENTRY_CHANNELS), step_of, 0)


def rows_of_step(refs, step, half, lanes):
    channels = ENTRY_CHANNELS
    rows = pl.ds(pl.multiple_of(step * channels, channels), channels)
    start = 2 * half * lanes
    return jnp.concatenate(
        [
            ref[pair, rows, start + part * lanes : start + (part + 1) * lanes]
            for ref in refs
            for pair in range(ref.shape[0])
            for part in range(2)
        ],
        0,
    )


def both_left(left_refs):
    sequences = left_refs[0].shape[1]
    return jnp.concatenate([ref[...] for ref in left_refs], 0) * (1.0 / sequences)


def right_kernel(blocks, weight_ref, cotangent_ref, left_ref, partial_ref, peer_ref, *refs):
    out_refs, (weight_cat, left_flip) = refs[:blocks], refs[blocks:]
    depth = cotangent_ref.shape[2]
    fold = fold_of(blocks * depth)
    lanes = fold * blocks * depth
    prepare_weight(weight_ref, weight_cat, fold)
    gradient_phase(peer_slots(blocks), fold, cotangent_ref, peer_ref, weight_cat)

    def store(step, found):
        found = found + partial_ref[step]
        for part in range(2):
            turned = found[:, part * lanes : (part + 1) * lanes].T
            for place in range(fold):
                for slot in range(blocks):
                    start = (place * blocks + slot) * depth
                    row = pl.multiple_of(((2 * step + part) * fold + place) * depth, depth)
                    out_refs[slot][pl.ds(row, depth), :] = turned[start : start + depth]

    right_phase(left_ref, peer_ref, left_flip, store)


def right_rows(right_refs, step, fold, depth):
    return jnp.concatenate(
        [
            ref[pl.ds(pl.multiple_of((step * fold + part) * depth, depth), depth), :]
            for part in range(fold)
            for ref in right_refs
        ],
        0,
    )


def weight_kernel(blocks, own_left, peer_left, own_cotangent, peer_cotangent, *refs):
    right_refs = refs[:blocks]
    keep_ref, send_ref, own_out, peer_out, own_ref, peer_ref, total, semaphores = refs[blocks:]
    channels = ENTRY_CHANNELS
    depth, pairs = own_cotangent.shape[2:]
    fold = fold_of(blocks * depth)
    lanes = fold * blocks * depth
    high, low = halves(both_left([own_left, peer_left]))
    left_cat = jnp.concatenate([high, low, high], 1)

    def copies(step):
        size = 2 * channels
        rows = pl.ds(pl.multiple_of(step * size, size), size)
        return [
            pltpu.make_async_copy(ref.at[:, rows], out.at[:, rows], semaphores.at[step, side])
            for side, (ref, out) in enumerate(((own_ref, own_out), (peer_ref, peer_out)))
        ]

    def outer_step(step, carry):
        right = [right_rows(right_refs, 2 * step + part, fold, depth) for part in range(2)]
        high, low = halves(jnp.concatenate(right, 0))
        found = dot_rows(left_cat, jnp.concatenate([high, high, low], 1))
        both = halves(found)
        for part in range(2):
            start = pl.multiple_of((2 * step + part) * channels, channels)
            row = 0
            for ref in (own_ref, peer_ref):
                for index in range(2 * ref.shape[0]):
                    for half in range(2):
                        lane = (2 * half + index % 2) * lanes
                        ref[index // 2, pl.ds(start, channels), lane : lane + lanes] = both[half][
                            row : row + channels, part * lanes : (part + 1) * lanes
                        ]
                    row += channels
        for copy in copies(step):
            copy.start()
        return carry

    lax.fori_loop(0, channels // (2 * fold), outer_step, 0)
    total[...] = jnp.zeros_like(total)

    def weight_step(pair, carry):
        lefts, rights = [], []
        for ref, cotangent_ref, slots in (
            (own_ref, own_cotangent, own_slots(blocks)),
            (peer_ref, peer_cotangent, peer_slots(blocks)),
        ):
            high, low = spread_of(cotangent_ref, pair, slots, fold)
            lefts += [ref[pair], ref[pair, :, : 2 * lanes]]
            rights += [high, high, low]
        total[...] += dot(jnp.concatenate(lefts, 1), jnp.concatenate(rights, 0))
        return carry

    lax.fori_loop(0, own_ref.shape[0], weight_step, 0)
    core = lax.rem(lax.axis_index("inner"), 2)
    steps = channels // (2 * fold)
    for out_ref, half in ((keep_ref, core), (send_ref, 1 - core)):
        for step in range(steps):
            start = pl.multiple_of((half * steps + step) * channels, channels)
            found = total[pl.ds(start, channels), :]
            for part in range(fold):
                y = step * fold + part
                out_ref[y * channels : (y + 1) * channels, :] = found[
                    :, part * pairs : (part + 1) * pairs
                ]

    def finish(step, carry):
        for copy in copies(step):
            copy.wait()
        return carry

    lax.fori_loop(0, channels // (2 * fold), finish, 0)


def left_kernel(blocks, depth, own_ref, peer_ref, *refs):
    right_refs, (own_out, peer_out, total, flipped) = refs[:blocks], refs[blocks:]
    lanes = own_ref.shape[2] // 4
    fold = lanes // (blocks * depth)
    sequences = right_refs[0].shape[1]
    group = 4
    total[...] = jnp.zeros_like(total)

    def step_of(step, carry):
        steps = [group * step + part for part in range(group)]
        right = [right_rows(right_refs, at, fold, depth) for at in steps]
        high, low = halves(jnp.concatenate(right, 0))
        grads = [
            jnp.concatenate([rows_of_step([own_ref, peer_ref], at, half, lanes) for at in steps], 1)
            for half in range(2)
        ]
        both = dot(grads[0], jnp.concatenate([high, low], 1))
        total[...] += both[:, :sequences] + both[:, sequences:] + dot(grads[1], high)
        return carry

    lax.fori_loop(0, ENTRY_CHANNELS // (fold * group), step_of, 0)
    flipped[...] = total[...].T * (1.0 / sequences)
    inner, size, width = own_out.shape
    here = lax.axis_index("inner")
    for slot in range(inner):
        start = pl.multiple_of(lax.bitwise_xor(here, slot) * size, size)
        own_out[slot] = flipped[pl.ds(start, size), :width]
        peer_out[slot] = flipped[pl.ds(start, size), width:]


def left_add_kernel(own_ref, other_ref, *out_refs):
    for slot, ref in enumerate(out_refs):
        ref[...] = own_ref[slot] + other_ref[slot]


def pair_kernel(final, blocks, outer_hbm, weight_ref, *refs):
    if final:
        other_ref, out_ref, outer_ref, weight_flip, weight_rows, semaphores = refs
    else:
        out_ref, outer_ref, weight_flip, weight_rows, semaphores = refs
    channels = ENTRY_CHANNELS
    depth, pairs = out_ref.shape[2:]
    count = outer_ref.shape[0]
    lanes = outer_ref.shape[2] // 4
    columns = blocks * depth
    fold = lanes // columns
    wide = fold * pairs

    def copy_of(pair):
        return pltpu.make_async_copy(outer_hbm.at[pair], outer_ref.at[pair], semaphores.at[pair])

    for pair in range(count):
        copy_of(pair).start()
    for step in range(channels // fold):
        weight_rows[step * channels : (step + 1) * channels, :] = folded_weight(
            weight_ref, step, fold
        )
    flip_high, flip_low = halves(weight_rows[...].T)
    weight_flip[:wide, :] = flip_high
    weight_flip[wide:, :] = flip_low
    slots = own_slots(blocks) if final else peer_slots(blocks)

    def step_of(pair, carry):
        copy_of(pair).wait()
        first = dot(weight_flip[...], outer_ref[pair, :, : 2 * lanes])
        second = dot(weight_flip[:wide, :], outer_ref[pair, :, 2 * lanes :])
        found = first[:wide] + first[wide:] + second
        for part in range(2):
            turned = []
            for place in range(fold):
                start = part * lanes
                piece = found[place * pairs : (place + 1) * pairs, start : start + lanes].T
                turned.append(piece[place * columns : (place + 1) * columns])
            turned = functools.reduce(jnp.add, turned)
            row = 2 * pair + part
            for slot in range(blocks):
                out_ref[row, slots[slot]] = turned[slot * depth : (slot + 1) * depth]
                if final:
                    other = 2 * slot + 1 - lax.rem(lax.axis_index("blk"), 2)
                    out_ref[row, other] = other_ref[row, slot]
        return carry

    lax.fori_loop(0, count, step_of, 0)


def spread_sum_kernel(in_ref, out_ref):
    found = in_ref[0]
    for part in range(1, in_ref.shape[0]):
        found = found + in_ref[part]
    for part in range(in_ref.shape[0]):
        out_ref[part] = found


def place_kernel(mine_ref, other_ref, out_ref):
    channels = ENTRY_CHANNELS
    core = lax.rem(lax.axis_index("inner"), 2)
    steps = mine_ref.shape[0] // channels
    for ref, half in ((mine_ref, core), (other_ref, 1 - core)):
        for step in range(steps):
            rows = ref[step * channels : (step + 1) * channels, :]
            out_ref[strided(half * steps + step, channels, channels), :] = rows


def shape(*sizes, kind=F32):
    return jax.ShapeDtypeStruct(sizes, kind)


def call(kernel, out_shape, scratch=(), name=None, limit=16 * MIB, far=(), after=(), out_specs=None):
    def run(*operands):
        vmem = pl.BlockSpec(memory_space=pltpu.VMEM)
        hbm = pl.BlockSpec(memory_space=pltpu.HBM)
        in_specs = [pl.BlockSpec(memory_space=pl.ANY)] * len(after)
        in_specs += [hbm if at in far else vmem for at in range(len(operands))]
        operands = [
            pltpu.with_memory_space_constraint(operand, pltpu.HBM) if at in far else operand
            for at, operand in enumerate(operands)
        ]
        extra = {} if out_specs is None else {"out_specs": out_specs}
        return pl.pallas_call(
            lambda *refs: kernel(*refs[len(after) :]),
            out_shape=out_shape,
            in_specs=in_specs,
            scratch_shapes=list(scratch),
            compiler_params=pltpu.CompilerParams(vmem_limit_bytes=limit),
            cost_estimate=pl.CostEstimate(flops=1, bytes_accessed=1, transcendentals=0),
            name=name,
            **extra,
        )(*after, *operands)

    return run


def local(alignment_left, alignment_right, projection_matrix, cotangent):
    rows, features = alignment_left.shape
    depth = alignment_right.shape[0]
    count = lax.axis_size("blk")
    inner = lax.axis_size("inner")
    channels = ENTRY_CHANNELS
    sequences = features // channels
    outer, pairs = projection_matrix.shape
    blocks = count // 2
    fold = fold_of(blocks * depth)
    lanes = fold * blocks * depth
    tall = outer // fold
    steps = channels // fold
    row_pairs = rows // 2
    everyone = ("blk", "inner")

    partner = [(here, here ^ 1) for here in range(count)]
    slot_moves = [[(here, here ^ (2 * slot)) for here in range(count)] for slot in range(blocks)]
    inner_moves = [[(here, here ^ slot) for here in range(inner)] for slot in range(inner)]
    cores = [(here, here ^ 1) for here in range(inner)]
    core_groups = [list(range(core, count * inner, 2)) for core in range(2)]

    limit = 20 * MIB * max(1, blocks * depth * fold // LANES * 2 // fold)
    large = functools.partial(call, limit=limit)

    right = alignment_right.reshape(depth, sequences, channels).transpose(2, 0, 1)
    right = right.reshape(channels * depth, sequences)
    rights = [right]
    for slot in range(1, blocks):
        rights.append(lax.ppermute(right, "blk", slot_moves[slot]))

    by_side = cotangent.reshape(rows, blocks, 2, depth, pairs)
    parity = lax.rem(lax.axis_index("blk"), 2)
    cotangent_peer = lax.ppermute(
        jnp.where(parity == 0, by_side[:, :, 1], by_side[:, :, 0]), "blk", partner
    )
    left = alignment_left.reshape(rows, sequences, channels).transpose(0, 2, 1)
    left = left.reshape(rows * channels, sequences)
    left_peer = lax.ppermute(left, "blk", partner)

    factor = shape(row_pairs, tall, 4 * lanes, kind=BF16)
    factor_scratch = pltpu.VMEM(factor.shape, BF16)
    weight_scratch = pltpu.VMEM((tall, 3 * fold * pairs), BF16)
    flip_scratch = pltpu.VMEM((2 * sequences, rows * channels), BF16)
    grad_own, partial = large(
        functools.partial(gradient_kernel, blocks),
        [factor, shape(steps // 2, sequences, 2 * lanes)],
        [weight_scratch, flip_scratch],
        "gradient_own",
    )(projection_matrix, cotangent, left)
    grad_peer, *right_parts = large(
        functools.partial(right_kernel, blocks),
        [factor] + [shape(channels * depth, sequences)] * blocks,
        [weight_scratch, flip_scratch],
        "right_parts",
    )(projection_matrix, cotangent_peer, left_peer, partial)
    right_found = [right_parts[0]]
    for slot in range(1, blocks):
        right_found.append(lax.ppermute(right_parts[slot], "blk", slot_moves[slot]))

    vmem = pl.BlockSpec(memory_space=pltpu.VMEM)
    hbm = pl.BlockSpec(memory_space=pltpu.HBM)
    keep, send, outer_own, outer_peer = large(
        functools.partial(weight_kernel, blocks),
        [shape(outer // 2, pairs)] * 2 + [pltpu.HBM(factor.shape, BF16)] * 2,
        [
            factor_scratch,
            factor_scratch,
            pltpu.VMEM((tall, fold * pairs), F32),
            pltpu.SemaphoreType.DMA((steps // 2, 2)),
        ],
        "weight",
        after=[right_parts[0]],
        out_specs=[vmem, vmem, hbm, hbm],
    )(left, left_peer, cotangent, cotangent_peer, *rights)
    sent = lax.ppermute(send, "inner", cores)

    size = sequences // inner
    left_own, left_other = large(
        functools.partial(left_kernel, blocks, depth),
        [shape(inner, size, rows * channels)] * 2,
        [
            pltpu.VMEM((2 * rows * channels, sequences), F32),
            pltpu.VMEM((sequences, 2 * rows * channels), F32),
        ],
        "left_parts",
        after=[keep],
    )(grad_own, grad_peer, *rights)
    left_other = lax.ppermute(left_other, "blk", partner)
    keep, left_own = lax.optimization_barrier((keep, left_own))
    members = count * inner // 2
    pieces = (keep + sent).reshape(members, outer // 2 // members, pairs)

    def pair(values, others, after, name):
        final = bool(others)
        return large(
            functools.partial(pair_kernel, final, blocks),
            shape(rows, count if final else blocks, depth, pairs),
            [
                factor_scratch,
                pltpu.VMEM((2 * fold * pairs, tall), BF16),
                pltpu.VMEM((tall, fold * pairs), F32),
                pltpu.SemaphoreType.DMA((row_pairs,)),
            ],
            name,
            far=[0],
            after=after,
        )(values, projection_matrix, *others)

    pair_own_rows = pair(outer_peer, [], [pieces], "pair_peer")
    pair_peer = lax.ppermute(pair_own_rows, "blk", partner)

    pieces = lax.all_to_all(pieces, everyone, 0, 0, axis_index_groups=core_groups)
    pieces = call(
        spread_sum_kernel, shape(*pieces.shape), name="weight_sum", after=[pair_own_rows]
    )(pieces)
    pieces = lax.all_to_all(pieces, everyone, 0, 0, axis_index_groups=core_groups)

    left_found = call(
        left_add_kernel, [shape(size, rows * channels)] * inner, name="left_add"
    )(left_own, left_other)
    left_found = [
        lax.ppermute(part, "inner", inner_moves[slot]) if slot else part
        for slot, part in enumerate(left_found)
    ]
    grad_left = call(
        functools.partial(turn_left_kernel, inner),
        shape(rows, features // inner),
        [
            pltpu.VMEM((size * rows * channels // LANES, LANES), F32),
            pltpu.VMEM((rows * features // inner // LANES, LANES), F32),
        ],
        name="turn_left",
    )(*left_found)

    grad_right = call(
        functools.partial(turn_right_kernel, blocks),
        shape(depth, features),
        [
            pltpu.VMEM((channels * depth, sequences), F32),
            pltpu.VMEM((LANES, LANES), F32),
            pltpu.VMEM((depth * features // LANES, LANES), F32),
        ],
        name="turn_right",
    )(*right_found)

    pair_update = pair(outer_own, [pair_peer], [], "pair_own")

    pieces, pair_update, grad_left, grad_right = lax.optimization_barrier(
        (pieces, pair_update, grad_left, grad_right)
    )
    mine = pieces.reshape(outer // 2, pairs)
    other = lax.ppermute(mine, "inner", cores)
    grad_weight = call(place_kernel, shape(outer, pairs), name="place")(mine, other)
    return (pair_update, grad_left, grad_right, grad_weight)


def solution(mesh):
    placed = (
        P(("groups", "blk"), None),
        P(("groups", "blk", "inner"), None),
        P(),
        P(("groups", "blk"), None, "inner", None),
    )
    return jax.shard_map(
        local,
        mesh=mesh,
        in_specs=placed,
        out_specs=(
            P(("groups", "blk"), None, "inner", None),
            P(("groups", "blk"), "inner"),
            P(("groups", "blk", "inner"), None),
            P("groups", None),
        ),
        check_vma=False,
    )
```

```python
import functools

import jax
import jax.numpy as jnp
from jax import lax
from jax.experimental import pallas as pl
from jax.experimental.pallas import tpu as pltpu
from jax.sharding import PartitionSpec as P

ENTRY_CHANNELS = 32
LANES = 128
PACK = LANES // ENTRY_CHANNELS
F32 = jnp.float32
BF16 = jnp.bfloat16
MIB = 1024 * 1024


def halves(values):
    high = values.astype(BF16)
    low = (values - high.astype(F32)).astype(BF16)
    return high, low


def dot(left, right):
    return jnp.dot(left, right, preferred_element_type=F32)


def dot_rows(left, right):
    return lax.dot_general(left, right, (((1,), (1,)), ((), ())), preferred_element_type=F32)


def fold_of(columns):
    return max(1, LANES // columns)


def strided(start, size, stride):
    return pl.ds(start, size, stride=stride)


def folded_weight(weight_ref, step, fold):
    channels = ENTRY_CHANNELS
    return jnp.concatenate(
        [weight_ref[strided(step * fold + part, channels, channels), :] for part in range(fold)], 1
    )


def own_slots(blocks):
    here = lax.axis_index("blk")
    return [lax.bitwise_xor(here, 2 * slot) for slot in range(blocks)]


def peer_slots(blocks):
    here = lax.axis_index("blk") // 2
    return [lax.bitwise_xor(here, slot) for slot in range(blocks)]


def spread_of(cotangent_ref, pair, slots, fold):
    columns = len(slots) * cotangent_ref.shape[2]
    empty = jnp.zeros((columns, cotangent_ref.shape[3]), BF16)
    spread = ([], [])
    for part in range(2):
        rows = jnp.concatenate([cotangent_ref[2 * pair + part, slot] for slot in slots], 0)
        for found, values in zip(spread, halves(rows)):
            for place in range(fold):
                found.append(
                    jnp.concatenate(
                        [values if place == other else empty for other in range(fold)], 1
                    )
                )
    return [jnp.concatenate(found, 0) for found in spread]


def turn_in(rows_minor, in_ref, out_ref, tiles, square):
    channels = ENTRY_CHANNELS
    rows, features = in_ref.shape
    count = features // LANES
    for tile in range(count):
        tiles[tile * rows : (tile + 1) * rows, :] = in_ref[:, tile * LANES : (tile + 1) * LANES]
    for group in range(rows // PACK):
        found = [tiles[strided(group * PACK + k, count, rows), :] for k in range(PACK)]
        for part in range(PACK):
            lanes = slice(part * channels, (part + 1) * channels)
            square[group, strided(part, count, PACK), :] = jnp.concatenate(
                [values[:, lanes] for values in found], 1
            )
        turned = square[group].T
        if rows_minor:
            for k in range(PACK):
                out_ref[strided(group * PACK + k, channels, rows), :] = turned[
                    k * channels : (k + 1) * channels
                ]
        else:
            out_ref[group * LANES : (group + 1) * LANES, :] = turned


def prepare_kernel(
    cotangent_hbm, right_ref, left_ref, right_out, left_out, send_ref, tiles, square, semaphore
):
    other = 1 - lax.rem(lax.axis_index("blk"), 2)
    copy = pltpu.make_async_copy(cotangent_hbm.at[:, :, other], send_ref, semaphore)
    copy.start()
    turn_in(True, right_ref, right_out, tiles.at[0], square.at[0])
    turn_in(False, left_ref, left_out, tiles.at[1], square.at[1])
    copy.wait()


def turn_right_kernel(parts, *refs):
    part_refs, (out_ref, total, square, tiles) = refs[:parts], refs[parts:]
    channels = ENTRY_CHANNELS
    rows, features = out_ref.shape
    count = features // LANES
    total[...] = functools.reduce(jnp.add, [ref[0] for ref in part_refs])
    for group in range(rows // PACK):
        stacked = [total[strided(group * PACK + k, channels, rows), :] for k in range(PACK)]
        square[...] = jnp.concatenate(stacked, 0).T
        pieces = [square[strided(part, count, PACK), :] for part in range(PACK)]
        for k in range(PACK):
            lanes = slice(k * channels, (k + 1) * channels)
            tiles[strided(group * PACK + k, count, rows), :] = jnp.concatenate(
                [piece[:, lanes] for piece in pieces], 1
            )
    for tile in range(count):
        out_ref[:, tile * LANES : (tile + 1) * LANES] = tiles[tile * rows : (tile + 1) * rows, :]


def turn_left_kernel(parts, *refs):
    part_refs, (out_ref, total, tiles) = refs[:parts], refs[parts:]
    channels = ENTRY_CHANNELS
    size, width = part_refs[0].shape
    rows, features = out_ref.shape
    count = features // LANES
    found = functools.reduce(jnp.add, [ref[...] for ref in part_refs])
    for tile in range(width // LANES):
        total[tile * size : (tile + 1) * size, :] = found[:, tile * LANES : (tile + 1) * LANES]
    for tile in range(width // LANES):
        pieces = [total[strided(tile * size + part, count, PACK), :] for part in range(PACK)]
        for k in range(PACK):
            lanes = slice(k * channels, (k + 1) * channels)
            tiles[strided(tile * PACK + k, count, rows), :] = jnp.concatenate(
                [piece[:, lanes] for piece in pieces], 1
            )
    for tile in range(count):
        out_ref[:, tile * LANES : (tile + 1) * LANES] = tiles[tile * rows : (tile + 1) * rows, :]


def prepare_weight(weight_ref, weight_cat, fold):
    channels = ENTRY_CHANNELS
    for step in range(channels // fold):
        high, low = halves(folded_weight(weight_ref, step, fold))
        weight_cat[step * channels : (step + 1) * channels, :] = jnp.concatenate(
            [high, low, high], 1
        )


def gradient_phase(slots, fold, cotangent_ref, out_ref, weight_cat):
    def step_of(pair, carry):
        high, low = spread_of(cotangent_ref, pair, slots, fold)
        found = dot_rows(weight_cat[...], jnp.concatenate([high, high, low], 1))
        out_ref[pair] = jnp.concatenate(halves(found), 1)
        return carry

    lax.fori_loop(0, out_ref.shape[0], step_of, 0)


def gradient_kernel(blocks, weight_ref, cotangent_ref, left_ref, out_ref, partial_ref, weight_cat, left_flip):
    fold = fold_of(blocks * cotangent_ref.shape[2])
    prepare_weight(weight_ref, weight_cat, fold)
    gradient_phase(own_slots(blocks), fold, cotangent_ref, out_ref, weight_cat)

    def store(step, found):
        partial_ref[step] = found

    right_phase(left_ref, out_ref, left_flip, store)


def right_phase(left_ref, factor_ref, left_flip, store):
    sequences = left_ref.shape[1]
    lanes = factor_ref.shape[2] // 4
    flip_high, flip_low = halves((left_ref[...] * (1.0 / sequences)).T)
    left_flip[:sequences, :] = flip_high
    left_flip[sequences:, :] = flip_low

    def step_of(step, carry):
        high, low = (
            jnp.concatenate(
                [rows_of_step([factor_ref], 2 * step + part, half, lanes) for part in range(2)], 1
            )
            for half in range(2)
        )
        first = dot(left_flip[...], high)
        second = dot(left_flip[:sequences, :], low)
        store(step, first[:sequences] + first[sequences:] + second)
        return carry

    lax.fori_loop(0, factor_ref.shape[1] // (2 * ENTRY_CHANNELS), step_of, 0)


def rows_of_step(refs, step, half, lanes):
    channels = ENTRY_CHANNELS
    rows = pl.ds(pl.multiple_of(step * channels, channels), channels)
    start = 2 * half * lanes
    return jnp.concatenate(
        [
            ref[pair, rows, start + part * lanes : start + (part + 1) * lanes]
            for ref in refs
            for pair in range(ref.shape[0])
            for part in range(2)
        ],
        0,
    )


def both_left(left_refs):
    sequences = left_refs[0].shape[1]
    return jnp.concatenate([ref[...] for ref in left_refs], 0) * (1.0 / sequences)


def right_kernel(blocks, weight_ref, cotangent_ref, left_ref, partial_ref, peer_ref, *refs):
    keep_ref, send_ref, weight_cat, left_flip = refs
    depth = cotangent_ref.shape[2]
    fold = fold_of(blocks * depth)
    lanes = fold * blocks * depth
    prepare_weight(weight_ref, weight_cat, fold)
    gradient_phase(peer_slots(blocks), fold, cotangent_ref, peer_ref, weight_cat)

    def store(step, found):
        found = found + partial_ref[step]
        for part in range(2):
            turned = found[:, part * lanes : (part + 1) * lanes].T
            for place in range(fold):
                for slot in range(blocks):
                    start = (place * blocks + slot) * depth
                    row = pl.multiple_of(((2 * step + part) * fold + place) * depth, depth)
                    out_ref = send_ref if slot % 2 else keep_ref
                    out_ref[slot // 2, pl.ds(row, depth), :] = turned[start : start + depth]

    right_phase(left_ref, peer_ref, left_flip, store)


def halve_kernel(keep_ref, found_ref, keep_out, send_out):
    for slot in range(keep_ref.shape[0]):
        out_ref = send_out if slot % 2 else keep_out
        out_ref[slot // 2] = keep_ref[slot] + found_ref[slot]


def right_rows(right_refs, step, fold, depth):
    return jnp.concatenate(
        [
            ref[pl.ds(pl.multiple_of((step * fold + part) * depth, depth), depth), :]
            for part in range(fold)
            for ref in right_refs
        ],
        0,
    )


def weight_kernel(blocks, own_left, peer_left, own_cotangent, peer_cotangent, *refs):
    right_refs = refs[:blocks]
    keep_ref, send_ref, own_out, peer_out, own_ref, peer_ref, total, semaphores = refs[blocks:]
    channels = ENTRY_CHANNELS
    depth, pairs = own_cotangent.shape[2:]
    fold = fold_of(blocks * depth)
    lanes = fold * blocks * depth
    high, low = halves(both_left([own_left, peer_left]))
    left_cat = jnp.concatenate([high, low, high], 1)

    def copies(step):
        size = 2 * channels
        rows = pl.ds(pl.multiple_of(step * size, size), size)
        return [
            pltpu.make_async_copy(ref.at[:, rows], out.at[:, rows], semaphores.at[step, side])
            for side, (ref, out) in enumerate(((own_ref, own_out), (peer_ref, peer_out)))
        ]

    def outer_step(step, carry):
        right = [right_rows(right_refs, 2 * step + part, fold, depth) for part in range(2)]
        high, low = halves(jnp.concatenate(right, 0))
        found = dot_rows(left_cat, jnp.concatenate([high, high, low], 1))
        both = halves(found)
        for part in range(2):
            start = pl.multiple_of((2 * step + part) * channels, channels)
            row = 0
            for ref in (own_ref, peer_ref):
                for index in range(2 * ref.shape[0]):
                    for half in range(2):
                        lane = (2 * half + index % 2) * lanes
                        ref[index // 2, pl.ds(start, channels), lane : lane + lanes] = both[half][
                            row : row + channels, part * lanes : (part + 1) * lanes
                        ]
                    row += channels
        for copy in copies(step):
            copy.start()
        return carry

    lax.fori_loop(0, channels // (2 * fold), outer_step, 0)
    total[...] = jnp.zeros_like(total)

    def weight_step(pair, carry):
        lefts, rights = [], []
        for ref, cotangent_ref, slots in (
            (own_ref, own_cotangent, own_slots(blocks)),
            (peer_ref, peer_cotangent, peer_slots(blocks)),
        ):
            high, low = spread_of(cotangent_ref, pair, slots, fold)
            lefts += [ref[pair], ref[pair, :, : 2 * lanes]]
            rights += [high, high, low]
        total[...] += dot(jnp.concatenate(lefts, 1), jnp.concatenate(rights, 0))
        return carry

    lax.fori_loop(0, own_ref.shape[0], weight_step, 0)
    core = lax.rem(lax.axis_index("inner"), 2)
    steps = channels // (2 * fold)
    for out_ref, half in ((keep_ref, core), (send_ref, 1 - core)):
        for step in range(steps):
            start = pl.multiple_of((half * steps + step) * channels, channels)
            found = total[pl.ds(start, channels), :]
            for part in range(fold):
                y = step * fold + part
                out_ref[y * channels : (y + 1) * channels, :] = found[
                    :, part * pairs : (part + 1) * pairs
                ]

    def finish(step, carry):
        for copy in copies(step):
            copy.wait()
        return carry

    lax.fori_loop(0, channels // (2 * fold), finish, 0)


def left_kernel(blocks, depth, own_ref, peer_ref, *refs):
    right_refs, (own_out, peer_out, total, flipped) = refs[:blocks], refs[blocks:]
    lanes = own_ref.shape[2] // 4
    fold = lanes // (blocks * depth)
    sequences = right_refs[0].shape[1]
    group = 4
    total[...] = jnp.zeros_like(total)

    def step_of(step, carry):
        steps = [group * step + part for part in range(group)]
        right = [right_rows(right_refs, at, fold, depth) for at in steps]
        high, low = halves(jnp.concatenate(right, 0))
        grads = [
            jnp.concatenate([rows_of_step([own_ref, peer_ref], at, half, lanes) for at in steps], 1)
            for half in range(2)
        ]
        both = dot(grads[0], jnp.concatenate([high, low], 1))
        total[...] += both[:, :sequences] + both[:, sequences:] + dot(grads[1], high)
        return carry

    lax.fori_loop(0, ENTRY_CHANNELS // (fold * group), step_of, 0)
    flipped[...] = total[...].T * (1.0 / sequences)
    inner, size, width = own_out.shape
    here = lax.axis_index("inner")
    for slot in range(inner):
        start = pl.multiple_of(lax.bitwise_xor(here, slot) * size, size)
        own_out[slot] = flipped[pl.ds(start, size), :width]
        peer_out[slot] = flipped[pl.ds(start, size), width:]


def left_add_kernel(own_ref, other_ref, *out_refs):
    for slot, ref in enumerate(out_refs):
        ref[...] = own_ref[slot] + other_ref[slot]


def pair_kernel(
    blocks, outer_hbm, weight_ref, out_ref, outer_ref, weight_flip, weight_rows, semaphores
):
    channels = ENTRY_CHANNELS
    depth, pairs = out_ref.shape[2:]
    count = outer_ref.shape[0]
    lanes = outer_ref.shape[2] // 4
    columns = blocks * depth
    fold = lanes // columns
    wide = fold * pairs

    def copy_of(pair):
        return pltpu.make_async_copy(outer_hbm.at[pair], outer_ref.at[pair], semaphores.at[pair])

    for pair in range(count):
        copy_of(pair).start()
    for step in range(channels // fold):
        weight_rows[step * channels : (step + 1) * channels, :] = folded_weight(
            weight_ref, step, fold
        )
    flip_high, flip_low = halves(weight_rows[...].T)
    weight_flip[:wide, :] = flip_high
    weight_flip[wide:, :] = flip_low
    slots = peer_slots(blocks)

    def step_of(pair, carry):
        copy_of(pair).wait()
        first = dot(weight_flip[...], outer_ref[pair, :, : 2 * lanes])
        second = dot(weight_flip[:wide, :], outer_ref[pair, :, 2 * lanes :])
        found = first[:wide] + first[wide:] + second
        for part in range(2):
            turned = []
            for place in range(fold):
                start = part * lanes
                piece = found[place * pairs : (place + 1) * pairs, start : start + lanes].T
                turned.append(piece[place * columns : (place + 1) * columns])
            turned = functools.reduce(jnp.add, turned)
            row = 2 * pair + part
            for slot in range(blocks):
                out_ref[row, slots[slot]] = turned[slot * depth : (slot + 1) * depth]
        return carry

    lax.fori_loop(0, count, step_of, 0)


def merge_kernel(own_ref, other_ref, out_ref, semaphores):
    parity = lax.rem(lax.axis_index("blk"), 2)
    copies = [
        pltpu.make_async_copy(ref, out_ref.at[:, :, side], semaphores.at[at])
        for at, (ref, side) in enumerate(((own_ref, parity), (other_ref, 1 - parity)))
    ]
    for copy in copies:
        copy.start()
    for copy in copies:
        copy.wait()


def spread_sum_kernel(in_ref, out_ref):
    found = in_ref[0]
    for part in range(1, in_ref.shape[0]):
        found = found + in_ref[part]
    for part in range(in_ref.shape[0]):
        out_ref[part] = found


def place_kernel(mine_ref, other_ref, out_ref):
    channels = ENTRY_CHANNELS
    core = lax.rem(lax.axis_index("inner"), 2)
    steps = mine_ref.shape[0] // channels
    for ref, half in ((mine_ref, core), (other_ref, 1 - core)):
        for step in range(steps):
            rows = ref[step * channels : (step + 1) * channels, :]
            out_ref[strided(half * steps + step, channels, channels), :] = rows


def shape(*sizes, kind=F32):
    return jax.ShapeDtypeStruct(sizes, kind)


def call(kernel, out_shape, scratch=(), name=None, limit=16 * MIB, far=(), after=(), out_specs=None):
    def run(*operands):
        vmem = pl.BlockSpec(memory_space=pltpu.VMEM)
        hbm = pl.BlockSpec(memory_space=pltpu.HBM)
        in_specs = [pl.BlockSpec(memory_space=pl.ANY)] * len(after)
        in_specs += [hbm if at in far else vmem for at in range(len(operands))]
        operands = [
            pltpu.with_memory_space_constraint(operand, pltpu.HBM) if at in far else operand
            for at, operand in enumerate(operands)
        ]
        extra = {} if out_specs is None else {"out_specs": out_specs}
        return pl.pallas_call(
            lambda *refs: kernel(*refs[len(after) :]),
            out_shape=out_shape,
            in_specs=in_specs,
            scratch_shapes=list(scratch),
            compiler_params=pltpu.CompilerParams(vmem_limit_bytes=limit),
            cost_estimate=pl.CostEstimate(flops=1, bytes_accessed=1, transcendentals=0),
            name=name,
            **extra,
        )(*after, *operands)

    return run


def local(alignment_left, alignment_right, projection_matrix, cotangent):
    rows, features = alignment_left.shape
    depth = alignment_right.shape[0]
    count = lax.axis_size("blk")
    inner = lax.axis_size("inner")
    channels = ENTRY_CHANNELS
    sequences = features // channels
    outer, pairs = projection_matrix.shape
    blocks = count // 2
    fold = fold_of(blocks * depth)
    lanes = fold * blocks * depth
    tall = outer // fold
    steps = channels // fold
    row_pairs = rows // 2
    everyone = ("blk", "inner")

    partner = [(here, here ^ 1) for here in range(count)]
    slot_moves = [[(here, here ^ (2 * slot)) for here in range(count)] for slot in range(blocks)]
    inner_moves = [[(here, here ^ slot) for here in range(inner)] for slot in range(inner)]
    cores = [(here, here ^ 1) for here in range(inner)]
    core_groups = [list(range(core, count * inner, 2)) for core in range(2)]

    limit = 20 * MIB * max(1, blocks * depth * fold // LANES * 2 // fold)
    large = functools.partial(call, limit=limit)

    by_side = cotangent.reshape(rows, blocks, 2, depth, pairs)
    right, left, cotangent_send = call(
        prepare_kernel,
        [
            shape(channels * depth, sequences),
            shape(rows * channels, sequences),
            shape(rows, blocks, depth, pairs),
        ],
        [
            pltpu.VMEM((2, rows * features // LANES, LANES), F32),
            pltpu.VMEM((2, rows // PACK, LANES, LANES), F32),
            pltpu.SemaphoreType.DMA,
        ],
        name="prepare",
        far=[0],
    )(by_side, alignment_right, alignment_left)
    rights = [right]
    for slot in range(1, blocks):
        rights.append(lax.ppermute(right, "blk", slot_moves[slot]))
    cotangent_peer = lax.ppermute(cotangent_send, "blk", partner)
    left_peer = lax.ppermute(left, "blk", partner)

    factor = shape(row_pairs, tall, 4 * lanes, kind=BF16)
    factor_scratch = pltpu.VMEM(factor.shape, BF16)
    weight_scratch = pltpu.VMEM((tall, 3 * fold * pairs), BF16)
    flip_scratch = pltpu.VMEM((2 * sequences, rows * channels), BF16)
    grad_own, partial = large(
        functools.partial(gradient_kernel, blocks),
        [factor, shape(steps // 2, sequences, 2 * lanes)],
        [weight_scratch, flip_scratch],
        "gradient_own",
    )(projection_matrix, cotangent, left)
    right_half = shape(blocks // 2, channels * depth, sequences)
    grad_peer, right_keep, right_send = large(
        functools.partial(right_kernel, blocks),
        [factor, right_half, right_half],
        [weight_scratch, flip_scratch],
        "right_parts",
    )(projection_matrix, cotangent_peer, left_peer, partial)
    right_send = lax.ppermute(right_send, "blk", slot_moves[1])

    vmem = pl.BlockSpec(memory_space=pltpu.VMEM)
    hbm = pl.BlockSpec(memory_space=pltpu.HBM)
    keep, send, outer_own, outer_peer = large(
        functools.partial(weight_kernel, blocks),
        [shape(outer // 2, pairs)] * 2 + [pltpu.HBM(factor.shape, BF16)] * 2,
        [
            factor_scratch,
            factor_scratch,
            pltpu.VMEM((tall, fold * pairs), F32),
            pltpu.SemaphoreType.DMA((steps // 2, 2)),
        ],
        "weight",
        after=[right_keep],
        out_specs=[vmem, vmem, hbm, hbm],
    )(left, left_peer, cotangent, cotangent_peer, *rights)
    sent = lax.ppermute(send, "inner", cores)

    size = sequences // inner
    left_own, left_other = large(
        functools.partial(left_kernel, blocks, depth),
        [shape(inner, size, rows * channels)] * 2,
        [
            pltpu.VMEM((2 * rows * channels, sequences), F32),
            pltpu.VMEM((sequences, 2 * rows * channels), F32),
        ],
        "left_parts",
        after=[keep],
    )(grad_own, grad_peer, *rights)
    left_other = lax.ppermute(left_other, "blk", partner)
    slot = 2
    while slot < blocks:
        part = shape(blocks // (2 * slot), channels * depth, sequences)
        right_keep, right_send = call(
            halve_kernel, [part, part], name="right_halve", after=[left_own]
        )(right_keep, right_send)
        right_send = lax.ppermute(right_send, "blk", slot_moves[slot])
        slot = 2 * slot
    keep, left_own, right_keep = lax.optimization_barrier((keep, left_own, right_keep))
    members = count * inner // 2
    pieces = (keep + sent).reshape(members, outer // 2 // members, pairs)

    def pair(values, after, name):
        return large(
            functools.partial(pair_kernel, blocks),
            shape(rows, blocks, depth, pairs),
            [
                factor_scratch,
                pltpu.VMEM((2 * fold * pairs, tall), BF16),
                pltpu.VMEM((tall, fold * pairs), F32),
                pltpu.SemaphoreType.DMA((row_pairs,)),
            ],
            name,
            far=[0],
            after=after,
        )(values, projection_matrix)

    pair_other = pair(outer_peer, [pieces], "pair_peer")
    pair_found = lax.ppermute(pair_other, "blk", partner)
    pair_own = pair(outer_own, [pair_other], "pair_own")

    pieces = lax.all_to_all(pieces, everyone, 0, 0, axis_index_groups=core_groups)
    left_found = call(
        left_add_kernel, [shape(size, rows * channels)] * inner, name="left_add"
    )(left_own, left_other)
    pieces = call(
        spread_sum_kernel,
        shape(*pieces.shape),
        name="weight_sum",
        after=[pair_own, left_found[0], right_send],
    )(pieces)
    pieces = lax.all_to_all(pieces, everyone, 0, 0, axis_index_groups=core_groups)

    left_found = [
        lax.ppermute(part, "inner", inner_moves[slot]) if slot else part
        for slot, part in enumerate(left_found)
    ]
    grad_left = call(
        functools.partial(turn_left_kernel, inner),
        shape(rows, features // inner),
        [
            pltpu.VMEM((size * rows * channels // LANES, LANES), F32),
            pltpu.VMEM((rows * features // inner // LANES, LANES), F32),
        ],
        name="turn_left",
    )(*left_found)

    grad_right = call(
        functools.partial(turn_right_kernel, 2),
        shape(depth, features),
        [
            pltpu.VMEM((channels * depth, sequences), F32),
            pltpu.VMEM((LANES, LANES), F32),
            pltpu.VMEM((depth * features // LANES, LANES), F32),
        ],
        name="turn_right",
    )(right_keep, right_send)

    pair_update = call(
        merge_kernel,
        pltpu.HBM(by_side.shape, F32),
        [pltpu.SemaphoreType.DMA((2,))],
        "merge",
        out_specs=hbm,
    )(pair_own, pair_found)
    pair_update = pair_update.reshape(cotangent.shape)

    pieces, pair_update, grad_left, grad_right = lax.optimization_barrier(
        (pieces, pair_update, grad_left, grad_right)
    )
    mine = pieces.reshape(outer // 2, pairs)
    other = lax.ppermute(mine, "inner", cores)
    grad_weight = call(place_kernel, shape(outer, pairs), name="place")(mine, other)
    return (pair_update, grad_left, grad_right, grad_weight)


def solution(mesh):
    placed = (
        P(("groups", "blk"), None),
        P(("groups", "blk", "inner"), None),
        P(),
        P(("groups", "blk"), None, "inner", None),
    )
    return jax.shard_map(
        local,
        mesh=mesh,
        in_specs=placed,
        out_specs=(
            P(("groups", "blk"), None, "inner", None),
            P(("groups", "blk"), "inner"),
            P(("groups", "blk", "inner"), None),
            P("groups", None),
        ),
        check_vma=False,
    )
```

```python
import functools

import jax
import jax.numpy as jnp
from jax import lax
from jax.experimental import pallas as pl
from jax.experimental.pallas import tpu as pltpu
from jax.sharding import PartitionSpec as P

ENTRY_CHANNELS = 32
LANES = 128
PACK = LANES // ENTRY_CHANNELS
F32 = jnp.float32
BF16 = jnp.bfloat16
MIB = 1024 * 1024


def halves(values):
    high = values.astype(BF16)
    low = (values - high.astype(F32)).astype(BF16)
    return high, low


def dot(left, right):
    return jnp.dot(left, right, preferred_element_type=F32)


def dot_rows(left, right):
    return lax.dot_general(left, right, (((1,), (1,)), ((), ())), preferred_element_type=F32)


def fold_of(columns):
    return max(1, LANES // columns)


def strided(start, size, stride):
    return pl.ds(start, size, stride=stride)


def folded_weight(weight_ref, step, fold):
    channels = ENTRY_CHANNELS
    return jnp.concatenate(
        [weight_ref[strided(step * fold + part, channels, channels), :] for part in range(fold)], 1
    )


def slots_of(blocks):
    here = lax.axis_index("blk") // 2
    return [lax.bitwise_xor(here, slot) for slot in range(blocks)]


def spread_of(cotangent_ref, pair, slots, fold):
    columns = len(slots) * cotangent_ref.shape[2]
    empty = jnp.zeros((columns, cotangent_ref.shape[3]), BF16)
    spread = ([], [])
    for part in range(2):
        rows = jnp.concatenate([cotangent_ref[2 * pair + part, slot] for slot in slots], 0)
        for found, values in zip(spread, halves(rows)):
            for place in range(fold):
                found.append(
                    jnp.concatenate(
                        [values if place == other else empty for other in range(fold)], 1
                    )
                )
    return [jnp.concatenate(found, 0) for found in spread]


def turn_in(rows_minor, in_ref, out_ref, tiles, square):
    channels = ENTRY_CHANNELS
    rows, features = in_ref.shape
    count = features // LANES
    for tile in range(count):
        tiles[tile * rows : (tile + 1) * rows, :] = in_ref[:, tile * LANES : (tile + 1) * LANES]
    for group in range(rows // PACK):
        found = [tiles[strided(group * PACK + k, count, rows), :] for k in range(PACK)]
        for part in range(PACK):
            lanes = slice(part * channels, (part + 1) * channels)
            square[group, strided(part, count, PACK), :] = jnp.concatenate(
                [values[:, lanes] for values in found], 1
            )
        turned = square[group].T
        if rows_minor:
            for k in range(PACK):
                out_ref[strided(group * PACK + k, channels, rows), :] = turned[
                    k * channels : (k + 1) * channels
                ]
        else:
            out_ref[group * LANES : (group + 1) * LANES, :] = turned


def prepare_kernel(
    cotangent_hbm,
    right_hbm,
    left_hbm,
    weight_hbm,
    right_out,
    left_out,
    send_out,
    own_out,
    weight_out,
    inputs,
    tiles,
    square,
    semaphores,
):
    parity = lax.rem(lax.axis_index("blk"), 2)
    moves = (
        (right_hbm, inputs.at[0]),
        (left_hbm, inputs.at[1]),
        (cotangent_hbm.at[:, :, 1 - parity], send_out),
        (cotangent_hbm.at[:, :, parity], own_out),
        (weight_hbm, weight_out),
    )
    copies = [
        pltpu.make_async_copy(source, target, semaphores.at[at])
        for at, (source, target) in enumerate(moves)
    ]
    for copy in copies:
        copy.start()
    copies[0].wait()
    turn_in(True, inputs.at[0], right_out, tiles.at[0], square.at[0])
    copies[1].wait()
    turn_in(False, inputs.at[1], left_out, tiles.at[1], square.at[1])
    for copy in copies[2:]:
        copy.wait()


def turn_right_kernel(parts, *refs):
    part_refs, (out_ref, total, square, tiles) = refs[:parts], refs[parts:]
    channels = ENTRY_CHANNELS
    rows, features = out_ref.shape
    count = features // LANES
    total[...] = functools.reduce(jnp.add, [ref[0] for ref in part_refs])
    for group in range(rows // PACK):
        stacked = [total[strided(group * PACK + k, channels, rows), :] for k in range(PACK)]
        square[...] = jnp.concatenate(stacked, 0).T
        pieces = [square[strided(part, count, PACK), :] for part in range(PACK)]
        for k in range(PACK):
            lanes = slice(k * channels, (k + 1) * channels)
            tiles[strided(group * PACK + k, count, rows), :] = jnp.concatenate(
                [piece[:, lanes] for piece in pieces], 1
            )
    for tile in range(count):
        out_ref[:, tile * LANES : (tile + 1) * LANES] = tiles[tile * rows : (tile + 1) * rows, :]


def turn_left_kernel(parts, *refs):
    part_refs, (out_ref, total, tiles) = refs[:parts], refs[parts:]
    channels = ENTRY_CHANNELS
    size, width = part_refs[0].shape
    rows, features = out_ref.shape
    count = features // LANES
    found = functools.reduce(jnp.add, [ref[...] for ref in part_refs])
    for tile in range(width // LANES):
        total[tile * size : (tile + 1) * size, :] = found[:, tile * LANES : (tile + 1) * LANES]
    for tile in range(width // LANES):
        pieces = [total[strided(tile * size + part, count, PACK), :] for part in range(PACK)]
        for k in range(PACK):
            lanes = slice(k * channels, (k + 1) * channels)
            tiles[strided(tile * PACK + k, count, rows), :] = jnp.concatenate(
                [piece[:, lanes] for piece in pieces], 1
            )
    for tile in range(count):
        out_ref[:, tile * LANES : (tile + 1) * LANES] = tiles[tile * rows : (tile + 1) * rows, :]


def prepare_weight(weight_ref, weight_cat, fold):
    channels = ENTRY_CHANNELS
    for step in range(channels // fold):
        high, low = halves(folded_weight(weight_ref, step, fold))
        weight_cat[step * channels : (step + 1) * channels, :] = jnp.concatenate(
            [high, low, high], 1
        )


def gradient_phase(blocks, cotangent_ref, out_ref, weight_cat):
    fold = fold_of(blocks * cotangent_ref.shape[2])
    slots = slots_of(blocks)

    def step_of(pair, carry):
        high, low = spread_of(cotangent_ref, pair, slots, fold)
        found = dot_rows(weight_cat[...], jnp.concatenate([high, high, low], 1))
        out_ref[pair] = jnp.concatenate(halves(found), 1)
        return carry

    lax.fori_loop(0, out_ref.shape[0], step_of, 0)


def gradient_kernel(
    blocks, weight_ref, cotangent_ref, left_ref, out_ref, partial_ref, weight_cat, left_flip
):
    prepare_weight(weight_ref, weight_cat, fold_of(blocks * cotangent_ref.shape[2]))
    gradient_phase(blocks, cotangent_ref, out_ref, weight_cat)

    def store(step, found):
        partial_ref[step] = found

    right_phase(left_ref, out_ref, left_flip, store)


def right_phase(left_ref, factor_ref, left_flip, store):
    sequences = left_ref.shape[1]
    lanes = factor_ref.shape[2] // 4
    flip_high, flip_low = halves((left_ref[...] * (1.0 / sequences)).T)
    left_flip[:sequences, :] = flip_high
    left_flip[sequences:, :] = flip_low

    def step_of(step, carry):
        high, low = (
            jnp.concatenate(
                [rows_of_step([factor_ref], 2 * step + part, half, lanes) for part in range(2)], 1
            )
            for half in range(2)
        )
        first = dot(left_flip[...], high)
        second = dot(left_flip[:sequences, :], low)
        store(step, first[:sequences] + first[sequences:] + second)
        return carry

    lax.fori_loop(0, factor_ref.shape[1] // (2 * ENTRY_CHANNELS), step_of, 0)


def rows_of_step(refs, step, half, lanes):
    channels = ENTRY_CHANNELS
    rows = pl.ds(pl.multiple_of(step * channels, channels), channels)
    start = 2 * half * lanes
    return jnp.concatenate(
        [
            ref[pair, rows, start + part * lanes : start + (part + 1) * lanes]
            for ref in refs
            for pair in range(ref.shape[0])
            for part in range(2)
        ],
        0,
    )


def both_left(left_refs):
    sequences = left_refs[0].shape[1]
    return jnp.concatenate([ref[...] for ref in left_refs], 0) * (1.0 / sequences)


def right_kernel(
    blocks,
    weight_cat,
    cotangent_ref,
    left_ref,
    partial_ref,
    peer_ref,
    keep_ref,
    send_ref,
    left_flip,
):
    depth = cotangent_ref.shape[2]
    fold = fold_of(blocks * depth)
    lanes = fold * blocks * depth
    gradient_phase(blocks, cotangent_ref, peer_ref, weight_cat)

    def store(step, found):
        found = found + partial_ref[step]
        for part in range(2):
            turned = found[:, part * lanes : (part + 1) * lanes].T
            for place in range(fold):
                for slot in range(blocks):
                    start = (place * blocks + slot) * depth
                    row = pl.multiple_of(((2 * step + part) * fold + place) * depth, depth)
                    out_ref = send_ref if slot % 2 else keep_ref
                    out_ref[slot // 2, pl.ds(row, depth), :] = turned[start : start + depth]

    right_phase(left_ref, peer_ref, left_flip, store)


def halve_kernel(keep_ref, found_ref, keep_out, send_out):
    for slot in range(keep_ref.shape[0]):
        out_ref = send_out if slot % 2 else keep_out
        out_ref[slot // 2] = keep_ref[slot] + found_ref[slot]


def right_rows(right_refs, step, fold, depth):
    return jnp.concatenate(
        [
            ref[pl.ds(pl.multiple_of((step * fold + part) * depth, depth), depth), :]
            for part in range(fold)
            for ref in right_refs
        ],
        0,
    )


def weight_kernel(blocks, own_left, peer_left, own_cotangent, peer_cotangent, *refs):
    right_refs = refs[:blocks]
    keep_ref, send_ref, own_out, peer_out, own_ref, peer_ref, total, semaphores = refs[blocks:]
    channels = ENTRY_CHANNELS
    depth, pairs = own_cotangent.shape[2:]
    fold = fold_of(blocks * depth)
    lanes = fold * blocks * depth
    high, low = halves(both_left([own_left, peer_left]))
    left_cat = jnp.concatenate([high, low, high], 1)

    def copies(step):
        size = 2 * channels
        rows = pl.ds(pl.multiple_of(step * size, size), size)
        return [
            pltpu.make_async_copy(ref.at[:, rows], out.at[:, rows], semaphores.at[step, side])
            for side, (ref, out) in enumerate(((own_ref, own_out), (peer_ref, peer_out)))
        ]

    def outer_step(step, carry):
        right = [right_rows(right_refs, 2 * step + part, fold, depth) for part in range(2)]
        high, low = halves(jnp.concatenate(right, 0))
        found = dot_rows(left_cat, jnp.concatenate([high, high, low], 1))
        both = halves(found)
        for part in range(2):
            start = pl.multiple_of((2 * step + part) * channels, channels)
            row = 0
            for ref in (own_ref, peer_ref):
                for index in range(2 * ref.shape[0]):
                    for half in range(2):
                        lane = (2 * half + index % 2) * lanes
                        ref[index // 2, pl.ds(start, channels), lane : lane + lanes] = both[half][
                            row : row + channels, part * lanes : (part + 1) * lanes
                        ]
                    row += channels
        for copy in copies(step):
            copy.start()
        return carry

    lax.fori_loop(0, channels // (2 * fold), outer_step, 0)
    total[...] = jnp.zeros_like(total)

    def weight_step(pair, carry):
        lefts, rights = [], []
        for ref, cotangent_ref in ((own_ref, own_cotangent), (peer_ref, peer_cotangent)):
            high, low = spread_of(cotangent_ref, pair, slots_of(blocks), fold)
            lefts += [ref[pair], ref[pair, :, : 2 * lanes]]
            rights += [high, high, low]
        total[...] += dot(jnp.concatenate(lefts, 1), jnp.concatenate(rights, 0))
        return carry

    lax.fori_loop(0, own_ref.shape[0], weight_step, 0)
    core = lax.rem(lax.axis_index("inner"), 2)
    steps = channels // (2 * fold)
    for out_ref, half in ((keep_ref, core), (send_ref, 1 - core)):
        for step in range(steps):
            start = pl.multiple_of((half * steps + step) * channels, channels)
            found = total[pl.ds(start, channels), :]
            for part in range(fold):
                y = step * fold + part
                out_ref[y * channels : (y + 1) * channels, :] = found[
                    :, part * pairs : (part + 1) * pairs
                ]

    def finish(step, carry):
        for copy in copies(step):
            copy.wait()
        return carry

    lax.fori_loop(0, channels // (2 * fold), finish, 0)


def left_kernel(blocks, depth, own_ref, peer_ref, *refs):
    right_refs, (own_out, peer_out, total, flipped) = refs[:blocks], refs[blocks:]
    lanes = own_ref.shape[2] // 4
    fold = lanes // (blocks * depth)
    sequences = right_refs[0].shape[1]
    group = 4
    total[...] = jnp.zeros_like(total)

    def step_of(step, carry):
        steps = [group * step + part for part in range(group)]
        right = [right_rows(right_refs, at, fold, depth) for at in steps]
        high, low = halves(jnp.concatenate(right, 0))
        grads = [
            jnp.concatenate([rows_of_step([own_ref, peer_ref], at, half, lanes) for at in steps], 1)
            for half in range(2)
        ]
        both = dot(grads[0], jnp.concatenate([high, low], 1))
        total[...] += both[:, :sequences] + both[:, sequences:] + dot(grads[1], high)
        return carry

    lax.fori_loop(0, ENTRY_CHANNELS // (fold * group), step_of, 0)
    flipped[...] = total[...].T * (1.0 / sequences)
    inner, size, width = own_out.shape
    here = lax.axis_index("inner")
    for slot in range(inner):
        start = pl.multiple_of(lax.bitwise_xor(here, slot) * size, size)
        own_out[slot] = flipped[pl.ds(start, size), :width]
        peer_out[slot] = flipped[pl.ds(start, size), width:]


def left_add_kernel(own_ref, other_ref, *out_refs):
    for slot, ref in enumerate(out_refs):
        ref[...] = own_ref[slot] + other_ref[slot]


def pair_kernel(
    blocks,
    outer_hbm,
    weight_hbm,
    out_ref,
    outer_ref,
    weight_ref,
    weight_flip,
    weight_rows,
    semaphores,
):
    channels = ENTRY_CHANNELS
    depth, pairs = out_ref.shape[2:]
    count = outer_ref.shape[0]
    lanes = outer_ref.shape[2] // 4
    columns = blocks * depth
    fold = lanes // columns
    wide = fold * pairs

    def copy_of(pair):
        return pltpu.make_async_copy(outer_hbm.at[pair], outer_ref.at[pair], semaphores.at[pair])

    weight_copy = pltpu.make_async_copy(weight_hbm, weight_ref, semaphores.at[count])
    weight_copy.start()
    for pair in range(count):
        copy_of(pair).start()
    weight_copy.wait()
    for step in range(channels // fold):
        weight_rows[step * channels : (step + 1) * channels, :] = folded_weight(
            weight_ref, step, fold
        )
    flip_high, flip_low = halves(weight_rows[...].T)
    weight_flip[:wide, :] = flip_high
    weight_flip[wide:, :] = flip_low
    slots = slots_of(blocks)

    def step_of(pair, carry):
        copy_of(pair).wait()
        first = dot(weight_flip[...], outer_ref[pair, :, : 2 * lanes])
        second = dot(weight_flip[:wide, :], outer_ref[pair, :, 2 * lanes :])
        found = first[:wide] + first[wide:] + second
        for part in range(2):
            turned = []
            for place in range(fold):
                start = part * lanes
                piece = found[place * pairs : (place + 1) * pairs, start : start + lanes].T
                turned.append(piece[place * columns : (place + 1) * columns])
            turned = functools.reduce(jnp.add, turned)
            row = 2 * pair + part
            for slot in range(blocks):
                out_ref[row, slots[slot]] = turned[slot * depth : (slot + 1) * depth]
        return carry

    lax.fori_loop(0, count, step_of, 0)


def merge_kernel(own_ref, other_ref, out_ref, semaphores):
    parity = lax.rem(lax.axis_index("blk"), 2)
    copies = [
        pltpu.make_async_copy(ref, out_ref.at[:, :, side], semaphores.at[at])
        for at, (ref, side) in enumerate(((own_ref, parity), (other_ref, 1 - parity)))
    ]
    for copy in copies:
        copy.start()
    for copy in copies:
        copy.wait()


def spread_sum_kernel(in_ref, out_ref):
    found = in_ref[0]
    for part in range(1, in_ref.shape[0]):
        found = found + in_ref[part]
    for part in range(in_ref.shape[0]):
        out_ref[part] = found


def place_kernel(mine_ref, other_ref, out_ref):
    channels = ENTRY_CHANNELS
    core = lax.rem(lax.axis_index("inner"), 2)
    steps = mine_ref.shape[0] // channels
    for ref, half in ((mine_ref, core), (other_ref, 1 - core)):
        for step in range(steps):
            rows = ref[step * channels : (step + 1) * channels, :]
            out_ref[strided(half * steps + step, channels, channels), :] = rows


def shape(*sizes, kind=F32):
    return jax.ShapeDtypeStruct(sizes, kind)


def call(kernel, out_shape, scratch=(), name=None, limit=16 * MIB, far=(), after=(), out_specs=None):
    def run(*operands):
        vmem = pl.BlockSpec(memory_space=pltpu.VMEM)
        hbm = pl.BlockSpec(memory_space=pltpu.HBM)
        in_specs = [pl.BlockSpec(memory_space=pl.ANY)] * len(after)
        in_specs += [hbm if at in far else vmem for at in range(len(operands))]
        operands = [
            pltpu.with_memory_space_constraint(operand, pltpu.HBM) if at in far else operand
            for at, operand in enumerate(operands)
        ]
        extra = {} if out_specs is None else {"out_specs": out_specs}
        return pl.pallas_call(
            lambda *refs: kernel(*refs[len(after) :]),
            out_shape=out_shape,
            in_specs=in_specs,
            scratch_shapes=list(scratch),
            compiler_params=pltpu.CompilerParams(vmem_limit_bytes=limit),
            cost_estimate=pl.CostEstimate(flops=1, bytes_accessed=1, transcendentals=0),
            name=name,
            **extra,
        )(*after, *operands)

    return run


def local(alignment_left, alignment_right, projection_matrix, cotangent):
    rows, features = alignment_left.shape
    depth = alignment_right.shape[0]
    count = lax.axis_size("blk")
    inner = lax.axis_size("inner")
    channels = ENTRY_CHANNELS
    sequences = features // channels
    outer, pairs = projection_matrix.shape
    blocks = count // 2
    fold = fold_of(blocks * depth)
    lanes = fold * blocks * depth
    tall = outer // fold
    steps = channels // fold
    row_pairs = rows // 2
    everyone = ("blk", "inner")

    partner = [(here, here ^ 1) for here in range(count)]
    slot_moves = [[(here, here ^ (2 * slot)) for here in range(count)] for slot in range(blocks)]
    inner_moves = [[(here, here ^ slot) for here in range(inner)] for slot in range(inner)]
    cores = [(here, here ^ 1) for here in range(inner)]
    core_groups = [list(range(core, count * inner, 2)) for core in range(2)]

    limit = 20 * MIB * max(1, blocks * depth * fold // LANES * 2 // fold)
    large = functools.partial(call, limit=limit)

    by_side = cotangent.reshape(rows, blocks, 2, depth, pairs)
    half_cotangent = shape(rows, blocks, depth, pairs)
    right, left, cotangent_send, cotangent_own, weight = call(
        prepare_kernel,
        [
            shape(channels * depth, sequences),
            shape(rows * channels, sequences),
            half_cotangent,
            half_cotangent,
            shape(outer, pairs),
        ],
        [
            pltpu.VMEM((2, rows, features), F32),
            pltpu.VMEM((2, rows * features // LANES, LANES), F32),
            pltpu.VMEM((2, rows // PACK, LANES, LANES), F32),
            pltpu.SemaphoreType.DMA((5,)),
        ],
        name="prepare",
        far=range(4),
    )(by_side, alignment_right, alignment_left, projection_matrix)
    rights = [right]
    for slot in range(1, blocks):
        rights.append(lax.ppermute(right, "blk", slot_moves[slot]))
    cotangent_peer = lax.ppermute(cotangent_send, "blk", partner)
    left_peer = lax.ppermute(left, "blk", partner)

    factor = shape(row_pairs, tall, 4 * lanes, kind=BF16)
    factor_scratch = pltpu.VMEM(factor.shape, BF16)
    weight_cat = shape(tall, 3 * fold * pairs, kind=BF16)
    flip_scratch = pltpu.VMEM((2 * sequences, rows * channels), BF16)
    grad_own, partial, weight_cat = large(
        functools.partial(gradient_kernel, blocks),
        [factor, shape(steps // 2, sequences, 2 * lanes), weight_cat],
        [flip_scratch],
        "gradient_own",
    )(weight, cotangent_own, left)
    right_half = shape(blocks // 2, channels * depth, sequences)
    grad_peer, right_keep, right_send = large(
        functools.partial(right_kernel, blocks),
        [factor, right_half, right_half],
        [flip_scratch],
        "right_parts",
    )(weight_cat, cotangent_peer, left_peer, partial)

    vmem = pl.BlockSpec(memory_space=pltpu.VMEM)
    hbm = pl.BlockSpec(memory_space=pltpu.HBM)
    keep, send, outer_own, outer_peer = large(
        functools.partial(weight_kernel, blocks),
        [shape(outer // 2, pairs)] * 2 + [pltpu.HBM(factor.shape, BF16)] * 2,
        [
            factor_scratch,
            factor_scratch,
            pltpu.VMEM((tall, fold * pairs), F32),
            pltpu.SemaphoreType.DMA((steps // 2, 2)),
        ],
        "weight",
        after=[right_keep],
        out_specs=[vmem, vmem, hbm, hbm],
    )(left, left_peer, cotangent_own, cotangent_peer, *rights)
    sent = lax.ppermute(send, "inner", cores)

    size = sequences // inner
    left_own, left_other = large(
        functools.partial(left_kernel, blocks, depth),
        [shape(inner, size, rows * channels)] * 2,
        [
            pltpu.VMEM((2 * rows * channels, sequences), F32),
            pltpu.VMEM((sequences, 2 * rows * channels), F32),
        ],
        "left_parts",
        after=[keep],
    )(grad_own, grad_peer, *rights)
    left_other = lax.ppermute(left_other, "blk", partner)
    keep, left_own, right_send = lax.optimization_barrier((keep, left_own, right_send))
    right_send = lax.ppermute(right_send, "blk", slot_moves[1])
    slot = 2
    while slot < blocks:
        part = shape(blocks // (2 * slot), channels * depth, sequences)
        right_keep, right_send = call(halve_kernel, [part, part], name="right_halve")(
            right_keep, right_send
        )
        right_send = lax.ppermute(right_send, "blk", slot_moves[slot])
        slot = 2 * slot
    members = count * inner // 2
    pieces = (keep + sent).reshape(members, outer // 2 // members, pairs)

    def pair(values, after, name):
        return large(
            functools.partial(pair_kernel, blocks),
            shape(rows, blocks, depth, pairs),
            [
                factor_scratch,
                pltpu.VMEM((outer, pairs), F32),
                pltpu.VMEM((2 * fold * pairs, tall), BF16),
                pltpu.VMEM((tall, fold * pairs), F32),
                pltpu.SemaphoreType.DMA((row_pairs + 1,)),
            ],
            name,
            far=[0, 1],
            after=after,
        )(values, projection_matrix)

    pair_other = pair(outer_peer, [pieces], "pair_peer")
    pair_found = lax.ppermute(pair_other, "blk", partner)

    pieces = lax.all_to_all(pieces, everyone, 0, 0, axis_index_groups=core_groups)
    left_found = call(
        left_add_kernel,
        [shape(size, rows * channels)] * inner,
        name="left_add",
        after=[pieces],
    )(left_own, left_other)
    pieces = call(
        spread_sum_kernel,
        shape(*pieces.shape),
        name="weight_sum",
        after=[pair_other, left_found[0], right_keep],
    )(pieces)
    pair_own = pair(outer_own, [pieces], "pair_own")
    pieces = lax.all_to_all(pieces, everyone, 0, 0, axis_index_groups=core_groups)

    left_found = [
        lax.ppermute(part, "inner", inner_moves[slot]) if slot else part
        for slot, part in enumerate(left_found)
    ]
    grad_left = call(
        functools.partial(turn_left_kernel, inner),
        shape(rows, features // inner),
        [
            pltpu.VMEM((size * rows * channels // LANES, LANES), F32),
            pltpu.VMEM((rows * features // inner // LANES, LANES), F32),
        ],
        name="turn_left",
    )(*left_found)

    grad_right = call(
        functools.partial(turn_right_kernel, 2),
        shape(depth, features),
        [
            pltpu.VMEM((channels * depth, sequences), F32),
            pltpu.VMEM((LANES, LANES), F32),
            pltpu.VMEM((depth * features // LANES, LANES), F32),
        ],
        name="turn_right",
    )(right_keep, right_send)

    pair_update = call(
        merge_kernel,
        pltpu.HBM(by_side.shape, F32),
        [pltpu.SemaphoreType.DMA((2,))],
        "merge",
        out_specs=hbm,
    )(pair_own, pair_found)
    pair_update = pair_update.reshape(cotangent.shape)

    pieces, pair_update, grad_left, grad_right = lax.optimization_barrier(
        (pieces, pair_update, grad_left, grad_right)
    )
    mine = pieces.reshape(outer // 2, pairs)
    other = lax.ppermute(mine, "inner", cores)
    grad_weight = call(place_kernel, shape(outer, pairs), name="place")(mine, other)
    return (pair_update, grad_left, grad_right, grad_weight)


def solution(mesh):
    placed = (
        P(("groups", "blk"), None),
        P(("groups", "blk", "inner"), None),
        P(),
        P(("groups", "blk"), None, "inner", None),
    )
    return jax.shard_map(
        local,
        mesh=mesh,
        in_specs=placed,
        out_specs=(
            P(("groups", "blk"), None, "inner", None),
            P(("groups", "blk"), "inner"),
            P(("groups", "blk", "inner"), None),
            P("groups", None),
        ),
        check_vma=False,
    )
```

```python
import functools

import jax
import jax.numpy as jnp
from jax import lax
from jax.experimental import pallas as pl
from jax.experimental.pallas import tpu as pltpu
from jax.sharding import PartitionSpec as P

ENTRY_CHANNELS = 32
LANES = 128
PACK = LANES // ENTRY_CHANNELS
F32 = jnp.float32
BF16 = jnp.bfloat16
MIB = 1024 * 1024


def halves(values):
    high = values.astype(BF16)
    low = (values - high.astype(F32)).astype(BF16)
    return high, low


def dot(left, right):
    return jnp.dot(left, right, preferred_element_type=F32)


def dot_rows(left, right):
    return lax.dot_general(left, right, (((1,), (1,)), ((), ())), preferred_element_type=F32)


def fold_of(columns):
    return max(1, LANES // columns)


def strided(start, size, stride):
    return pl.ds(start, size, stride=stride)


def folded_weight(weight_ref, step, fold):
    channels = ENTRY_CHANNELS
    return jnp.concatenate(
        [weight_ref[strided(step * fold + part, channels, channels), :] for part in range(fold)], 1
    )


def slots_of(blocks):
    here = lax.axis_index("blk") // 2
    return [lax.bitwise_xor(here, slot) for slot in range(blocks)]


def spread_of(cotangent_ref, pair, slots, fold):
    columns = len(slots) * cotangent_ref.shape[2]
    empty = jnp.zeros((columns, cotangent_ref.shape[3]), BF16)
    spread = ([], [])
    for part in range(2):
        rows = jnp.concatenate([cotangent_ref[2 * pair + part, slot] for slot in slots], 0)
        for found, values in zip(spread, halves(rows)):
            for place in range(fold):
                found.append(
                    jnp.concatenate(
                        [values if place == other else empty for other in range(fold)], 1
                    )
                )
    return [jnp.concatenate(found, 0) for found in spread]


def turn_in(rows_minor, in_ref, out_ref, tiles, square):
    channels = ENTRY_CHANNELS
    rows, features = in_ref.shape
    count = features // LANES
    for tile in range(count):
        tiles[tile * rows : (tile + 1) * rows, :] = in_ref[:, tile * LANES : (tile + 1) * LANES]
    for group in range(rows // PACK):
        found = [tiles[strided(group * PACK + k, count, rows), :] for k in range(PACK)]
        for part in range(PACK):
            lanes = slice(part * channels, (part + 1) * channels)
            square[group, strided(part, count, PACK), :] = jnp.concatenate(
                [values[:, lanes] for values in found], 1
            )
        turned = square[group].T
        if rows_minor:
            for k in range(PACK):
                out_ref[strided(group * PACK + k, channels, rows), :] = turned[
                    k * channels : (k + 1) * channels
                ]
        else:
            out_ref[group * LANES : (group + 1) * LANES, :] = turned


def prepare_kernel(
    cotangent_hbm,
    right_hbm,
    left_hbm,
    weight_hbm,
    right_out,
    left_out,
    send_out,
    own_out,
    weight_out,
    inputs,
    tiles,
    square,
    semaphores,
):
    parity = lax.rem(lax.axis_index("blk"), 2)
    moves = (
        (right_hbm, inputs.at[0]),
        (left_hbm, inputs.at[1]),
        (cotangent_hbm.at[:, :, 1 - parity], send_out),
        (cotangent_hbm.at[:, :, parity], own_out),
        (weight_hbm, weight_out),
    )
    copies = [
        pltpu.make_async_copy(source, target, semaphores.at[at])
        for at, (source, target) in enumerate(moves)
    ]
    for copy in copies:
        copy.start()
    copies[0].wait()
    turn_in(True, inputs.at[0], right_out, tiles.at[0], square.at[0])
    copies[1].wait()
    turn_in(False, inputs.at[1], left_out, tiles.at[1], square.at[1])
    for copy in copies[2:]:
        copy.wait()


def turn_right_kernel(in_ref, out_ref, square, tiles):
    channels = ENTRY_CHANNELS
    rows, features = out_ref.shape
    count = features // LANES
    for group in range(rows // PACK):
        stacked = [in_ref[strided(group * PACK + k, channels, rows), :] for k in range(PACK)]
        square[group] = jnp.concatenate(stacked, 0).T
        pieces = [square[group, strided(part, count, PACK), :] for part in range(PACK)]
        for k in range(PACK):
            lanes = slice(k * channels, (k + 1) * channels)
            tiles[strided(group * PACK + k, count, rows), :] = jnp.concatenate(
                [piece[:, lanes] for piece in pieces], 1
            )
    for tile in range(count):
        out_ref[:, tile * LANES : (tile + 1) * LANES] = tiles[tile * rows : (tile + 1) * rows, :]


def turn_left_kernel(parts, *refs):
    part_refs, (out_ref, total, tiles) = refs[:parts], refs[parts:]
    channels = ENTRY_CHANNELS
    size, width = part_refs[0].shape
    rows, features = out_ref.shape
    count = features // LANES
    found = functools.reduce(jnp.add, [ref[...] for ref in part_refs])
    for tile in range(width // LANES):
        total[tile * size : (tile + 1) * size, :] = found[:, tile * LANES : (tile + 1) * LANES]
    for tile in range(width // LANES):
        pieces = [total[strided(tile * size + part, count, PACK), :] for part in range(PACK)]
        for k in range(PACK):
            lanes = slice(k * channels, (k + 1) * channels)
            tiles[strided(tile * PACK + k, count, rows), :] = jnp.concatenate(
                [piece[:, lanes] for piece in pieces], 1
            )
    for tile in range(count):
        out_ref[:, tile * LANES : (tile + 1) * LANES] = tiles[tile * rows : (tile + 1) * rows, :]


def prepare_weight(weight_ref, weight_cat, fold):
    channels = ENTRY_CHANNELS
    for step in range(channels // fold):
        high, low = halves(folded_weight(weight_ref, step, fold))
        weight_cat[step * channels : (step + 1) * channels, :] = jnp.concatenate(
            [high, low, high], 1
        )


def gradient_phase(blocks, cotangent_ref, factor_ref, out_hbm, weight_cat, semaphores):
    fold = fold_of(blocks * cotangent_ref.shape[2])
    slots = slots_of(blocks)

    def copy_of(pair):
        return pltpu.make_async_copy(factor_ref.at[pair], out_hbm.at[pair], semaphores.at[pair])

    def step_of(pair, carry):
        high, low = spread_of(cotangent_ref, pair, slots, fold)
        found = dot_rows(weight_cat[...], jnp.concatenate([high, high, low], 1))
        factor_ref[pair] = jnp.concatenate(halves(found), 1)
        copy_of(pair).start()
        return carry

    lax.fori_loop(0, factor_ref.shape[0], step_of, 0)
    return [copy_of(pair) for pair in range(factor_ref.shape[0])]


def gradient_kernel(
    blocks,
    weight_ref,
    cotangent_ref,
    left_ref,
    out_hbm,
    partial_ref,
    weight_cat,
    factor_ref,
    left_flip,
    semaphores,
):
    prepare_weight(weight_ref, weight_cat, fold_of(blocks * cotangent_ref.shape[2]))
    copies = gradient_phase(blocks, cotangent_ref, factor_ref, out_hbm, weight_cat, semaphores)

    def store(step, found):
        partial_ref[step] = found

    right_phase(left_ref, factor_ref, left_flip, store)
    for copy in copies:
        copy.wait()


def right_phase(left_ref, factor_ref, left_flip, store):
    sequences = left_ref.shape[1]
    lanes = factor_ref.shape[2] // 4
    flip_high, flip_low = halves((left_ref[...] * (1.0 / sequences)).T)
    left_flip[:sequences, :] = flip_high
    left_flip[sequences:, :] = flip_low

    def step_of(step, carry):
        high, low = (
            jnp.concatenate(
                [rows_of_step([factor_ref], 2 * step + part, half, lanes) for part in range(2)], 1
            )
            for half in range(2)
        )
        first = dot(left_flip[...], high)
        second = dot(left_flip[:sequences, :], low)
        store(step, first[:sequences] + first[sequences:] + second)
        return carry

    lax.fori_loop(0, factor_ref.shape[1] // (2 * ENTRY_CHANNELS), step_of, 0)


def rows_of_step(refs, step, half, lanes):
    channels = ENTRY_CHANNELS
    rows = pl.ds(pl.multiple_of(step * channels, channels), channels)
    start = 2 * half * lanes
    return jnp.concatenate(
        [
            ref[pair, rows, start + part * lanes : start + (part + 1) * lanes]
            for ref in refs
            for pair in range(ref.shape[0])
            for part in range(2)
        ],
        0,
    )


def both_left(left_refs):
    sequences = left_refs[0].shape[1]
    return jnp.concatenate([ref[...] for ref in left_refs], 0) * (1.0 / sequences)


def right_kernel(
    blocks,
    weight_cat,
    cotangent_ref,
    left_ref,
    partial_ref,
    out_hbm,
    out_ref,
    factor_ref,
    left_flip,
    semaphores,
):
    depth = cotangent_ref.shape[2]
    fold = fold_of(blocks * depth)
    lanes = fold * blocks * depth
    copies = gradient_phase(blocks, cotangent_ref, factor_ref, out_hbm, weight_cat, semaphores)
    slots = slots_of(blocks)

    def store(step, found):
        found = found + partial_ref[step]
        for part in range(2):
            turned = found[:, part * lanes : (part + 1) * lanes].T
            for place in range(fold):
                for slot in range(blocks):
                    start = (place * blocks + slot) * depth
                    row = pl.multiple_of(((2 * step + part) * fold + place) * depth, depth)
                    out_ref[slots[slot], pl.ds(row, depth), :] = turned[start : start + depth]

    right_phase(left_ref, factor_ref, left_flip, store)
    for copy in copies:
        copy.wait()


def right_rows(right_refs, step, fold, depth):
    return jnp.concatenate(
        [
            ref[pl.ds(pl.multiple_of((step * fold + part) * depth, depth), depth), :]
            for part in range(fold)
            for ref in right_refs
        ],
        0,
    )


def weight_kernel(blocks, own_left, peer_left, own_cotangent, peer_cotangent, *refs):
    right_refs = refs[:blocks]
    keep_ref, send_ref, own_out, peer_out, own_ref, peer_ref, total, semaphores = refs[blocks:]
    channels = ENTRY_CHANNELS
    depth, pairs = own_cotangent.shape[2:]
    fold = fold_of(blocks * depth)
    lanes = fold * blocks * depth
    high, low = halves(both_left([own_left, peer_left]))
    left_cat = jnp.concatenate([high, low, high], 1)

    def copies(step):
        size = 2 * channels
        rows = pl.ds(pl.multiple_of(step * size, size), size)
        return [
            pltpu.make_async_copy(ref.at[:, rows], out.at[:, rows], semaphores.at[step, side])
            for side, (ref, out) in enumerate(((own_ref, own_out), (peer_ref, peer_out)))
        ]

    def outer_step(step, carry):
        right = [right_rows(right_refs, 2 * step + part, fold, depth) for part in range(2)]
        high, low = halves(jnp.concatenate(right, 0))
        found = dot_rows(left_cat, jnp.concatenate([high, high, low], 1))
        both = halves(found)
        for part in range(2):
            start = pl.multiple_of((2 * step + part) * channels, channels)
            row = 0
            for ref in (own_ref, peer_ref):
                for index in range(2 * ref.shape[0]):
                    for half in range(2):
                        lane = (2 * half + index % 2) * lanes
                        ref[index // 2, pl.ds(start, channels), lane : lane + lanes] = both[half][
                            row : row + channels, part * lanes : (part + 1) * lanes
                        ]
                    row += channels
        for copy in copies(step):
            copy.start()
        return carry

    lax.fori_loop(0, channels // (2 * fold), outer_step, 0)
    total[...] = jnp.zeros_like(total)

    def weight_step(pair, carry):
        lefts, rights = [], []
        for ref, cotangent_ref in ((own_ref, own_cotangent), (peer_ref, peer_cotangent)):
            high, low = spread_of(cotangent_ref, pair, slots_of(blocks), fold)
            lefts += [ref[pair], ref[pair, :, : 2 * lanes]]
            rights += [high, high, low]
        total[...] += dot(jnp.concatenate(lefts, 1), jnp.concatenate(rights, 0))
        return carry

    lax.fori_loop(0, own_ref.shape[0], weight_step, 0)
    core = lax.rem(lax.axis_index("inner"), 2)
    steps = channels // (2 * fold)
    for out_ref, half in ((keep_ref, core), (send_ref, 1 - core)):
        for step in range(steps):
            start = pl.multiple_of((half * steps + step) * channels, channels)
            found = total[pl.ds(start, channels), :]
            for part in range(fold):
                y = step * fold + part
                out_ref[y * channels : (y + 1) * channels, :] = found[
                    :, part * pairs : (part + 1) * pairs
                ]

    def finish(step, carry):
        for copy in copies(step):
            copy.wait()
        return carry

    lax.fori_loop(0, channels // (2 * fold), finish, 0)


def left_kernel(blocks, depth, own_hbm, peer_hbm, *refs):
    right_refs, refs = refs[:blocks], refs[blocks:]
    own_out, peer_out, own_ref, peer_ref, total, flipped, semaphores = refs
    lanes = own_ref.shape[2] // 4
    fold = lanes // (blocks * depth)
    sequences = right_refs[0].shape[1]
    group = 4
    count = ENTRY_CHANNELS // (fold * group)

    def copies(step):
        size = group * ENTRY_CHANNELS
        rows = pl.ds(pl.multiple_of(step * size, size), size)
        return [
            pltpu.make_async_copy(hbm.at[:, rows], ref.at[:, rows], semaphores.at[step, side])
            for side, (hbm, ref) in enumerate(((own_hbm, own_ref), (peer_hbm, peer_ref)))
        ]

    for step in range(count):
        for copy in copies(step):
            copy.start()
    total[...] = jnp.zeros_like(total)

    def step_of(step, carry):
        for copy in copies(step):
            copy.wait()
        steps = [group * step + part for part in range(group)]
        right = [right_rows(right_refs, at, fold, depth) for at in steps]
        high, low = halves(jnp.concatenate(right, 0))
        grads = [
            jnp.concatenate([rows_of_step([own_ref, peer_ref], at, half, lanes) for at in steps], 1)
            for half in range(2)
        ]
        both = dot(grads[0], jnp.concatenate([high, low], 1))
        total[...] += both[:, :sequences] + both[:, sequences:] + dot(grads[1], high)
        return carry

    lax.fori_loop(0, count, step_of, 0)
    flipped[...] = total[...].T * (1.0 / sequences)
    inner, size, width = own_out.shape
    here = lax.axis_index("inner")
    for slot in range(inner):
        start = pl.multiple_of(lax.bitwise_xor(here, slot) * size, size)
        own_out[slot] = flipped[pl.ds(start, size), :width]
        peer_out[slot] = flipped[pl.ds(start, size), width:]


def left_add_kernel(own_ref, other_ref, *out_refs):
    for slot, ref in enumerate(out_refs):
        ref[...] = own_ref[slot] + other_ref[slot]


def pair_kernel(
    blocks,
    outer_hbm,
    weight_hbm,
    out_ref,
    outer_ref,
    weight_ref,
    weight_flip,
    weight_rows,
    semaphores,
):
    channels = ENTRY_CHANNELS
    depth, pairs = out_ref.shape[2:]
    count = outer_ref.shape[0]
    lanes = outer_ref.shape[2] // 4
    columns = blocks * depth
    fold = lanes // columns
    wide = fold * pairs

    def copy_of(pair):
        return pltpu.make_async_copy(outer_hbm.at[pair], outer_ref.at[pair], semaphores.at[pair])

    weight_copy = pltpu.make_async_copy(weight_hbm, weight_ref, semaphores.at[count])
    weight_copy.start()
    for pair in range(count):
        copy_of(pair).start()
    weight_copy.wait()
    for step in range(channels // fold):
        weight_rows[step * channels : (step + 1) * channels, :] = folded_weight(
            weight_ref, step, fold
        )
    flip_high, flip_low = halves(weight_rows[...].T)
    weight_flip[:wide, :] = flip_high
    weight_flip[wide:, :] = flip_low
    slots = slots_of(blocks)

    def step_of(pair, carry):
        copy_of(pair).wait()
        first = dot(weight_flip[...], outer_ref[pair, :, : 2 * lanes])
        second = dot(weight_flip[:wide, :], outer_ref[pair, :, 2 * lanes :])
        found = first[:wide] + first[wide:] + second
        for part in range(2):
            turned = []
            for place in range(fold):
                start = part * lanes
                piece = found[place * pairs : (place + 1) * pairs, start : start + lanes].T
                turned.append(piece[place * columns : (place + 1) * columns])
            turned = functools.reduce(jnp.add, turned)
            row = 2 * pair + part
            for slot in range(blocks):
                out_ref[row, slots[slot]] = turned[slot * depth : (slot + 1) * depth]
        return carry

    lax.fori_loop(0, count, step_of, 0)


def merge_kernel(own_ref, other_ref, out_ref, semaphores):
    parity = lax.rem(lax.axis_index("blk"), 2)
    copies = [
        pltpu.make_async_copy(ref, out_ref.at[:, :, side], semaphores.at[at])
        for at, (ref, side) in enumerate(((own_ref, parity), (other_ref, 1 - parity)))
    ]
    for copy in copies:
        copy.start()
    for copy in copies:
        copy.wait()


def spread_sum_kernel(in_ref, out_ref):
    found = in_ref[0]
    for part in range(1, in_ref.shape[0]):
        found = found + in_ref[part]
    for part in range(in_ref.shape[0]):
        out_ref[part] = found


def place_kernel(mine_ref, other_ref, out_ref):
    channels = ENTRY_CHANNELS
    core = lax.rem(lax.axis_index("inner"), 2)
    steps = mine_ref.shape[0] // channels
    for ref, half in ((mine_ref, core), (other_ref, 1 - core)):
        for step in range(steps):
            rows = ref[step * channels : (step + 1) * channels, :]
            out_ref[strided(half * steps + step, channels, channels), :] = rows


def shape(*sizes, kind=F32):
    return jax.ShapeDtypeStruct(sizes, kind)


def call(kernel, out_shape, scratch=(), name=None, limit=16 * MIB, far=(), after=(), out_specs=None):
    def run(*operands):
        vmem = pl.BlockSpec(memory_space=pltpu.VMEM)
        hbm = pl.BlockSpec(memory_space=pltpu.HBM)
        in_specs = [pl.BlockSpec(memory_space=pl.ANY)] * len(after)
        in_specs += [hbm if at in far else vmem for at in range(len(operands))]
        operands = [
            pltpu.with_memory_space_constraint(operand, pltpu.HBM) if at in far else operand
            for at, operand in enumerate(operands)
        ]
        extra = {} if out_specs is None else {"out_specs": out_specs}
        return pl.pallas_call(
            lambda *refs: kernel(*refs[len(after) :]),
            out_shape=out_shape,
            in_specs=in_specs,
            scratch_shapes=list(scratch),
            compiler_params=pltpu.CompilerParams(vmem_limit_bytes=limit),
            cost_estimate=pl.CostEstimate(flops=1, bytes_accessed=1, transcendentals=0),
            name=name,
            **extra,
        )(*after, *operands)

    return run


def local(alignment_left, alignment_right, projection_matrix, cotangent):
    rows, features = alignment_left.shape
    depth = alignment_right.shape[0]
    count = lax.axis_size("blk")
    inner = lax.axis_size("inner")
    channels = ENTRY_CHANNELS
    sequences = features // channels
    outer, pairs = projection_matrix.shape
    blocks = count // 2
    fold = fold_of(blocks * depth)
    lanes = fold * blocks * depth
    tall = outer // fold
    steps = channels // fold
    row_pairs = rows // 2
    everyone = ("blk", "inner")

    partner = [(here, here ^ 1) for here in range(count)]
    slot_moves = [[(here, here ^ (2 * slot)) for here in range(count)] for slot in range(blocks)]
    same_parity = [[2 * block + side for block in range(blocks)] for side in range(2)]
    inner_moves = [[(here, here ^ slot) for here in range(inner)] for slot in range(inner)]
    cores = [(here, here ^ 1) for here in range(inner)]
    core_groups = [list(range(core, count * inner, 2)) for core in range(2)]

    limit = 20 * MIB * max(1, blocks * depth * fold // LANES * 2 // fold)
    large = functools.partial(call, limit=limit)

    by_side = cotangent.reshape(rows, blocks, 2, depth, pairs)
    half_cotangent = shape(rows, blocks, depth, pairs)
    right, left, cotangent_send, cotangent_own, weight = call(
        prepare_kernel,
        [
            shape(channels * depth, sequences),
            shape(rows * channels, sequences),
            half_cotangent,
            half_cotangent,
            shape(outer, pairs),
        ],
        [
            pltpu.VMEM((2, rows, features), F32),
            pltpu.VMEM((2, rows * features // LANES, LANES), F32),
            pltpu.VMEM((2, rows // PACK, LANES, LANES), F32),
            pltpu.SemaphoreType.DMA((5,)),
        ],
        name="prepare",
        far=range(4),
    )(by_side, alignment_right, alignment_left, projection_matrix)
    rights = [right]
    for slot in range(1, blocks):
        rights.append(lax.ppermute(right, "blk", slot_moves[slot]))
    cotangent_peer = lax.ppermute(cotangent_send, "blk", partner)
    left_peer = lax.ppermute(left, "blk", partner)

    vmem = pl.BlockSpec(memory_space=pltpu.VMEM)
    hbm = pl.BlockSpec(memory_space=pltpu.HBM)
    factor = shape(row_pairs, tall, 4 * lanes, kind=BF16)
    factor_scratch = pltpu.VMEM(factor.shape, BF16)
    weight_cat = shape(tall, 3 * fold * pairs, kind=BF16)
    flip_scratch = pltpu.VMEM((2 * sequences, rows * channels), BF16)
    factor_hbm = pltpu.HBM(factor.shape, BF16)
    factor_copies = pltpu.SemaphoreType.DMA((row_pairs,))
    grad_own, partial, weight_cat = large(
        functools.partial(gradient_kernel, blocks),
        [factor_hbm, shape(steps // 2, sequences, 2 * lanes), weight_cat],
        [factor_scratch, flip_scratch, factor_copies],
        "gradient_own",
        out_specs=[hbm, vmem, vmem],
    )(weight, cotangent_own, left)
    grad_peer, right_parts = large(
        functools.partial(right_kernel, blocks),
        [factor_hbm, shape(blocks, channels * depth, sequences)],
        [factor_scratch, flip_scratch, factor_copies],
        "right_parts",
        out_specs=[hbm, vmem],
    )(weight_cat, cotangent_peer, left_peer, partial)
    right_sum = lax.psum_scatter(
        right_parts, "blk", scatter_dimension=0, axis_index_groups=same_parity
    )

    keep, send, outer_own, outer_peer = large(
        functools.partial(weight_kernel, blocks),
        [shape(outer // 2, pairs)] * 2 + [factor_hbm] * 2,
        [
            factor_scratch,
            factor_scratch,
            pltpu.VMEM((tall, fold * pairs), F32),
            pltpu.SemaphoreType.DMA((steps // 2, 2)),
        ],
        "weight",
        after=[right_parts],
        out_specs=[vmem, vmem, hbm, hbm],
    )(left, left_peer, cotangent_own, cotangent_peer, *rights)
    sent = lax.ppermute(send, "inner", cores)

    size = sequences // inner
    left_own, left_other = large(
        functools.partial(left_kernel, blocks, depth),
        [shape(inner, size, rows * channels)] * 2,
        [
            factor_scratch,
            factor_scratch,
            pltpu.VMEM((2 * rows * channels, sequences), F32),
            pltpu.VMEM((sequences, 2 * rows * channels), F32),
            pltpu.SemaphoreType.DMA((steps // 4, 2)),
        ],
        "left_parts",
        far=[0, 1],
        after=[keep],
    )(grad_own, grad_peer, *rights)
    left_other = lax.ppermute(left_other, "blk", partner)
    keep, left_own = lax.optimization_barrier((keep, left_own))
    members = count * inner // 2
    pieces = (keep + sent).reshape(members, outer // 2 // members, pairs)

    def pair(values, after, name):
        return large(
            functools.partial(pair_kernel, blocks),
            shape(rows, blocks, depth, pairs),
            [
                factor_scratch,
                pltpu.VMEM((outer, pairs), F32),
                pltpu.VMEM((2 * fold * pairs, tall), BF16),
                pltpu.VMEM((tall, fold * pairs), F32),
                pltpu.SemaphoreType.DMA((row_pairs + 1,)),
            ],
            name,
            far=[0, 1],
            after=after,
        )(values, projection_matrix)

    pair_other = pair(outer_peer, [pieces], "pair_peer")
    pair_found = lax.ppermute(pair_other, "blk", partner)

    pieces = lax.all_to_all(pieces, everyone, 0, 0, axis_index_groups=core_groups)
    left_found = call(
        left_add_kernel,
        [shape(size, rows * channels)] * inner,
        name="left_add",
        after=[pieces],
    )(left_own, left_other)
    pieces = call(
        spread_sum_kernel,
        shape(*pieces.shape),
        name="weight_sum",
        after=[pair_other],
    )(pieces)
    pair_own = pair(outer_own, [pieces], "pair_own")
    pieces = lax.all_to_all(pieces, everyone, 0, 0, axis_index_groups=core_groups)

    left_found = [
        lax.ppermute(part, "inner", inner_moves[slot]) if slot else part
        for slot, part in enumerate(left_found)
    ]
    grad_left = call(
        functools.partial(turn_left_kernel, inner),
        shape(rows, features // inner),
        [
            pltpu.VMEM((size * rows * channels // LANES, LANES), F32),
            pltpu.VMEM((rows * features // inner // LANES, LANES), F32),
        ],
        name="turn_left",
    )(*left_found)

    grad_right = call(
        turn_right_kernel,
        shape(depth, features),
        [
            pltpu.VMEM((depth // PACK, LANES, LANES), F32),
            pltpu.VMEM((depth * features // LANES, LANES), F32),
        ],
        name="turn_right",
    )(right_sum)

    pair_update = call(
        merge_kernel,
        pltpu.HBM(by_side.shape, F32),
        [pltpu.SemaphoreType.DMA((2,))],
        "merge",
        out_specs=hbm,
    )(pair_own, pair_found)
    pair_update = pair_update.reshape(cotangent.shape)

    pieces, pair_update, grad_left, grad_right = lax.optimization_barrier(
        (pieces, pair_update, grad_left, grad_right)
    )
    mine = pieces.reshape(outer // 2, pairs)
    other = lax.ppermute(mine, "inner", cores)
    grad_weight = call(place_kernel, shape(outer, pairs), name="place")(mine, other)
    return (pair_update, grad_left, grad_right, grad_weight)


def solution(mesh):
    placed = (
        P(("groups", "blk"), None),
        P(("groups", "blk", "inner"), None),
        P(),
        P(("groups", "blk"), None, "inner", None),
    )
    return jax.shard_map(
        local,
        mesh=mesh,
        in_specs=placed,
        out_specs=(
            P(("groups", "blk"), None, "inner", None),
            P(("groups", "blk"), "inner"),
            P(("groups", "blk", "inner"), None),
            P("groups", None),
        ),
        check_vma=False,
    )
```

```python
import functools

import jax
import jax.numpy as jnp
from jax import lax
from jax.experimental import pallas as pl
from jax.experimental.pallas import tpu as pltpu
from jax.sharding import PartitionSpec as P

ENTRY_CHANNELS = 32
LANES = 128
PACK = LANES // ENTRY_CHANNELS
F32 = jnp.float32
BF16 = jnp.bfloat16
MIB = 1024 * 1024


def halves(values):
    high = values.astype(BF16)
    low = (values - high.astype(F32)).astype(BF16)
    return high, low


def dot(left, right):
    return jnp.dot(left, right, preferred_element_type=F32)


def dot_rows(left, right):
    return lax.dot_general(left, right, (((1,), (1,)), ((), ())), preferred_element_type=F32)


def fold_of(columns):
    return max(1, LANES // columns)


def strided(start, size, stride):
    return pl.ds(start, size, stride=stride)


def folded_weight(weight_ref, step, fold):
    channels = ENTRY_CHANNELS
    return jnp.concatenate(
        [weight_ref[strided(step * fold + part, channels, channels), :] for part in range(fold)], 1
    )


def slots_of(blocks):
    here = lax.axis_index("blk") // 2
    return [lax.bitwise_xor(here, slot) for slot in range(blocks)]


def spread_of(cotangent_ref, pair, slots, fold):
    columns = len(slots) * cotangent_ref.shape[2]
    empty = jnp.zeros((columns, cotangent_ref.shape[3]), BF16)
    spread = ([], [])
    for part in range(2):
        rows = jnp.concatenate([cotangent_ref[2 * pair + part, slot] for slot in slots], 0)
        for found, values in zip(spread, halves(rows)):
            for place in range(fold):
                found.append(
                    jnp.concatenate(
                        [values if place == other else empty for other in range(fold)], 1
                    )
                )
    return [jnp.concatenate(found, 0) for found in spread]


def turn_in(rows_minor, in_ref, out_ref, tiles, square):
    channels = ENTRY_CHANNELS
    rows, features = in_ref.shape
    count = features // LANES
    for tile in range(count):
        tiles[tile * rows : (tile + 1) * rows, :] = in_ref[:, tile * LANES : (tile + 1) * LANES]
    for group in range(rows // PACK):
        found = [tiles[strided(group * PACK + k, count, rows), :] for k in range(PACK)]
        for part in range(PACK):
            lanes = slice(part * channels, (part + 1) * channels)
            square[group, strided(part, count, PACK), :] = jnp.concatenate(
                [values[:, lanes] for values in found], 1
            )
        turned = square[group].T
        if rows_minor:
            for k in range(PACK):
                out_ref[strided(group * PACK + k, channels, rows), :] = turned[
                    k * channels : (k + 1) * channels
                ]
        else:
            out_ref[group * LANES : (group + 1) * LANES, :] = turned


def prepare_kernel(
    cotangent_hbm,
    right_hbm,
    left_hbm,
    weight_hbm,
    right_out,
    left_out,
    send_out,
    own_out,
    weight_out,
    inputs,
    tiles,
    square,
    semaphores,
):
    parity = lax.rem(lax.axis_index("blk"), 2)
    moves = (
        (right_hbm, inputs.at[0]),
        (left_hbm, inputs.at[1]),
        (cotangent_hbm.at[:, :, 1 - parity], send_out),
        (cotangent_hbm.at[:, :, parity], own_out),
        (weight_hbm, weight_out),
    )
    copies = [
        pltpu.make_async_copy(source, target, semaphores.at[at])
        for at, (source, target) in enumerate(moves)
    ]
    for copy in copies:
        copy.start()
    copies[0].wait()
    turn_in(True, inputs.at[0], right_out, tiles.at[0], square.at[0])
    copies[1].wait()
    turn_in(False, inputs.at[1], left_out, tiles.at[1], square.at[1])
    for copy in copies[2:]:
        copy.wait()


def turn_right_kernel(in_ref, out_ref, square, tiles):
    channels = ENTRY_CHANNELS
    rows, features = out_ref.shape
    count = features // LANES
    for group in range(rows // PACK):
        stacked = [in_ref[strided(group * PACK + k, channels, rows), :] for k in range(PACK)]
        square[group] = jnp.concatenate(stacked, 0).T
        pieces = [square[group, strided(part, count, PACK), :] for part in range(PACK)]
        for k in range(PACK):
            lanes = slice(k * channels, (k + 1) * channels)
            tiles[strided(group * PACK + k, count, rows), :] = jnp.concatenate(
                [piece[:, lanes] for piece in pieces], 1
            )
    for tile in range(count):
        out_ref[:, tile * LANES : (tile + 1) * LANES] = tiles[tile * rows : (tile + 1) * rows, :]


def turn_left_kernel(parts, *refs):
    part_refs, (out_ref, total, tiles) = refs[:parts], refs[parts:]
    channels = ENTRY_CHANNELS
    size, width = part_refs[0].shape
    rows, features = out_ref.shape
    count = features // LANES
    found = functools.reduce(jnp.add, [ref[...] for ref in part_refs])
    for tile in range(width // LANES):
        total[tile * size : (tile + 1) * size, :] = found[:, tile * LANES : (tile + 1) * LANES]
    for tile in range(width // LANES):
        pieces = [total[strided(tile * size + part, count, PACK), :] for part in range(PACK)]
        for k in range(PACK):
            lanes = slice(k * channels, (k + 1) * channels)
            tiles[strided(tile * PACK + k, count, rows), :] = jnp.concatenate(
                [piece[:, lanes] for piece in pieces], 1
            )
    for tile in range(count):
        out_ref[:, tile * LANES : (tile + 1) * LANES] = tiles[tile * rows : (tile + 1) * rows, :]


def prepare_weight(weight_ref, weight_cat, fold):
    channels = ENTRY_CHANNELS
    for step in range(channels // fold):
        high, low = halves(folded_weight(weight_ref, step, fold))
        weight_cat[step * channels : (step + 1) * channels, :] = jnp.concatenate(
            [high, low, high], 1
        )


def gradient_phase(blocks, cotangent_ref, factor_ref, out_hbm, weight_cat, semaphores):
    fold = fold_of(blocks * cotangent_ref.shape[2])
    slots = slots_of(blocks)

    def copy_of(pair):
        return pltpu.make_async_copy(factor_ref.at[pair], out_hbm.at[pair], semaphores.at[pair])

    def step_of(pair, carry):
        high, low = spread_of(cotangent_ref, pair, slots, fold)
        found = dot_rows(weight_cat[...], jnp.concatenate([high, high, low], 1))
        factor_ref[pair] = jnp.concatenate(halves(found), 1)
        copy_of(pair).start()
        return carry

    lax.fori_loop(0, factor_ref.shape[0], step_of, 0)
    return [copy_of(pair) for pair in range(factor_ref.shape[0])]


def gradient_kernel(
    blocks,
    weight_ref,
    cotangent_ref,
    left_ref,
    out_hbm,
    partial_ref,
    weight_cat,
    factor_ref,
    left_flip,
    semaphores,
):
    prepare_weight(weight_ref, weight_cat, fold_of(blocks * cotangent_ref.shape[2]))
    copies = gradient_phase(blocks, cotangent_ref, factor_ref, out_hbm, weight_cat, semaphores)

    def store(step, found):
        partial_ref[step] = found

    right_phase(left_ref, factor_ref, left_flip, store)
    for copy in copies:
        copy.wait()


def right_phase(left_ref, factor_ref, left_flip, store):
    sequences = left_ref.shape[1]
    lanes = factor_ref.shape[2] // 4
    flip_high, flip_low = halves((left_ref[...] * (1.0 / sequences)).T)
    left_flip[:sequences, :] = flip_high
    left_flip[sequences:, :] = flip_low

    def step_of(step, carry):
        high, low = (
            jnp.concatenate(
                [rows_of_step([factor_ref], 2 * step + part, half, lanes) for part in range(2)], 1
            )
            for half in range(2)
        )
        first = dot(left_flip[...], high)
        second = dot(left_flip[:sequences, :], low)
        store(step, first[:sequences] + first[sequences:] + second)
        return carry

    lax.fori_loop(0, factor_ref.shape[1] // (2 * ENTRY_CHANNELS), step_of, 0)


def rows_of_step(refs, step, half, lanes):
    channels = ENTRY_CHANNELS
    rows = pl.ds(pl.multiple_of(step * channels, channels), channels)
    start = 2 * half * lanes
    return jnp.concatenate(
        [
            ref[pair, rows, start + part * lanes : start + (part + 1) * lanes]
            for ref in refs
            for pair in range(ref.shape[0])
            for part in range(2)
        ],
        0,
    )


def both_left(left_refs):
    sequences = left_refs[0].shape[1]
    return jnp.concatenate([ref[...] for ref in left_refs], 0) * (1.0 / sequences)


def right_kernel(
    blocks,
    weight_cat,
    cotangent_ref,
    left_ref,
    partial_ref,
    out_hbm,
    out_ref,
    factor_ref,
    left_flip,
    semaphores,
):
    depth = cotangent_ref.shape[2]
    fold = fold_of(blocks * depth)
    lanes = fold * blocks * depth
    copies = gradient_phase(blocks, cotangent_ref, factor_ref, out_hbm, weight_cat, semaphores)
    slots = slots_of(blocks)

    def store(step, found):
        found = found + partial_ref[step]
        for part in range(2):
            turned = found[:, part * lanes : (part + 1) * lanes].T
            for place in range(fold):
                for slot in range(blocks):
                    start = (place * blocks + slot) * depth
                    row = pl.multiple_of(((2 * step + part) * fold + place) * depth, depth)
                    out_ref[slots[slot], pl.ds(row, depth), :] = turned[start : start + depth]

    right_phase(left_ref, factor_ref, left_flip, store)
    for copy in copies:
        copy.wait()


def right_rows(right_refs, step, fold, depth):
    return jnp.concatenate(
        [
            ref[pl.ds(pl.multiple_of((step * fold + part) * depth, depth), depth), :]
            for part in range(fold)
            for ref in right_refs
        ],
        0,
    )


def weight_kernel(blocks, own_left, peer_left, own_cotangent, peer_cotangent, *refs):
    right_refs = refs[:blocks]
    keep_ref, send_ref, own_out, peer_out, own_ref, peer_ref, total, semaphores = refs[blocks:]
    channels = ENTRY_CHANNELS
    depth, pairs = own_cotangent.shape[2:]
    fold = fold_of(blocks * depth)
    lanes = fold * blocks * depth
    high, low = halves(both_left([own_left, peer_left]))
    left_cat = jnp.concatenate([high, low, high], 1)

    def copies(step):
        size = 2 * channels
        rows = pl.ds(pl.multiple_of(step * size, size), size)
        return [
            pltpu.make_async_copy(ref.at[:, rows], out.at[:, rows], semaphores.at[step, side])
            for side, (ref, out) in enumerate(((own_ref, own_out), (peer_ref, peer_out)))
        ]

    def outer_step(step, carry):
        right = [right_rows(right_refs, 2 * step + part, fold, depth) for part in range(2)]
        high, low = halves(jnp.concatenate(right, 0))
        found = dot_rows(left_cat, jnp.concatenate([high, high, low], 1))
        both = halves(found)
        for part in range(2):
            start = pl.multiple_of((2 * step + part) * channels, channels)
            row = 0
            for ref in (own_ref, peer_ref):
                for index in range(2 * ref.shape[0]):
                    for half in range(2):
                        lane = (2 * half + index % 2) * lanes
                        ref[index // 2, pl.ds(start, channels), lane : lane + lanes] = both[half][
                            row : row + channels, part * lanes : (part + 1) * lanes
                        ]
                    row += channels
        for copy in copies(step):
            copy.start()
        return carry

    lax.fori_loop(0, channels // (2 * fold), outer_step, 0)
    total[...] = jnp.zeros_like(total)

    def weight_step(pair, carry):
        lefts, rights = [], []
        for ref, cotangent_ref in ((own_ref, own_cotangent), (peer_ref, peer_cotangent)):
            high, low = spread_of(cotangent_ref, pair, slots_of(blocks), fold)
            lefts += [ref[pair], ref[pair, :, : 2 * lanes]]
            rights += [high, high, low]
        total[...] += dot(jnp.concatenate(lefts, 1), jnp.concatenate(rights, 0))
        return carry

    lax.fori_loop(0, own_ref.shape[0], weight_step, 0)
    core = lax.rem(lax.axis_index("inner"), 2)
    steps = channels // (2 * fold)
    for out_ref, half in ((keep_ref, core), (send_ref, 1 - core)):
        for step in range(steps):
            start = pl.multiple_of((half * steps + step) * channels, channels)
            found = total[pl.ds(start, channels), :]
            for part in range(fold):
                y = step * fold + part
                out_ref[y * channels : (y + 1) * channels, :] = found[
                    :, part * pairs : (part + 1) * pairs
                ]

    def finish(step, carry):
        for copy in copies(step):
            copy.wait()
        return carry

    lax.fori_loop(0, channels // (2 * fold), finish, 0)


def left_kernel(blocks, depth, own_hbm, peer_hbm, *refs):
    right_refs, refs = refs[:blocks], refs[blocks:]
    own_out, peer_out, own_ref, peer_ref, total, flipped, semaphores = refs
    lanes = own_ref.shape[2] // 4
    fold = lanes // (blocks * depth)
    sequences = right_refs[0].shape[1]
    group = 4
    count = ENTRY_CHANNELS // (fold * group)

    def copies(step):
        size = group * ENTRY_CHANNELS
        rows = pl.ds(pl.multiple_of(step * size, size), size)
        return [
            pltpu.make_async_copy(hbm.at[:, rows], ref.at[:, rows], semaphores.at[step, side])
            for side, (hbm, ref) in enumerate(((own_hbm, own_ref), (peer_hbm, peer_ref)))
        ]

    for step in range(count):
        for copy in copies(step):
            copy.start()
    total[...] = jnp.zeros_like(total)

    def step_of(step, carry):
        for copy in copies(step):
            copy.wait()
        steps = [group * step + part for part in range(group)]
        right = [right_rows(right_refs, at, fold, depth) for at in steps]
        high, low = halves(jnp.concatenate(right, 0))
        grads = [
            jnp.concatenate([rows_of_step([own_ref, peer_ref], at, half, lanes) for at in steps], 1)
            for half in range(2)
        ]
        both = dot(grads[0], jnp.concatenate([high, low], 1))
        total[...] += both[:, :sequences] + both[:, sequences:] + dot(grads[1], high)
        return carry

    lax.fori_loop(0, count, step_of, 0)
    flipped[...] = total[...].T * (1.0 / sequences)
    inner, size, width = own_out.shape
    here = lax.axis_index("inner")
    for slot in range(inner):
        start = pl.multiple_of(lax.bitwise_xor(here, slot) * size, size)
        own_out[slot] = flipped[pl.ds(start, size), :width]
        peer_out[slot] = flipped[pl.ds(start, size), width:]


def left_add_kernel(own_ref, other_ref, *out_refs):
    for slot, ref in enumerate(out_refs):
        ref[...] = own_ref[slot] + other_ref[slot]


def pair_kernel(
    blocks,
    outer_hbm,
    weight_hbm,
    out_ref,
    outer_ref,
    weight_ref,
    weight_flip,
    weight_rows,
    semaphores,
):
    channels = ENTRY_CHANNELS
    depth, pairs = out_ref.shape[2:]
    count = outer_ref.shape[0]
    lanes = outer_ref.shape[2] // 4
    columns = blocks * depth
    fold = lanes // columns
    wide = fold * pairs

    def copy_of(pair):
        return pltpu.make_async_copy(outer_hbm.at[pair], outer_ref.at[pair], semaphores.at[pair])

    weight_copy = pltpu.make_async_copy(weight_hbm, weight_ref, semaphores.at[count])
    weight_copy.start()
    for pair in range(count):
        copy_of(pair).start()
    weight_copy.wait()
    for step in range(channels // fold):
        weight_rows[step * channels : (step + 1) * channels, :] = folded_weight(
            weight_ref, step, fold
        )
    flip_high, flip_low = halves(weight_rows[...].T)
    weight_flip[:wide, :] = flip_high
    weight_flip[wide:, :] = flip_low
    slots = slots_of(blocks)

    def step_of(pair, carry):
        copy_of(pair).wait()
        first = dot(weight_flip[...], outer_ref[pair, :, : 2 * lanes])
        second = dot(weight_flip[:wide, :], outer_ref[pair, :, 2 * lanes :])
        found = first[:wide] + first[wide:] + second
        for part in range(2):
            turned = []
            for place in range(fold):
                start = part * lanes
                piece = found[place * pairs : (place + 1) * pairs, start : start + lanes].T
                turned.append(piece[place * columns : (place + 1) * columns])
            turned = functools.reduce(jnp.add, turned)
            row = 2 * pair + part
            for slot in range(blocks):
                out_ref[row, slots[slot]] = turned[slot * depth : (slot + 1) * depth]
        return carry

    lax.fori_loop(0, count, step_of, 0)


def merge_kernel(own_ref, other_ref, out_ref, semaphores):
    parity = lax.rem(lax.axis_index("blk"), 2)
    copies = [
        pltpu.make_async_copy(ref, out_ref.at[:, :, side], semaphores.at[at])
        for at, (ref, side) in enumerate(((own_ref, parity), (other_ref, 1 - parity)))
    ]
    for copy in copies:
        copy.start()
    for copy in copies:
        copy.wait()


def spread_sum_kernel(in_ref, out_ref):
    found = in_ref[0]
    for part in range(1, in_ref.shape[0]):
        found = found + in_ref[part]
    for part in range(in_ref.shape[0]):
        out_ref[part] = found


def place_kernel(mine_ref, other_ref, out_ref):
    channels = ENTRY_CHANNELS
    core = lax.rem(lax.axis_index("inner"), 2)
    steps = mine_ref.shape[0] // channels
    for ref, half in ((mine_ref, core), (other_ref, 1 - core)):
        for step in range(steps):
            rows = ref[step * channels : (step + 1) * channels, :]
            out_ref[strided(half * steps + step, channels, channels), :] = rows


def shape(*sizes, kind=F32):
    return jax.ShapeDtypeStruct(sizes, kind)


def call(
    kernel,
    out_shape,
    scratch=(),
    name=None,
    limit=16 * MIB,
    far=(),
    after=(),
    out_specs=None,
    flops=1,
):
    def run(*operands):
        vmem = pl.BlockSpec(memory_space=pltpu.VMEM)
        hbm = pl.BlockSpec(memory_space=pltpu.HBM)
        in_specs = [pl.BlockSpec(memory_space=pl.ANY)] * len(after)
        in_specs += [hbm if at in far else vmem for at in range(len(operands))]
        operands = [
            pltpu.with_memory_space_constraint(operand, pltpu.HBM) if at in far else operand
            for at, operand in enumerate(operands)
        ]
        extra = {} if out_specs is None else {"out_specs": out_specs}
        return pl.pallas_call(
            lambda *refs: kernel(*refs[len(after) :]),
            out_shape=out_shape,
            in_specs=in_specs,
            scratch_shapes=list(scratch),
            compiler_params=pltpu.CompilerParams(vmem_limit_bytes=limit),
            cost_estimate=pl.CostEstimate(flops=flops, bytes_accessed=1, transcendentals=0),
            name=name,
            **extra,
        )(*after, *operands)

    return run


def local(alignment_left, alignment_right, projection_matrix, cotangent):
    rows, features = alignment_left.shape
    depth = alignment_right.shape[0]
    count = lax.axis_size("blk")
    inner = lax.axis_size("inner")
    channels = ENTRY_CHANNELS
    sequences = features // channels
    outer, pairs = projection_matrix.shape
    blocks = count // 2
    fold = fold_of(blocks * depth)
    lanes = fold * blocks * depth
    tall = outer // fold
    steps = channels // fold
    row_pairs = rows // 2
    everyone = ("blk", "inner")

    partner = [(here, here ^ 1) for here in range(count)]
    slot_moves = [[(here, here ^ (2 * slot)) for here in range(count)] for slot in range(blocks)]
    same_parity = [[2 * block + side for block in range(blocks)] for side in range(2)]
    inner_moves = [[(here, here ^ slot) for here in range(inner)] for slot in range(inner)]
    cores = [(here, here ^ 1) for here in range(inner)]
    core_groups = [list(range(core, count * inner, 2)) for core in range(2)]

    limit = 20 * MIB * max(1, blocks * depth * fold // LANES * 2 // fold)
    large = functools.partial(call, limit=limit)
    work = 4 * 2 * rows * 2 * blocks * depth * outer * pairs * 3

    by_side = cotangent.reshape(rows, blocks, 2, depth, pairs)
    half_cotangent = shape(rows, blocks, depth, pairs)
    right, left, cotangent_send, cotangent_own, weight = call(
        prepare_kernel,
        [
            shape(channels * depth, sequences),
            shape(rows * channels, sequences),
            half_cotangent,
            half_cotangent,
            shape(outer, pairs),
        ],
        [
            pltpu.VMEM((2, rows, features), F32),
            pltpu.VMEM((2, rows * features // LANES, LANES), F32),
            pltpu.VMEM((2, rows // PACK, LANES, LANES), F32),
            pltpu.SemaphoreType.DMA((5,)),
        ],
        name="prepare",
        far=range(4),
    )(by_side, alignment_right, alignment_left, projection_matrix)
    rights = [right]
    for slot in range(1, blocks):
        rights.append(lax.ppermute(right, "blk", slot_moves[slot]))
    cotangent_peer = lax.ppermute(cotangent_send, "blk", partner)
    left_peer = lax.ppermute(left, "blk", partner)

    vmem = pl.BlockSpec(memory_space=pltpu.VMEM)
    hbm = pl.BlockSpec(memory_space=pltpu.HBM)
    factor = shape(row_pairs, tall, 4 * lanes, kind=BF16)
    factor_scratch = pltpu.VMEM(factor.shape, BF16)
    weight_cat = shape(tall, 3 * fold * pairs, kind=BF16)
    flip_scratch = pltpu.VMEM((2 * sequences, rows * channels), BF16)
    factor_hbm = pltpu.HBM(factor.shape, BF16)
    factor_copies = pltpu.SemaphoreType.DMA((row_pairs,))
    grad_own, partial, weight_cat = large(
        functools.partial(gradient_kernel, blocks),
        [factor_hbm, shape(steps // 2, sequences, 2 * lanes), weight_cat],
        [factor_scratch, flip_scratch, factor_copies],
        "gradient_own",
        out_specs=[hbm, vmem, vmem],
    )(weight, cotangent_own, left)
    grad_peer, right_parts = large(
        functools.partial(right_kernel, blocks),
        [factor_hbm, shape(blocks, channels * depth, sequences)],
        [factor_scratch, flip_scratch, factor_copies],
        "right_parts",
        out_specs=[hbm, vmem],
    )(weight_cat, cotangent_peer, left_peer, partial)
    right_sum = lax.psum_scatter(
        right_parts, "blk", scatter_dimension=0, axis_index_groups=same_parity
    )

    keep, send, outer_own, outer_peer = large(
        functools.partial(weight_kernel, blocks),
        [shape(outer // 2, pairs)] * 2 + [factor_hbm] * 2,
        [
            factor_scratch,
            factor_scratch,
            pltpu.VMEM((tall, fold * pairs), F32),
            pltpu.SemaphoreType.DMA((steps // 2, 2)),
        ],
        "weight",
        after=[right_parts],
        flops=2 * work,
        out_specs=[vmem, vmem, hbm, hbm],
    )(left, left_peer, cotangent_own, cotangent_peer, *rights)
    sent = lax.ppermute(send, "inner", cores)

    size = sequences // inner
    left_own, left_other = large(
        functools.partial(left_kernel, blocks, depth),
        [shape(inner, size, rows * channels)] * 2,
        [
            factor_scratch,
            factor_scratch,
            pltpu.VMEM((2 * rows * channels, sequences), F32),
            pltpu.VMEM((sequences, 2 * rows * channels), F32),
            pltpu.SemaphoreType.DMA((steps // 4, 2)),
        ],
        "left_parts",
        far=[0, 1],
        after=[keep],
        flops=work,
    )(grad_own, grad_peer, *rights)
    left_other = lax.ppermute(left_other, "blk", partner)
    keep, left_own = lax.optimization_barrier((keep, left_own))
    members = count * inner // 2
    pieces = (keep + sent).reshape(members, outer // 2 // members, pairs)

    def pair(values, after, name):
        return large(
            functools.partial(pair_kernel, blocks),
            shape(rows, blocks, depth, pairs),
            [
                factor_scratch,
                pltpu.VMEM((outer, pairs), F32),
                pltpu.VMEM((2 * fold * pairs, tall), BF16),
                pltpu.VMEM((tall, fold * pairs), F32),
                pltpu.SemaphoreType.DMA((row_pairs + 1,)),
            ],
            name,
            far=[0, 1],
            after=after,
            flops=work,
        )(values, projection_matrix)

    pair_other = pair(outer_peer, [pieces], "pair_peer")
    pair_found = lax.ppermute(pair_other, "blk", partner)

    pieces = lax.all_to_all(pieces, everyone, 0, 0, axis_index_groups=core_groups)
    left_found = call(
        left_add_kernel,
        [shape(size, rows * channels)] * inner,
        name="left_add",
        after=[pieces],
    )(left_own, left_other)
    pieces = call(
        spread_sum_kernel,
        shape(*pieces.shape),
        name="weight_sum",
        after=[pair_other],
    )(pieces)
    pair_own = pair(outer_own, [pieces], "pair_own")
    pieces = lax.all_to_all(pieces, everyone, 0, 0, axis_index_groups=core_groups)

    left_found = [
        lax.ppermute(part, "inner", inner_moves[slot]) if slot else part
        for slot, part in enumerate(left_found)
    ]
    grad_left = call(
        functools.partial(turn_left_kernel, inner),
        shape(rows, features // inner),
        [
            pltpu.VMEM((size * rows * channels // LANES, LANES), F32),
            pltpu.VMEM((rows * features // inner // LANES, LANES), F32),
        ],
        name="turn_left",
    )(*left_found)

    grad_right = call(
        turn_right_kernel,
        shape(depth, features),
        [
            pltpu.VMEM((depth // PACK, LANES, LANES), F32),
            pltpu.VMEM((depth * features // LANES, LANES), F32),
        ],
        name="turn_right",
    )(right_sum)

    pair_update = call(
        merge_kernel,
        pltpu.HBM(by_side.shape, F32),
        [pltpu.SemaphoreType.DMA((2,))],
        "merge",
        out_specs=hbm,
    )(pair_own, pair_found)
    pair_update = pair_update.reshape(cotangent.shape)

    pieces, pair_update, grad_left, grad_right = lax.optimization_barrier(
        (pieces, pair_update, grad_left, grad_right)
    )
    mine = pieces.reshape(outer // 2, pairs)
    other = lax.ppermute(mine, "inner", cores)
    grad_weight = call(place_kernel, shape(outer, pairs), name="place")(mine, other)
    return (pair_update, grad_left, grad_right, grad_weight)


def solution(mesh):
    placed = (
        P(("groups", "blk"), None),
        P(("groups", "blk", "inner"), None),
        P(),
        P(("groups", "blk"), None, "inner", None),
    )
    return jax.shard_map(
        local,
        mesh=mesh,
        in_specs=placed,
        out_specs=(
            P(("groups", "blk"), None, "inner", None),
            P(("groups", "blk"), "inner"),
            P(("groups", "blk", "inner"), None),
            P("groups", None),
        ),
        check_vma=False,
    )
```

```python
import functools

import jax
import jax.numpy as jnp
from jax import lax
from jax.experimental import pallas as pl
from jax.experimental.pallas import tpu as pltpu
from jax.sharding import PartitionSpec as P

ENTRY_CHANNELS = 32
LANES = 128
PACK = LANES // ENTRY_CHANNELS
F32 = jnp.float32
BF16 = jnp.bfloat16
MIB = 1024 * 1024


def halves(values):
    high = values.astype(BF16)
    low = (values - high.astype(F32)).astype(BF16)
    return high, low


def dot(left, right):
    return jnp.dot(left, right, preferred_element_type=F32)


def dot_rows(left, right):
    return lax.dot_general(left, right, (((1,), (1,)), ((), ())), preferred_element_type=F32)


def fold_of(columns):
    return max(1, LANES // columns)


def strided(start, size, stride):
    return pl.ds(start, size, stride=stride)


def folded_weight(weight_ref, step, fold):
    channels = ENTRY_CHANNELS
    return jnp.concatenate(
        [weight_ref[strided(step * fold + part, channels, channels), :] for part in range(fold)], 1
    )


def slots_of(blocks):
    here = lax.axis_index("blk") // 2
    return [lax.bitwise_xor(here, slot) for slot in range(blocks)]


def spread_of(cotangent_ref, pair, slots, fold):
    columns = len(slots) * cotangent_ref.shape[2]
    empty = jnp.zeros((columns, cotangent_ref.shape[3]), BF16)
    spread = ([], [])
    for part in range(2):
        rows = jnp.concatenate([cotangent_ref[2 * pair + part, slot] for slot in slots], 0)
        for found, values in zip(spread, halves(rows)):
            for place in range(fold):
                found.append(
                    jnp.concatenate(
                        [values if place == other else empty for other in range(fold)], 1
                    )
                )
    return [jnp.concatenate(found, 0) for found in spread]


def turn_in(rows_minor, in_ref, out_ref, tiles, square):
    channels = ENTRY_CHANNELS
    rows, features = in_ref.shape
    count = features // LANES
    for tile in range(count):
        tiles[tile * rows : (tile + 1) * rows, :] = in_ref[:, tile * LANES : (tile + 1) * LANES]
    for group in range(rows // PACK):
        found = [tiles[strided(group * PACK + k, count, rows), :] for k in range(PACK)]
        for part in range(PACK):
            lanes = slice(part * channels, (part + 1) * channels)
            square[group, strided(part, count, PACK), :] = jnp.concatenate(
                [values[:, lanes] for values in found], 1
            )
        turned = square[group].T
        if rows_minor:
            for k in range(PACK):
                out_ref[strided(group * PACK + k, channels, rows), :] = turned[
                    k * channels : (k + 1) * channels
                ]
        else:
            out_ref[group * LANES : (group + 1) * LANES, :] = turned


def prepare_kernel(
    cotangent_hbm,
    right_hbm,
    left_hbm,
    weight_hbm,
    right_out,
    left_out,
    send_out,
    own_out,
    weight_out,
    inputs,
    tiles,
    square,
    semaphores,
):
    parity = lax.rem(lax.axis_index("blk"), 2)
    moves = (
        (right_hbm, inputs.at[0]),
        (left_hbm, inputs.at[1]),
        (cotangent_hbm.at[:, :, 1 - parity], send_out),
        (cotangent_hbm.at[:, :, parity], own_out),
        (weight_hbm, weight_out),
    )
    copies = [
        pltpu.make_async_copy(source, target, semaphores.at[at])
        for at, (source, target) in enumerate(moves)
    ]
    for copy in copies:
        copy.start()
    copies[0].wait()
    turn_in(True, inputs.at[0], right_out, tiles.at[0], square.at[0])
    copies[1].wait()
    turn_in(False, inputs.at[1], left_out, tiles.at[1], square.at[1])
    for copy in copies[2:]:
        copy.wait()


def turn_right_kernel(parts, *refs):
    part_refs, (out_ref, total, square, tiles) = refs[:parts], refs[parts:]
    channels = ENTRY_CHANNELS
    rows, features = out_ref.shape
    count = features // LANES
    total[...] = functools.reduce(jnp.add, [ref[0] for ref in part_refs])
    for group in range(rows // PACK):
        stacked = [total[strided(group * PACK + k, channels, rows), :] for k in range(PACK)]
        square[...] = jnp.concatenate(stacked, 0).T
        pieces = [square[strided(part, count, PACK), :] for part in range(PACK)]
        for k in range(PACK):
            lanes = slice(k * channels, (k + 1) * channels)
            tiles[strided(group * PACK + k, count, rows), :] = jnp.concatenate(
                [piece[:, lanes] for piece in pieces], 1
            )
    for tile in range(count):
        out_ref[:, tile * LANES : (tile + 1) * LANES] = tiles[tile * rows : (tile + 1) * rows, :]


def turn_left_kernel(parts, *refs):
    part_refs, (out_ref, total, tiles) = refs[:parts], refs[parts:]
    channels = ENTRY_CHANNELS
    size, width = part_refs[0].shape
    rows, features = out_ref.shape
    count = features // LANES
    found = functools.reduce(jnp.add, [ref[...] for ref in part_refs])
    for tile in range(width // LANES):
        total[tile * size : (tile + 1) * size, :] = found[:, tile * LANES : (tile + 1) * LANES]
    for tile in range(width // LANES):
        pieces = [total[strided(tile * size + part, count, PACK), :] for part in range(PACK)]
        for k in range(PACK):
            lanes = slice(k * channels, (k + 1) * channels)
            tiles[strided(tile * PACK + k, count, rows), :] = jnp.concatenate(
                [piece[:, lanes] for piece in pieces], 1
            )
    for tile in range(count):
        out_ref[:, tile * LANES : (tile + 1) * LANES] = tiles[tile * rows : (tile + 1) * rows, :]


def prepare_weight(weight_ref, weight_cat, fold):
    channels = ENTRY_CHANNELS
    for step in range(channels // fold):
        high, low = halves(folded_weight(weight_ref, step, fold))
        weight_cat[step * channels : (step + 1) * channels, :] = jnp.concatenate(
            [high, low, high], 1
        )


def gradient_phase(blocks, cotangent_ref, out_ref, weight_cat):
    fold = fold_of(blocks * cotangent_ref.shape[2])
    slots = slots_of(blocks)

    def step_of(pair, carry):
        high, low = spread_of(cotangent_ref, pair, slots, fold)
        found = dot_rows(weight_cat[...], jnp.concatenate([high, high, low], 1))
        out_ref[pair] = jnp.concatenate(halves(found), 1)
        return carry

    lax.fori_loop(0, out_ref.shape[0], step_of, 0)


def gradient_kernel(
    blocks, weight_ref, cotangent_ref, left_ref, out_ref, partial_ref, weight_cat, left_flip
):
    prepare_weight(weight_ref, weight_cat, fold_of(blocks * cotangent_ref.shape[2]))
    gradient_phase(blocks, cotangent_ref, out_ref, weight_cat)

    def store(step, found):
        partial_ref[step] = found

    right_phase(left_ref, out_ref, left_flip, store)


def right_phase(left_ref, factor_ref, left_flip, store):
    sequences = left_ref.shape[1]
    lanes = factor_ref.shape[2] // 4
    flip_high, flip_low = halves((left_ref[...] * (1.0 / sequences)).T)
    left_flip[:sequences, :] = flip_high
    left_flip[sequences:, :] = flip_low

    def step_of(step, carry):
        high, low = (
            jnp.concatenate(
                [rows_of_step([factor_ref], 2 * step + part, half, lanes) for part in range(2)], 1
            )
            for half in range(2)
        )
        first = dot(left_flip[...], high)
        second = dot(left_flip[:sequences, :], low)
        store(step, first[:sequences] + first[sequences:] + second)
        return carry

    lax.fori_loop(0, factor_ref.shape[1] // (2 * ENTRY_CHANNELS), step_of, 0)


def rows_of_step(refs, step, half, lanes):
    channels = ENTRY_CHANNELS
    rows = pl.ds(pl.multiple_of(step * channels, channels), channels)
    start = 2 * half * lanes
    return jnp.concatenate(
        [
            ref[pair, rows, start + part * lanes : start + (part + 1) * lanes]
            for ref in refs
            for pair in range(ref.shape[0])
            for part in range(2)
        ],
        0,
    )


def both_left(left_refs):
    sequences = left_refs[0].shape[1]
    return jnp.concatenate([ref[...] for ref in left_refs], 0) * (1.0 / sequences)


def right_kernel(
    blocks,
    weight_cat,
    cotangent_ref,
    left_ref,
    partial_ref,
    peer_ref,
    keep_ref,
    send_ref,
    left_flip,
):
    depth = cotangent_ref.shape[2]
    fold = fold_of(blocks * depth)
    lanes = fold * blocks * depth
    gradient_phase(blocks, cotangent_ref, peer_ref, weight_cat)

    def store(step, found):
        found = found + partial_ref[step]
        for part in range(2):
            turned = found[:, part * lanes : (part + 1) * lanes].T
            for place in range(fold):
                for slot in range(blocks):
                    start = (place * blocks + slot) * depth
                    row = pl.multiple_of(((2 * step + part) * fold + place) * depth, depth)
                    out_ref = send_ref if slot >= blocks // 2 else keep_ref
                    place_of = slot % (blocks // 2)
                    out_ref[place_of, pl.ds(row, depth), :] = turned[start : start + depth]

    right_phase(left_ref, peer_ref, left_flip, store)


def halve_kernel(keep_ref, found_ref, keep_out, send_out):
    half = keep_ref.shape[0] // 2
    for slot in range(half):
        keep_out[slot] = keep_ref[slot] + found_ref[slot]
        send_out[slot] = keep_ref[half + slot] + found_ref[half + slot]


def right_rows(right_refs, step, fold, depth):
    return jnp.concatenate(
        [
            ref[pl.ds(pl.multiple_of((step * fold + part) * depth, depth), depth), :]
            for part in range(fold)
            for ref in right_refs
        ],
        0,
    )


def weight_kernel(blocks, own_left, peer_left, own_cotangent, peer_cotangent, *refs):
    right_refs = refs[:blocks]
    keep_ref, send_ref, own_out, peer_out, own_ref, peer_ref, total, semaphores = refs[blocks:]
    channels = ENTRY_CHANNELS
    depth, pairs = own_cotangent.shape[2:]
    fold = fold_of(blocks * depth)
    lanes = fold * blocks * depth
    high, low = halves(both_left([own_left, peer_left]))
    left_cat = jnp.concatenate([high, low, high], 1)

    def copies(step):
        size = 2 * channels
        rows = pl.ds(pl.multiple_of(step * size, size), size)
        return [
            pltpu.make_async_copy(ref.at[:, rows], out.at[:, rows], semaphores.at[step, side])
            for side, (ref, out) in enumerate(((own_ref, own_out), (peer_ref, peer_out)))
        ]

    def outer_step(step, carry):
        right = [right_rows(right_refs, 2 * step + part, fold, depth) for part in range(2)]
        high, low = halves(jnp.concatenate(right, 0))
        found = dot_rows(left_cat, jnp.concatenate([high, high, low], 1))
        both = halves(found)
        for part in range(2):
            start = pl.multiple_of((2 * step + part) * channels, channels)
            row = 0
            for ref in (own_ref, peer_ref):
                for index in range(2 * ref.shape[0]):
                    for half in range(2):
                        lane = (2 * half + index % 2) * lanes
                        ref[index // 2, pl.ds(start, channels), lane : lane + lanes] = both[half][
                            row : row + channels, part * lanes : (part + 1) * lanes
                        ]
                    row += channels
        for copy in copies(step):
            copy.start()
        return carry

    lax.fori_loop(0, channels // (2 * fold), outer_step, 0)
    total[...] = jnp.zeros_like(total)

    def weight_step(pair, carry):
        lefts, rights = [], []
        for ref, cotangent_ref in ((own_ref, own_cotangent), (peer_ref, peer_cotangent)):
            high, low = spread_of(cotangent_ref, pair, slots_of(blocks), fold)
            lefts += [ref[pair], ref[pair, :, : 2 * lanes]]
            rights += [high, high, low]
        total[...] += dot(jnp.concatenate(lefts, 1), jnp.concatenate(rights, 0))
        return carry

    lax.fori_loop(0, own_ref.shape[0], weight_step, 0)
    core = lax.rem(lax.axis_index("inner"), 2)
    steps = channels // (2 * fold)
    for out_ref, half in ((keep_ref, core), (send_ref, 1 - core)):
        for step in range(steps):
            start = pl.multiple_of((half * steps + step) * channels, channels)
            found = total[pl.ds(start, channels), :]
            for part in range(fold):
                y = step * fold + part
                out_ref[y * channels : (y + 1) * channels, :] = found[
                    :, part * pairs : (part + 1) * pairs
                ]

    def finish(step, carry):
        for copy in copies(step):
            copy.wait()
        return carry

    lax.fori_loop(0, channels // (2 * fold), finish, 0)


def left_kernel(blocks, depth, own_ref, peer_ref, *refs):
    right_refs, (own_out, peer_out, total, flipped) = refs[:blocks], refs[blocks:]
    lanes = own_ref.shape[2] // 4
    fold = lanes // (blocks * depth)
    sequences = right_refs[0].shape[1]
    group = 4
    total[...] = jnp.zeros_like(total)

    def step_of(step, carry):
        steps = [group * step + part for part in range(group)]
        right = [right_rows(right_refs, at, fold, depth) for at in steps]
        high, low = halves(jnp.concatenate(right, 0))
        grads = [
            jnp.concatenate([rows_of_step([own_ref, peer_ref], at, half, lanes) for at in steps], 1)
            for half in range(2)
        ]
        both = dot(grads[0], jnp.concatenate([high, low], 1))
        total[...] += both[:, :sequences] + both[:, sequences:] + dot(grads[1], high)
        return carry

    lax.fori_loop(0, ENTRY_CHANNELS // (fold * group), step_of, 0)
    flipped[...] = total[...].T * (1.0 / sequences)
    inner, size, width = own_out.shape
    here = lax.axis_index("inner")
    for slot in range(inner):
        start = pl.multiple_of(lax.bitwise_xor(here, slot) * size, size)
        own_out[slot] = flipped[pl.ds(start, size), :width]
        peer_out[slot] = flipped[pl.ds(start, size), width:]


def left_add_kernel(own_ref, other_ref, *out_refs):
    for slot, ref in enumerate(out_refs):
        ref[...] = own_ref[slot] + other_ref[slot]


def pair_kernel(
    blocks,
    outer_hbm,
    weight_hbm,
    out_ref,
    outer_ref,
    weight_ref,
    weight_flip,
    weight_rows,
    semaphores,
):
    channels = ENTRY_CHANNELS
    depth, pairs = out_ref.shape[2:]
    count = outer_ref.shape[0]
    lanes = outer_ref.shape[2] // 4
    columns = blocks * depth
    fold = lanes // columns
    wide = fold * pairs

    def copy_of(pair):
        return pltpu.make_async_copy(outer_hbm.at[pair], outer_ref.at[pair], semaphores.at[pair])

    weight_copy = pltpu.make_async_copy(weight_hbm, weight_ref, semaphores.at[count])
    weight_copy.start()
    for pair in range(count):
        copy_of(pair).start()
    weight_copy.wait()
    for step in range(channels // fold):
        weight_rows[step * channels : (step + 1) * channels, :] = folded_weight(
            weight_ref, step, fold
        )
    flip_high, flip_low = halves(weight_rows[...].T)
    weight_flip[:wide, :] = flip_high
    weight_flip[wide:, :] = flip_low
    slots = slots_of(blocks)

    def step_of(pair, carry):
        copy_of(pair).wait()
        first = dot(weight_flip[...], outer_ref[pair, :, : 2 * lanes])
        second = dot(weight_flip[:wide, :], outer_ref[pair, :, 2 * lanes :])
        found = first[:wide] + first[wide:] + second
        for part in range(2):
            turned = []
            for place in range(fold):
                start = part * lanes
                piece = found[place * pairs : (place + 1) * pairs, start : start + lanes].T
                turned.append(piece[place * columns : (place + 1) * columns])
            turned = functools.reduce(jnp.add, turned)
            row = 2 * pair + part
            for slot in range(blocks):
                out_ref[row, slots[slot]] = turned[slot * depth : (slot + 1) * depth]
        return carry

    lax.fori_loop(0, count, step_of, 0)


def merge_kernel(own_ref, other_ref, out_ref, semaphores):
    parity = lax.rem(lax.axis_index("blk"), 2)
    copies = [
        pltpu.make_async_copy(ref, out_ref.at[:, :, side], semaphores.at[at])
        for at, (ref, side) in enumerate(((own_ref, parity), (other_ref, 1 - parity)))
    ]
    for copy in copies:
        copy.start()
    for copy in copies:
        copy.wait()


def spread_sum_kernel(in_ref, out_ref):
    found = in_ref[0]
    for part in range(1, in_ref.shape[0]):
        found = found + in_ref[part]
    for part in range(in_ref.shape[0]):
        out_ref[part] = found


def place_kernel(mine_ref, other_ref, out_ref):
    channels = ENTRY_CHANNELS
    core = lax.rem(lax.axis_index("inner"), 2)
    steps = mine_ref.shape[0] // channels
    for ref, half in ((mine_ref, core), (other_ref, 1 - core)):
        for step in range(steps):
            rows = ref[step * channels : (step + 1) * channels, :]
            out_ref[strided(half * steps + step, channels, channels), :] = rows


def shape(*sizes, kind=F32):
    return jax.ShapeDtypeStruct(sizes, kind)


def call(
    kernel,
    out_shape,
    scratch=(),
    name=None,
    limit=16 * MIB,
    far=(),
    after=(),
    out_specs=None,
    flops=1,
):
    def run(*operands):
        vmem = pl.BlockSpec(memory_space=pltpu.VMEM)
        hbm = pl.BlockSpec(memory_space=pltpu.HBM)
        in_specs = [pl.BlockSpec(memory_space=pl.ANY)] * len(after)
        in_specs += [hbm if at in far else vmem for at in range(len(operands))]
        operands = [
            pltpu.with_memory_space_constraint(operand, pltpu.HBM) if at in far else operand
            for at, operand in enumerate(operands)
        ]
        extra = {} if out_specs is None else {"out_specs": out_specs}
        return pl.pallas_call(
            lambda *refs: kernel(*refs[len(after) :]),
            out_shape=out_shape,
            in_specs=in_specs,
            scratch_shapes=list(scratch),
            compiler_params=pltpu.CompilerParams(vmem_limit_bytes=limit),
            cost_estimate=pl.CostEstimate(flops=flops, bytes_accessed=1, transcendentals=0),
            name=name,
            **extra,
        )(*after, *operands)

    return run


def local(alignment_left, alignment_right, projection_matrix, cotangent):
    rows, features = alignment_left.shape
    depth = alignment_right.shape[0]
    count = lax.axis_size("blk")
    inner = lax.axis_size("inner")
    channels = ENTRY_CHANNELS
    sequences = features // channels
    outer, pairs = projection_matrix.shape
    blocks = count // 2
    fold = fold_of(blocks * depth)
    lanes = fold * blocks * depth
    tall = outer // fold
    steps = channels // fold
    row_pairs = rows // 2
    everyone = ("blk", "inner")

    partner = [(here, here ^ 1) for here in range(count)]
    slot_moves = [[(here, here ^ (2 * slot)) for here in range(count)] for slot in range(blocks)]
    inner_moves = [[(here, here ^ slot) for here in range(inner)] for slot in range(inner)]
    cores = [(here, here ^ 1) for here in range(inner)]
    core_groups = [list(range(core, count * inner, 2)) for core in range(2)]

    limit = 20 * MIB * max(1, blocks * depth * fold // LANES * 2 // fold)
    large = functools.partial(call, limit=limit)
    work = 4 * 2 * rows * 2 * blocks * depth * outer * pairs * 3

    by_side = cotangent.reshape(rows, blocks, 2, depth, pairs)
    half_cotangent = shape(rows, blocks, depth, pairs)
    right, left, cotangent_send, cotangent_own, weight = call(
        prepare_kernel,
        [
            shape(channels * depth, sequences),
            shape(rows * channels, sequences),
            half_cotangent,
            half_cotangent,
            shape(outer, pairs),
        ],
        [
            pltpu.VMEM((2, rows, features), F32),
            pltpu.VMEM((2, rows * features // LANES, LANES), F32),
            pltpu.VMEM((2, rows // PACK, LANES, LANES), F32),
            pltpu.SemaphoreType.DMA((5,)),
        ],
        name="prepare",
        far=range(4),
    )(by_side, alignment_right, alignment_left, projection_matrix)
    rights = [right]
    for slot in range(1, blocks):
        rights.append(lax.ppermute(right, "blk", slot_moves[slot]))
    cotangent_peer = lax.ppermute(cotangent_send, "blk", partner)
    left_peer = lax.ppermute(left, "blk", partner)

    factor = shape(row_pairs, tall, 4 * lanes, kind=BF16)
    factor_scratch = pltpu.VMEM(factor.shape, BF16)
    weight_cat = shape(tall, 3 * fold * pairs, kind=BF16)
    flip_scratch = pltpu.VMEM((2 * sequences, rows * channels), BF16)
    grad_own, partial, weight_cat = large(
        functools.partial(gradient_kernel, blocks),
        [factor, shape(steps // 2, sequences, 2 * lanes), weight_cat],
        [flip_scratch],
        "gradient_own",
    )(weight, cotangent_own, left)
    right_half = shape(blocks // 2, channels * depth, sequences)
    grad_peer, right_keep, right_send = large(
        functools.partial(right_kernel, blocks),
        [factor, right_half, right_half],
        [flip_scratch],
        "right_parts",
    )(weight_cat, cotangent_peer, left_peer, partial)
    right_send = lax.ppermute(right_send, "blk", slot_moves[blocks // 2])

    vmem = pl.BlockSpec(memory_space=pltpu.VMEM)
    hbm = pl.BlockSpec(memory_space=pltpu.HBM)
    keep, send, outer_own, outer_peer = large(
        functools.partial(weight_kernel, blocks),
        [shape(outer // 2, pairs)] * 2 + [pltpu.HBM(factor.shape, BF16)] * 2,
        [
            factor_scratch,
            factor_scratch,
            pltpu.VMEM((tall, fold * pairs), F32),
            pltpu.SemaphoreType.DMA((steps // 2, 2)),
        ],
        "weight",
        after=[right_keep],
        flops=2 * work,
        out_specs=[vmem, vmem, hbm, hbm],
    )(left, left_peer, cotangent_own, cotangent_peer, *rights)
    sent = lax.ppermute(send, "inner", cores)

    size = sequences // inner
    left_own, left_other = large(
        functools.partial(left_kernel, blocks, depth),
        [shape(inner, size, rows * channels)] * 2,
        [
            pltpu.VMEM((2 * rows * channels, sequences), F32),
            pltpu.VMEM((sequences, 2 * rows * channels), F32),
        ],
        "left_parts",
        after=[keep],
        flops=work,
    )(grad_own, grad_peer, *rights)
    keep, left_own = lax.optimization_barrier((keep, left_own))
    members = count * inner // 2
    pieces = (keep + sent).reshape(members, outer // 2 // members, pairs)

    def pair(values, after, name):
        return large(
            functools.partial(pair_kernel, blocks),
            shape(rows, blocks, depth, pairs),
            [
                factor_scratch,
                pltpu.VMEM((outer, pairs), F32),
                pltpu.VMEM((2 * fold * pairs, tall), BF16),
                pltpu.VMEM((tall, fold * pairs), F32),
                pltpu.SemaphoreType.DMA((row_pairs + 1,)),
            ],
            name,
            far=[0, 1],
            after=after,
            flops=work,
        )(values, projection_matrix)

    pieces, left_other = lax.optimization_barrier((pieces, left_other))
    left_other = lax.ppermute(left_other, "blk", partner)
    slot = blocks // 4
    while slot:
        part = shape(slot, channels * depth, sequences)
        right_keep, right_send = call(
            halve_kernel, [part, part], name="right_halve", after=[pieces]
        )(right_keep, right_send)
        right_send = lax.ppermute(right_send, "blk", slot_moves[slot])
        slot = slot // 2

    pair_other = pair(outer_peer, [pieces], "pair_peer")
    pair_found = lax.ppermute(pair_other, "blk", partner)

    pieces = lax.all_to_all(pieces, everyone, 0, 0, axis_index_groups=core_groups)
    pieces = call(
        spread_sum_kernel,
        shape(*pieces.shape),
        name="weight_sum",
        after=[pair_other, right_keep],
    )(pieces)
    pair_own = pair(outer_own, [pieces], "pair_own")
    left_found = call(
        left_add_kernel,
        [shape(size, rows * channels)] * inner,
        name="left_add",
        after=[pieces],
    )(left_own, left_other)
    pieces = lax.all_to_all(pieces, everyone, 0, 0, axis_index_groups=core_groups)

    left_found = [
        lax.ppermute(part, "inner", inner_moves[slot]) if slot else part
        for slot, part in enumerate(left_found)
    ]
    grad_left = call(
        functools.partial(turn_left_kernel, inner),
        shape(rows, features // inner),
        [
            pltpu.VMEM((size * rows * channels // LANES, LANES), F32),
            pltpu.VMEM((rows * features // inner // LANES, LANES), F32),
        ],
        name="turn_left",
    )(*left_found)

    grad_right = call(
        functools.partial(turn_right_kernel, 2),
        shape(depth, features),
        [
            pltpu.VMEM((channels * depth, sequences), F32),
            pltpu.VMEM((LANES, LANES), F32),
            pltpu.VMEM((depth * features // LANES, LANES), F32),
        ],
        name="turn_right",
    )(right_keep, right_send)

    pair_update = call(
        merge_kernel,
        pltpu.HBM(by_side.shape, F32),
        [pltpu.SemaphoreType.DMA((2,))],
        "merge",
        out_specs=hbm,
    )(pair_own, pair_found)
    pair_update = pair_update.reshape(cotangent.shape)

    pieces, pair_update, grad_left, grad_right = lax.optimization_barrier(
        (pieces, pair_update, grad_left, grad_right)
    )
    mine = pieces.reshape(outer // 2, pairs)
    other = lax.ppermute(mine, "inner", cores)
    grad_weight = call(place_kernel, shape(outer, pairs), name="place")(mine, other)
    return (pair_update, grad_left, grad_right, grad_weight)


def solution(mesh):
    placed = (
        P(("groups", "blk"), None),
        P(("groups", "blk", "inner"), None),
        P(),
        P(("groups", "blk"), None, "inner", None),
    )
    return jax.shard_map(
        local,
        mesh=mesh,
        in_specs=placed,
        out_specs=(
            P(("groups", "blk"), None, "inner", None),
            P(("groups", "blk"), "inner"),
            P(("groups", "blk", "inner"), None),
            P("groups", None),
        ),
        check_vma=False,
    )
```

```python
import functools

import jax
import jax.numpy as jnp
from jax import lax
from jax.experimental import pallas as pl
from jax.experimental.pallas import tpu as pltpu
from jax.sharding import PartitionSpec as P

ENTRY_CHANNELS = 32
LANES = 128
PACK = LANES // ENTRY_CHANNELS
F32 = jnp.float32
BF16 = jnp.bfloat16
MIB = 1024 * 1024


def halves(values):
    high = values.astype(BF16)
    low = (values - high.astype(F32)).astype(BF16)
    return high, low


def dot(left, right):
    return jnp.dot(left, right, preferred_element_type=F32)


def dot_rows(left, right):
    return lax.dot_general(left, right, (((1,), (1,)), ((), ())), preferred_element_type=F32)


def fold_of(columns):
    return max(1, LANES // columns)


def strided(start, size, stride):
    return pl.ds(start, size, stride=stride)


def folded_weight(weight_ref, step, fold):
    channels = ENTRY_CHANNELS
    return jnp.concatenate(
        [weight_ref[strided(step * fold + part, channels, channels), :] for part in range(fold)], 1
    )


def slots_of(blocks):
    here = lax.axis_index("blk") // 2
    return [lax.bitwise_xor(here, slot) for slot in range(blocks)]


def spread_of(cotangent_ref, pair, slots, fold):
    columns = len(slots) * cotangent_ref.shape[2]
    empty = jnp.zeros((columns, cotangent_ref.shape[3]), BF16)
    spread = ([], [])
    for part in range(2):
        rows = jnp.concatenate([cotangent_ref[2 * pair + part, slot] for slot in slots], 0)
        for found, values in zip(spread, halves(rows)):
            for place in range(fold):
                found.append(
                    jnp.concatenate(
                        [values if place == other else empty for other in range(fold)], 1
                    )
                )
    return [jnp.concatenate(found, 0) for found in spread]


def turn_in(rows_minor, in_ref, out_ref, tiles, square):
    channels = ENTRY_CHANNELS
    rows, features = in_ref.shape
    count = features // LANES
    for tile in range(count):
        tiles[tile * rows : (tile + 1) * rows, :] = in_ref[:, tile * LANES : (tile + 1) * LANES]
    for group in range(rows // PACK):
        found = [tiles[strided(group * PACK + k, count, rows), :] for k in range(PACK)]
        for part in range(PACK):
            lanes = slice(part * channels, (part + 1) * channels)
            square[group, strided(part, count, PACK), :] = jnp.concatenate(
                [values[:, lanes] for values in found], 1
            )
        turned = square[group].T
        if rows_minor:
            for k in range(PACK):
                out_ref[strided(group * PACK + k, channels, rows), :] = turned[
                    k * channels : (k + 1) * channels
                ]
        else:
            out_ref[group * LANES : (group + 1) * LANES, :] = turned


def prepare_kernel(
    cotangent_hbm,
    right_hbm,
    left_hbm,
    weight_hbm,
    right_out,
    left_out,
    send_out,
    own_out,
    weight_out,
    inputs,
    tiles,
    square,
    semaphores,
):
    parity = lax.rem(lax.axis_index("blk"), 2)
    moves = (
        (right_hbm, inputs.at[0]),
        (left_hbm, inputs.at[1]),
        (cotangent_hbm.at[:, :, 1 - parity], send_out),
        (cotangent_hbm.at[:, :, parity], own_out),
        (weight_hbm, weight_out),
    )
    copies = [
        pltpu.make_async_copy(source, target, semaphores.at[at])
        for at, (source, target) in enumerate(moves)
    ]
    for copy in copies:
        copy.start()
    copies[0].wait()
    turn_in(True, inputs.at[0], right_out, tiles.at[0], square.at[0])
    copies[1].wait()
    turn_in(False, inputs.at[1], left_out, tiles.at[1], square.at[1])
    for copy in copies[2:]:
        copy.wait()


def turn_right(part_refs, out_ref, total, square, tiles):
    channels = ENTRY_CHANNELS
    rows, features = out_ref.shape
    count = features // LANES
    total[...] = functools.reduce(jnp.add, [ref[0] for ref in part_refs])
    for group in range(rows // PACK):
        stacked = [total[strided(group * PACK + k, channels, rows), :] for k in range(PACK)]
        square[group] = jnp.concatenate(stacked, 0).T
        pieces = [square[group, strided(part, count, PACK), :] for part in range(PACK)]
        for k in range(PACK):
            lanes = slice(k * channels, (k + 1) * channels)
            tiles[strided(group * PACK + k, count, rows), :] = jnp.concatenate(
                [piece[:, lanes] for piece in pieces], 1
            )
    for tile in range(count):
        out_ref[:, tile * LANES : (tile + 1) * LANES] = tiles[tile * rows : (tile + 1) * rows, :]


def turn_left(part_refs, out_ref, total, tiles):
    channels = ENTRY_CHANNELS
    size, width = part_refs[0].shape
    rows, features = out_ref.shape
    count = features // LANES
    found = functools.reduce(jnp.add, [ref[...] for ref in part_refs])
    for tile in range(width // LANES):
        total[tile * size : (tile + 1) * size, :] = found[:, tile * LANES : (tile + 1) * LANES]
    for tile in range(width // LANES):
        pieces = [total[strided(tile * size + part, count, PACK), :] for part in range(PACK)]
        for k in range(PACK):
            lanes = slice(k * channels, (k + 1) * channels)
            tiles[strided(tile * PACK + k, count, rows), :] = jnp.concatenate(
                [piece[:, lanes] for piece in pieces], 1
            )
    for tile in range(count):
        out_ref[:, tile * LANES : (tile + 1) * LANES] = tiles[tile * rows : (tile + 1) * rows, :]


def prepare_weight(weight_ref, weight_cat, fold):
    channels = ENTRY_CHANNELS
    for step in range(channels // fold):
        high, low = halves(folded_weight(weight_ref, step, fold))
        weight_cat[step * channels : (step + 1) * channels, :] = jnp.concatenate(
            [high, low, high], 1
        )


def gradient_phase(blocks, cotangent_ref, out_ref, weight_cat):
    fold = fold_of(blocks * cotangent_ref.shape[2])
    slots = slots_of(blocks)

    def step_of(pair, carry):
        high, low = spread_of(cotangent_ref, pair, slots, fold)
        found = dot_rows(weight_cat[...], jnp.concatenate([high, high, low], 1))
        out_ref[pair] = jnp.concatenate(halves(found), 1)
        return carry

    lax.fori_loop(0, out_ref.shape[0], step_of, 0, unroll=2)


def gradient_kernel(
    blocks,
    weight_ref,
    cotangent_ref,
    left_ref,
    out_ref,
    partial_ref,
    weight_cat,
    flip_hbm,
    left_flip,
    weight_rows,
    weight_flip,
    semaphore,
):
    fold = fold_of(blocks * cotangent_ref.shape[2])
    prepare_weight(weight_ref, weight_cat, fold)
    gradient_phase(blocks, cotangent_ref, out_ref, weight_cat)

    def store(step, found):
        partial_ref[step] = found

    right_phase(left_ref, out_ref, left_flip, store)
    channels = ENTRY_CHANNELS
    wide = weight_rows.shape[1]
    for step in range(channels // fold):
        weight_rows[step * channels : (step + 1) * channels, :] = folded_weight(
            weight_ref, step, fold
        )
    flip_high, flip_low = halves(weight_rows[...].T)
    weight_flip[:wide, :] = flip_high
    weight_flip[wide:, :] = flip_low
    copy = pltpu.make_async_copy(weight_flip, flip_hbm, semaphore)
    copy.start()
    copy.wait()


def peer_kernel(blocks, weight_cat, cotangent_ref, out_ref):
    gradient_phase(blocks, cotangent_ref, out_ref, weight_cat)


def right_phase(left_ref, factor_ref, left_flip, store):
    sequences = left_ref.shape[1]
    lanes = factor_ref.shape[2] // 4
    flip_high, flip_low = halves((left_ref[...] * (1.0 / sequences)).T)
    left_flip[:sequences, :] = flip_high
    left_flip[sequences:, :] = flip_low

    def step_of(step, carry):
        high, low = (
            jnp.concatenate(
                [rows_of_step([factor_ref], 2 * step + part, half, lanes) for part in range(2)], 1
            )
            for half in range(2)
        )
        first = dot(left_flip[...], high)
        second = dot(left_flip[:sequences, :], low)
        store(step, first[:sequences] + first[sequences:] + second)
        return carry

    lax.fori_loop(0, factor_ref.shape[1] // (2 * ENTRY_CHANNELS), step_of, 0, unroll=2)


def rows_of_step(refs, step, half, lanes):
    channels = ENTRY_CHANNELS
    rows = pl.ds(pl.multiple_of(step * channels, channels), channels)
    start = 2 * half * lanes
    return jnp.concatenate(
        [
            ref[pair, rows, start + part * lanes : start + (part + 1) * lanes]
            for ref in refs
            for pair in range(ref.shape[0])
            for part in range(2)
        ],
        0,
    )


def both_left(left_refs):
    sequences = left_refs[0].shape[1]
    return jnp.concatenate([ref[...] for ref in left_refs], 0) * (1.0 / sequences)


def right_kernel(
    blocks, depth, peer_ref, left_ref, partial_ref, keep_ref, send_ref, left_flip
):
    fold = fold_of(blocks * depth)
    lanes = fold * blocks * depth

    def store(step, found):
        found = found + partial_ref[step]
        for part in range(2):
            turned = found[:, part * lanes : (part + 1) * lanes].T
            for place in range(fold):
                for slot in range(blocks):
                    start = (place * blocks + slot) * depth
                    row = pl.multiple_of(((2 * step + part) * fold + place) * depth, depth)
                    out_ref = send_ref if slot >= blocks // 2 else keep_ref
                    place_of = slot % (blocks // 2)
                    out_ref[place_of, pl.ds(row, depth), :] = turned[start : start + depth]

    right_phase(left_ref, peer_ref, left_flip, store)


def halve_kernel(keep_ref, found_ref, keep_out, send_out):
    half = keep_ref.shape[0] // 2
    for slot in range(half):
        keep_out[slot] = keep_ref[slot] + found_ref[slot]
        send_out[slot] = keep_ref[half + slot] + found_ref[half + slot]


def right_rows(right_refs, step, fold, depth):
    return jnp.concatenate(
        [
            ref[pl.ds(pl.multiple_of((step * fold + part) * depth, depth), depth), :]
            for part in range(fold)
            for ref in right_refs
        ],
        0,
    )


def weight_kernel(blocks, own_left, peer_left, own_cotangent, peer_cotangent, *refs):
    right_refs = refs[:blocks]
    keep_ref, send_ref, own_out, peer_out, own_ref, peer_ref, total, semaphores = refs[blocks:]
    channels = ENTRY_CHANNELS
    depth, pairs = own_cotangent.shape[2:]
    fold = fold_of(blocks * depth)
    lanes = fold * blocks * depth
    high, low = halves(both_left([own_left, peer_left]))
    left_cat = jnp.concatenate([high, low, high], 1)

    def copies(step):
        size = 2 * channels
        rows = pl.ds(pl.multiple_of(step * size, size), size)
        return [
            pltpu.make_async_copy(ref.at[:, rows], out.at[:, rows], semaphores.at[step, side])
            for side, (ref, out) in enumerate(((own_ref, own_out), (peer_ref, peer_out)))
        ]

    def outer_step(step, carry):
        right = [right_rows(right_refs, 2 * step + part, fold, depth) for part in range(2)]
        high, low = halves(jnp.concatenate(right, 0))
        found = dot_rows(left_cat, jnp.concatenate([high, high, low], 1))
        both = halves(found)
        for part in range(2):
            start = pl.multiple_of((2 * step + part) * channels, channels)
            row = 0
            for ref in (own_ref, peer_ref):
                for index in range(2 * ref.shape[0]):
                    for half in range(2):
                        lane = (2 * half + index % 2) * lanes
                        ref[index // 2, pl.ds(start, channels), lane : lane + lanes] = both[half][
                            row : row + channels, part * lanes : (part + 1) * lanes
                        ]
                    row += channels
        for copy in copies(step):
            copy.start()
        return carry

    lax.fori_loop(0, channels // (2 * fold), outer_step, 0, unroll=2)
    total[...] = jnp.zeros_like(total)

    def weight_step(pair, carry):
        lefts, rights = [], []
        for ref, cotangent_ref in ((own_ref, own_cotangent), (peer_ref, peer_cotangent)):
            high, low = spread_of(cotangent_ref, pair, slots_of(blocks), fold)
            lefts += [ref[pair], ref[pair, :, : 2 * lanes]]
            rights += [high, high, low]
        total[...] += dot(jnp.concatenate(lefts, 1), jnp.concatenate(rights, 0))
        return carry

    lax.fori_loop(0, own_ref.shape[0], weight_step, 0, unroll=2)
    core = lax.rem(lax.axis_index("inner"), 2)
    steps = channels // (2 * fold)
    for out_ref, half in ((keep_ref, core), (send_ref, 1 - core)):
        for step in range(steps):
            start = pl.multiple_of((half * steps + step) * channels, channels)
            found = total[pl.ds(start, channels), :]
            for part in range(fold):
                y = step * fold + part
                out_ref[y * channels : (y + 1) * channels, :] = found[
                    :, part * pairs : (part + 1) * pairs
                ]

    def finish(step, carry):
        for copy in copies(step):
            copy.wait()
        return carry

    lax.fori_loop(0, channels // (2 * fold), finish, 0)


def left_kernel(blocks, depth, own_ref, peer_ref, *refs):
    right_refs, (own_out, peer_out, total, flipped) = refs[:blocks], refs[blocks:]
    lanes = own_ref.shape[2] // 4
    fold = lanes // (blocks * depth)
    sequences = right_refs[0].shape[1]
    group = 4
    total[...] = jnp.zeros_like(total)

    def step_of(step, carry):
        steps = [group * step + part for part in range(group)]
        right = [right_rows(right_refs, at, fold, depth) for at in steps]
        high, low = halves(jnp.concatenate(right, 0))
        grads = [
            jnp.concatenate([rows_of_step([own_ref, peer_ref], at, half, lanes) for at in steps], 1)
            for half in range(2)
        ]
        both = dot(grads[0], jnp.concatenate([high, low], 1))
        total[...] += both[:, :sequences] + both[:, sequences:] + dot(grads[1], high)
        return carry

    lax.fori_loop(0, ENTRY_CHANNELS // (fold * group), step_of, 0, unroll=2)
    flipped[...] = total[...].T * (1.0 / sequences)
    inner, size, width = own_out.shape
    here = lax.axis_index("inner")
    for slot in range(inner):
        start = pl.multiple_of(lax.bitwise_xor(here, slot) * size, size)
        own_out[slot] = flipped[pl.ds(start, size), :width]
        peer_out[slot] = flipped[pl.ds(start, size), width:]


def left_add_kernel(own_ref, other_ref, *out_refs):
    for slot, ref in enumerate(out_refs):
        ref[...] = own_ref[slot] + other_ref[slot]


def pair_kernel(blocks, outer_hbm, flip_hbm, out_ref, outer_ref, weight_flip, semaphores):
    depth, pairs = out_ref.shape[2:]
    count = outer_ref.shape[0]
    lanes = outer_ref.shape[2] // 4
    columns = blocks * depth
    fold = lanes // columns
    wide = fold * pairs

    def copy_of(pair):
        return pltpu.make_async_copy(outer_hbm.at[pair], outer_ref.at[pair], semaphores.at[pair])

    flip_copy = pltpu.make_async_copy(flip_hbm, weight_flip, semaphores.at[count])
    flip_copy.start()
    for pair in range(count):
        copy_of(pair).start()
    flip_copy.wait()
    slots = slots_of(blocks)

    def step_of(pair, carry):
        copy_of(pair).wait()
        first = dot(weight_flip[...], outer_ref[pair, :, : 2 * lanes])
        second = dot(weight_flip[:wide, :], outer_ref[pair, :, 2 * lanes :])
        found = first[:wide] + first[wide:] + second
        for part in range(2):
            turned = []
            for place in range(fold):
                start = part * lanes
                piece = found[place * pairs : (place + 1) * pairs, start : start + lanes].T
                turned.append(piece[place * columns : (place + 1) * columns])
            turned = functools.reduce(jnp.add, turned)
            row = 2 * pair + part
            for slot in range(blocks):
                out_ref[row, slots[slot]] = turned[slot * depth : (slot + 1) * depth]
        return carry

    lax.fori_loop(0, count, step_of, 0, unroll=2)


def finish_kernel(own_ref, other_ref, keep_ref, found_ref, *refs):
    left_refs, refs = refs[:-9], refs[-9:]
    pair_hbm, left_out, right_out = refs[:3]
    right_total, right_square, right_tiles, left_total, left_tiles, semaphores = refs[3:]
    parity = lax.rem(lax.axis_index("blk"), 2)
    copies = [
        pltpu.make_async_copy(ref, pair_hbm.at[:, :, side], semaphores.at[at])
        for at, (ref, side) in enumerate(((own_ref, parity), (other_ref, 1 - parity)))
    ]
    for copy in copies:
        copy.start()
    turn_right([keep_ref, found_ref], right_out, right_total, right_square, right_tiles)
    turn_left(left_refs, left_out, left_total, left_tiles)
    for copy in copies:
        copy.wait()


def spread_sum_kernel(in_ref, out_ref):
    found = in_ref[0]
    for part in range(1, in_ref.shape[0]):
        found = found + in_ref[part]
    for part in range(in_ref.shape[0]):
        out_ref[part] = found


def place_kernel(mine_ref, other_ref, out_ref):
    channels = ENTRY_CHANNELS
    core = lax.rem(lax.axis_index("inner"), 2)
    steps = mine_ref.shape[0] // channels
    for ref, half in ((mine_ref, core), (other_ref, 1 - core)):
        for step in range(steps):
            rows = ref[step * channels : (step + 1) * channels, :]
            out_ref[strided(half * steps + step, channels, channels), :] = rows


def shape(*sizes, kind=F32):
    return jax.ShapeDtypeStruct(sizes, kind)


def call(
    kernel,
    out_shape,
    scratch=(),
    name=None,
    limit=16 * MIB,
    far=(),
    after=(),
    out_specs=None,
    flops=1,
):
    def run(*operands):
        vmem = pl.BlockSpec(memory_space=pltpu.VMEM)
        hbm = pl.BlockSpec(memory_space=pltpu.HBM)
        in_specs = [pl.BlockSpec(memory_space=pl.ANY)] * len(after)
        in_specs += [hbm if at in far else vmem for at in range(len(operands))]
        operands = [
            pltpu.with_memory_space_constraint(operand, pltpu.HBM) if at in far else operand
            for at, operand in enumerate(operands)
        ]
        extra = {} if out_specs is None else {"out_specs": out_specs}
        return pl.pallas_call(
            lambda *refs: kernel(*refs[len(after) :]),
            out_shape=out_shape,
            in_specs=in_specs,
            scratch_shapes=list(scratch),
            compiler_params=pltpu.CompilerParams(vmem_limit_bytes=limit),
            cost_estimate=pl.CostEstimate(flops=flops, bytes_accessed=1, transcendentals=0),
            name=name,
            **extra,
        )(*after, *operands)

    return run


def local(alignment_left, alignment_right, projection_matrix, cotangent):
    rows, features = alignment_left.shape
    depth = alignment_right.shape[0]
    count = lax.axis_size("blk")
    inner = lax.axis_size("inner")
    channels = ENTRY_CHANNELS
    sequences = features // channels
    outer, pairs = projection_matrix.shape
    blocks = count // 2
    fold = fold_of(blocks * depth)
    lanes = fold * blocks * depth
    tall = outer // fold
    steps = channels // fold
    row_pairs = rows // 2
    everyone = ("blk", "inner")

    partner = [(here, here ^ 1) for here in range(count)]
    slot_moves = [[(here, here ^ (2 * slot)) for here in range(count)] for slot in range(blocks)]
    inner_moves = [[(here, here ^ slot) for here in range(inner)] for slot in range(inner)]
    cores = [(here, here ^ 1) for here in range(inner)]
    core_groups = [list(range(core, count * inner, 2)) for core in range(2)]

    limit = 20 * MIB * max(1, blocks * depth * fold // LANES * 2 // fold)
    large = functools.partial(call, limit=limit)
    work = 4 * 2 * rows * 2 * blocks * depth * outer * pairs * 3

    by_side = cotangent.reshape(rows, blocks, 2, depth, pairs)
    half_cotangent = shape(rows, blocks, depth, pairs)
    right, left, cotangent_send, cotangent_own, weight = call(
        prepare_kernel,
        [
            shape(channels * depth, sequences),
            shape(rows * channels, sequences),
            half_cotangent,
            half_cotangent,
            shape(outer, pairs),
        ],
        [
            pltpu.VMEM((2, rows, features), F32),
            pltpu.VMEM((2, rows * features // LANES, LANES), F32),
            pltpu.VMEM((2, rows // PACK, LANES, LANES), F32),
            pltpu.SemaphoreType.DMA((5,)),
        ],
        name="prepare",
        far=range(4),
    )(by_side, alignment_right, alignment_left, projection_matrix)
    rights = [right]
    for slot in range(1, blocks):
        rights.append(lax.ppermute(right, "blk", slot_moves[slot]))
    cotangent_peer = lax.ppermute(cotangent_send, "blk", partner)
    left_peer = lax.ppermute(left, "blk", partner)

    vmem = pl.BlockSpec(memory_space=pltpu.VMEM)
    hbm = pl.BlockSpec(memory_space=pltpu.HBM)
    factor = shape(row_pairs, tall, 4 * lanes, kind=BF16)
    factor_scratch = pltpu.VMEM(factor.shape, BF16)
    weight_cat = shape(tall, 3 * fold * pairs, kind=BF16)
    flip_scratch = pltpu.VMEM((2 * sequences, rows * channels), BF16)
    flip_sizes = (2 * fold * pairs, tall)
    grad_own, partial, weight_cat, weight_flip = large(
        functools.partial(gradient_kernel, blocks),
        [
            factor,
            shape(steps // 2, sequences, 2 * lanes),
            weight_cat,
            pltpu.HBM(flip_sizes, BF16),
        ],
        [
            flip_scratch,
            pltpu.VMEM((tall, fold * pairs), F32),
            pltpu.VMEM(flip_sizes, BF16),
            pltpu.SemaphoreType.DMA,
        ],
        "gradient_own",
        out_specs=[vmem, vmem, vmem, hbm],
    )(weight, cotangent_own, left)
    grad_peer = large(functools.partial(peer_kernel, blocks), factor, [], "gradient_peer")(
        weight_cat, cotangent_peer
    )
    right_half = shape(blocks // 2, channels * depth, sequences)
    right_keep, right_send = large(
        functools.partial(right_kernel, blocks, depth),
        [right_half, right_half],
        [flip_scratch],
        "right_parts",
    )(grad_peer, left_peer, partial)
    right_send = lax.ppermute(right_send, "blk", slot_moves[blocks // 2])

    keep, send, outer_own, outer_peer = large(
        functools.partial(weight_kernel, blocks),
        [shape(outer // 2, pairs)] * 2 + [pltpu.HBM(factor.shape, BF16)] * 2,
        [
            factor_scratch,
            factor_scratch,
            pltpu.VMEM((tall, fold * pairs), F32),
            pltpu.SemaphoreType.DMA((steps // 2, 2)),
        ],
        "weight",
        after=[right_keep],
        flops=2 * work,
        out_specs=[vmem, vmem, hbm, hbm],
    )(left, left_peer, cotangent_own, cotangent_peer, *rights)
    sent = lax.ppermute(send, "inner", cores)

    size = sequences // inner
    left_own, left_other = large(
        functools.partial(left_kernel, blocks, depth),
        [shape(inner, size, rows * channels)] * 2,
        [
            pltpu.VMEM((2 * rows * channels, sequences), F32),
            pltpu.VMEM((sequences, 2 * rows * channels), F32),
        ],
        "left_parts",
        after=[keep],
        flops=work,
    )(grad_own, grad_peer, *rights)
    keep, left_own = lax.optimization_barrier((keep, left_own))
    members = count * inner // 2
    pieces = (keep + sent).reshape(members, outer // 2 // members, pairs)

    def pair(values, after, name):
        return large(
            functools.partial(pair_kernel, blocks),
            shape(rows, blocks, depth, pairs),
            [
                factor_scratch,
                pltpu.VMEM(flip_sizes, BF16),
                pltpu.SemaphoreType.DMA((row_pairs + 1,)),
            ],
            name,
            far=[0, 1],
            after=after,
            flops=work,
        )(values, weight_flip)

    pieces, left_other = lax.optimization_barrier((pieces, left_other))
    left_other = lax.ppermute(left_other, "blk", partner)
    slot = blocks // 4
    while slot:
        part = shape(slot, channels * depth, sequences)
        right_keep, right_send = call(
            halve_kernel, [part, part], name="right_halve", after=[pieces]
        )(right_keep, right_send)
        right_send = lax.ppermute(right_send, "blk", slot_moves[slot])
        slot = slot // 2

    pair_other = pair(outer_peer, [pieces], "pair_peer")
    pair_found = lax.ppermute(pair_other, "blk", partner)

    pieces = lax.all_to_all(pieces, everyone, 0, 0, axis_index_groups=core_groups)
    pieces = call(
        spread_sum_kernel,
        shape(*pieces.shape),
        name="weight_sum",
        after=[pair_other, right_keep],
    )(pieces)
    pair_own = pair(outer_own, [pieces], "pair_own")
    left_found = call(
        left_add_kernel,
        [shape(size, rows * channels)] * inner,
        name="left_add",
        after=[pieces],
    )(left_own, left_other)
    pieces = lax.all_to_all(pieces, everyone, 0, 0, axis_index_groups=core_groups)

    left_found = [
        lax.ppermute(part, "inner", inner_moves[slot]) if slot else part
        for slot, part in enumerate(left_found)
    ]
    pair_update, grad_left, grad_right = call(
        finish_kernel,
        [
            pltpu.HBM(by_side.shape, F32),
            shape(rows, features // inner),
            shape(depth, features),
        ],
        [
            pltpu.VMEM((channels * depth, sequences), F32),
            pltpu.VMEM((depth // PACK, LANES, LANES), F32),
            pltpu.VMEM((depth * features // LANES, LANES), F32),
            pltpu.VMEM((size * rows * channels // LANES, LANES), F32),
            pltpu.VMEM((rows * features // inner // LANES, LANES), F32),
            pltpu.SemaphoreType.DMA((2,)),
        ],
        "finish",
        out_specs=[hbm, vmem, vmem],
    )(pair_own, pair_found, right_keep, right_send, *left_found)
    pair_update = pair_update.reshape(cotangent.shape)

    pieces, pair_update, grad_left, grad_right = lax.optimization_barrier(
        (pieces, pair_update, grad_left, grad_right)
    )
    mine = pieces.reshape(outer // 2, pairs)
    other = lax.ppermute(mine, "inner", cores)
    grad_weight = call(place_kernel, shape(outer, pairs), name="place")(mine, other)
    return (pair_update, grad_left, grad_right, grad_weight)


def solution(mesh):
    placed = (
        P(("groups", "blk"), None),
        P(("groups", "blk", "inner"), None),
        P(),
        P(("groups", "blk"), None, "inner", None),
    )
    return jax.shard_map(
        local,
        mesh=mesh,
        in_specs=placed,
        out_specs=(
            P(("groups", "blk"), None, "inner", None),
            P(("groups", "blk"), "inner"),
            P(("groups", "blk", "inner"), None),
            P("groups", None),
        ),
        check_vma=False,
    )
```

```python
import functools

import jax
import jax.numpy as jnp
from jax import lax
from jax.experimental import pallas as pl
from jax.experimental.pallas import tpu as pltpu
from jax.sharding import PartitionSpec as P

ENTRY_CHANNELS = 32
LANES = 128
PACK = LANES // ENTRY_CHANNELS
F32 = jnp.float32
BF16 = jnp.bfloat16
MIB = 1024 * 1024


def halves(values):
    high = values.astype(BF16)
    low = (values - high.astype(F32)).astype(BF16)
    return high, low


def dot(left, right):
    return jnp.dot(left, right, preferred_element_type=F32)


def dot_rows(left, right):
    return lax.dot_general(left, right, (((1,), (1,)), ((), ())), preferred_element_type=F32)


def fold_of(columns):
    return max(1, LANES // columns)


def strided(start, size, stride):
    return pl.ds(start, size, stride=stride)


def folded_weight(weight_ref, step, fold):
    channels = ENTRY_CHANNELS
    return jnp.concatenate(
        [weight_ref[strided(step * fold + part, channels, channels), :] for part in range(fold)], 1
    )


def slots_of(blocks):
    here = lax.axis_index("blk") // 2
    return [lax.bitwise_xor(here, slot) for slot in range(blocks)]


def spread_of(cotangent_ref, pair, slots, fold):
    columns = len(slots) * cotangent_ref.shape[2]
    empty = jnp.zeros((columns, cotangent_ref.shape[3]), BF16)
    spread = ([], [])
    for part in range(2):
        rows = jnp.concatenate([cotangent_ref[2 * pair + part, slot] for slot in slots], 0)
        for found, values in zip(spread, halves(rows)):
            for place in range(fold):
                found.append(
                    jnp.concatenate(
                        [values if place == other else empty for other in range(fold)], 1
                    )
                )
    return [jnp.concatenate(found, 0) for found in spread]


def turn_in(rows_minor, in_ref, out_ref, tiles, square):
    channels = ENTRY_CHANNELS
    rows, features = in_ref.shape
    count = features // LANES
    for tile in range(count):
        tiles[tile * rows : (tile + 1) * rows, :] = in_ref[:, tile * LANES : (tile + 1) * LANES]
    for group in range(rows // PACK):
        found = [tiles[strided(group * PACK + k, count, rows), :] for k in range(PACK)]
        for part in range(PACK):
            lanes = slice(part * channels, (part + 1) * channels)
            square[group, strided(part, count, PACK), :] = jnp.concatenate(
                [values[:, lanes] for values in found], 1
            )
        turned = square[group].T
        if rows_minor:
            for k in range(PACK):
                out_ref[strided(group * PACK + k, channels, rows), :] = turned[
                    k * channels : (k + 1) * channels
                ]
        else:
            out_ref[group * LANES : (group + 1) * LANES, :] = turned


def prepare_kernel(
    cotangent_hbm,
    right_hbm,
    left_hbm,
    weight_hbm,
    right_out,
    left_out,
    send_out,
    own_out,
    weight_out,
    inputs,
    tiles,
    square,
    semaphores,
):
    parity = lax.rem(lax.axis_index("blk"), 2)
    moves = (
        (right_hbm, inputs.at[0]),
        (left_hbm, inputs.at[1]),
        (cotangent_hbm.at[:, :, 1 - parity], send_out),
        (cotangent_hbm.at[:, :, parity], own_out),
        (weight_hbm, weight_out),
    )
    copies = [
        pltpu.make_async_copy(source, target, semaphores.at[at])
        for at, (source, target) in enumerate(moves)
    ]
    for copy in copies:
        copy.start()
    copies[0].wait()
    turn_in(True, inputs.at[0], right_out, tiles.at[0], square.at[0])
    copies[1].wait()
    turn_in(False, inputs.at[1], left_out, tiles.at[1], square.at[1])
    for copy in copies[2:]:
        copy.wait()


def turn_right(part_refs, out_ref, total, square, tiles):
    channels = ENTRY_CHANNELS
    rows, features = out_ref.shape
    count = features // LANES
    total[...] = functools.reduce(jnp.add, [ref[0] for ref in part_refs])
    for group in range(rows // PACK):
        stacked = [total[strided(group * PACK + k, channels, rows), :] for k in range(PACK)]
        square[group] = jnp.concatenate(stacked, 0).T
        pieces = [square[group, strided(part, count, PACK), :] for part in range(PACK)]
        for k in range(PACK):
            lanes = slice(k * channels, (k + 1) * channels)
            tiles[strided(group * PACK + k, count, rows), :] = jnp.concatenate(
                [piece[:, lanes] for piece in pieces], 1
            )
    for tile in range(count):
        out_ref[:, tile * LANES : (tile + 1) * LANES] = tiles[tile * rows : (tile + 1) * rows, :]


def turn_left(part_refs, out_ref, total, tiles):
    channels = ENTRY_CHANNELS
    size, width = part_refs[0].shape
    rows, features = out_ref.shape
    count = features // LANES
    found = functools.reduce(jnp.add, [ref[...] for ref in part_refs])
    for tile in range(width // LANES):
        total[tile * size : (tile + 1) * size, :] = found[:, tile * LANES : (tile + 1) * LANES]
    for tile in range(width // LANES):
        pieces = [total[strided(tile * size + part, count, PACK), :] for part in range(PACK)]
        for k in range(PACK):
            lanes = slice(k * channels, (k + 1) * channels)
            tiles[strided(tile * PACK + k, count, rows), :] = jnp.concatenate(
                [piece[:, lanes] for piece in pieces], 1
            )
    for tile in range(count):
        out_ref[:, tile * LANES : (tile + 1) * LANES] = tiles[tile * rows : (tile + 1) * rows, :]


def prepare_weight(weight_ref, weight_cat, fold):
    channels = ENTRY_CHANNELS
    for step in range(channels // fold):
        high, low = halves(folded_weight(weight_ref, step, fold))
        weight_cat[step * channels : (step + 1) * channels, :] = jnp.concatenate(
            [high, low, high], 1
        )


def gradient_phase(blocks, cotangent_ref, out_ref, spread_ref, weight_cat):
    fold = fold_of(blocks * cotangent_ref.shape[2])
    slots = slots_of(blocks)

    def step_of(pair, carry):
        high, low = spread_of(cotangent_ref, pair, slots, fold)
        spread_ref[pair, 0] = high
        spread_ref[pair, 1] = low
        found = dot_rows(weight_cat[...], jnp.concatenate([high, high, low], 1))
        out_ref[pair] = jnp.concatenate(halves(found), 1)
        return carry

    lax.fori_loop(0, out_ref.shape[0], step_of, 0, unroll=2)


def gradient_kernel(
    blocks,
    weight_ref,
    cotangent_ref,
    left_ref,
    out_ref,
    spread_ref,
    partial_ref,
    weight_cat,
    flip_hbm,
    left_flip,
    weight_rows,
    weight_flip,
    semaphore,
):
    fold = fold_of(blocks * cotangent_ref.shape[2])
    prepare_weight(weight_ref, weight_cat, fold)
    gradient_phase(blocks, cotangent_ref, out_ref, spread_ref, weight_cat)

    def store(step, found):
        partial_ref[step] = found

    right_phase(left_ref, out_ref, left_flip, store)
    channels = ENTRY_CHANNELS
    wide = weight_rows.shape[1]
    for step in range(channels // fold):
        weight_rows[step * channels : (step + 1) * channels, :] = folded_weight(
            weight_ref, step, fold
        )
    flip_high, flip_low = halves(weight_rows[...].T)
    weight_flip[:wide, :] = flip_high
    weight_flip[wide:, :] = flip_low
    copy = pltpu.make_async_copy(weight_flip, flip_hbm, semaphore)
    copy.start()
    copy.wait()


def peer_kernel(blocks, weight_cat, cotangent_ref, out_ref, spread_ref):
    gradient_phase(blocks, cotangent_ref, out_ref, spread_ref, weight_cat)


def right_phase(left_ref, factor_ref, left_flip, store):
    sequences = left_ref.shape[1]
    lanes = factor_ref.shape[2] // 4
    flip_high, flip_low = halves((left_ref[...] * (1.0 / sequences)).T)
    left_flip[:sequences, :] = flip_high
    left_flip[sequences:, :] = flip_low

    def step_of(step, carry):
        high, low = (
            jnp.concatenate(
                [rows_of_step([factor_ref], 2 * step + part, half, lanes) for part in range(2)], 1
            )
            for half in range(2)
        )
        first = dot(left_flip[...], high)
        second = dot(left_flip[:sequences, :], low)
        store(step, first[:sequences] + first[sequences:] + second)
        return carry

    lax.fori_loop(0, factor_ref.shape[1] // (2 * ENTRY_CHANNELS), step_of, 0, unroll=2)


def rows_of_step(refs, step, half, lanes):
    channels = ENTRY_CHANNELS
    rows = pl.ds(pl.multiple_of(step * channels, channels), channels)
    start = 2 * half * lanes
    return jnp.concatenate(
        [
            ref[pair, rows, start + part * lanes : start + (part + 1) * lanes]
            for ref in refs
            for pair in range(ref.shape[0])
            for part in range(2)
        ],
        0,
    )


def both_left(left_refs):
    sequences = left_refs[0].shape[1]
    return jnp.concatenate([ref[...] for ref in left_refs], 0) * (1.0 / sequences)


def right_kernel(
    blocks, depth, peer_ref, left_ref, partial_ref, keep_ref, send_ref, left_flip
):
    fold = fold_of(blocks * depth)
    lanes = fold * blocks * depth

    def store(step, found):
        found = found + partial_ref[step]
        for part in range(2):
            turned = found[:, part * lanes : (part + 1) * lanes].T
            for place in range(fold):
                for slot in range(blocks):
                    start = (place * blocks + slot) * depth
                    row = pl.multiple_of(((2 * step + part) * fold + place) * depth, depth)
                    out_ref = send_ref if slot % 2 else keep_ref
                    out_ref[slot // 2, pl.ds(row, depth), :] = turned[start : start + depth]

    right_phase(left_ref, peer_ref, left_flip, store)


def halve_kernel(keep_ref, found_ref, keep_out, send_out):
    for slot in range(keep_ref.shape[0]):
        out_ref = send_out if slot % 2 else keep_out
        out_ref[slot // 2] = keep_ref[slot] + found_ref[slot]


def right_rows(right_refs, step, fold, depth):
    return jnp.concatenate(
        [
            ref[pl.ds(pl.multiple_of((step * fold + part) * depth, depth), depth), :]
            for part in range(fold)
            for ref in right_refs
        ],
        0,
    )


def weight_kernel(blocks, depth, own_left, peer_left, own_spread, peer_spread, *refs):
    right_refs = refs[:blocks]
    keep_ref, send_ref, own_out, peer_out, own_ref, peer_ref, total, semaphores = refs[blocks:]
    channels = ENTRY_CHANNELS
    fold = fold_of(blocks * depth)
    lanes = fold * blocks * depth
    pairs = total.shape[1] // fold
    high, low = halves(both_left([own_left, peer_left]))
    left_cat = jnp.concatenate([high, low, high], 1)

    def copies(step):
        size = 2 * channels
        rows = pl.ds(pl.multiple_of(step * size, size), size)
        return [
            pltpu.make_async_copy(ref.at[:, rows], out.at[:, rows], semaphores.at[step, side])
            for side, (ref, out) in enumerate(((own_ref, own_out), (peer_ref, peer_out)))
        ]

    def outer_step(step, carry):
        right = [right_rows(right_refs, 2 * step + part, fold, depth) for part in range(2)]
        high, low = halves(jnp.concatenate(right, 0))
        found = dot_rows(left_cat, jnp.concatenate([high, high, low], 1))
        both = halves(found)
        for part in range(2):
            start = pl.multiple_of((2 * step + part) * channels, channels)
            row = 0
            for ref in (own_ref, peer_ref):
                for index in range(2 * ref.shape[0]):
                    for half in range(2):
                        lane = (2 * half + index % 2) * lanes
                        ref[index // 2, pl.ds(start, channels), lane : lane + lanes] = both[half][
                            row : row + channels, part * lanes : (part + 1) * lanes
                        ]
                    row += channels
        for copy in copies(step):
            copy.start()
        return carry

    lax.fori_loop(0, channels // (2 * fold), outer_step, 0, unroll=2)
    total[...] = jnp.zeros_like(total)

    def weight_step(pair, carry):
        lefts, rights = [], []
        for ref, spread_ref in ((own_ref, own_spread), (peer_ref, peer_spread)):
            high = spread_ref[pair, 0]
            lefts += [ref[pair], ref[pair, :, : 2 * lanes]]
            rights += [high, high, spread_ref[pair, 1]]
        total[...] += dot(jnp.concatenate(lefts, 1), jnp.concatenate(rights, 0))
        return carry

    lax.fori_loop(0, own_ref.shape[0], weight_step, 0, unroll=2)
    core = lax.rem(lax.axis_index("inner"), 2)
    steps = channels // (2 * fold)
    for out_ref, half in ((keep_ref, core), (send_ref, 1 - core)):
        for step in range(steps):
            start = pl.multiple_of((half * steps + step) * channels, channels)
            found = total[pl.ds(start, channels), :]
            for part in range(fold):
                y = step * fold + part
                out_ref[y * channels : (y + 1) * channels, :] = found[
                    :, part * pairs : (part + 1) * pairs
                ]

    def finish(step, carry):
        for copy in copies(step):
            copy.wait()
        return carry

    lax.fori_loop(0, channels // (2 * fold), finish, 0)


def left_kernel(blocks, depth, own_ref, peer_ref, *refs):
    right_refs, (own_out, peer_out, total, flipped) = refs[:blocks], refs[blocks:]
    lanes = own_ref.shape[2] // 4
    fold = lanes // (blocks * depth)
    sequences = right_refs[0].shape[1]
    group = 4
    total[...] = jnp.zeros_like(total)

    def step_of(step, carry):
        steps = [group * step + part for part in range(group)]
        right = [right_rows(right_refs, at, fold, depth) for at in steps]
        high, low = halves(jnp.concatenate(right, 0))
        grads = [
            jnp.concatenate([rows_of_step([own_ref, peer_ref], at, half, lanes) for at in steps], 1)
            for half in range(2)
        ]
        both = dot(grads[0], jnp.concatenate([high, low], 1))
        total[...] += both[:, :sequences] + both[:, sequences:] + dot(grads[1], high)
        return carry

    lax.fori_loop(0, ENTRY_CHANNELS // (fold * group), step_of, 0, unroll=2)
    flipped[...] = total[...].T * (1.0 / sequences)
    inner, size, width = own_out.shape
    here = lax.axis_index("inner")
    for slot in range(inner):
        start = pl.multiple_of(lax.bitwise_xor(here, slot) * size, size)
        own_out[slot] = flipped[pl.ds(start, size), :width]
        peer_out[slot] = flipped[pl.ds(start, size), width:]


def left_add_kernel(own_ref, other_ref, *out_refs):
    for slot, ref in enumerate(out_refs):
        ref[...] = own_ref[slot] + other_ref[slot]


def pair_kernel(blocks, outer_hbm, flip_hbm, out_ref, outer_ref, weight_flip, semaphores):
    depth, pairs = out_ref.shape[2:]
    count = outer_ref.shape[0]
    lanes = outer_ref.shape[2] // 4
    columns = blocks * depth
    fold = lanes // columns
    wide = fold * pairs

    def copy_of(pair):
        return pltpu.make_async_copy(outer_hbm.at[pair], outer_ref.at[pair], semaphores.at[pair])

    flip_copy = pltpu.make_async_copy(flip_hbm, weight_flip, semaphores.at[count])
    flip_copy.start()
    for pair in range(count):
        copy_of(pair).start()
    flip_copy.wait()
    slots = slots_of(blocks)

    def step_of(pair, carry):
        copy_of(pair).wait()
        first = dot(weight_flip[...], outer_ref[pair, :, : 2 * lanes])
        second = dot(weight_flip[:wide, :], outer_ref[pair, :, 2 * lanes :])
        found = first[:wide] + first[wide:] + second
        for part in range(2):
            turned = []
            for place in range(fold):
                start = part * lanes
                piece = found[place * pairs : (place + 1) * pairs, start : start + lanes].T
                turned.append(piece[place * columns : (place + 1) * columns])
            turned = functools.reduce(jnp.add, turned)
            row = 2 * pair + part
            for slot in range(blocks):
                out_ref[row, slots[slot]] = turned[slot * depth : (slot + 1) * depth]
        return carry

    lax.fori_loop(0, count, step_of, 0)


def finish_kernel(own_ref, other_ref, keep_ref, found_ref, *refs):
    left_refs, refs = refs[:-9], refs[-9:]
    pair_hbm, left_out, right_out = refs[:3]
    right_total, right_square, right_tiles, left_total, left_tiles, semaphores = refs[3:]
    parity = lax.rem(lax.axis_index("blk"), 2)
    copies = [
        pltpu.make_async_copy(ref, pair_hbm.at[:, :, side], semaphores.at[at])
        for at, (ref, side) in enumerate(((own_ref, parity), (other_ref, 1 - parity)))
    ]
    for copy in copies:
        copy.start()
    turn_right([keep_ref, found_ref], right_out, right_total, right_square, right_tiles)
    turn_left(left_refs, left_out, left_total, left_tiles)
    for copy in copies:
        copy.wait()


def spread_sum_kernel(in_ref, out_ref):
    found = in_ref[0]
    for part in range(1, in_ref.shape[0]):
        found = found + in_ref[part]
    for part in range(in_ref.shape[0]):
        out_ref[part] = found


def place_kernel(mine_ref, other_ref, out_ref):
    channels = ENTRY_CHANNELS
    core = lax.rem(lax.axis_index("inner"), 2)
    steps = mine_ref.shape[0] // channels
    for ref, half in ((mine_ref, core), (other_ref, 1 - core)):
        for step in range(steps):
            rows = ref[step * channels : (step + 1) * channels, :]
            out_ref[strided(half * steps + step, channels, channels), :] = rows


def shape(*sizes, kind=F32):
    return jax.ShapeDtypeStruct(sizes, kind)


def call(
    kernel,
    out_shape,
    scratch=(),
    name=None,
    limit=16 * MIB,
    far=(),
    after=(),
    out_specs=None,
    flops=1,
):
    def run(*operands):
        vmem = pl.BlockSpec(memory_space=pltpu.VMEM)
        hbm = pl.BlockSpec(memory_space=pltpu.HBM)
        in_specs = [pl.BlockSpec(memory_space=pl.ANY)] * len(after)
        in_specs += [hbm if at in far else vmem for at in range(len(operands))]
        operands = [
            pltpu.with_memory_space_constraint(operand, pltpu.HBM) if at in far else operand
            for at, operand in enumerate(operands)
        ]
        extra = {} if out_specs is None else {"out_specs": out_specs}
        return pl.pallas_call(
            lambda *refs: kernel(*refs[len(after) :]),
            out_shape=out_shape,
            in_specs=in_specs,
            scratch_shapes=list(scratch),
            compiler_params=pltpu.CompilerParams(vmem_limit_bytes=limit),
            cost_estimate=pl.CostEstimate(flops=flops, bytes_accessed=1, transcendentals=0),
            name=name,
            **extra,
        )(*after, *operands)

    return run


def local(alignment_left, alignment_right, projection_matrix, cotangent):
    rows, features = alignment_left.shape
    depth = alignment_right.shape[0]
    count = lax.axis_size("blk")
    inner = lax.axis_size("inner")
    channels = ENTRY_CHANNELS
    sequences = features // channels
    outer, pairs = projection_matrix.shape
    blocks = count // 2
    fold = fold_of(blocks * depth)
    lanes = fold * blocks * depth
    tall = outer // fold
    steps = channels // fold
    row_pairs = rows // 2
    everyone = ("blk", "inner")

    partner = [(here, here ^ 1) for here in range(count)]
    slot_moves = [[(here, here ^ (2 * slot)) for here in range(count)] for slot in range(blocks)]
    inner_moves = [[(here, here ^ slot) for here in range(inner)] for slot in range(inner)]
    cores = [(here, here ^ 1) for here in range(inner)]
    core_groups = [list(range(core, count * inner, 2)) for core in range(2)]

    limit = 20 * MIB * max(1, blocks * depth * fold // LANES * 2 // fold)
    large = functools.partial(call, limit=limit)
    work = 4 * 2 * rows * 2 * blocks * depth * outer * pairs * 3

    by_side = cotangent.reshape(rows, blocks, 2, depth, pairs)
    half_cotangent = shape(rows, blocks, depth, pairs)
    right, left, cotangent_send, cotangent_own, weight = call(
        prepare_kernel,
        [
            shape(channels * depth, sequences),
            shape(rows * channels, sequences),
            half_cotangent,
            half_cotangent,
            shape(outer, pairs),
        ],
        [
            pltpu.VMEM((2, rows, features), F32),
            pltpu.VMEM((2, rows * features // LANES, LANES), F32),
            pltpu.VMEM((2, rows // PACK, LANES, LANES), F32),
            pltpu.SemaphoreType.DMA((5,)),
        ],
        name="prepare",
        far=range(4),
    )(by_side, alignment_right, alignment_left, projection_matrix)
    rights = [right]
    for slot in range(1, blocks):
        rights.append(lax.ppermute(right, "blk", slot_moves[slot]))
    cotangent_peer = lax.ppermute(cotangent_send, "blk", partner)
    left_peer = lax.ppermute(left, "blk", partner)

    vmem = pl.BlockSpec(memory_space=pltpu.VMEM)
    hbm = pl.BlockSpec(memory_space=pltpu.HBM)
    factor = shape(row_pairs, tall, 4 * lanes, kind=BF16)
    factor_scratch = pltpu.VMEM(factor.shape, BF16)
    weight_cat = shape(tall, 3 * fold * pairs, kind=BF16)
    flip_scratch = pltpu.VMEM((2 * sequences, rows * channels), BF16)
    flip_sizes = (2 * fold * pairs, tall)
    spread = shape(row_pairs, 2, 2 * lanes, fold * pairs, kind=BF16)
    grad_own, spread_own, partial, weight_cat, weight_flip = large(
        functools.partial(gradient_kernel, blocks),
        [
            factor,
            spread,
            shape(steps // 2, sequences, 2 * lanes),
            weight_cat,
            pltpu.HBM(flip_sizes, BF16),
        ],
        [
            flip_scratch,
            pltpu.VMEM((tall, fold * pairs), F32),
            pltpu.VMEM(flip_sizes, BF16),
            pltpu.SemaphoreType.DMA,
        ],
        "gradient_own",
        out_specs=[vmem, vmem, vmem, vmem, hbm],
    )(weight, cotangent_own, left)
    grad_peer, spread_peer = large(
        functools.partial(peer_kernel, blocks), [factor, spread], [], "gradient_peer"
    )(weight_cat, cotangent_peer)
    right_half = shape(blocks // 2, channels * depth, sequences)
    right_keep, right_send = large(
        functools.partial(right_kernel, blocks, depth),
        [right_half, right_half],
        [flip_scratch],
        "right_parts",
    )(grad_peer, left_peer, partial)
    right_send = lax.ppermute(right_send, "blk", slot_moves[1])

    keep, send, outer_own, outer_peer = large(
        functools.partial(weight_kernel, blocks, depth),
        [shape(outer // 2, pairs)] * 2 + [pltpu.HBM(factor.shape, BF16)] * 2,
        [
            factor_scratch,
            factor_scratch,
            pltpu.VMEM((tall, fold * pairs), F32),
            pltpu.SemaphoreType.DMA((steps // 2, 2)),
        ],
        "weight",
        after=[right_keep],
        flops=2 * work,
        out_specs=[vmem, vmem, hbm, hbm],
    )(left, left_peer, spread_own, spread_peer, *rights)
    sent = lax.ppermute(send, "inner", cores)

    size = sequences // inner
    left_own, left_other = large(
        functools.partial(left_kernel, blocks, depth),
        [shape(inner, size, rows * channels)] * 2,
        [
            pltpu.VMEM((2 * rows * channels, sequences), F32),
            pltpu.VMEM((sequences, 2 * rows * channels), F32),
        ],
        "left_parts",
        after=[keep],
        flops=work,
    )(grad_own, grad_peer, *rights)
    keep, left_own = lax.optimization_barrier((keep, left_own))
    members = count * inner // 2
    pieces = (keep + sent).reshape(members, outer // 2 // members, pairs)

    def pair(values, after, name):
        return large(
            functools.partial(pair_kernel, blocks),
            shape(rows, blocks, depth, pairs),
            [
                factor_scratch,
                pltpu.VMEM(flip_sizes, BF16),
                pltpu.SemaphoreType.DMA((row_pairs + 1,)),
            ],
            name,
            far=[0, 1],
            after=after,
            flops=work,
        )(values, weight_flip)

    pieces, left_other = lax.optimization_barrier((pieces, left_other))
    left_other = lax.ppermute(left_other, "blk", partner)
    slot = 2
    while slot < blocks:
        part = shape(blocks // (2 * slot), channels * depth, sequences)
        right_keep, right_send = call(
            halve_kernel, [part, part], name="right_halve", after=[pieces]
        )(right_keep, right_send)
        right_send = lax.ppermute(right_send, "blk", slot_moves[slot])
        slot = 2 * slot

    pair_other = pair(outer_peer, [pieces], "pair_peer")
    pair_found = lax.ppermute(pair_other, "blk", partner)

    pieces = lax.all_to_all(pieces, everyone, 0, 0, axis_index_groups=core_groups)
    pieces = call(
        spread_sum_kernel,
        shape(*pieces.shape),
        name="weight_sum",
        after=[pair_other, right_keep],
    )(pieces)
    pair_own = pair(outer_own, [pieces], "pair_own")
    left_found = call(
        left_add_kernel,
        [shape(size, rows * channels)] * inner,
        name="left_add",
        after=[pieces],
    )(left_own, left_other)
    pieces = lax.all_to_all(pieces, everyone, 0, 0, axis_index_groups=core_groups)

    left_found = [
        lax.ppermute(part, "inner", inner_moves[slot]) if slot else part
        for slot, part in enumerate(left_found)
    ]
    pair_update, grad_left, grad_right = call(
        finish_kernel,
        [
            pltpu.HBM(by_side.shape, F32),
            shape(rows, features // inner),
            shape(depth, features),
        ],
        [
            pltpu.VMEM((channels * depth, sequences), F32),
            pltpu.VMEM((depth // PACK, LANES, LANES), F32),
            pltpu.VMEM((depth * features // LANES, LANES), F32),
            pltpu.VMEM((size * rows * channels // LANES, LANES), F32),
            pltpu.VMEM((rows * features // inner // LANES, LANES), F32),
            pltpu.SemaphoreType.DMA((2,)),
        ],
        "finish",
        out_specs=[hbm, vmem, vmem],
    )(pair_own, pair_found, right_keep, right_send, *left_found)
    pair_update = pair_update.reshape(cotangent.shape)

    pieces, pair_update, grad_left, grad_right = lax.optimization_barrier(
        (pieces, pair_update, grad_left, grad_right)
    )
    mine = pieces.reshape(outer // 2, pairs)
    other = lax.ppermute(mine, "inner", cores)
    grad_weight = call(place_kernel, shape(outer, pairs), name="place")(mine, other)
    return (pair_update, grad_left, grad_right, grad_weight)


def solution(mesh):
    placed = (
        P(("groups", "blk"), None),
        P(("groups", "blk", "inner"), None),
        P(),
        P(("groups", "blk"), None, "inner", None),
    )
    return jax.shard_map(
        local,
        mesh=mesh,
        in_specs=placed,
        out_specs=(
            P(("groups", "blk"), None, "inner", None),
            P(("groups", "blk"), "inner"),
            P(("groups", "blk", "inner"), None),
            P("groups", None),
        ),
        check_vma=False,
    )
```

```python
import functools

import jax
import jax.numpy as jnp
from jax import lax
from jax.experimental import pallas as pl
from jax.experimental.pallas import tpu as pltpu
from jax.sharding import PartitionSpec as P

ENTRY_CHANNELS = 32
LANES = 128
PACK = LANES // ENTRY_CHANNELS
F32 = jnp.float32
BF16 = jnp.bfloat16
MIB = 1024 * 1024


def halves(values):
    high = values.astype(BF16)
    low = (values - high.astype(F32)).astype(BF16)
    return high, low


def dot(left, right):
    return jnp.dot(left, right, preferred_element_type=F32)


def dot_rows(left, right):
    return lax.dot_general(left, right, (((1,), (1,)), ((), ())), preferred_element_type=F32)


def fold_of(columns):
    return max(1, LANES // columns)


def strided(start, size, stride):
    return pl.ds(start, size, stride=stride)


def folded_weight(weight_ref, step, fold):
    channels = ENTRY_CHANNELS
    return jnp.concatenate(
        [weight_ref[strided(step * fold + part, channels, channels), :] for part in range(fold)], 1
    )


def slots_of(blocks):
    here = lax.axis_index("blk") // 2
    return [lax.bitwise_xor(here, slot) for slot in range(blocks)]


def spread_of(cotangent_ref, pair, slots, fold):
    columns = len(slots) * cotangent_ref.shape[2]
    empty = jnp.zeros((columns, cotangent_ref.shape[3]), BF16)
    spread = ([], [])
    for part in range(2):
        rows = jnp.concatenate([cotangent_ref[2 * pair + part, slot] for slot in slots], 0)
        for found, values in zip(spread, halves(rows)):
            for place in range(fold):
                found.append(
                    jnp.concatenate(
                        [values if place == other else empty for other in range(fold)], 1
                    )
                )
    return [jnp.concatenate(found, 0) for found in spread]


def turn_in(rows_minor, in_ref, out_ref, tiles, square):
    channels = ENTRY_CHANNELS
    rows, features = in_ref.shape
    count = features // LANES
    for tile in range(count):
        tiles[tile * rows : (tile + 1) * rows, :] = in_ref[:, tile * LANES : (tile + 1) * LANES]
    for group in range(rows // PACK):
        found = [tiles[strided(group * PACK + k, count, rows), :] for k in range(PACK)]
        for part in range(PACK):
            lanes = slice(part * channels, (part + 1) * channels)
            square[group, strided(part, count, PACK), :] = jnp.concatenate(
                [values[:, lanes] for values in found], 1
            )
        turned = square[group].T
        if rows_minor:
            for k in range(PACK):
                out_ref[strided(group * PACK + k, channels, rows), :] = turned[
                    k * channels : (k + 1) * channels
                ]
        else:
            out_ref[group * LANES : (group + 1) * LANES, :] = turned


def prepare_kernel(
    cotangent_hbm,
    right_hbm,
    left_hbm,
    weight_hbm,
    right_out,
    left_out,
    send_out,
    own_out,
    weight_out,
    inputs,
    tiles,
    square,
    semaphores,
):
    parity = lax.rem(lax.axis_index("blk"), 2)
    moves = (
        (right_hbm, inputs.at[0]),
        (left_hbm, inputs.at[1]),
        (cotangent_hbm.at[:, :, 1 - parity], send_out),
        (cotangent_hbm.at[:, :, parity], own_out),
        (weight_hbm, weight_out),
    )
    copies = [
        pltpu.make_async_copy(source, target, semaphores.at[at])
        for at, (source, target) in enumerate(moves)
    ]
    for copy in copies:
        copy.start()
    copies[0].wait()
    turn_in(True, inputs.at[0], right_out, tiles.at[0], square.at[0])
    copies[1].wait()
    turn_in(False, inputs.at[1], left_out, tiles.at[1], square.at[1])
    for copy in copies[2:]:
        copy.wait()


def turn_right(part_refs, out_ref, total, square, tiles):
    channels = ENTRY_CHANNELS
    rows, features = out_ref.shape
    count = features // LANES
    total[...] = functools.reduce(jnp.add, [ref[0] for ref in part_refs])
    for group in range(rows // PACK):
        stacked = [total[strided(group * PACK + k, channels, rows), :] for k in range(PACK)]
        square[group] = jnp.concatenate(stacked, 0).T
        pieces = [square[group, strided(part, count, PACK), :] for part in range(PACK)]
        for k in range(PACK):
            lanes = slice(k * channels, (k + 1) * channels)
            tiles[strided(group * PACK + k, count, rows), :] = jnp.concatenate(
                [piece[:, lanes] for piece in pieces], 1
            )
    for tile in range(count):
        out_ref[:, tile * LANES : (tile + 1) * LANES] = tiles[tile * rows : (tile + 1) * rows, :]


def turn_left(part_refs, out_ref, total, tiles):
    channels = ENTRY_CHANNELS
    size, width = part_refs[0].shape
    rows, features = out_ref.shape
    count = features // LANES
    found = functools.reduce(jnp.add, [ref[...] for ref in part_refs])
    for tile in range(width // LANES):
        total[tile * size : (tile + 1) * size, :] = found[:, tile * LANES : (tile + 1) * LANES]
    for tile in range(width // LANES):
        pieces = [total[strided(tile * size + part, count, PACK), :] for part in range(PACK)]
        for k in range(PACK):
            lanes = slice(k * channels, (k + 1) * channels)
            tiles[strided(tile * PACK + k, count, rows), :] = jnp.concatenate(
                [piece[:, lanes] for piece in pieces], 1
            )
    for tile in range(count):
        out_ref[:, tile * LANES : (tile + 1) * LANES] = tiles[tile * rows : (tile + 1) * rows, :]


def prepare_weight(weight_ref, weight_cat, fold):
    channels = ENTRY_CHANNELS
    for step in range(channels // fold):
        high, low = halves(folded_weight(weight_ref, step, fold))
        weight_cat[step * channels : (step + 1) * channels, :] = jnp.concatenate(
            [high, low, high], 1
        )


def gradient_phase(blocks, cotangent_ref, out_ref, spread_ref, weight_cat):
    fold = fold_of(blocks * cotangent_ref.shape[2])
    slots = slots_of(blocks)

    def step_of(pair, carry):
        high, low = spread_of(cotangent_ref, pair, slots, fold)
        spread_ref[pair, 0] = high
        spread_ref[pair, 1] = low
        found = dot_rows(weight_cat[...], jnp.concatenate([high, high, low], 1))
        out_ref[pair] = jnp.concatenate(halves(found), 1)
        return carry

    lax.fori_loop(0, out_ref.shape[0], step_of, 0, unroll=2)


def gradient_kernel(
    blocks,
    weight_ref,
    cotangent_ref,
    left_ref,
    out_ref,
    spread_ref,
    partial_ref,
    weight_cat,
    flip_hbm,
    left_flip,
    weight_rows,
    weight_flip,
    semaphore,
):
    fold = fold_of(blocks * cotangent_ref.shape[2])
    prepare_weight(weight_ref, weight_cat, fold)
    gradient_phase(blocks, cotangent_ref, out_ref, spread_ref, weight_cat)

    def store(step, found):
        partial_ref[step] = found

    right_phase(left_ref, out_ref, left_flip, store)
    channels = ENTRY_CHANNELS
    wide = weight_rows.shape[1]
    for step in range(channels // fold):
        weight_rows[step * channels : (step + 1) * channels, :] = folded_weight(
            weight_ref, step, fold
        )
    flip_high, flip_low = halves(weight_rows[...].T)
    weight_flip[:wide, :] = flip_high
    weight_flip[wide:, :] = flip_low
    copy = pltpu.make_async_copy(weight_flip, flip_hbm, semaphore)
    copy.start()
    copy.wait()


def peer_kernel(blocks, weight_cat, cotangent_ref, out_ref, spread_ref):
    gradient_phase(blocks, cotangent_ref, out_ref, spread_ref, weight_cat)


def right_phase(left_ref, factor_ref, left_flip, store):
    sequences = left_ref.shape[1]
    lanes = factor_ref.shape[2] // 4
    flip_high, flip_low = halves((left_ref[...] * (1.0 / sequences)).T)
    left_flip[:sequences, :] = flip_high
    left_flip[sequences:, :] = flip_low

    def step_of(step, carry):
        high, low = (
            jnp.concatenate(
                [rows_of_step([factor_ref], 2 * step + part, half, lanes) for part in range(2)], 1
            )
            for half in range(2)
        )
        first = dot(left_flip[...], high)
        second = dot(left_flip[:sequences, :], low)
        store(step, first[:sequences] + first[sequences:] + second)
        return carry

    lax.fori_loop(0, factor_ref.shape[1] // (2 * ENTRY_CHANNELS), step_of, 0, unroll=2)


def rows_of_step(refs, step, half, lanes):
    channels = ENTRY_CHANNELS
    rows = pl.ds(pl.multiple_of(step * channels, channels), channels)
    start = 2 * half * lanes
    return jnp.concatenate(
        [
            ref[pair, rows, start + part * lanes : start + (part + 1) * lanes]
            for ref in refs
            for pair in range(ref.shape[0])
            for part in range(2)
        ],
        0,
    )


def both_left(left_refs):
    sequences = left_refs[0].shape[1]
    return jnp.concatenate([ref[...] for ref in left_refs], 0) * (1.0 / sequences)


def right_kernel(
    blocks, depth, peer_ref, left_ref, partial_ref, keep_ref, send_ref, left_flip
):
    fold = fold_of(blocks * depth)
    lanes = fold * blocks * depth

    def store(step, found):
        found = found + partial_ref[step]
        for part in range(2):
            turned = found[:, part * lanes : (part + 1) * lanes].T
            for place in range(fold):
                for slot in range(blocks):
                    start = (place * blocks + slot) * depth
                    row = pl.multiple_of(((2 * step + part) * fold + place) * depth, depth)
                    out_ref = send_ref if slot % 2 else keep_ref
                    out_ref[slot // 2, pl.ds(row, depth), :] = turned[start : start + depth]

    right_phase(left_ref, peer_ref, left_flip, store)


def halve_kernel(keep_ref, found_ref, keep_out, send_out):
    for slot in range(keep_ref.shape[0]):
        out_ref = send_out if slot % 2 else keep_out
        out_ref[slot // 2] = keep_ref[slot] + found_ref[slot]


def right_rows(right_refs, step, fold, depth):
    return jnp.concatenate(
        [
            ref[pl.ds(pl.multiple_of((step * fold + part) * depth, depth), depth), :]
            for part in range(fold)
            for ref in right_refs
        ],
        0,
    )


def weight_kernel(blocks, depth, own_left, peer_left, own_spread, peer_spread, *refs):
    right_refs = refs[:blocks]
    keep_ref, send_ref, own_out, peer_out, own_ref, peer_ref, total, semaphores = refs[blocks:]
    channels = ENTRY_CHANNELS
    fold = fold_of(blocks * depth)
    lanes = fold * blocks * depth
    pairs = total.shape[1] // fold
    high, low = halves(both_left([own_left, peer_left]))
    left_cat = jnp.concatenate([high, low, high], 1)

    def copies(step):
        size = 2 * channels
        rows = pl.ds(pl.multiple_of(step * size, size), size)
        return [
            pltpu.make_async_copy(ref.at[:, rows], out.at[:, rows], semaphores.at[step, side])
            for side, (ref, out) in enumerate(((own_ref, own_out), (peer_ref, peer_out)))
        ]

    def outer_step(step, carry):
        right = [right_rows(right_refs, 2 * step + part, fold, depth) for part in range(2)]
        high, low = halves(jnp.concatenate(right, 0))
        found = dot_rows(left_cat, jnp.concatenate([high, high, low], 1))
        both = halves(found)
        for part in range(2):
            start = pl.multiple_of((2 * step + part) * channels, channels)
            row = 0
            for ref in (own_ref, peer_ref):
                for index in range(2 * ref.shape[0]):
                    for half in range(2):
                        lane = (2 * half + index % 2) * lanes
                        ref[index // 2, pl.ds(start, channels), lane : lane + lanes] = both[half][
                            row : row + channels, part * lanes : (part + 1) * lanes
                        ]
                    row += channels
        for copy in copies(step):
            copy.start()
        return carry

    lax.fori_loop(0, channels // (2 * fold), outer_step, 0, unroll=2)
    total[...] = jnp.zeros_like(total)

    def weight_step(pair, carry):
        lefts, rights = [], []
        for ref, spread_ref in ((own_ref, own_spread), (peer_ref, peer_spread)):
            high = spread_ref[pair, 0]
            lefts += [ref[pair], ref[pair, :, : 2 * lanes]]
            rights += [high, high, spread_ref[pair, 1]]
        total[...] += dot(jnp.concatenate(lefts, 1), jnp.concatenate(rights, 0))
        return carry

    lax.fori_loop(0, own_ref.shape[0], weight_step, 0, unroll=2)
    core = lax.rem(lax.axis_index("inner"), 2)
    steps = channels // (2 * fold)
    for out_ref, half in ((keep_ref, core), (send_ref, 1 - core)):
        for step in range(steps):
            start = pl.multiple_of((half * steps + step) * channels, channels)
            found = total[pl.ds(start, channels), :]
            for part in range(fold):
                y = step * fold + part
                out_ref[y * channels : (y + 1) * channels, :] = found[
                    :, part * pairs : (part + 1) * pairs
                ]

    def finish(step, carry):
        for copy in copies(step):
            copy.wait()
        return carry

    lax.fori_loop(0, channels // (2 * fold), finish, 0)


def left_kernel(blocks, depth, own_ref, peer_ref, *refs):
    right_refs, (own_out, peer_out, total, flipped) = refs[:blocks], refs[blocks:]
    lanes = own_ref.shape[2] // 4
    fold = lanes // (blocks * depth)
    sequences = right_refs[0].shape[1]
    group = 4
    total[...] = jnp.zeros_like(total)

    def step_of(step, carry):
        steps = [group * step + part for part in range(group)]
        right = [right_rows(right_refs, at, fold, depth) for at in steps]
        high, low = halves(jnp.concatenate(right, 0))
        grads = [
            jnp.concatenate([rows_of_step([own_ref, peer_ref], at, half, lanes) for at in steps], 1)
            for half in range(2)
        ]
        both = dot(grads[0], jnp.concatenate([high, low], 1))
        total[...] += both[:, :sequences] + both[:, sequences:] + dot(grads[1], high)
        return carry

    lax.fori_loop(0, ENTRY_CHANNELS // (fold * group), step_of, 0, unroll=2)
    flipped[...] = total[...].T * (1.0 / sequences)
    inner, size, width = own_out.shape
    here = lax.axis_index("inner")
    for slot in range(inner):
        start = pl.multiple_of(lax.bitwise_xor(here, slot) * size, size)
        own_out[slot] = flipped[pl.ds(start, size), :width]
        peer_out[slot] = flipped[pl.ds(start, size), width:]


def left_add_kernel(own_ref, other_ref, *out_refs):
    for slot, ref in enumerate(out_refs):
        ref[...] = own_ref[slot] + other_ref[slot]


def pair_kernel(blocks, outer_hbm, flip_hbm, out_ref, outer_ref, weight_flip, semaphores):
    depth, pairs = out_ref.shape[2:]
    count = outer_ref.shape[0]
    lanes = outer_ref.shape[2] // 4
    columns = blocks * depth
    fold = lanes // columns
    wide = fold * pairs

    def copy_of(pair):
        return pltpu.make_async_copy(outer_hbm.at[pair], outer_ref.at[pair], semaphores.at[pair])

    flip_copy = pltpu.make_async_copy(flip_hbm, weight_flip, semaphores.at[count])
    flip_copy.start()
    for pair in range(count):
        copy_of(pair).start()
    flip_copy.wait()
    slots = slots_of(blocks)

    def step_of(pair, carry):
        copy_of(pair).wait()
        first = dot(weight_flip[...], outer_ref[pair, :, : 2 * lanes])
        second = dot(weight_flip[:wide, :], outer_ref[pair, :, 2 * lanes :])
        found = first[:wide] + first[wide:] + second
        for part in range(2):
            turned = []
            for place in range(fold):
                start = part * lanes
                piece = found[place * pairs : (place + 1) * pairs, start : start + lanes].T
                turned.append(piece[place * columns : (place + 1) * columns])
            turned = functools.reduce(jnp.add, turned)
            row = 2 * pair + part
            for slot in range(blocks):
                out_ref[row, slots[slot]] = turned[slot * depth : (slot + 1) * depth]
        return carry

    lax.fori_loop(0, count, step_of, 0)


def finish_kernel(own_ref, other_ref, keep_ref, found_ref, *refs):
    left_refs, refs = refs[:-9], refs[-9:]
    pair_hbm, left_out, right_out = refs[:3]
    right_total, right_square, right_tiles, left_total, left_tiles, semaphores = refs[3:]
    parity = lax.rem(lax.axis_index("blk"), 2)
    copies = [
        pltpu.make_async_copy(ref, pair_hbm.at[:, :, side], semaphores.at[at])
        for at, (ref, side) in enumerate(((own_ref, parity), (other_ref, 1 - parity)))
    ]
    for copy in copies:
        copy.start()
    turn_right([keep_ref, found_ref], right_out, right_total, right_square, right_tiles)
    turn_left(left_refs, left_out, left_total, left_tiles)
    for copy in copies:
        copy.wait()


def spread_sum_kernel(in_ref, out_ref):
    found = in_ref[0]
    for part in range(1, in_ref.shape[0]):
        found = found + in_ref[part]
    for part in range(in_ref.shape[0]):
        out_ref[part] = found


def place_kernel(mine_ref, other_ref, out_ref):
    channels = ENTRY_CHANNELS
    core = lax.rem(lax.axis_index("inner"), 2)
    steps = mine_ref.shape[0] // channels
    for ref, half in ((mine_ref, core), (other_ref, 1 - core)):
        for step in range(steps):
            rows = ref[step * channels : (step + 1) * channels, :]
            out_ref[strided(half * steps + step, channels, channels), :] = rows


def shape(*sizes, kind=F32):
    return jax.ShapeDtypeStruct(sizes, kind)


def call(
    kernel,
    out_shape,
    scratch=(),
    name=None,
    limit=16 * MIB,
    far=(),
    after=(),
    out_specs=None,
    flops=1,
):
    def run(*operands):
        vmem = pl.BlockSpec(memory_space=pltpu.VMEM)
        hbm = pl.BlockSpec(memory_space=pltpu.HBM)
        in_specs = [pl.BlockSpec(memory_space=pl.ANY)] * len(after)
        in_specs += [hbm if at in far else vmem for at in range(len(operands))]
        operands = [
            pltpu.with_memory_space_constraint(operand, pltpu.HBM) if at in far else operand
            for at, operand in enumerate(operands)
        ]
        extra = {} if out_specs is None else {"out_specs": out_specs}
        return pl.pallas_call(
            lambda *refs: kernel(*refs[len(after) :]),
            out_shape=out_shape,
            in_specs=in_specs,
            scratch_shapes=list(scratch),
            compiler_params=pltpu.CompilerParams(vmem_limit_bytes=limit),
            cost_estimate=pl.CostEstimate(flops=flops, bytes_accessed=1, transcendentals=0),
            name=name,
            **extra,
        )(*after, *operands)

    return run


def local(alignment_left, alignment_right, projection_matrix, cotangent):
    rows, features = alignment_left.shape
    depth = alignment_right.shape[0]
    count = lax.axis_size("blk")
    inner = lax.axis_size("inner")
    channels = ENTRY_CHANNELS
    sequences = features // channels
    outer, pairs = projection_matrix.shape
    blocks = count // 2
    fold = fold_of(blocks * depth)
    lanes = fold * blocks * depth
    tall = outer // fold
    steps = channels // fold
    row_pairs = rows // 2
    everyone = ("blk", "inner")

    partner = [(here, here ^ 1) for here in range(count)]
    slot_moves = [[(here, here ^ (2 * slot)) for here in range(count)] for slot in range(blocks)]
    inner_moves = [[(here, here ^ slot) for here in range(inner)] for slot in range(inner)]
    cores = [(here, here ^ 1) for here in range(inner)]
    core_groups = [list(range(core, count * inner, 2)) for core in range(2)]

    limit = 20 * MIB * max(1, blocks * depth * fold // LANES * 2 // fold)
    large = functools.partial(call, limit=limit)
    work = 4 * 2 * rows * 2 * blocks * depth * outer * pairs * 3

    by_side = cotangent.reshape(rows, blocks, 2, depth, pairs)
    half_cotangent = shape(rows, blocks, depth, pairs)
    right, left, cotangent_send, cotangent_own, weight = call(
        prepare_kernel,
        [
            shape(channels * depth, sequences),
            shape(rows * channels, sequences),
            half_cotangent,
            half_cotangent,
            shape(outer, pairs),
        ],
        [
            pltpu.VMEM((2, rows, features), F32),
            pltpu.VMEM((2, rows * features // LANES, LANES), F32),
            pltpu.VMEM((2, rows // PACK, LANES, LANES), F32),
            pltpu.SemaphoreType.DMA((5,)),
        ],
        name="prepare",
        far=range(4),
    )(by_side, alignment_right, alignment_left, projection_matrix)
    cotangent_peer = lax.ppermute(cotangent_send, "blk", partner)
    left_peer = lax.ppermute(left, "blk", partner)

    vmem = pl.BlockSpec(memory_space=pltpu.VMEM)
    hbm = pl.BlockSpec(memory_space=pltpu.HBM)
    factor = shape(row_pairs, tall, 4 * lanes, kind=BF16)
    factor_scratch = pltpu.VMEM(factor.shape, BF16)
    weight_cat = shape(tall, 3 * fold * pairs, kind=BF16)
    flip_scratch = pltpu.VMEM((2 * sequences, rows * channels), BF16)
    flip_sizes = (2 * fold * pairs, tall)
    spread = shape(row_pairs, 2, 2 * lanes, fold * pairs, kind=BF16)
    grad_own, spread_own, partial, weight_cat, weight_flip = large(
        functools.partial(gradient_kernel, blocks),
        [
            factor,
            spread,
            shape(steps // 2, sequences, 2 * lanes),
            weight_cat,
            pltpu.HBM(flip_sizes, BF16),
        ],
        [
            flip_scratch,
            pltpu.VMEM((tall, fold * pairs), F32),
            pltpu.VMEM(flip_sizes, BF16),
            pltpu.SemaphoreType.DMA,
        ],
        "gradient_own",
        out_specs=[vmem, vmem, vmem, vmem, hbm],
    )(weight, cotangent_own, left)
    rights = {0: right}
    distance = blocks // 2
    while distance:
        for slot in list(rights):
            sent = rights[slot]
            if slot:
                sent, _ = lax.optimization_barrier((sent, grad_own))
            rights[slot + distance] = lax.ppermute(sent, "blk", slot_moves[distance])
        distance = distance // 2
    rights = [rights[slot] for slot in range(blocks)]
    grad_peer, spread_peer = large(
        functools.partial(peer_kernel, blocks), [factor, spread], [], "gradient_peer"
    )(weight_cat, cotangent_peer)
    right_half = shape(blocks // 2, channels * depth, sequences)
    right_keep, right_send = large(
        functools.partial(right_kernel, blocks, depth),
        [right_half, right_half],
        [flip_scratch],
        "right_parts",
    )(grad_peer, left_peer, partial)
    right_send = lax.ppermute(right_send, "blk", slot_moves[1])

    keep, send, outer_own, outer_peer = large(
        functools.partial(weight_kernel, blocks, depth),
        [shape(outer // 2, pairs)] * 2 + [pltpu.HBM(factor.shape, BF16)] * 2,
        [
            factor_scratch,
            factor_scratch,
            pltpu.VMEM((tall, fold * pairs), F32),
            pltpu.SemaphoreType.DMA((steps // 2, 2)),
        ],
        "weight",
        after=[right_keep],
        flops=2 * work,
        out_specs=[vmem, vmem, hbm, hbm],
    )(left, left_peer, spread_own, spread_peer, *rights)
    sent = lax.ppermute(send, "inner", cores)

    size = sequences // inner
    left_own, left_other = large(
        functools.partial(left_kernel, blocks, depth),
        [shape(inner, size, rows * channels)] * 2,
        [
            pltpu.VMEM((2 * rows * channels, sequences), F32),
            pltpu.VMEM((sequences, 2 * rows * channels), F32),
        ],
        "left_parts",
        after=[keep],
        flops=work,
    )(grad_own, grad_peer, *rights)
    keep, left_own = lax.optimization_barrier((keep, left_own))
    members = count * inner // 2
    pieces = (keep + sent).reshape(members, outer // 2 // members, pairs)

    def pair(values, after, name):
        return large(
            functools.partial(pair_kernel, blocks),
            shape(rows, blocks, depth, pairs),
            [
                factor_scratch,
                pltpu.VMEM(flip_sizes, BF16),
                pltpu.SemaphoreType.DMA((row_pairs + 1,)),
            ],
            name,
            far=[0, 1],
            after=after,
            flops=work,
        )(values, weight_flip)

    pieces, left_other = lax.optimization_barrier((pieces, left_other))
    left_other = lax.ppermute(left_other, "blk", partner)
    slot = 2
    while slot < blocks:
        part = shape(blocks // (2 * slot), channels * depth, sequences)
        right_keep, right_send = call(
            halve_kernel, [part, part], name="right_halve", after=[pieces]
        )(right_keep, right_send)
        right_send = lax.ppermute(right_send, "blk", slot_moves[slot])
        slot = 2 * slot

    pair_other = pair(outer_peer, [pieces, right_keep], "pair_peer")
    pair_found = lax.ppermute(pair_other, "blk", partner)

    pieces = lax.all_to_all(pieces, everyone, 0, 0, axis_index_groups=core_groups)
    pieces = call(
        spread_sum_kernel,
        shape(*pieces.shape),
        name="weight_sum",
        after=[pair_other, right_keep],
    )(pieces)
    pair_own = pair(outer_own, [pieces], "pair_own")
    left_found = call(
        left_add_kernel,
        [shape(size, rows * channels)] * inner,
        name="left_add",
        after=[pieces],
    )(left_own, left_other)
    pieces = lax.all_to_all(pieces, everyone, 0, 0, axis_index_groups=core_groups)

    left_found = [
        lax.ppermute(part, "inner", inner_moves[slot]) if slot else part
        for slot, part in enumerate(left_found)
    ]
    pair_update, grad_left, grad_right = call(
        finish_kernel,
        [
            pltpu.HBM(by_side.shape, F32),
            shape(rows, features // inner),
            shape(depth, features),
        ],
        [
            pltpu.VMEM((channels * depth, sequences), F32),
            pltpu.VMEM((depth // PACK, LANES, LANES), F32),
            pltpu.VMEM((depth * features // LANES, LANES), F32),
            pltpu.VMEM((size * rows * channels // LANES, LANES), F32),
            pltpu.VMEM((rows * features // inner // LANES, LANES), F32),
            pltpu.SemaphoreType.DMA((2,)),
        ],
        "finish",
        out_specs=[hbm, vmem, vmem],
    )(pair_own, pair_found, right_keep, right_send, *left_found)
    pair_update = pair_update.reshape(cotangent.shape)

    pieces, pair_update, grad_left, grad_right = lax.optimization_barrier(
        (pieces, pair_update, grad_left, grad_right)
    )
    mine = pieces.reshape(outer // 2, pairs)
    other = lax.ppermute(mine, "inner", cores)
    grad_weight = call(place_kernel, shape(outer, pairs), name="place")(mine, other)
    return (pair_update, grad_left, grad_right, grad_weight)


def solution(mesh):
    placed = (
        P(("groups", "blk"), None),
        P(("groups", "blk", "inner"), None),
        P(),
        P(("groups", "blk"), None, "inner", None),
    )
    return jax.shard_map(
        local,
        mesh=mesh,
        in_specs=placed,
        out_specs=(
            P(("groups", "blk"), None, "inner", None),
            P(("groups", "blk"), "inner"),
            P(("groups", "blk", "inner"), None),
            P("groups", None),
        ),
        check_vma=False,
    )
```

```python
import functools

import jax
import jax.numpy as jnp
from jax import lax
from jax.experimental import pallas as pl
from jax.experimental.pallas import tpu as pltpu
from jax.sharding import PartitionSpec as P

ENTRY_CHANNELS = 32
LANES = 128
PACK = LANES // ENTRY_CHANNELS
F32 = jnp.float32
BF16 = jnp.bfloat16
MIB = 1024 * 1024


def halves(values):
    high = values.astype(BF16)
    low = (values - high.astype(F32)).astype(BF16)
    return high, low


def dot(left, right):
    return jnp.dot(left, right, preferred_element_type=F32)


def dot_rows(left, right):
    return lax.dot_general(left, right, (((1,), (1,)), ((), ())), preferred_element_type=F32)


def fold_of(columns):
    return max(1, LANES // columns)


def strided(start, size, stride):
    return pl.ds(start, size, stride=stride)


def folded_weight(weight_ref, step, fold):
    channels = ENTRY_CHANNELS
    return jnp.concatenate(
        [weight_ref[strided(step * fold + part, channels, channels), :] for part in range(fold)], 1
    )


def slots_of(blocks):
    here = lax.axis_index("blk") // 2
    return [lax.bitwise_xor(here, slot) for slot in range(blocks)]


def spread_of(cotangent_ref, pair, slots, fold):
    columns = len(slots) * cotangent_ref.shape[2]
    empty = jnp.zeros((columns, cotangent_ref.shape[3]), BF16)
    spread = ([], [])
    for part in range(2):
        rows = jnp.concatenate([cotangent_ref[2 * pair + part, slot] for slot in slots], 0)
        for found, values in zip(spread, halves(rows)):
            for place in range(fold):
                found.append(
                    jnp.concatenate(
                        [values if place == other else empty for other in range(fold)], 1
                    )
                )
    return [jnp.concatenate(found, 0) for found in spread]


def turn_in(rows_minor, in_ref, out_ref, tiles, square):
    channels = ENTRY_CHANNELS
    rows, features = in_ref.shape
    count = features // LANES
    for tile in range(count):
        tiles[tile * rows : (tile + 1) * rows, :] = in_ref[:, tile * LANES : (tile + 1) * LANES]
    for group in range(rows // PACK):
        found = [tiles[strided(group * PACK + k, count, rows), :] for k in range(PACK)]
        for part in range(PACK):
            lanes = slice(part * channels, (part + 1) * channels)
            square[group, strided(part, count, PACK), :] = jnp.concatenate(
                [values[:, lanes] for values in found], 1
            )
        turned = square[group].T
        if rows_minor:
            for k in range(PACK):
                out_ref[strided(group * PACK + k, channels, rows), :] = turned[
                    k * channels : (k + 1) * channels
                ]
        else:
            out_ref[group * LANES : (group + 1) * LANES, :] = turned


def prepare_kernel(
    cotangent_hbm,
    right_hbm,
    left_hbm,
    weight_hbm,
    right_out,
    left_out,
    send_out,
    own_out,
    weight_out,
    inputs,
    tiles,
    square,
    semaphores,
):
    parity = lax.rem(lax.axis_index("blk"), 2)
    moves = (
        (right_hbm, inputs.at[0]),
        (left_hbm, inputs.at[1]),
        (cotangent_hbm.at[:, :, 1 - parity], send_out),
        (cotangent_hbm.at[:, :, parity], own_out),
        (weight_hbm, weight_out),
    )
    copies = [
        pltpu.make_async_copy(source, target, semaphores.at[at])
        for at, (source, target) in enumerate(moves)
    ]
    for copy in copies:
        copy.start()
    copies[0].wait()
    turn_in(True, inputs.at[0], right_out, tiles.at[0], square.at[0])
    copies[1].wait()
    turn_in(False, inputs.at[1], left_out, tiles.at[1], square.at[1])
    for copy in copies[2:]:
        copy.wait()


def turn_right(part_refs, out_ref, total, square, tiles):
    channels = ENTRY_CHANNELS
    rows, features = out_ref.shape
    count = features // LANES
    total[...] = functools.reduce(jnp.add, [ref[...] for ref in part_refs])
    for group in range(rows // PACK):
        stacked = [total[strided(group * PACK + k, channels, rows), :] for k in range(PACK)]
        square[group] = jnp.concatenate(stacked, 0).T
        pieces = [square[group, strided(part, count, PACK), :] for part in range(PACK)]
        for k in range(PACK):
            lanes = slice(k * channels, (k + 1) * channels)
            tiles[strided(group * PACK + k, count, rows), :] = jnp.concatenate(
                [piece[:, lanes] for piece in pieces], 1
            )
    for tile in range(count):
        out_ref[:, tile * LANES : (tile + 1) * LANES] = tiles[tile * rows : (tile + 1) * rows, :]


def turn_left(part_refs, out_ref, total, tiles):
    channels = ENTRY_CHANNELS
    size, width = part_refs[0].shape
    rows, features = out_ref.shape
    count = features // LANES
    found = functools.reduce(jnp.add, [ref[...] for ref in part_refs])
    for tile in range(width // LANES):
        total[tile * size : (tile + 1) * size, :] = found[:, tile * LANES : (tile + 1) * LANES]
    for tile in range(width // LANES):
        pieces = [total[strided(tile * size + part, count, PACK), :] for part in range(PACK)]
        for k in range(PACK):
            lanes = slice(k * channels, (k + 1) * channels)
            tiles[strided(tile * PACK + k, count, rows), :] = jnp.concatenate(
                [piece[:, lanes] for piece in pieces], 1
            )
    for tile in range(count):
        out_ref[:, tile * LANES : (tile + 1) * LANES] = tiles[tile * rows : (tile + 1) * rows, :]


def prepare_weight(weight_ref, weight_cat, fold):
    channels = ENTRY_CHANNELS
    for step in range(channels // fold):
        high, low = halves(folded_weight(weight_ref, step, fold))
        weight_cat[step * channels : (step + 1) * channels, :] = jnp.concatenate(
            [high, low, high], 1
        )


def gradient_phase(blocks, cotangent_ref, out_ref, spread_ref, weight_cat):
    fold = fold_of(blocks * cotangent_ref.shape[2])
    slots = slots_of(blocks)

    def step_of(pair, carry):
        high, low = spread_of(cotangent_ref, pair, slots, fold)
        spread_ref[pair, 0] = high
        spread_ref[pair, 1] = low
        found = dot_rows(weight_cat[...], jnp.concatenate([high, high, low], 1))
        out_ref[pair] = jnp.concatenate(halves(found), 1)
        return carry

    lax.fori_loop(0, out_ref.shape[0], step_of, 0, unroll=2)


def gradient_kernel(
    blocks,
    weight_ref,
    cotangent_ref,
    left_ref,
    out_ref,
    spread_ref,
    partial_ref,
    weight_cat,
    flip_hbm,
    left_flip,
    weight_rows,
    weight_flip,
    semaphore,
):
    fold = fold_of(blocks * cotangent_ref.shape[2])
    prepare_weight(weight_ref, weight_cat, fold)
    gradient_phase(blocks, cotangent_ref, out_ref, spread_ref, weight_cat)

    def store(step, found):
        partial_ref[step] = found

    right_phase(left_ref, out_ref, left_flip, store)
    channels = ENTRY_CHANNELS
    wide = weight_rows.shape[1]
    for step in range(channels // fold):
        weight_rows[step * channels : (step + 1) * channels, :] = folded_weight(
            weight_ref, step, fold
        )
    flip_high, flip_low = halves(weight_rows[...].T)
    weight_flip[:wide, :] = flip_high
    weight_flip[wide:, :] = flip_low
    copy = pltpu.make_async_copy(weight_flip, flip_hbm, semaphore)
    copy.start()
    copy.wait()


def peer_kernel(blocks, weight_cat, cotangent_ref, out_ref, spread_ref):
    gradient_phase(blocks, cotangent_ref, out_ref, spread_ref, weight_cat)


def right_phase(left_ref, factor_ref, left_flip, store):
    sequences = left_ref.shape[1]
    lanes = factor_ref.shape[2] // 4
    flip_high, flip_low = halves((left_ref[...] * (1.0 / sequences)).T)
    left_flip[:sequences, :] = flip_high
    left_flip[sequences:, :] = flip_low

    def step_of(step, carry):
        high, low = (
            jnp.concatenate(
                [rows_of_step([factor_ref], 2 * step + part, half, lanes) for part in range(2)], 1
            )
            for half in range(2)
        )
        first = dot(left_flip[...], high)
        second = dot(left_flip[:sequences, :], low)
        store(step, first[:sequences] + first[sequences:] + second)
        return carry

    lax.fori_loop(0, factor_ref.shape[1] // (2 * ENTRY_CHANNELS), step_of, 0, unroll=2)


def rows_of_step(refs, step, half, lanes):
    channels = ENTRY_CHANNELS
    rows = pl.ds(pl.multiple_of(step * channels, channels), channels)
    start = 2 * half * lanes
    return jnp.concatenate(
        [
            ref[pair, rows, start + part * lanes : start + (part + 1) * lanes]
            for ref in refs
            for pair in range(ref.shape[0])
            for part in range(2)
        ],
        0,
    )


def both_left(left_refs):
    sequences = left_refs[0].shape[1]
    return jnp.concatenate([ref[...] for ref in left_refs], 0) * (1.0 / sequences)


def right_kernel(blocks, depth, peer_ref, left_ref, partial_ref, *refs):
    out_refs, left_flip = refs[:blocks], refs[blocks]
    fold = fold_of(blocks * depth)
    lanes = fold * blocks * depth

    def store(step, found):
        found = found + partial_ref[step]
        for part in range(2):
            turned = found[:, part * lanes : (part + 1) * lanes].T
            for place in range(fold):
                for slot in range(blocks):
                    start = (place * blocks + slot) * depth
                    row = pl.multiple_of(((2 * step + part) * fold + place) * depth, depth)
                    out_refs[slot][pl.ds(row, depth), :] = turned[start : start + depth]

    right_phase(left_ref, peer_ref, left_flip, store)


def right_rows(right_refs, step, fold, depth):
    return jnp.concatenate(
        [
            ref[pl.ds(pl.multiple_of((step * fold + part) * depth, depth), depth), :]
            for part in range(fold)
            for ref in right_refs
        ],
        0,
    )


def weight_kernel(blocks, depth, own_left, peer_left, own_spread, peer_spread, *refs):
    right_refs = refs[:blocks]
    keep_ref, send_ref, own_out, peer_out, own_ref, peer_ref, total, semaphores = refs[blocks:]
    channels = ENTRY_CHANNELS
    fold = fold_of(blocks * depth)
    lanes = fold * blocks * depth
    pairs = total.shape[1] // fold
    high, low = halves(both_left([own_left, peer_left]))
    left_cat = jnp.concatenate([high, low, high], 1)

    def copies(step):
        size = 2 * channels
        rows = pl.ds(pl.multiple_of(step * size, size), size)
        return [
            pltpu.make_async_copy(ref.at[:, rows], out.at[:, rows], semaphores.at[step, side])
            for side, (ref, out) in enumerate(((own_ref, own_out), (peer_ref, peer_out)))
        ]

    def outer_step(step, carry):
        right = [right_rows(right_refs, 2 * step + part, fold, depth) for part in range(2)]
        high, low = halves(jnp.concatenate(right, 0))
        found = dot_rows(left_cat, jnp.concatenate([high, high, low], 1))
        both = halves(found)
        for part in range(2):
            start = pl.multiple_of((2 * step + part) * channels, channels)
            row = 0
            for ref in (own_ref, peer_ref):
                for index in range(2 * ref.shape[0]):
                    for half in range(2):
                        lane = (2 * half + index % 2) * lanes
                        ref[index // 2, pl.ds(start, channels), lane : lane + lanes] = both[half][
                            row : row + channels, part * lanes : (part + 1) * lanes
                        ]
                    row += channels
        for copy in copies(step):
            copy.start()
        return carry

    lax.fori_loop(0, channels // (2 * fold), outer_step, 0, unroll=2)
    total[...] = jnp.zeros_like(total)

    def weight_step(pair, carry):
        lefts, rights = [], []
        for ref, spread_ref in ((own_ref, own_spread), (peer_ref, peer_spread)):
            high = spread_ref[pair, 0]
            lefts += [ref[pair], ref[pair, :, : 2 * lanes]]
            rights += [high, high, spread_ref[pair, 1]]
        total[...] += dot(jnp.concatenate(lefts, 1), jnp.concatenate(rights, 0))
        return carry

    lax.fori_loop(0, own_ref.shape[0], weight_step, 0, unroll=2)
    core = lax.rem(lax.axis_index("inner"), 2)
    steps = channels // (2 * fold)
    for out_ref, half in ((keep_ref, core), (send_ref, 1 - core)):
        for step in range(steps):
            start = pl.multiple_of((half * steps + step) * channels, channels)
            found = total[pl.ds(start, channels), :]
            for part in range(fold):
                y = step * fold + part
                out_ref[y * channels : (y + 1) * channels, :] = found[
                    :, part * pairs : (part + 1) * pairs
                ]

    def finish(step, carry):
        for copy in copies(step):
            copy.wait()
        return carry

    lax.fori_loop(0, channels // (2 * fold), finish, 0)


def left_kernel(blocks, depth, own_ref, peer_ref, *refs):
    right_refs, (own_out, peer_out, total, flipped) = refs[:blocks], refs[blocks:]
    lanes = own_ref.shape[2] // 4
    fold = lanes // (blocks * depth)
    sequences = right_refs[0].shape[1]
    group = 4
    total[...] = jnp.zeros_like(total)

    def step_of(step, carry):
        steps = [group * step + part for part in range(group)]
        right = [right_rows(right_refs, at, fold, depth) for at in steps]
        high, low = halves(jnp.concatenate(right, 0))
        grads = [
            jnp.concatenate([rows_of_step([own_ref, peer_ref], at, half, lanes) for at in steps], 1)
            for half in range(2)
        ]
        both = dot(grads[0], jnp.concatenate([high, low], 1))
        total[...] += both[:, :sequences] + both[:, sequences:] + dot(grads[1], high)
        return carry

    lax.fori_loop(0, ENTRY_CHANNELS // (fold * group), step_of, 0, unroll=2)
    flipped[...] = total[...].T * (1.0 / sequences)
    inner, size, width = own_out.shape
    here = lax.axis_index("inner")
    for slot in range(inner):
        start = pl.multiple_of(lax.bitwise_xor(here, slot) * size, size)
        own_out[slot] = flipped[pl.ds(start, size), :width]
        peer_out[slot] = flipped[pl.ds(start, size), width:]


def left_add_kernel(own_ref, other_ref, *out_refs):
    for slot, ref in enumerate(out_refs):
        ref[...] = own_ref[slot] + other_ref[slot]


def pair_kernel(blocks, outer_hbm, flip_hbm, out_ref, outer_ref, weight_flip, semaphores):
    depth, pairs = out_ref.shape[2:]
    count = outer_ref.shape[0]
    lanes = outer_ref.shape[2] // 4
    columns = blocks * depth
    fold = lanes // columns
    wide = fold * pairs

    def copy_of(pair):
        return pltpu.make_async_copy(outer_hbm.at[pair], outer_ref.at[pair], semaphores.at[pair])

    flip_copy = pltpu.make_async_copy(flip_hbm, weight_flip, semaphores.at[count])
    flip_copy.start()
    for pair in range(count):
        copy_of(pair).start()
    flip_copy.wait()
    slots = slots_of(blocks)

    def step_of(pair, carry):
        copy_of(pair).wait()
        first = dot(weight_flip[...], outer_ref[pair, :, : 2 * lanes])
        second = dot(weight_flip[:wide, :], outer_ref[pair, :, 2 * lanes :])
        found = first[:wide] + first[wide:] + second
        for part in range(2):
            turned = []
            for place in range(fold):
                start = part * lanes
                piece = found[place * pairs : (place + 1) * pairs, start : start + lanes].T
                turned.append(piece[place * columns : (place + 1) * columns])
            turned = functools.reduce(jnp.add, turned)
            row = 2 * pair + part
            for slot in range(blocks):
                out_ref[row, slots[slot]] = turned[slot * depth : (slot + 1) * depth]
        return carry

    lax.fori_loop(0, count, step_of, 0)


def finish_kernel(blocks, own_ref, other_ref, *refs):
    right_refs, left_refs, refs = refs[:blocks], refs[blocks:-9], refs[-9:]
    pair_hbm, left_out, right_out = refs[:3]
    right_total, right_square, right_tiles, left_total, left_tiles, semaphores = refs[3:]
    parity = lax.rem(lax.axis_index("blk"), 2)
    copies = [
        pltpu.make_async_copy(ref, pair_hbm.at[:, :, side], semaphores.at[at])
        for at, (ref, side) in enumerate(((own_ref, parity), (other_ref, 1 - parity)))
    ]
    for copy in copies:
        copy.start()
    turn_right(right_refs, right_out, right_total, right_square, right_tiles)
    turn_left(left_refs, left_out, left_total, left_tiles)
    for copy in copies:
        copy.wait()


def spread_sum_kernel(in_ref, out_ref):
    found = in_ref[0]
    for part in range(1, in_ref.shape[0]):
        found = found + in_ref[part]
    for part in range(in_ref.shape[0]):
        out_ref[part] = found


def place_kernel(mine_ref, other_ref, out_ref):
    channels = ENTRY_CHANNELS
    core = lax.rem(lax.axis_index("inner"), 2)
    steps = mine_ref.shape[0] // channels
    for ref, half in ((mine_ref, core), (other_ref, 1 - core)):
        for step in range(steps):
            rows = ref[step * channels : (step + 1) * channels, :]
            out_ref[strided(half * steps + step, channels, channels), :] = rows


def shape(*sizes, kind=F32):
    return jax.ShapeDtypeStruct(sizes, kind)


def call(
    kernel,
    out_shape,
    scratch=(),
    name=None,
    limit=16 * MIB,
    far=(),
    after=(),
    out_specs=None,
    flops=1,
):
    def run(*operands):
        vmem = pl.BlockSpec(memory_space=pltpu.VMEM)
        hbm = pl.BlockSpec(memory_space=pltpu.HBM)
        in_specs = [pl.BlockSpec(memory_space=pl.ANY)] * len(after)
        in_specs += [hbm if at in far else vmem for at in range(len(operands))]
        operands = [
            pltpu.with_memory_space_constraint(operand, pltpu.HBM) if at in far else operand
            for at, operand in enumerate(operands)
        ]
        extra = {} if out_specs is None else {"out_specs": out_specs}
        return pl.pallas_call(
            lambda *refs: kernel(*refs[len(after) :]),
            out_shape=out_shape,
            in_specs=in_specs,
            scratch_shapes=list(scratch),
            compiler_params=pltpu.CompilerParams(vmem_limit_bytes=limit),
            cost_estimate=pl.CostEstimate(flops=flops, bytes_accessed=1, transcendentals=0),
            name=name,
            **extra,
        )(*after, *operands)

    return run


def local(alignment_left, alignment_right, projection_matrix, cotangent):
    rows, features = alignment_left.shape
    depth = alignment_right.shape[0]
    count = lax.axis_size("blk")
    inner = lax.axis_size("inner")
    channels = ENTRY_CHANNELS
    sequences = features // channels
    outer, pairs = projection_matrix.shape
    blocks = count // 2
    fold = fold_of(blocks * depth)
    lanes = fold * blocks * depth
    tall = outer // fold
    steps = channels // fold
    row_pairs = rows // 2
    everyone = ("blk", "inner")

    partner = [(here, here ^ 1) for here in range(count)]
    slot_moves = [[(here, here ^ (2 * slot)) for here in range(count)] for slot in range(blocks)]
    inner_moves = [[(here, here ^ slot) for here in range(inner)] for slot in range(inner)]
    cores = [(here, here ^ 1) for here in range(inner)]
    core_groups = [list(range(core, count * inner, 2)) for core in range(2)]

    limit = 20 * MIB * max(1, blocks * depth * fold // LANES * 2 // fold)
    large = functools.partial(call, limit=limit)
    work = 4 * 2 * rows * 2 * blocks * depth * outer * pairs * 3

    by_side = cotangent.reshape(rows, blocks, 2, depth, pairs)
    half_cotangent = shape(rows, blocks, depth, pairs)
    right, left, cotangent_send, cotangent_own, weight = call(
        prepare_kernel,
        [
            shape(channels * depth, sequences),
            shape(rows * channels, sequences),
            half_cotangent,
            half_cotangent,
            shape(outer, pairs),
        ],
        [
            pltpu.VMEM((2, rows, features), F32),
            pltpu.VMEM((2, rows * features // LANES, LANES), F32),
            pltpu.VMEM((2, rows // PACK, LANES, LANES), F32),
            pltpu.SemaphoreType.DMA((5,)),
        ],
        name="prepare",
        far=range(4),
    )(by_side, alignment_right, alignment_left, projection_matrix)
    cotangent_peer = lax.ppermute(cotangent_send, "blk", partner)
    left_peer = lax.ppermute(left, "blk", partner)

    vmem = pl.BlockSpec(memory_space=pltpu.VMEM)
    hbm = pl.BlockSpec(memory_space=pltpu.HBM)
    factor = shape(row_pairs, tall, 4 * lanes, kind=BF16)
    factor_scratch = pltpu.VMEM(factor.shape, BF16)
    weight_cat = shape(tall, 3 * fold * pairs, kind=BF16)
    flip_scratch = pltpu.VMEM((2 * sequences, rows * channels), BF16)
    flip_sizes = (2 * fold * pairs, tall)
    spread = shape(row_pairs, 2, 2 * lanes, fold * pairs, kind=BF16)
    grad_own, spread_own, partial, weight_cat, weight_flip = large(
        functools.partial(gradient_kernel, blocks),
        [
            factor,
            spread,
            shape(steps // 2, sequences, 2 * lanes),
            weight_cat,
            pltpu.HBM(flip_sizes, BF16),
        ],
        [
            flip_scratch,
            pltpu.VMEM((tall, fold * pairs), F32),
            pltpu.VMEM(flip_sizes, BF16),
            pltpu.SemaphoreType.DMA,
        ],
        "gradient_own",
        out_specs=[vmem, vmem, vmem, vmem, hbm],
    )(weight, cotangent_own, left)
    rights = {0: right}
    distance = blocks // 2
    while distance:
        for slot in list(rights):
            sent = rights[slot]
            if slot:
                sent, _ = lax.optimization_barrier((sent, grad_own))
            rights[slot + distance] = lax.ppermute(sent, "blk", slot_moves[distance])
        distance = distance // 2
    rights = [rights[slot] for slot in range(blocks)]
    grad_peer, spread_peer = large(
        functools.partial(peer_kernel, blocks), [factor, spread], [], "gradient_peer"
    )(weight_cat, cotangent_peer)
    right_parts = large(
        functools.partial(right_kernel, blocks, depth),
        [shape(channels * depth, sequences)] * blocks,
        [flip_scratch],
        "right_parts",
    )(grad_peer, left_peer, partial)
    right_found = [
        lax.ppermute(part, "blk", slot_moves[slot]) if slot else part
        for slot, part in enumerate(right_parts)
    ]

    keep, send, outer_own, outer_peer = large(
        functools.partial(weight_kernel, blocks, depth),
        [shape(outer // 2, pairs)] * 2 + [pltpu.HBM(factor.shape, BF16)] * 2,
        [
            factor_scratch,
            factor_scratch,
            pltpu.VMEM((tall, fold * pairs), F32),
            pltpu.SemaphoreType.DMA((steps // 2, 2)),
        ],
        "weight",
        after=[right_parts[0]],
        flops=2 * work,
        out_specs=[vmem, vmem, hbm, hbm],
    )(left, left_peer, spread_own, spread_peer, *rights)
    sent = lax.ppermute(send, "inner", cores)

    size = sequences // inner
    left_own, left_other = large(
        functools.partial(left_kernel, blocks, depth),
        [shape(inner, size, rows * channels)] * 2,
        [
            pltpu.VMEM((2 * rows * channels, sequences), F32),
            pltpu.VMEM((sequences, 2 * rows * channels), F32),
        ],
        "left_parts",
        after=[keep],
        flops=work,
    )(grad_own, grad_peer, *rights)
    keep, left_own = lax.optimization_barrier((keep, left_own))
    members = count * inner // 2
    pieces = (keep + sent).reshape(members, outer // 2 // members, pairs)

    def pair(values, after, name):
        return large(
            functools.partial(pair_kernel, blocks),
            shape(rows, blocks, depth, pairs),
            [
                factor_scratch,
                pltpu.VMEM(flip_sizes, BF16),
                pltpu.SemaphoreType.DMA((row_pairs + 1,)),
            ],
            name,
            far=[0, 1],
            after=after,
            flops=work,
        )(values, weight_flip)

    pieces, left_other = lax.optimization_barrier((pieces, left_other))
    left_other = lax.ppermute(left_other, "blk", partner)
    pair_other = pair(outer_peer, [pieces], "pair_peer")
    pair_found = lax.ppermute(pair_other, "blk", partner)

    pieces = lax.all_to_all(pieces, everyone, 0, 0, axis_index_groups=core_groups)
    pieces = call(
        spread_sum_kernel,
        shape(*pieces.shape),
        name="weight_sum",
        after=[pair_other],
    )(pieces)
    pair_own = pair(outer_own, [pieces], "pair_own")
    left_found = call(
        left_add_kernel,
        [shape(size, rows * channels)] * inner,
        name="left_add",
        after=[pieces],
    )(left_own, left_other)
    pieces = lax.all_to_all(pieces, everyone, 0, 0, axis_index_groups=core_groups)

    left_found = [
        lax.ppermute(part, "inner", inner_moves[slot]) if slot else part
        for slot, part in enumerate(left_found)
    ]
    pair_update, grad_left, grad_right = call(
        functools.partial(finish_kernel, blocks),
        [
            pltpu.HBM(by_side.shape, F32),
            shape(rows, features // inner),
            shape(depth, features),
        ],
        [
            pltpu.VMEM((channels * depth, sequences), F32),
            pltpu.VMEM((depth // PACK, LANES, LANES), F32),
            pltpu.VMEM((depth * features // LANES, LANES), F32),
            pltpu.VMEM((size * rows * channels // LANES, LANES), F32),
            pltpu.VMEM((rows * features // inner // LANES, LANES), F32),
            pltpu.SemaphoreType.DMA((2,)),
        ],
        "finish",
        out_specs=[hbm, vmem, vmem],
    )(pair_own, pair_found, *right_found, *left_found)
    pair_update = pair_update.reshape(cotangent.shape)

    pieces, pair_update, grad_left, grad_right = lax.optimization_barrier(
        (pieces, pair_update, grad_left, grad_right)
    )
    mine = pieces.reshape(outer // 2, pairs)
    other = lax.ppermute(mine, "inner", cores)
    grad_weight = call(place_kernel, shape(outer, pairs), name="place")(mine, other)
    return (pair_update, grad_left, grad_right, grad_weight)


def solution(mesh):
    placed = (
        P(("groups", "blk"), None),
        P(("groups", "blk", "inner"), None),
        P(),
        P(("groups", "blk"), None, "inner", None),
    )
    return jax.shard_map(
        local,
        mesh=mesh,
        in_specs=placed,
        out_specs=(
            P(("groups", "blk"), None, "inner", None),
            P(("groups", "blk"), "inner"),
            P(("groups", "blk", "inner"), None),
            P("groups", None),
        ),
        check_vma=False,
    )
```

```python
import functools

import jax
import jax.numpy as jnp
from jax import lax
from jax.experimental import pallas as pl
from jax.experimental.pallas import tpu as pltpu
from jax.sharding import PartitionSpec as P

ENTRY_CHANNELS = 32
LANES = 128
PACK = LANES // ENTRY_CHANNELS
F32 = jnp.float32
BF16 = jnp.bfloat16
MIB = 1024 * 1024


def halves(values):
    high = values.astype(BF16)
    low = (values - high.astype(F32)).astype(BF16)
    return high, low


def dot(left, right):
    return jnp.dot(left, right, preferred_element_type=F32)


def dot_rows(left, right):
    return lax.dot_general(left, right, (((1,), (1,)), ((), ())), preferred_element_type=F32)


def fold_of(columns):
    return max(1, LANES // columns)


def strided(start, size, stride):
    return pl.ds(start, size, stride=stride)


def folded_weight(weight_ref, step, fold):
    channels = ENTRY_CHANNELS
    return jnp.concatenate(
        [weight_ref[strided(step * fold + part, channels, channels), :] for part in range(fold)], 1
    )


def slots_of(blocks):
    here = lax.axis_index("blk") // 2
    return [lax.bitwise_xor(here, slot) for slot in range(blocks)]


def spread_of(cotangent_ref, pair, slots, fold):
    columns = len(slots) * cotangent_ref.shape[2]
    empty = jnp.zeros((columns, cotangent_ref.shape[3]), BF16)
    spread = ([], [])
    for part in range(2):
        rows = jnp.concatenate([cotangent_ref[2 * pair + part, slot] for slot in slots], 0)
        for found, values in zip(spread, halves(rows)):
            for place in range(fold):
                found.append(
                    jnp.concatenate(
                        [values if place == other else empty for other in range(fold)], 1
                    )
                )
    return [jnp.concatenate(found, 0) for found in spread]


def turn_in(rows_minor, in_ref, out_ref, tiles, square):
    channels = ENTRY_CHANNELS
    rows, features = in_ref.shape
    count = features // LANES
    for tile in range(count):
        tiles[tile * rows : (tile + 1) * rows, :] = in_ref[:, tile * LANES : (tile + 1) * LANES]
    for group in range(rows // PACK):
        found = [tiles[strided(group * PACK + k, count, rows), :] for k in range(PACK)]
        for part in range(PACK):
            lanes = slice(part * channels, (part + 1) * channels)
            square[group, strided(part, count, PACK), :] = jnp.concatenate(
                [values[:, lanes] for values in found], 1
            )
        turned = square[group].T
        if rows_minor:
            for k in range(PACK):
                out_ref[strided(group * PACK + k, channels, rows), :] = turned[
                    k * channels : (k + 1) * channels
                ]
        else:
            out_ref[group * LANES : (group + 1) * LANES, :] = turned


def prepare_kernel(
    cotangent_hbm,
    right_hbm,
    left_hbm,
    weight_hbm,
    right_out,
    left_out,
    send_out,
    own_out,
    weight_out,
    inputs,
    tiles,
    square,
    semaphores,
):
    parity = lax.rem(lax.axis_index("blk"), 2)
    moves = (
        (right_hbm, inputs.at[0]),
        (left_hbm, inputs.at[1]),
        (cotangent_hbm.at[:, :, 1 - parity], send_out),
        (cotangent_hbm.at[:, :, parity], own_out),
        (weight_hbm, weight_out),
    )
    copies = [
        pltpu.make_async_copy(source, target, semaphores.at[at])
        for at, (source, target) in enumerate(moves)
    ]
    for copy in copies:
        copy.start()
    copies[0].wait()
    turn_in(True, inputs.at[0], right_out, tiles.at[0], square.at[0])
    copies[1].wait()
    turn_in(False, inputs.at[1], left_out, tiles.at[1], square.at[1])
    for copy in copies[2:]:
        copy.wait()


def turn_right(part_refs, out_ref, total, square, tiles):
    channels = ENTRY_CHANNELS
    rows, features = out_ref.shape
    count = features // LANES
    total[...] = functools.reduce(jnp.add, [ref[0] for ref in part_refs])
    for group in range(rows // PACK):
        stacked = [total[strided(group * PACK + k, channels, rows), :] for k in range(PACK)]
        square[group] = jnp.concatenate(stacked, 0).T
        pieces = [square[group, strided(part, count, PACK), :] for part in range(PACK)]
        for k in range(PACK):
            lanes = slice(k * channels, (k + 1) * channels)
            tiles[strided(group * PACK + k, count, rows), :] = jnp.concatenate(
                [piece[:, lanes] for piece in pieces], 1
            )
    for tile in range(count):
        out_ref[:, tile * LANES : (tile + 1) * LANES] = tiles[tile * rows : (tile + 1) * rows, :]


def turn_left(part_refs, out_ref, total, tiles):
    channels = ENTRY_CHANNELS
    size, width = part_refs[0].shape
    rows, features = out_ref.shape
    count = features // LANES
    found = functools.reduce(jnp.add, [ref[...] for ref in part_refs])
    for tile in range(width // LANES):
        total[tile * size : (tile + 1) * size, :] = found[:, tile * LANES : (tile + 1) * LANES]
    for tile in range(width // LANES):
        pieces = [total[strided(tile * size + part, count, PACK), :] for part in range(PACK)]
        for k in range(PACK):
            lanes = slice(k * channels, (k + 1) * channels)
            tiles[strided(tile * PACK + k, count, rows), :] = jnp.concatenate(
                [piece[:, lanes] for piece in pieces], 1
            )
    for tile in range(count):
        out_ref[:, tile * LANES : (tile + 1) * LANES] = tiles[tile * rows : (tile + 1) * rows, :]


def prepare_weight(weight_ref, weight_cat, fold):
    channels = ENTRY_CHANNELS
    for step in range(channels // fold):
        high, low = halves(folded_weight(weight_ref, step, fold))
        weight_cat[step * channels : (step + 1) * channels, :] = jnp.concatenate(
            [high, low, high], 1
        )


def gradient_phase(blocks, cotangent_ref, out_ref, spread_ref, weight_cat):
    fold = fold_of(blocks * cotangent_ref.shape[2])
    slots = slots_of(blocks)

    def step_of(pair, carry):
        high, low = spread_of(cotangent_ref, pair, slots, fold)
        spread_ref[pair, 0] = high
        spread_ref[pair, 1] = low
        found = dot_rows(weight_cat[...], jnp.concatenate([high, high, low], 1))
        out_ref[pair] = jnp.concatenate(halves(found), 1)
        return carry

    lax.fori_loop(0, out_ref.shape[0], step_of, 0, unroll=2)


def gradient_kernel(
    blocks,
    weight_ref,
    cotangent_ref,
    left_ref,
    out_ref,
    spread_ref,
    partial_ref,
    weight_cat,
    flip_hbm,
    left_flip,
    weight_rows,
    weight_flip,
    semaphore,
):
    fold = fold_of(blocks * cotangent_ref.shape[2])
    prepare_weight(weight_ref, weight_cat, fold)
    gradient_phase(blocks, cotangent_ref, out_ref, spread_ref, weight_cat)

    def store(step, found):
        partial_ref[step] = found

    right_phase(left_ref, out_ref, left_flip, store)
    channels = ENTRY_CHANNELS
    wide = weight_rows.shape[1]
    for step in range(channels // fold):
        weight_rows[step * channels : (step + 1) * channels, :] = folded_weight(
            weight_ref, step, fold
        )
    flip_high, flip_low = halves(weight_rows[...].T)
    weight_flip[:wide, :] = flip_high
    weight_flip[wide:, :] = flip_low
    copy = pltpu.make_async_copy(weight_flip, flip_hbm, semaphore)
    copy.start()
    copy.wait()


def peer_kernel(blocks, weight_cat, cotangent_ref, out_ref, spread_ref):
    gradient_phase(blocks, cotangent_ref, out_ref, spread_ref, weight_cat)


def right_phase(left_ref, factor_ref, left_flip, store):
    sequences = left_ref.shape[1]
    lanes = factor_ref.shape[2] // 4
    flip_high, flip_low = halves((left_ref[...] * (1.0 / sequences)).T)
    left_flip[:sequences, :] = flip_high
    left_flip[sequences:, :] = flip_low

    def step_of(step, carry):
        high, low = (
            jnp.concatenate(
                [rows_of_step([factor_ref], 2 * step + part, half, lanes) for part in range(2)], 1
            )
            for half in range(2)
        )
        first = dot(left_flip[...], high)
        second = dot(left_flip[:sequences, :], low)
        store(step, first[:sequences] + first[sequences:] + second)
        return carry

    lax.fori_loop(0, factor_ref.shape[1] // (2 * ENTRY_CHANNELS), step_of, 0, unroll=2)


def rows_of_step(refs, step, half, lanes):
    channels = ENTRY_CHANNELS
    rows = pl.ds(pl.multiple_of(step * channels, channels), channels)
    start = 2 * half * lanes
    return jnp.concatenate(
        [
            ref[pair, rows, start + part * lanes : start + (part + 1) * lanes]
            for ref in refs
            for pair in range(ref.shape[0])
            for part in range(2)
        ],
        0,
    )


def both_left(left_refs):
    sequences = left_refs[0].shape[1]
    return jnp.concatenate([ref[...] for ref in left_refs], 0) * (1.0 / sequences)


def right_kernel(
    blocks, depth, peer_ref, left_ref, partial_ref, keep_ref, send_ref, left_flip
):
    fold = fold_of(blocks * depth)
    lanes = fold * blocks * depth

    def store(step, found):
        found = found + partial_ref[step]
        for part in range(2):
            turned = found[:, part * lanes : (part + 1) * lanes].T
            for place in range(fold):
                for slot in range(blocks):
                    start = (place * blocks + slot) * depth
                    row = pl.multiple_of(((2 * step + part) * fold + place) * depth, depth)
                    out_ref = keep_ref if slot < blocks // 2 else send_ref
                    out_ref[slot % (blocks // 2), pl.ds(row, depth), :] = turned[
                        start : start + depth
                    ]

    right_phase(left_ref, peer_ref, left_flip, store)


def halve_kernel(keep_ref, found_ref, keep_out, send_out):
    half = keep_ref.shape[0] // 2
    for slot in range(half):
        keep_out[slot] = keep_ref[slot] + found_ref[slot]
        send_out[slot] = keep_ref[half + slot] + found_ref[half + slot]


def right_rows(right_refs, step, fold, depth):
    return jnp.concatenate(
        [
            ref[pl.ds(pl.multiple_of((step * fold + part) * depth, depth), depth), :]
            for part in range(fold)
            for ref in right_refs
        ],
        0,
    )


def weight_kernel(blocks, depth, own_left, peer_left, own_spread, peer_spread, *refs):
    right_refs = refs[:blocks]
    keep_ref, send_ref, own_out, peer_out, own_ref, peer_ref, total, semaphores = refs[blocks:]
    channels = ENTRY_CHANNELS
    fold = fold_of(blocks * depth)
    lanes = fold * blocks * depth
    pairs = total.shape[1] // fold
    high, low = halves(both_left([own_left, peer_left]))
    left_cat = jnp.concatenate([high, low, high], 1)

    def copies(step):
        size = 2 * channels
        rows = pl.ds(pl.multiple_of(step * size, size), size)
        return [
            pltpu.make_async_copy(ref.at[:, rows], out.at[:, rows], semaphores.at[step, side])
            for side, (ref, out) in enumerate(((own_ref, own_out), (peer_ref, peer_out)))
        ]

    def outer_step(step, carry):
        right = [right_rows(right_refs, 2 * step + part, fold, depth) for part in range(2)]
        high, low = halves(jnp.concatenate(right, 0))
        found = dot_rows(left_cat, jnp.concatenate([high, high, low], 1))
        both = halves(found)
        for part in range(2):
            start = pl.multiple_of((2 * step + part) * channels, channels)
            row = 0
            for ref in (own_ref, peer_ref):
                for index in range(2 * ref.shape[0]):
                    for half in range(2):
                        lane = (2 * half + index % 2) * lanes
                        ref[index // 2, pl.ds(start, channels), lane : lane + lanes] = both[half][
                            row : row + channels, part * lanes : (part + 1) * lanes
                        ]
                    row += channels
        for copy in copies(step):
            copy.start()
        return carry

    lax.fori_loop(0, channels // (2 * fold), outer_step, 0, unroll=2)
    total[...] = jnp.zeros_like(total)

    def weight_step(pair, carry):
        lefts, rights = [], []
        for ref, spread_ref in ((own_ref, own_spread), (peer_ref, peer_spread)):
            high = spread_ref[pair, 0]
            lefts += [ref[pair], ref[pair, :, : 2 * lanes]]
            rights += [high, high, spread_ref[pair, 1]]
        total[...] += dot(jnp.concatenate(lefts, 1), jnp.concatenate(rights, 0))
        return carry

    lax.fori_loop(0, own_ref.shape[0], weight_step, 0, unroll=2)
    core = lax.rem(lax.axis_index("inner"), 2)
    steps = channels // (2 * fold)
    for out_ref, half in ((keep_ref, core), (send_ref, 1 - core)):
        for step in range(steps):
            start = pl.multiple_of((half * steps + step) * channels, channels)
            found = total[pl.ds(start, channels), :]
            for part in range(fold):
                y = step * fold + part
                out_ref[y * channels : (y + 1) * channels, :] = found[
                    :, part * pairs : (part + 1) * pairs
                ]

    def finish(step, carry):
        for copy in copies(step):
            copy.wait()
        return carry

    lax.fori_loop(0, channels // (2 * fold), finish, 0)


def left_kernel(blocks, depth, own_ref, peer_ref, *refs):
    right_refs, out_refs, (total, flipped) = refs[:blocks], refs[blocks:-2], refs[-2:]
    lanes = own_ref.shape[2] // 4
    fold = lanes // (blocks * depth)
    sequences = right_refs[0].shape[1]
    group = 4
    total[...] = jnp.zeros_like(total)

    def step_of(step, carry):
        steps = [group * step + part for part in range(group)]
        right = [right_rows(right_refs, at, fold, depth) for at in steps]
        high, low = halves(jnp.concatenate(right, 0))
        grads = [
            jnp.concatenate([rows_of_step([own_ref, peer_ref], at, half, lanes) for at in steps], 1)
            for half in range(2)
        ]
        both = dot(grads[0], jnp.concatenate([high, low], 1))
        total[...] += both[:, :sequences] + both[:, sequences:] + dot(grads[1], high)
        return carry

    lax.fori_loop(0, ENTRY_CHANNELS // (fold * group), step_of, 0, unroll=2)
    flipped[...] = total[...].T * (1.0 / sequences)
    here = lax.axis_index("inner")
    size, width = out_refs[0].shape[1:]
    for slot, ref in enumerate(out_refs):
        start = pl.multiple_of(lax.bitwise_xor(here, slot) * size, size)
        for side in range(2):
            ref[side] = flipped[pl.ds(start, size), side * width : (side + 1) * width]


def left_add_kernel(*refs):
    parts, (own_out, send_out) = refs[:-2], refs[-2:]
    for side, ref in enumerate((own_out, send_out)):
        ref[...] = functools.reduce(jnp.add, [part[side] for part in parts])


def pair_kernel(blocks, outer_hbm, flip_hbm, out_ref, outer_ref, weight_flip, semaphores):
    depth, pairs = out_ref.shape[2:]
    count = outer_ref.shape[0]
    lanes = outer_ref.shape[2] // 4
    columns = blocks * depth
    fold = lanes // columns
    wide = fold * pairs

    def copy_of(pair):
        return pltpu.make_async_copy(outer_hbm.at[pair], outer_ref.at[pair], semaphores.at[pair])

    flip_copy = pltpu.make_async_copy(flip_hbm, weight_flip, semaphores.at[count])
    flip_copy.start()
    for pair in range(count):
        copy_of(pair).start()
    flip_copy.wait()
    slots = slots_of(blocks)

    def step_of(pair, carry):
        copy_of(pair).wait()
        first = dot(weight_flip[...], outer_ref[pair, :, : 2 * lanes])
        second = dot(weight_flip[:wide, :], outer_ref[pair, :, 2 * lanes :])
        found = first[:wide] + first[wide:] + second
        for part in range(2):
            turned = []
            for place in range(fold):
                start = part * lanes
                piece = found[place * pairs : (place + 1) * pairs, start : start + lanes].T
                turned.append(piece[place * columns : (place + 1) * columns])
            turned = functools.reduce(jnp.add, turned)
            row = 2 * pair + part
            for slot in range(blocks):
                out_ref[row, slots[slot]] = turned[slot * depth : (slot + 1) * depth]
        return carry

    lax.fori_loop(0, count, step_of, 0)


def finish_kernel(own_ref, other_ref, keep_ref, found_ref, *refs):
    left_refs, refs = refs[:-9], refs[-9:]
    pair_hbm, left_out, right_out = refs[:3]
    right_total, right_square, right_tiles, left_total, left_tiles, semaphores = refs[3:]
    parity = lax.rem(lax.axis_index("blk"), 2)
    copies = [
        pltpu.make_async_copy(ref, pair_hbm.at[:, :, side], semaphores.at[at])
        for at, (ref, side) in enumerate(((own_ref, parity), (other_ref, 1 - parity)))
    ]
    for copy in copies:
        copy.start()
    turn_right([keep_ref, found_ref], right_out, right_total, right_square, right_tiles)
    turn_left(left_refs, left_out, left_total, left_tiles)
    for copy in copies:
        copy.wait()


def spread_sum_kernel(in_ref, out_ref):
    found = in_ref[0]
    for part in range(1, in_ref.shape[0]):
        found = found + in_ref[part]
    for part in range(in_ref.shape[0]):
        out_ref[part] = found


def place_kernel(mine_ref, other_ref, out_ref):
    channels = ENTRY_CHANNELS
    core = lax.rem(lax.axis_index("inner"), 2)
    steps = mine_ref.shape[0] // channels
    for ref, half in ((mine_ref, core), (other_ref, 1 - core)):
        for step in range(steps):
            rows = ref[step * channels : (step + 1) * channels, :]
            out_ref[strided(half * steps + step, channels, channels), :] = rows


def shape(*sizes, kind=F32):
    return jax.ShapeDtypeStruct(sizes, kind)


def call(
    kernel,
    out_shape,
    scratch=(),
    name=None,
    limit=16 * MIB,
    far=(),
    after=(),
    out_specs=None,
    flops=1,
):
    def run(*operands):
        vmem = pl.BlockSpec(memory_space=pltpu.VMEM)
        hbm = pl.BlockSpec(memory_space=pltpu.HBM)
        in_specs = [pl.BlockSpec(memory_space=pl.ANY)] * len(after)
        in_specs += [hbm if at in far else vmem for at in range(len(operands))]
        operands = [
            pltpu.with_memory_space_constraint(operand, pltpu.HBM) if at in far else operand
            for at, operand in enumerate(operands)
        ]
        extra = {} if out_specs is None else {"out_specs": out_specs}
        return pl.pallas_call(
            lambda *refs: kernel(*refs[len(after) :]),
            out_shape=out_shape,
            in_specs=in_specs,
            scratch_shapes=list(scratch),
            compiler_params=pltpu.CompilerParams(vmem_limit_bytes=limit),
            cost_estimate=pl.CostEstimate(flops=flops, bytes_accessed=1, transcendentals=0),
            name=name,
            **extra,
        )(*after, *operands)

    return run


def local(alignment_left, alignment_right, projection_matrix, cotangent):
    rows, features = alignment_left.shape
    depth = alignment_right.shape[0]
    count = lax.axis_size("blk")
    inner = lax.axis_size("inner")
    channels = ENTRY_CHANNELS
    sequences = features // channels
    outer, pairs = projection_matrix.shape
    blocks = count // 2
    fold = fold_of(blocks * depth)
    lanes = fold * blocks * depth
    tall = outer // fold
    steps = channels // fold
    row_pairs = rows // 2
    everyone = ("blk", "inner")

    partner = [(here, here ^ 1) for here in range(count)]
    slot_moves = [[(here, here ^ (2 * slot)) for here in range(count)] for slot in range(blocks)]
    inner_moves = [[(here, here ^ slot) for here in range(inner)] for slot in range(inner)]
    cores = [(here, here ^ 1) for here in range(inner)]
    core_groups = [list(range(core, count * inner, 2)) for core in range(2)]

    limit = 20 * MIB * max(1, blocks * depth * fold // LANES * 2 // fold)
    large = functools.partial(call, limit=limit)
    work = 4 * 2 * rows * 2 * blocks * depth * outer * pairs * 3

    by_side = cotangent.reshape(rows, blocks, 2, depth, pairs)
    half_cotangent = shape(rows, blocks, depth, pairs)
    right, left, cotangent_send, cotangent_own, weight = call(
        prepare_kernel,
        [
            shape(channels * depth, sequences),
            shape(rows * channels, sequences),
            half_cotangent,
            half_cotangent,
            shape(outer, pairs),
        ],
        [
            pltpu.VMEM((2, rows, features), F32),
            pltpu.VMEM((2, rows * features // LANES, LANES), F32),
            pltpu.VMEM((2, rows // PACK, LANES, LANES), F32),
            pltpu.SemaphoreType.DMA((5,)),
        ],
        name="prepare",
        far=range(4),
    )(by_side, alignment_right, alignment_left, projection_matrix)
    cotangent_peer = lax.ppermute(cotangent_send, "blk", partner)
    left_peer = lax.ppermute(left, "blk", partner)

    vmem = pl.BlockSpec(memory_space=pltpu.VMEM)
    hbm = pl.BlockSpec(memory_space=pltpu.HBM)
    factor = shape(row_pairs, tall, 4 * lanes, kind=BF16)
    factor_scratch = pltpu.VMEM(factor.shape, BF16)
    weight_cat = shape(tall, 3 * fold * pairs, kind=BF16)
    flip_scratch = pltpu.VMEM((2 * sequences, rows * channels), BF16)
    flip_sizes = (2 * fold * pairs, tall)
    spread = shape(row_pairs, 2, 2 * lanes, fold * pairs, kind=BF16)
    grad_own, spread_own, partial, weight_cat, weight_flip = large(
        functools.partial(gradient_kernel, blocks),
        [
            factor,
            spread,
            shape(steps // 2, sequences, 2 * lanes),
            weight_cat,
            pltpu.HBM(flip_sizes, BF16),
        ],
        [
            flip_scratch,
            pltpu.VMEM((tall, fold * pairs), F32),
            pltpu.VMEM(flip_sizes, BF16),
            pltpu.SemaphoreType.DMA,
        ],
        "gradient_own",
        out_specs=[vmem, vmem, vmem, vmem, hbm],
    )(weight, cotangent_own, left)
    rights = {0: right}
    distance = blocks // 2
    while distance:
        for slot in list(rights):
            sent = rights[slot]
            if slot:
                sent, _ = lax.optimization_barrier((sent, grad_own))
            rights[slot + distance] = lax.ppermute(sent, "blk", slot_moves[distance])
        distance = distance // 2
    rights = [rights[slot] for slot in range(blocks)]
    grad_peer, spread_peer = large(
        functools.partial(peer_kernel, blocks), [factor, spread], [], "gradient_peer"
    )(weight_cat, cotangent_peer)
    right_half = shape(blocks // 2, channels * depth, sequences)
    right_keep, right_send = large(
        functools.partial(right_kernel, blocks, depth),
        [right_half, right_half],
        [flip_scratch],
        "right_parts",
    )(grad_peer, left_peer, partial)
    right_send = lax.ppermute(right_send, "blk", slot_moves[blocks // 2])

    keep, send, outer_own, outer_peer = large(
        functools.partial(weight_kernel, blocks, depth),
        [shape(outer // 2, pairs)] * 2 + [pltpu.HBM(factor.shape, BF16)] * 2,
        [
            factor_scratch,
            factor_scratch,
            pltpu.VMEM((tall, fold * pairs), F32),
            pltpu.SemaphoreType.DMA((steps // 2, 2)),
        ],
        "weight",
        after=[right_keep],
        flops=2 * work,
        out_specs=[vmem, vmem, hbm, hbm],
    )(left, left_peer, spread_own, spread_peer, *rights)
    sent = lax.ppermute(send, "inner", cores)

    size = sequences // inner
    left_parts = large(
        functools.partial(left_kernel, blocks, depth),
        [shape(2, size, rows * channels)] * inner,
        [
            pltpu.VMEM((2 * rows * channels, sequences), F32),
            pltpu.VMEM((sequences, 2 * rows * channels), F32),
        ],
        "left_parts",
        after=[keep],
        flops=work,
    )(grad_own, grad_peer, *rights)
    keep, *left_parts = lax.optimization_barrier((keep, *left_parts))
    members = count * inner // 2
    pieces = (keep + sent).reshape(members, outer // 2 // members, pairs)

    def pair(values, after, name):
        return large(
            functools.partial(pair_kernel, blocks),
            shape(rows, blocks, depth, pairs),
            [
                factor_scratch,
                pltpu.VMEM(flip_sizes, BF16),
                pltpu.SemaphoreType.DMA((row_pairs + 1,)),
            ],
            name,
            far=[0, 1],
            after=after,
            flops=work,
        )(values, weight_flip)

    pieces, *left_parts = lax.optimization_barrier((pieces, *left_parts))
    left_parts = [
        lax.ppermute(part, "inner", inner_moves[slot]) if slot else part
        for slot, part in enumerate(left_parts)
    ]
    slot = blocks // 4
    while slot:
        part = shape(slot, channels * depth, sequences)
        right_keep, right_send = call(
            halve_kernel, [part, part], name="right_halve", after=[pieces]
        )(right_keep, right_send)
        right_send = lax.ppermute(right_send, "blk", slot_moves[slot])
        slot = slot // 2

    pair_other = pair(outer_peer, [pieces], "pair_peer")
    pair_found = lax.ppermute(pair_other, "blk", partner)

    pieces = lax.all_to_all(pieces, everyone, 0, 0, axis_index_groups=core_groups)
    pieces = call(
        spread_sum_kernel,
        shape(*pieces.shape),
        name="weight_sum",
        after=[pair_other, right_keep],
    )(pieces)
    pair_own = pair(outer_own, [pieces], "pair_own")
    left_own, left_send = call(
        left_add_kernel, [shape(size, rows * channels)] * 2, name="left_add", after=[pieces]
    )(*left_parts)
    pieces = lax.all_to_all(pieces, everyone, 0, 0, axis_index_groups=core_groups)

    left_found = [left_own, lax.ppermute(left_send, "blk", partner)]
    pair_update, grad_left, grad_right = call(
        finish_kernel,
        [
            pltpu.HBM(by_side.shape, F32),
            shape(rows, features // inner),
            shape(depth, features),
        ],
        [
            pltpu.VMEM((channels * depth, sequences), F32),
            pltpu.VMEM((depth // PACK, LANES, LANES), F32),
            pltpu.VMEM((depth * features // LANES, LANES), F32),
            pltpu.VMEM((size * rows * channels // LANES, LANES), F32),
            pltpu.VMEM((rows * features // inner // LANES, LANES), F32),
            pltpu.SemaphoreType.DMA((2,)),
        ],
        "finish",
        out_specs=[hbm, vmem, vmem],
    )(pair_own, pair_found, right_keep, right_send, *left_found)
    pair_update = pair_update.reshape(cotangent.shape)

    pieces, pair_update, grad_left, grad_right = lax.optimization_barrier(
        (pieces, pair_update, grad_left, grad_right)
    )
    mine = pieces.reshape(outer // 2, pairs)
    other = lax.ppermute(mine, "inner", cores)
    grad_weight = call(place_kernel, shape(outer, pairs), name="place")(mine, other)
    return (pair_update, grad_left, grad_right, grad_weight)


def solution(mesh):
    placed = (
        P(("groups", "blk"), None),
        P(("groups", "blk", "inner"), None),
        P(),
        P(("groups", "blk"), None, "inner", None),
    )
    return jax.shard_map(
        local,
        mesh=mesh,
        in_specs=placed,
        out_specs=(
            P(("groups", "blk"), None, "inner", None),
            P(("groups", "blk"), "inner"),
            P(("groups", "blk", "inner"), None),
            P("groups", None),
        ),
        check_vma=False,
    )
```

```python
import functools

import jax
import jax.numpy as jnp
from jax import lax
from jax.experimental import pallas as pl
from jax.experimental.pallas import tpu as pltpu
from jax.sharding import PartitionSpec as P

ENTRY_CHANNELS = 32
LANES = 128
PACK = LANES // ENTRY_CHANNELS
F32 = jnp.float32
BF16 = jnp.bfloat16
MIB = 1024 * 1024


def halves(values):
    high = values.astype(BF16)
    low = (values - high.astype(F32)).astype(BF16)
    return high, low


def dot(left, right):
    return jnp.dot(left, right, preferred_element_type=F32)


def dot_rows(left, right):
    return lax.dot_general(left, right, (((1,), (1,)), ((), ())), preferred_element_type=F32)


def fold_of(columns):
    return max(1, LANES // columns)


def strided(start, size, stride):
    return pl.ds(start, size, stride=stride)


def folded_weight(weight_ref, step, fold):
    channels = ENTRY_CHANNELS
    return jnp.concatenate(
        [weight_ref[strided(step * fold + part, channels, channels), :] for part in range(fold)], 1
    )


def slots_of(blocks):
    here = lax.axis_index("blk") // 2
    return [lax.bitwise_xor(here, slot) for slot in range(blocks)]


def spread_of(cotangent_ref, pair, slots, fold):
    columns = len(slots) * cotangent_ref.shape[2]
    empty = jnp.zeros((columns, cotangent_ref.shape[3]), BF16)
    spread = ([], [])
    for part in range(2):
        rows = jnp.concatenate([cotangent_ref[2 * pair + part, slot] for slot in slots], 0)
        for found, values in zip(spread, halves(rows)):
            for place in range(fold):
                found.append(
                    jnp.concatenate(
                        [values if place == other else empty for other in range(fold)], 1
                    )
                )
    return [jnp.concatenate(found, 0) for found in spread]


def turn_in(rows_minor, in_ref, out_ref, tiles, square):
    channels = ENTRY_CHANNELS
    rows, features = in_ref.shape
    count = features // LANES
    for tile in range(count):
        tiles[tile * rows : (tile + 1) * rows, :] = in_ref[:, tile * LANES : (tile + 1) * LANES]
    for group in range(rows // PACK):
        found = [tiles[strided(group * PACK + k, count, rows), :] for k in range(PACK)]
        for part in range(PACK):
            lanes = slice(part * channels, (part + 1) * channels)
            square[group, strided(part, count, PACK), :] = jnp.concatenate(
                [values[:, lanes] for values in found], 1
            )
        turned = square[group].T
        if rows_minor:
            for k in range(PACK):
                out_ref[strided(group * PACK + k, channels, rows), :] = turned[
                    k * channels : (k + 1) * channels
                ]
        else:
            out_ref[group * LANES : (group + 1) * LANES, :] = turned


def prepare_kernel(
    cotangent_hbm,
    right_hbm,
    left_hbm,
    weight_hbm,
    right_out,
    left_out,
    send_out,
    own_out,
    weight_out,
    inputs,
    tiles,
    square,
    semaphores,
):
    parity = lax.rem(lax.axis_index("blk"), 2)
    moves = (
        (right_hbm, inputs.at[0]),
        (left_hbm, inputs.at[1]),
        (cotangent_hbm.at[:, :, 1 - parity], send_out),
        (cotangent_hbm.at[:, :, parity], own_out),
        (weight_hbm, weight_out),
    )
    copies = [
        pltpu.make_async_copy(source, target, semaphores.at[at])
        for at, (source, target) in enumerate(moves)
    ]
    for copy in copies:
        copy.start()
    copies[0].wait()
    turn_in(True, inputs.at[0], right_out, tiles.at[0], square.at[0])
    copies[1].wait()
    turn_in(False, inputs.at[1], left_out, tiles.at[1], square.at[1])
    for copy in copies[2:]:
        copy.wait()


def turn_right(part_refs, out_ref, total, square, tiles):
    channels = ENTRY_CHANNELS
    rows, features = out_ref.shape
    count = features // LANES
    total[...] = functools.reduce(jnp.add, [ref[0] for ref in part_refs])
    for group in range(rows // PACK):
        stacked = [total[strided(group * PACK + k, channels, rows), :] for k in range(PACK)]
        square[group] = jnp.concatenate(stacked, 0).T
        pieces = [square[group, strided(part, count, PACK), :] for part in range(PACK)]
        for k in range(PACK):
            lanes = slice(k * channels, (k + 1) * channels)
            tiles[strided(group * PACK + k, count, rows), :] = jnp.concatenate(
                [piece[:, lanes] for piece in pieces], 1
            )
    for tile in range(count):
        out_ref[:, tile * LANES : (tile + 1) * LANES] = tiles[tile * rows : (tile + 1) * rows, :]


def turn_left(part_refs, out_ref, total, tiles):
    channels = ENTRY_CHANNELS
    size, width = part_refs[0].shape
    rows, features = out_ref.shape
    count = features // LANES
    found = functools.reduce(jnp.add, [ref[...] for ref in part_refs])
    for tile in range(width // LANES):
        total[tile * size : (tile + 1) * size, :] = found[:, tile * LANES : (tile + 1) * LANES]
    for tile in range(width // LANES):
        pieces = [total[strided(tile * size + part, count, PACK), :] for part in range(PACK)]
        for k in range(PACK):
            lanes = slice(k * channels, (k + 1) * channels)
            tiles[strided(tile * PACK + k, count, rows), :] = jnp.concatenate(
                [piece[:, lanes] for piece in pieces], 1
            )
    for tile in range(count):
        out_ref[:, tile * LANES : (tile + 1) * LANES] = tiles[tile * rows : (tile + 1) * rows, :]


def prepare_weight(weight_ref, weight_cat, fold):
    channels = ENTRY_CHANNELS
    for step in range(channels // fold):
        high, low = halves(folded_weight(weight_ref, step, fold))
        weight_cat[step * channels : (step + 1) * channels, :] = jnp.concatenate(
            [high, low, high], 1
        )


def gradient_phase(blocks, cotangent_ref, out_ref, spread_ref, weight_cat):
    fold = fold_of(blocks * cotangent_ref.shape[2])
    slots = slots_of(blocks)

    def step_of(pair, carry):
        high, low = spread_of(cotangent_ref, pair, slots, fold)
        spread_ref[pair, 0] = high
        spread_ref[pair, 1] = low
        found = dot_rows(weight_cat[...], jnp.concatenate([high, high, low], 1))
        out_ref[pair] = jnp.concatenate(halves(found), 1)
        return carry

    lax.fori_loop(0, out_ref.shape[0], step_of, 0, unroll=4)


def gradient_kernel(
    blocks,
    weight_ref,
    cotangent_ref,
    left_ref,
    out_ref,
    spread_ref,
    partial_ref,
    weight_cat,
    flip_hbm,
    left_flip,
    weight_rows,
    weight_flip,
    semaphore,
):
    fold = fold_of(blocks * cotangent_ref.shape[2])
    prepare_weight(weight_ref, weight_cat, fold)
    gradient_phase(blocks, cotangent_ref, out_ref, spread_ref, weight_cat)

    def store(step, found):
        partial_ref[step] = found

    right_phase(left_ref, out_ref, left_flip, store)
    channels = ENTRY_CHANNELS
    wide = weight_rows.shape[1]
    for step in range(channels // fold):
        weight_rows[step * channels : (step + 1) * channels, :] = folded_weight(
            weight_ref, step, fold
        )
    flip_high, flip_low = halves(weight_rows[...].T)
    weight_flip[:wide, :] = flip_high
    weight_flip[wide:, :] = flip_low
    copy = pltpu.make_async_copy(weight_flip, flip_hbm, semaphore)
    copy.start()
    copy.wait()


def peer_kernel(blocks, weight_cat, cotangent_ref, out_ref, spread_ref):
    gradient_phase(blocks, cotangent_ref, out_ref, spread_ref, weight_cat)


def right_phase(left_ref, factor_ref, left_flip, store):
    sequences = left_ref.shape[1]
    lanes = factor_ref.shape[2] // 4
    flip_high, flip_low = halves((left_ref[...] * (1.0 / sequences)).T)
    left_flip[:sequences, :] = flip_high
    left_flip[sequences:, :] = flip_low

    def step_of(step, carry):
        high, low = (
            jnp.concatenate(
                [rows_of_step([factor_ref], 2 * step + part, half, lanes) for part in range(2)], 1
            )
            for half in range(2)
        )
        first = dot(left_flip[...], high)
        second = dot(left_flip[:sequences, :], low)
        store(step, first[:sequences] + first[sequences:] + second)
        return carry

    lax.fori_loop(0, factor_ref.shape[1] // (2 * ENTRY_CHANNELS), step_of, 0, unroll=4)


def rows_of_step(refs, step, half, lanes):
    channels = ENTRY_CHANNELS
    rows = pl.ds(pl.multiple_of(step * channels, channels), channels)
    start = 2 * half * lanes
    return jnp.concatenate(
        [
            ref[pair, rows, start + part * lanes : start + (part + 1) * lanes]
            for ref in refs
            for pair in range(ref.shape[0])
            for part in range(2)
        ],
        0,
    )


def both_left(left_refs):
    sequences = left_refs[0].shape[1]
    return jnp.concatenate([ref[...] for ref in left_refs], 0) * (1.0 / sequences)


def right_kernel(
    blocks, depth, peer_ref, left_ref, partial_ref, keep_ref, send_ref, left_flip
):
    fold = fold_of(blocks * depth)
    lanes = fold * blocks * depth

    def store(step, found):
        found = found + partial_ref[step]
        for part in range(2):
            turned = found[:, part * lanes : (part + 1) * lanes].T
            for place in range(fold):
                for slot in range(blocks):
                    start = (place * blocks + slot) * depth
                    row = pl.multiple_of(((2 * step + part) * fold + place) * depth, depth)
                    out_ref = keep_ref if slot < blocks // 2 else send_ref
                    out_ref[slot % (blocks // 2), pl.ds(row, depth), :] = turned[
                        start : start + depth
                    ]

    right_phase(left_ref, peer_ref, left_flip, store)


def halve_kernel(keep_ref, found_ref, keep_out, send_out):
    half = keep_ref.shape[0] // 2
    for slot in range(half):
        keep_out[slot] = keep_ref[slot] + found_ref[slot]
        send_out[slot] = keep_ref[half + slot] + found_ref[half + slot]


def right_rows(right_refs, step, fold, depth):
    return jnp.concatenate(
        [
            ref[pl.ds(pl.multiple_of((step * fold + part) * depth, depth), depth), :]
            for part in range(fold)
            for ref in right_refs
        ],
        0,
    )


def weight_kernel(blocks, depth, own_left, peer_left, own_spread, peer_spread, *refs):
    right_refs = refs[:blocks]
    keep_ref, send_ref, own_out, peer_out, own_ref, peer_ref, total, semaphores = refs[blocks:]
    channels = ENTRY_CHANNELS
    fold = fold_of(blocks * depth)
    lanes = fold * blocks * depth
    pairs = total.shape[1] // fold
    high, low = halves(both_left([own_left, peer_left]))
    left_cat = jnp.concatenate([high, low, high], 1)

    def copies(step):
        size = 2 * channels
        rows = pl.ds(pl.multiple_of(step * size, size), size)
        return [
            pltpu.make_async_copy(ref.at[:, rows], out.at[:, rows], semaphores.at[step, side])
            for side, (ref, out) in enumerate(((own_ref, own_out), (peer_ref, peer_out)))
        ]

    def outer_step(step, carry):
        right = [right_rows(right_refs, 2 * step + part, fold, depth) for part in range(2)]
        high, low = halves(jnp.concatenate(right, 0))
        found = dot_rows(left_cat, jnp.concatenate([high, high, low], 1))
        both = halves(found)
        for part in range(2):
            start = pl.multiple_of((2 * step + part) * channels, channels)
            row = 0
            for ref in (own_ref, peer_ref):
                for index in range(2 * ref.shape[0]):
                    for half in range(2):
                        lane = (2 * half + index % 2) * lanes
                        ref[index // 2, pl.ds(start, channels), lane : lane + lanes] = both[half][
                            row : row + channels, part * lanes : (part + 1) * lanes
                        ]
                    row += channels
        for copy in copies(step):
            copy.start()
        return carry

    lax.fori_loop(0, channels // (2 * fold), outer_step, 0, unroll=4)
    total[...] = jnp.zeros_like(total)

    def weight_step(pair, carry):
        lefts, rights = [], []
        for ref, spread_ref in ((own_ref, own_spread), (peer_ref, peer_spread)):
            high = spread_ref[pair, 0]
            lefts += [ref[pair], ref[pair, :, : 2 * lanes]]
            rights += [high, high, spread_ref[pair, 1]]
        total[...] += dot(jnp.concatenate(lefts, 1), jnp.concatenate(rights, 0))
        return carry

    lax.fori_loop(0, own_ref.shape[0], weight_step, 0, unroll=4)
    core = lax.rem(lax.axis_index("inner"), 2)
    steps = channels // (2 * fold)
    for out_ref, half in ((keep_ref, core), (send_ref, 1 - core)):
        for step in range(steps):
            start = pl.multiple_of((half * steps + step) * channels, channels)
            found = total[pl.ds(start, channels), :]
            for part in range(fold):
                y = step * fold + part
                out_ref[y * channels : (y + 1) * channels, :] = found[
                    :, part * pairs : (part + 1) * pairs
                ]

    def finish(step, carry):
        for copy in copies(step):
            copy.wait()
        return carry

    lax.fori_loop(0, channels // (2 * fold), finish, 0)


def left_kernel(blocks, depth, own_ref, peer_ref, *refs):
    right_refs, out_refs, (total, flipped) = refs[:blocks], refs[blocks:-2], refs[-2:]
    lanes = own_ref.shape[2] // 4
    fold = lanes // (blocks * depth)
    sequences = right_refs[0].shape[1]
    group = 4
    total[...] = jnp.zeros_like(total)

    def step_of(step, carry):
        steps = [group * step + part for part in range(group)]
        right = [right_rows(right_refs, at, fold, depth) for at in steps]
        high, low = halves(jnp.concatenate(right, 0))
        grads = [
            jnp.concatenate([rows_of_step([own_ref, peer_ref], at, half, lanes) for at in steps], 1)
            for half in range(2)
        ]
        both = dot(grads[0], jnp.concatenate([high, low], 1))
        total[...] += both[:, :sequences] + both[:, sequences:] + dot(grads[1], high)
        return carry

    lax.fori_loop(0, ENTRY_CHANNELS // (fold * group), step_of, 0, unroll=4)
    flipped[...] = total[...].T * (1.0 / sequences)
    here = lax.axis_index("inner")
    size, width = out_refs[0].shape[1:]
    for slot, ref in enumerate(out_refs):
        start = pl.multiple_of(lax.bitwise_xor(here, slot) * size, size)
        for side in range(2):
            ref[side] = flipped[pl.ds(start, size), side * width : (side + 1) * width]


def left_add_kernel(*refs):
    parts, (own_out, send_out) = refs[:-2], refs[-2:]
    for side, ref in enumerate((own_out, send_out)):
        ref[...] = functools.reduce(jnp.add, [part[side] for part in parts])


def pair_kernel(blocks, outer_hbm, flip_hbm, out_ref, outer_ref, weight_flip, semaphores):
    depth, pairs = out_ref.shape[2:]
    count = outer_ref.shape[0]
    lanes = outer_ref.shape[2] // 4
    columns = blocks * depth
    fold = lanes // columns
    wide = fold * pairs

    def copy_of(pair):
        return pltpu.make_async_copy(outer_hbm.at[pair], outer_ref.at[pair], semaphores.at[pair])

    flip_copy = pltpu.make_async_copy(flip_hbm, weight_flip, semaphores.at[count])
    flip_copy.start()
    for pair in range(count):
        copy_of(pair).start()
    flip_copy.wait()
    slots = slots_of(blocks)

    def step_of(pair, carry):
        copy_of(pair).wait()
        first = dot(weight_flip[...], outer_ref[pair, :, : 2 * lanes])
        second = dot(weight_flip[:wide, :], outer_ref[pair, :, 2 * lanes :])
        found = first[:wide] + first[wide:] + second
        for part in range(2):
            turned = []
            for place in range(fold):
                start = part * lanes
                piece = found[place * pairs : (place + 1) * pairs, start : start + lanes].T
                turned.append(piece[place * columns : (place + 1) * columns])
            turned = functools.reduce(jnp.add, turned)
            row = 2 * pair + part
            for slot in range(blocks):
                out_ref[row, slots[slot]] = turned[slot * depth : (slot + 1) * depth]
        return carry

    lax.fori_loop(0, count, step_of, 0)


def finish_kernel(own_ref, other_ref, keep_ref, found_ref, *refs):
    left_refs, refs = refs[:-9], refs[-9:]
    pair_hbm, left_out, right_out = refs[:3]
    right_total, right_square, right_tiles, left_total, left_tiles, semaphores = refs[3:]
    parity = lax.rem(lax.axis_index("blk"), 2)
    copies = [
        pltpu.make_async_copy(ref, pair_hbm.at[:, :, side], semaphores.at[at])
        for at, (ref, side) in enumerate(((own_ref, parity), (other_ref, 1 - parity)))
    ]
    for copy in copies:
        copy.start()
    turn_right([keep_ref, found_ref], right_out, right_total, right_square, right_tiles)
    turn_left(left_refs, left_out, left_total, left_tiles)
    for copy in copies:
        copy.wait()


def spread_sum_kernel(in_ref, out_ref):
    found = in_ref[0]
    for part in range(1, in_ref.shape[0]):
        found = found + in_ref[part]
    for part in range(in_ref.shape[0]):
        out_ref[part] = found


def place_kernel(mine_ref, other_ref, out_ref):
    channels = ENTRY_CHANNELS
    core = lax.rem(lax.axis_index("inner"), 2)
    steps = mine_ref.shape[0] // channels
    for ref, half in ((mine_ref, core), (other_ref, 1 - core)):
        for step in range(steps):
            rows = ref[step * channels : (step + 1) * channels, :]
            out_ref[strided(half * steps + step, channels, channels), :] = rows


def shape(*sizes, kind=F32):
    return jax.ShapeDtypeStruct(sizes, kind)


def call(
    kernel,
    out_shape,
    scratch=(),
    name=None,
    limit=16 * MIB,
    far=(),
    after=(),
    out_specs=None,
    flops=1,
):
    def run(*operands):
        vmem = pl.BlockSpec(memory_space=pltpu.VMEM)
        hbm = pl.BlockSpec(memory_space=pltpu.HBM)
        in_specs = [pl.BlockSpec(memory_space=pl.ANY)] * len(after)
        in_specs += [hbm if at in far else vmem for at in range(len(operands))]
        operands = [
            pltpu.with_memory_space_constraint(operand, pltpu.HBM) if at in far else operand
            for at, operand in enumerate(operands)
        ]
        extra = {} if out_specs is None else {"out_specs": out_specs}
        return pl.pallas_call(
            lambda *refs: kernel(*refs[len(after) :]),
            out_shape=out_shape,
            in_specs=in_specs,
            scratch_shapes=list(scratch),
            compiler_params=pltpu.CompilerParams(vmem_limit_bytes=limit),
            cost_estimate=pl.CostEstimate(flops=flops, bytes_accessed=1, transcendentals=0),
            name=name,
            **extra,
        )(*after, *operands)

    return run


def local(alignment_left, alignment_right, projection_matrix, cotangent):
    rows, features = alignment_left.shape
    depth = alignment_right.shape[0]
    count = lax.axis_size("blk")
    inner = lax.axis_size("inner")
    channels = ENTRY_CHANNELS
    sequences = features // channels
    outer, pairs = projection_matrix.shape
    blocks = count // 2
    fold = fold_of(blocks * depth)
    lanes = fold * blocks * depth
    tall = outer // fold
    steps = channels // fold
    row_pairs = rows // 2
    everyone = ("blk", "inner")

    partner = [(here, here ^ 1) for here in range(count)]
    slot_moves = [[(here, here ^ (2 * slot)) for here in range(count)] for slot in range(blocks)]
    inner_moves = [[(here, here ^ slot) for here in range(inner)] for slot in range(inner)]
    cores = [(here, here ^ 1) for here in range(inner)]
    core_groups = [list(range(core, count * inner, 2)) for core in range(2)]

    limit = 20 * MIB * max(1, blocks * depth * fold // LANES * 2 // fold)
    large = functools.partial(call, limit=limit)
    work = 4 * 2 * rows * 2 * blocks * depth * outer * pairs * 3

    by_side = cotangent.reshape(rows, blocks, 2, depth, pairs)
    half_cotangent = shape(rows, blocks, depth, pairs)
    right, left, cotangent_send, cotangent_own, weight = call(
        prepare_kernel,
        [
            shape(channels * depth, sequences),
            shape(rows * channels, sequences),
            half_cotangent,
            half_cotangent,
            shape(outer, pairs),
        ],
        [
            pltpu.VMEM((2, rows, features), F32),
            pltpu.VMEM((2, rows * features // LANES, LANES), F32),
            pltpu.VMEM((2, rows // PACK, LANES, LANES), F32),
            pltpu.SemaphoreType.DMA((5,)),
        ],
        name="prepare",
        far=range(4),
    )(by_side, alignment_right, alignment_left, projection_matrix)
    cotangent_peer = lax.ppermute(cotangent_send, "blk", partner)
    left_peer = lax.ppermute(left, "blk", partner)

    vmem = pl.BlockSpec(memory_space=pltpu.VMEM)
    hbm = pl.BlockSpec(memory_space=pltpu.HBM)
    factor = shape(row_pairs, tall, 4 * lanes, kind=BF16)
    factor_scratch = pltpu.VMEM(factor.shape, BF16)
    weight_cat = shape(tall, 3 * fold * pairs, kind=BF16)
    flip_scratch = pltpu.VMEM((2 * sequences, rows * channels), BF16)
    flip_sizes = (2 * fold * pairs, tall)
    spread = shape(row_pairs, 2, 2 * lanes, fold * pairs, kind=BF16)
    grad_own, spread_own, partial, weight_cat, weight_flip = large(
        functools.partial(gradient_kernel, blocks),
        [
            factor,
            spread,
            shape(steps // 2, sequences, 2 * lanes),
            weight_cat,
            pltpu.HBM(flip_sizes, BF16),
        ],
        [
            flip_scratch,
            pltpu.VMEM((tall, fold * pairs), F32),
            pltpu.VMEM(flip_sizes, BF16),
            pltpu.SemaphoreType.DMA,
        ],
        "gradient_own",
        out_specs=[vmem, vmem, vmem, vmem, hbm],
    )(weight, cotangent_own, left)
    grad_peer, spread_peer = large(
        functools.partial(peer_kernel, blocks), [factor, spread], [], "gradient_peer"
    )(weight_cat, cotangent_peer)
    rights = {0: right}
    distance = blocks // 2
    while distance:
        for slot in list(rights):
            sent = rights[slot]
            if slot:
                sent, _ = lax.optimization_barrier((sent, grad_peer))
            rights[slot + distance] = lax.ppermute(sent, "blk", slot_moves[distance])
        distance = distance // 2
    rights = [rights[slot] for slot in range(blocks)]
    right_half = shape(blocks // 2, channels * depth, sequences)
    right_keep, right_send = large(
        functools.partial(right_kernel, blocks, depth),
        [right_half, right_half],
        [flip_scratch],
        "right_parts",
    )(grad_peer, left_peer, partial)
    right_send = lax.ppermute(right_send, "blk", slot_moves[blocks // 2])

    keep, send, outer_own, outer_peer = large(
        functools.partial(weight_kernel, blocks, depth),
        [shape(outer // 2, pairs)] * 2 + [pltpu.HBM(factor.shape, BF16)] * 2,
        [
            factor_scratch,
            factor_scratch,
            pltpu.VMEM((tall, fold * pairs), F32),
            pltpu.SemaphoreType.DMA((steps // 2, 2)),
        ],
        "weight",
        after=[right_keep],
        flops=2 * work,
        out_specs=[vmem, vmem, hbm, hbm],
    )(left, left_peer, spread_own, spread_peer, *rights)
    sent = lax.ppermute(send, "inner", cores)

    size = sequences // inner
    left_parts = large(
        functools.partial(left_kernel, blocks, depth),
        [shape(2, size, rows * channels)] * inner,
        [
            pltpu.VMEM((2 * rows * channels, sequences), F32),
            pltpu.VMEM((sequences, 2 * rows * channels), F32),
        ],
        "left_parts",
        after=[keep],
        flops=work,
    )(grad_own, grad_peer, *rights)
    keep, *left_parts = lax.optimization_barrier((keep, *left_parts))
    members = count * inner // 2
    pieces = (keep + sent).reshape(members, outer // 2 // members, pairs)

    def pair(values, after, name):
        return large(
            functools.partial(pair_kernel, blocks),
            shape(rows, blocks, depth, pairs),
            [
                factor_scratch,
                pltpu.VMEM(flip_sizes, BF16),
                pltpu.SemaphoreType.DMA((row_pairs + 1,)),
            ],
            name,
            far=[0, 1],
            after=after,
            flops=work,
        )(values, weight_flip)

    pieces, *left_parts = lax.optimization_barrier((pieces, *left_parts))
    left_parts = [
        lax.ppermute(part, "inner", inner_moves[slot]) if slot else part
        for slot, part in enumerate(left_parts)
    ]
    slot = blocks // 4
    while slot:
        part = shape(slot, channels * depth, sequences)
        right_keep, right_send = call(
            halve_kernel, [part, part], name="right_halve", after=[pieces]
        )(right_keep, right_send)
        right_send = lax.ppermute(right_send, "blk", slot_moves[slot])
        slot = slot // 2

    pair_other = pair(outer_peer, [pieces], "pair_peer")
    pair_found = lax.ppermute(pair_other, "blk", partner)

    pieces = lax.all_to_all(pieces, everyone, 0, 0, axis_index_groups=core_groups)
    pieces = call(
        spread_sum_kernel,
        shape(*pieces.shape),
        name="weight_sum",
        after=[pair_other, right_keep],
    )(pieces)
    pair_own = pair(outer_own, [pieces], "pair_own")
    left_own, left_send = call(
        left_add_kernel, [shape(size, rows * channels)] * 2, name="left_add", after=[pieces]
    )(*left_parts)
    pieces = lax.all_to_all(pieces, everyone, 0, 0, axis_index_groups=core_groups)

    left_found = [left_own, lax.ppermute(left_send, "blk", partner)]
    pair_update, grad_left, grad_right = call(
        finish_kernel,
        [
            pltpu.HBM(by_side.shape, F32),
            shape(rows, features // inner),
            shape(depth, features),
        ],
        [
            pltpu.VMEM((channels * depth, sequences), F32),
            pltpu.VMEM((depth // PACK, LANES, LANES), F32),
            pltpu.VMEM((depth * features // LANES, LANES), F32),
            pltpu.VMEM((size * rows * channels // LANES, LANES), F32),
            pltpu.VMEM((rows * features // inner // LANES, LANES), F32),
            pltpu.SemaphoreType.DMA((2,)),
        ],
        "finish",
        out_specs=[hbm, vmem, vmem],
    )(pair_own, pair_found, right_keep, right_send, *left_found)
    pair_update = pair_update.reshape(cotangent.shape)

    pieces, pair_update, grad_left, grad_right = lax.optimization_barrier(
        (pieces, pair_update, grad_left, grad_right)
    )
    mine = pieces.reshape(outer // 2, pairs)
    other = lax.ppermute(mine, "inner", cores)
    grad_weight = call(place_kernel, shape(outer, pairs), name="place")(mine, other)
    return (pair_update, grad_left, grad_right, grad_weight)


def solution(mesh):
    placed = (
        P(("groups", "blk"), None),
        P(("groups", "blk", "inner"), None),
        P(),
        P(("groups", "blk"), None, "inner", None),
    )
    return jax.shard_map(
        local,
        mesh=mesh,
        in_specs=placed,
        out_specs=(
            P(("groups", "blk"), None, "inner", None),
            P(("groups", "blk"), "inner"),
            P(("groups", "blk", "inner"), None),
            P("groups", None),
        ),
        check_vma=False,
    )
```

```python
import functools

import jax
import jax.numpy as jnp
from jax import lax
from jax.experimental import pallas as pl
from jax.experimental.pallas import tpu as pltpu
from jax.sharding import PartitionSpec as P

ENTRY_CHANNELS = 32
LANES = 128
PACK = LANES // ENTRY_CHANNELS
F32 = jnp.float32
BF16 = jnp.bfloat16
MIB = 1024 * 1024


def halves(values):
    high = values.astype(BF16)
    low = (values - high.astype(F32)).astype(BF16)
    return high, low


def dot(left, right):
    return jnp.dot(left, right, preferred_element_type=F32)


def dot_rows(left, right):
    return lax.dot_general(left, right, (((1,), (1,)), ((), ())), preferred_element_type=F32)


def fold_of(columns):
    return max(1, LANES // columns)


def strided(start, size, stride):
    return pl.ds(start, size, stride=stride)


def folded_weight(weight_ref, step, fold):
    channels = ENTRY_CHANNELS
    return jnp.concatenate(
        [weight_ref[strided(step * fold + part, channels, channels), :] for part in range(fold)], 1
    )


def slots_of(blocks):
    here = lax.axis_index("blk") // 2
    return [lax.bitwise_xor(here, slot) for slot in range(blocks)]


def spread_of(cotangent_ref, pair, slots, fold):
    columns = len(slots) * cotangent_ref.shape[2]
    empty = jnp.zeros((columns, cotangent_ref.shape[3]), BF16)
    spread = ([], [])
    for part in range(2):
        rows = jnp.concatenate([cotangent_ref[2 * pair + part, slot] for slot in slots], 0)
        for found, values in zip(spread, halves(rows)):
            for place in range(fold):
                found.append(
                    jnp.concatenate(
                        [values if place == other else empty for other in range(fold)], 1
                    )
                )
    return [jnp.concatenate(found, 0) for found in spread]


def turn_in(rows_minor, in_ref, out_ref, tiles, square):
    channels = ENTRY_CHANNELS
    rows, features = in_ref.shape
    count = features // LANES
    for tile in range(count):
        tiles[tile * rows : (tile + 1) * rows, :] = in_ref[:, tile * LANES : (tile + 1) * LANES]
    for group in range(rows // PACK):
        found = [tiles[strided(group * PACK + k, count, rows), :] for k in range(PACK)]
        for part in range(PACK):
            lanes = slice(part * channels, (part + 1) * channels)
            square[group, strided(part, count, PACK), :] = jnp.concatenate(
                [values[:, lanes] for values in found], 1
            )
        turned = square[group].T
        if rows_minor:
            for k in range(PACK):
                out_ref[strided(group * PACK + k, channels, rows), :] = turned[
                    k * channels : (k + 1) * channels
                ]
        else:
            out_ref[group * LANES : (group + 1) * LANES, :] = turned


def prepare_kernel(
    cotangent_hbm,
    right_hbm,
    left_hbm,
    weight_hbm,
    right_out,
    left_out,
    send_out,
    own_out,
    weight_out,
    inputs,
    tiles,
    square,
    semaphores,
):
    parity = lax.rem(lax.axis_index("blk"), 2)
    moves = (
        (right_hbm, inputs.at[0]),
        (left_hbm, inputs.at[1]),
        (cotangent_hbm.at[:, :, 1 - parity], send_out),
        (cotangent_hbm.at[:, :, parity], own_out),
        (weight_hbm, weight_out),
    )
    copies = [
        pltpu.make_async_copy(source, target, semaphores.at[at])
        for at, (source, target) in enumerate(moves)
    ]
    for copy in copies:
        copy.start()
    copies[0].wait()
    turn_in(True, inputs.at[0], right_out, tiles.at[0], square.at[0])
    copies[1].wait()
    turn_in(False, inputs.at[1], left_out, tiles.at[1], square.at[1])
    for copy in copies[2:]:
        copy.wait()


def turn_right(part_refs, out_ref, total, square, tiles):
    channels = ENTRY_CHANNELS
    rows, features = out_ref.shape
    count = features // LANES
    total[...] = functools.reduce(jnp.add, [ref[0] for ref in part_refs])
    for group in range(rows // PACK):
        stacked = [total[strided(group * PACK + k, channels, rows), :] for k in range(PACK)]
        square[group] = jnp.concatenate(stacked, 0).T
        pieces = [square[group, strided(part, count, PACK), :] for part in range(PACK)]
        for k in range(PACK):
            lanes = slice(k * channels, (k + 1) * channels)
            tiles[strided(group * PACK + k, count, rows), :] = jnp.concatenate(
                [piece[:, lanes] for piece in pieces], 1
            )
    for tile in range(count):
        out_ref[:, tile * LANES : (tile + 1) * LANES] = tiles[tile * rows : (tile + 1) * rows, :]


def turn_left(part_refs, out_ref, total, tiles):
    channels = ENTRY_CHANNELS
    size, width = part_refs[0].shape
    rows, features = out_ref.shape
    count = features // LANES
    found = functools.reduce(jnp.add, [ref[...] for ref in part_refs])
    for tile in range(width // LANES):
        total[tile * size : (tile + 1) * size, :] = found[:, tile * LANES : (tile + 1) * LANES]
    for tile in range(width // LANES):
        pieces = [total[strided(tile * size + part, count, PACK), :] for part in range(PACK)]
        for k in range(PACK):
            lanes = slice(k * channels, (k + 1) * channels)
            tiles[strided(tile * PACK + k, count, rows), :] = jnp.concatenate(
                [piece[:, lanes] for piece in pieces], 1
            )
    for tile in range(count):
        out_ref[:, tile * LANES : (tile + 1) * LANES] = tiles[tile * rows : (tile + 1) * rows, :]


def prepare_weight(weight_ref, weight_cat, fold):
    channels = ENTRY_CHANNELS
    for step in range(channels // fold):
        high, low = halves(folded_weight(weight_ref, step, fold))
        weight_cat[step * channels : (step + 1) * channels, :] = jnp.concatenate(
            [high, low, high], 1
        )


def gradient_phase(blocks, cotangent_ref, out_ref, spread_ref, weight_cat):
    fold = fold_of(blocks * cotangent_ref.shape[2])
    slots = slots_of(blocks)

    def step_of(pair, carry):
        high, low = spread_of(cotangent_ref, pair, slots, fold)
        spread_ref[pair, 0] = high
        spread_ref[pair, 1] = low
        found = dot_rows(weight_cat[...], jnp.concatenate([high, high, low], 1))
        out_ref[pair] = jnp.concatenate(halves(found), 1)
        return carry

    lax.fori_loop(0, out_ref.shape[0], step_of, 0, unroll=8)


def gradient_kernel(
    blocks,
    weight_ref,
    cotangent_ref,
    left_ref,
    out_ref,
    spread_ref,
    partial_ref,
    weight_cat,
    flip_hbm,
    left_flip,
    weight_rows,
    weight_flip,
    semaphore,
):
    fold = fold_of(blocks * cotangent_ref.shape[2])
    prepare_weight(weight_ref, weight_cat, fold)
    gradient_phase(blocks, cotangent_ref, out_ref, spread_ref, weight_cat)

    def store(step, found):
        partial_ref[step] = found

    right_phase(left_ref, out_ref, left_flip, store)
    channels = ENTRY_CHANNELS
    wide = weight_rows.shape[1]
    for step in range(channels // fold):
        weight_rows[step * channels : (step + 1) * channels, :] = folded_weight(
            weight_ref, step, fold
        )
    flip_high, flip_low = halves(weight_rows[...].T)
    weight_flip[:wide, :] = flip_high
    weight_flip[wide:, :] = flip_low
    copy = pltpu.make_async_copy(weight_flip, flip_hbm, semaphore)
    copy.start()
    copy.wait()


def peer_kernel(blocks, weight_cat, cotangent_ref, out_ref, spread_ref):
    gradient_phase(blocks, cotangent_ref, out_ref, spread_ref, weight_cat)


def right_phase(left_ref, factor_ref, left_flip, store):
    sequences = left_ref.shape[1]
    lanes = factor_ref.shape[2] // 4
    flip_high, flip_low = halves((left_ref[...] * (1.0 / sequences)).T)
    left_flip[:sequences, :] = flip_high
    left_flip[sequences:, :] = flip_low

    def step_of(step, carry):
        high, low = (
            jnp.concatenate(
                [rows_of_step([factor_ref], 2 * step + part, half, lanes) for part in range(2)], 1
            )
            for half in range(2)
        )
        first = dot(left_flip[...], high)
        second = dot(left_flip[:sequences, :], low)
        store(step, first[:sequences] + first[sequences:] + second)
        return carry

    lax.fori_loop(0, factor_ref.shape[1] // (2 * ENTRY_CHANNELS), step_of, 0, unroll=8)


def rows_of_step(refs, step, half, lanes):
    channels = ENTRY_CHANNELS
    rows = pl.ds(pl.multiple_of(step * channels, channels), channels)
    start = 2 * half * lanes
    return jnp.concatenate(
        [
            ref[pair, rows, start + part * lanes : start + (part + 1) * lanes]
            for ref in refs
            for pair in range(ref.shape[0])
            for part in range(2)
        ],
        0,
    )


def both_left(left_refs):
    sequences = left_refs[0].shape[1]
    return jnp.concatenate([ref[...] for ref in left_refs], 0) * (1.0 / sequences)


def right_kernel(
    blocks, depth, peer_ref, left_ref, partial_ref, keep_ref, send_ref, left_flip
):
    fold = fold_of(blocks * depth)
    lanes = fold * blocks * depth

    def store(step, found):
        found = found + partial_ref[step]
        for part in range(2):
            turned = found[:, part * lanes : (part + 1) * lanes].T
            for place in range(fold):
                for slot in range(blocks):
                    start = (place * blocks + slot) * depth
                    row = pl.multiple_of(((2 * step + part) * fold + place) * depth, depth)
                    out_ref = keep_ref if slot < blocks // 2 else send_ref
                    out_ref[slot % (blocks // 2), pl.ds(row, depth), :] = turned[
                        start : start + depth
                    ]

    right_phase(left_ref, peer_ref, left_flip, store)


def halve_kernel(keep_ref, found_ref, keep_out, send_out):
    half = keep_ref.shape[0] // 2
    for slot in range(half):
        keep_out[slot] = keep_ref[slot] + found_ref[slot]
        send_out[slot] = keep_ref[half + slot] + found_ref[half + slot]


def right_rows(right_refs, step, fold, depth):
    return jnp.concatenate(
        [
            ref[pl.ds(pl.multiple_of((step * fold + part) * depth, depth), depth), :]
            for part in range(fold)
            for ref in right_refs
        ],
        0,
    )


def weight_kernel(blocks, depth, own_left, peer_left, own_spread, peer_spread, *refs):
    right_refs = refs[:blocks]
    keep_ref, send_ref, own_out, peer_out, own_ref, peer_ref, total, semaphores = refs[blocks:]
    channels = ENTRY_CHANNELS
    fold = fold_of(blocks * depth)
    lanes = fold * blocks * depth
    pairs = total.shape[1] // fold
    high, low = halves(both_left([own_left, peer_left]))
    left_cat = jnp.concatenate([high, low, high], 1)

    def copies(step):
        size = 2 * channels
        rows = pl.ds(pl.multiple_of(step * size, size), size)
        return [
            pltpu.make_async_copy(ref.at[:, rows], out.at[:, rows], semaphores.at[step, side])
            for side, (ref, out) in enumerate(((own_ref, own_out), (peer_ref, peer_out)))
        ]

    def outer_step(step, carry):
        right = [right_rows(right_refs, 2 * step + part, fold, depth) for part in range(2)]
        high, low = halves(jnp.concatenate(right, 0))
        found = dot_rows(left_cat, jnp.concatenate([high, high, low], 1))
        both = halves(found)
        for part in range(2):
            start = pl.multiple_of((2 * step + part) * channels, channels)
            row = 0
            for ref in (own_ref, peer_ref):
                for index in range(2 * ref.shape[0]):
                    for half in range(2):
                        lane = (2 * half + index % 2) * lanes
                        ref[index // 2, pl.ds(start, channels), lane : lane + lanes] = both[half][
                            row : row + channels, part * lanes : (part + 1) * lanes
                        ]
                    row += channels
        for copy in copies(step):
            copy.start()
        return carry

    lax.fori_loop(0, channels // (2 * fold), outer_step, 0, unroll=8)
    total[...] = jnp.zeros_like(total)

    def weight_step(pair, carry):
        lefts, rights = [], []
        for ref, spread_ref in ((own_ref, own_spread), (peer_ref, peer_spread)):
            high = spread_ref[pair, 0]
            lefts += [ref[pair], ref[pair, :, : 2 * lanes]]
            rights += [high, high, spread_ref[pair, 1]]
        total[...] += dot(jnp.concatenate(lefts, 1), jnp.concatenate(rights, 0))
        return carry

    lax.fori_loop(0, own_ref.shape[0], weight_step, 0, unroll=8)
    core = lax.rem(lax.axis_index("inner"), 2)
    steps = channels // (2 * fold)
    for out_ref, half in ((keep_ref, core), (send_ref, 1 - core)):
        for step in range(steps):
            start = pl.multiple_of((half * steps + step) * channels, channels)
            found = total[pl.ds(start, channels), :]
            for part in range(fold):
                y = step * fold + part
                out_ref[y * channels : (y + 1) * channels, :] = found[
                    :, part * pairs : (part + 1) * pairs
                ]

    def finish(step, carry):
        for copy in copies(step):
            copy.wait()
        return carry

    lax.fori_loop(0, channels // (2 * fold), finish, 0)


def left_kernel(blocks, depth, own_ref, peer_ref, *refs):
    right_refs, out_refs, (total, flipped) = refs[:blocks], refs[blocks:-2], refs[-2:]
    lanes = own_ref.shape[2] // 4
    fold = lanes // (blocks * depth)
    sequences = right_refs[0].shape[1]
    group = 4
    total[...] = jnp.zeros_like(total)

    def step_of(step, carry):
        steps = [group * step + part for part in range(group)]
        right = [right_rows(right_refs, at, fold, depth) for at in steps]
        high, low = halves(jnp.concatenate(right, 0))
        grads = [
            jnp.concatenate([rows_of_step([own_ref, peer_ref], at, half, lanes) for at in steps], 1)
            for half in range(2)
        ]
        both = dot(grads[0], jnp.concatenate([high, low], 1))
        total[...] += both[:, :sequences] + both[:, sequences:] + dot(grads[1], high)
        return carry

    lax.fori_loop(0, ENTRY_CHANNELS // (fold * group), step_of, 0, unroll=4)
    flipped[...] = total[...].T * (1.0 / sequences)
    here = lax.axis_index("inner")
    size, width = out_refs[0].shape[1:]
    for slot, ref in enumerate(out_refs):
        start = pl.multiple_of(lax.bitwise_xor(here, slot) * size, size)
        for side in range(2):
            ref[side] = flipped[pl.ds(start, size), side * width : (side + 1) * width]


def left_add_kernel(*refs):
    parts, (own_out, send_out) = refs[:-2], refs[-2:]
    for side, ref in enumerate((own_out, send_out)):
        ref[...] = functools.reduce(jnp.add, [part[side] for part in parts])


def pair_kernel(blocks, outer_hbm, flip_hbm, out_ref, outer_ref, weight_flip, semaphores):
    depth, pairs = out_ref.shape[2:]
    count = outer_ref.shape[0]
    lanes = outer_ref.shape[2] // 4
    columns = blocks * depth
    fold = lanes // columns
    wide = fold * pairs

    def copy_of(pair):
        return pltpu.make_async_copy(outer_hbm.at[pair], outer_ref.at[pair], semaphores.at[pair])

    flip_copy = pltpu.make_async_copy(flip_hbm, weight_flip, semaphores.at[count])
    flip_copy.start()
    for pair in range(count):
        copy_of(pair).start()
    flip_copy.wait()
    slots = slots_of(blocks)

    def step_of(pair, carry):
        copy_of(pair).wait()
        first = dot(weight_flip[...], outer_ref[pair, :, : 2 * lanes])
        second = dot(weight_flip[:wide, :], outer_ref[pair, :, 2 * lanes :])
        found = first[:wide] + first[wide:] + second
        for part in range(2):
            turned = []
            for place in range(fold):
                start = part * lanes
                piece = found[place * pairs : (place + 1) * pairs, start : start + lanes].T
                turned.append(piece[place * columns : (place + 1) * columns])
            turned = functools.reduce(jnp.add, turned)
            row = 2 * pair + part
            for slot in range(blocks):
                out_ref[row, slots[slot]] = turned[slot * depth : (slot + 1) * depth]
        return carry

    lax.fori_loop(0, count, step_of, 0)


def finish_kernel(own_ref, other_ref, keep_ref, found_ref, *refs):
    left_refs, refs = refs[:-9], refs[-9:]
    pair_hbm, left_out, right_out = refs[:3]
    right_total, right_square, right_tiles, left_total, left_tiles, semaphores = refs[3:]
    parity = lax.rem(lax.axis_index("blk"), 2)
    copies = [
        pltpu.make_async_copy(ref, pair_hbm.at[:, :, side], semaphores.at[at])
        for at, (ref, side) in enumerate(((own_ref, parity), (other_ref, 1 - parity)))
    ]
    for copy in copies:
        copy.start()
    turn_right([keep_ref, found_ref], right_out, right_total, right_square, right_tiles)
    turn_left(left_refs, left_out, left_total, left_tiles)
    for copy in copies:
        copy.wait()


def spread_sum_kernel(in_ref, out_ref):
    found = in_ref[0]
    for part in range(1, in_ref.shape[0]):
        found = found + in_ref[part]
    for part in range(in_ref.shape[0]):
        out_ref[part] = found


def place_kernel(mine_ref, other_ref, out_ref):
    channels = ENTRY_CHANNELS
    core = lax.rem(lax.axis_index("inner"), 2)
    steps = mine_ref.shape[0] // channels
    for ref, half in ((mine_ref, core), (other_ref, 1 - core)):
        for step in range(steps):
            rows = ref[step * channels : (step + 1) * channels, :]
            out_ref[strided(half * steps + step, channels, channels), :] = rows


def shape(*sizes, kind=F32):
    return jax.ShapeDtypeStruct(sizes, kind)


def call(
    kernel,
    out_shape,
    scratch=(),
    name=None,
    limit=16 * MIB,
    far=(),
    after=(),
    out_specs=None,
    flops=1,
):
    def run(*operands):
        vmem = pl.BlockSpec(memory_space=pltpu.VMEM)
        hbm = pl.BlockSpec(memory_space=pltpu.HBM)
        in_specs = [pl.BlockSpec(memory_space=pl.ANY)] * len(after)
        in_specs += [hbm if at in far else vmem for at in range(len(operands))]
        operands = [
            pltpu.with_memory_space_constraint(operand, pltpu.HBM) if at in far else operand
            for at, operand in enumerate(operands)
        ]
        extra = {} if out_specs is None else {"out_specs": out_specs}
        return pl.pallas_call(
            lambda *refs: kernel(*refs[len(after) :]),
            out_shape=out_shape,
            in_specs=in_specs,
            scratch_shapes=list(scratch),
            compiler_params=pltpu.CompilerParams(vmem_limit_bytes=limit),
            cost_estimate=pl.CostEstimate(flops=flops, bytes_accessed=1, transcendentals=0),
            name=name,
            **extra,
        )(*after, *operands)

    return run


def local(alignment_left, alignment_right, projection_matrix, cotangent):
    rows, features = alignment_left.shape
    depth = alignment_right.shape[0]
    count = lax.axis_size("blk")
    inner = lax.axis_size("inner")
    channels = ENTRY_CHANNELS
    sequences = features // channels
    outer, pairs = projection_matrix.shape
    blocks = count // 2
    fold = fold_of(blocks * depth)
    lanes = fold * blocks * depth
    tall = outer // fold
    steps = channels // fold
    row_pairs = rows // 2
    everyone = ("blk", "inner")

    partner = [(here, here ^ 1) for here in range(count)]
    slot_moves = [[(here, here ^ (2 * slot)) for here in range(count)] for slot in range(blocks)]
    inner_moves = [[(here, here ^ slot) for here in range(inner)] for slot in range(inner)]
    cores = [(here, here ^ 1) for here in range(inner)]
    core_groups = [list(range(core, count * inner, 2)) for core in range(2)]

    limit = 20 * MIB * max(1, blocks * depth * fold // LANES * 2 // fold)
    large = functools.partial(call, limit=limit)
    work = 4 * 2 * rows * 2 * blocks * depth * outer * pairs * 3

    by_side = cotangent.reshape(rows, blocks, 2, depth, pairs)
    half_cotangent = shape(rows, blocks, depth, pairs)
    right, left, cotangent_send, cotangent_own, weight = call(
        prepare_kernel,
        [
            shape(channels * depth, sequences),
            shape(rows * channels, sequences),
            half_cotangent,
            half_cotangent,
            shape(outer, pairs),
        ],
        [
            pltpu.VMEM((2, rows, features), F32),
            pltpu.VMEM((2, rows * features // LANES, LANES), F32),
            pltpu.VMEM((2, rows // PACK, LANES, LANES), F32),
            pltpu.SemaphoreType.DMA((5,)),
        ],
        name="prepare",
        far=range(4),
    )(by_side, alignment_right, alignment_left, projection_matrix)
    cotangent_peer = lax.ppermute(cotangent_send, "blk", partner)
    left_peer = lax.ppermute(left, "blk", partner)

    vmem = pl.BlockSpec(memory_space=pltpu.VMEM)
    hbm = pl.BlockSpec(memory_space=pltpu.HBM)
    factor = shape(row_pairs, tall, 4 * lanes, kind=BF16)
    factor_scratch = pltpu.VMEM(factor.shape, BF16)
    weight_cat = shape(tall, 3 * fold * pairs, kind=BF16)
    flip_scratch = pltpu.VMEM((2 * sequences, rows * channels), BF16)
    flip_sizes = (2 * fold * pairs, tall)
    spread = shape(row_pairs, 2, 2 * lanes, fold * pairs, kind=BF16)
    grad_own, spread_own, partial, weight_cat, weight_flip = large(
        functools.partial(gradient_kernel, blocks),
        [
            factor,
            spread,
            shape(steps // 2, sequences, 2 * lanes),
            weight_cat,
            pltpu.HBM(flip_sizes, BF16),
        ],
        [
            flip_scratch,
            pltpu.VMEM((tall, fold * pairs), F32),
            pltpu.VMEM(flip_sizes, BF16),
            pltpu.SemaphoreType.DMA,
        ],
        "gradient_own",
        out_specs=[vmem, vmem, vmem, vmem, hbm],
    )(weight, cotangent_own, left)
    grad_peer, spread_peer = large(
        functools.partial(peer_kernel, blocks), [factor, spread], [], "gradient_peer"
    )(weight_cat, cotangent_peer)
    rights = {0: right}
    distance = blocks // 2
    while distance:
        for slot in list(rights):
            sent = rights[slot]
            if slot:
                sent, _ = lax.optimization_barrier((sent, grad_peer))
            rights[slot + distance] = lax.ppermute(sent, "blk", slot_moves[distance])
        distance = distance // 2
    rights = [rights[slot] for slot in range(blocks)]
    right_half = shape(blocks // 2, channels * depth, sequences)
    right_keep, right_send = large(
        functools.partial(right_kernel, blocks, depth),
        [right_half, right_half],
        [flip_scratch],
        "right_parts",
    )(grad_peer, left_peer, partial)
    right_send = lax.ppermute(right_send, "blk", slot_moves[blocks // 2])

    keep, send, outer_own, outer_peer = large(
        functools.partial(weight_kernel, blocks, depth),
        [shape(outer // 2, pairs)] * 2 + [pltpu.HBM(factor.shape, BF16)] * 2,
        [
            factor_scratch,
            factor_scratch,
            pltpu.VMEM((tall, fold * pairs), F32),
            pltpu.SemaphoreType.DMA((steps // 2, 2)),
        ],
        "weight",
        after=[right_keep],
        flops=2 * work,
        out_specs=[vmem, vmem, hbm, hbm],
    )(left, left_peer, spread_own, spread_peer, *rights)
    sent = lax.ppermute(send, "inner", cores)

    size = sequences // inner
    left_parts = large(
        functools.partial(left_kernel, blocks, depth),
        [shape(2, size, rows * channels)] * inner,
        [
            pltpu.VMEM((2 * rows * channels, sequences), F32),
            pltpu.VMEM((sequences, 2 * rows * channels), F32),
        ],
        "left_parts",
        after=[keep],
        flops=work,
    )(grad_own, grad_peer, *rights)
    keep, *left_parts = lax.optimization_barrier((keep, *left_parts))
    members = count * inner // 2
    pieces = (keep + sent).reshape(members, outer // 2 // members, pairs)

    def pair(values, after, name):
        return large(
            functools.partial(pair_kernel, blocks),
            shape(rows, blocks, depth, pairs),
            [
                factor_scratch,
                pltpu.VMEM(flip_sizes, BF16),
                pltpu.SemaphoreType.DMA((row_pairs + 1,)),
            ],
            name,
            far=[0, 1],
            after=after,
            flops=work,
        )(values, weight_flip)

    pieces, *left_parts = lax.optimization_barrier((pieces, *left_parts))
    left_parts = [
        lax.ppermute(part, "inner", inner_moves[slot]) if slot else part
        for slot, part in enumerate(left_parts)
    ]
    pair_other = pair(outer_peer, [pieces], "pair_peer")
    pair_found = lax.ppermute(pair_other, "blk", partner)
    slot = blocks // 4
    while slot:
        part = shape(slot, channels * depth, sequences)
        right_keep, right_send = call(
            halve_kernel, [part, part], name="right_halve", after=[pair_other]
        )(right_keep, right_send)
        right_send = lax.ppermute(right_send, "blk", slot_moves[slot])
        slot = slot // 2

    pieces = lax.all_to_all(pieces, everyone, 0, 0, axis_index_groups=core_groups)
    pieces = call(
        spread_sum_kernel,
        shape(*pieces.shape),
        name="weight_sum",
        after=[pair_other, right_keep],
    )(pieces)
    pair_own = pair(outer_own, [pieces], "pair_own")
    left_own, left_send = call(
        left_add_kernel, [shape(size, rows * channels)] * 2, name="left_add", after=[pieces]
    )(*left_parts)
    pieces = lax.all_to_all(pieces, everyone, 0, 0, axis_index_groups=core_groups)

    left_found = [left_own, lax.ppermute(left_send, "blk", partner)]
    pair_update, grad_left, grad_right = call(
        finish_kernel,
        [
            pltpu.HBM(by_side.shape, F32),
            shape(rows, features // inner),
            shape(depth, features),
        ],
        [
            pltpu.VMEM((channels * depth, sequences), F32),
            pltpu.VMEM((depth // PACK, LANES, LANES), F32),
            pltpu.VMEM((depth * features // LANES, LANES), F32),
            pltpu.VMEM((size * rows * channels // LANES, LANES), F32),
            pltpu.VMEM((rows * features // inner // LANES, LANES), F32),
            pltpu.SemaphoreType.DMA((2,)),
        ],
        "finish",
        out_specs=[hbm, vmem, vmem],
    )(pair_own, pair_found, right_keep, right_send, *left_found)
    pair_update = pair_update.reshape(cotangent.shape)

    pieces, pair_update, grad_left, grad_right = lax.optimization_barrier(
        (pieces, pair_update, grad_left, grad_right)
    )
    mine = pieces.reshape(outer // 2, pairs)
    other = lax.ppermute(mine, "inner", cores)
    grad_weight = call(place_kernel, shape(outer, pairs), name="place")(mine, other)
    return (pair_update, grad_left, grad_right, grad_weight)


def solution(mesh):
    placed = (
        P(("groups", "blk"), None),
        P(("groups", "blk", "inner"), None),
        P(),
        P(("groups", "blk"), None, "inner", None),
    )
    return jax.shard_map(
        local,
        mesh=mesh,
        in_specs=placed,
        out_specs=(
            P(("groups", "blk"), None, "inner", None),
            P(("groups", "blk"), "inner"),
            P(("groups", "blk", "inner"), None),
            P("groups", None),
        ),
        check_vma=False,
    )
```

```python
import functools

import jax
import jax.numpy as jnp
from jax import lax
from jax.experimental import pallas as pl
from jax.experimental.pallas import tpu as pltpu
from jax.sharding import PartitionSpec as P

ENTRY_CHANNELS = 32
LANES = 128
PACK = LANES // ENTRY_CHANNELS
F32 = jnp.float32
BF16 = jnp.bfloat16
MIB = 1024 * 1024


def halves(values):
    high = values.astype(BF16)
    low = (values - high.astype(F32)).astype(BF16)
    return high, low


def dot(left, right):
    return jnp.dot(left, right, preferred_element_type=F32)


def dot_rows(left, right):
    return lax.dot_general(left, right, (((1,), (1,)), ((), ())), preferred_element_type=F32)


def fold_of(columns):
    return max(1, LANES // columns)


def strided(start, size, stride):
    return pl.ds(start, size, stride=stride)


def folded_weight(weight_ref, step, fold):
    channels = ENTRY_CHANNELS
    return jnp.concatenate(
        [weight_ref[strided(step * fold + part, channels, channels), :] for part in range(fold)], 1
    )


def slots_of(blocks):
    here = lax.axis_index("blk") // 2
    return [lax.bitwise_xor(here, slot) for slot in range(blocks)]


def spread_of(cotangent_ref, pair, slots, fold):
    columns = len(slots) * cotangent_ref.shape[2]
    empty = jnp.zeros((columns, cotangent_ref.shape[3]), BF16)
    spread = ([], [])
    for part in range(2):
        rows = jnp.concatenate([cotangent_ref[2 * pair + part, slot] for slot in slots], 0)
        for found, values in zip(spread, halves(rows)):
            for place in range(fold):
                found.append(
                    jnp.concatenate(
                        [values if place == other else empty for other in range(fold)], 1
                    )
                )
    return [jnp.concatenate(found, 0) for found in spread]


def turn_in(rows_minor, in_ref, out_ref, tiles, square):
    channels = ENTRY_CHANNELS
    rows, features = in_ref.shape
    count = features // LANES
    for tile in range(count):
        tiles[tile * rows : (tile + 1) * rows, :] = in_ref[:, tile * LANES : (tile + 1) * LANES]
    for group in range(rows // PACK):
        found = [tiles[strided(group * PACK + k, count, rows), :] for k in range(PACK)]
        for part in range(PACK):
            lanes = slice(part * channels, (part + 1) * channels)
            square[group, strided(part, count, PACK), :] = jnp.concatenate(
                [values[:, lanes] for values in found], 1
            )
        turned = square[group].T
        if rows_minor:
            for k in range(PACK):
                out_ref[strided(group * PACK + k, channels, rows), :] = turned[
                    k * channels : (k + 1) * channels
                ]
        else:
            out_ref[group * LANES : (group + 1) * LANES, :] = turned


def prepare_kernel(
    cotangent_hbm,
    right_hbm,
    left_hbm,
    weight_hbm,
    right_out,
    left_out,
    send_out,
    own_out,
    weight_out,
    inputs,
    tiles,
    square,
    semaphores,
):
    parity = lax.rem(lax.axis_index("blk"), 2)
    moves = (
        (right_hbm, inputs.at[0]),
        (left_hbm, inputs.at[1]),
        (cotangent_hbm.at[:, :, 1 - parity], send_out),
        (cotangent_hbm.at[:, :, parity], own_out),
        (weight_hbm, weight_out),
    )
    copies = [
        pltpu.make_async_copy(source, target, semaphores.at[at])
        for at, (source, target) in enumerate(moves)
    ]
    for copy in copies:
        copy.start()
    copies[0].wait()
    turn_in(True, inputs.at[0], right_out, tiles.at[0], square.at[0])
    copies[1].wait()
    turn_in(False, inputs.at[1], left_out, tiles.at[1], square.at[1])
    for copy in copies[2:]:
        copy.wait()


def turn_right(part_refs, out_ref, total, square, tiles):
    channels = ENTRY_CHANNELS
    rows, features = out_ref.shape
    count = features // LANES
    total[...] = functools.reduce(jnp.add, [ref[0] for ref in part_refs])
    for group in range(rows // PACK):
        stacked = [total[strided(group * PACK + k, channels, rows), :] for k in range(PACK)]
        square[group] = jnp.concatenate(stacked, 0).T
        pieces = [square[group, strided(part, count, PACK), :] for part in range(PACK)]
        for k in range(PACK):
            lanes = slice(k * channels, (k + 1) * channels)
            tiles[strided(group * PACK + k, count, rows), :] = jnp.concatenate(
                [piece[:, lanes] for piece in pieces], 1
            )
    for tile in range(count):
        out_ref[:, tile * LANES : (tile + 1) * LANES] = tiles[tile * rows : (tile + 1) * rows, :]


def turn_left(part_refs, out_ref, total, tiles):
    channels = ENTRY_CHANNELS
    size, width = part_refs[0].shape
    rows, features = out_ref.shape
    count = features // LANES
    found = functools.reduce(jnp.add, [ref[...] for ref in part_refs])
    for tile in range(width // LANES):
        total[tile * size : (tile + 1) * size, :] = found[:, tile * LANES : (tile + 1) * LANES]
    for tile in range(width // LANES):
        pieces = [total[strided(tile * size + part, count, PACK), :] for part in range(PACK)]
        for k in range(PACK):
            lanes = slice(k * channels, (k + 1) * channels)
            tiles[strided(tile * PACK + k, count, rows), :] = jnp.concatenate(
                [piece[:, lanes] for piece in pieces], 1
            )
    for tile in range(count):
        out_ref[:, tile * LANES : (tile + 1) * LANES] = tiles[tile * rows : (tile + 1) * rows, :]


def prepare_weight(weight_ref, weight_cat, fold):
    channels = ENTRY_CHANNELS
    for step in range(channels // fold):
        high, low = halves(folded_weight(weight_ref, step, fold))
        weight_cat[step * channels : (step + 1) * channels, :] = jnp.concatenate(
            [high, low, high], 1
        )


def gradient_phase(blocks, cotangent_ref, out_ref, spread_ref, weight_cat):
    fold = fold_of(blocks * cotangent_ref.shape[2])
    slots = slots_of(blocks)

    def step_of(pair, carry):
        high, low = spread_of(cotangent_ref, pair, slots, fold)
        spread_ref[pair, 0] = high
        spread_ref[pair, 1] = low
        found = dot_rows(weight_cat[...], jnp.concatenate([high, high, low], 1))
        out_ref[pair] = jnp.concatenate(halves(found), 1)
        return carry

    lax.fori_loop(0, out_ref.shape[0], step_of, 0, unroll=8)


def gradient_kernel(
    blocks,
    weight_ref,
    cotangent_ref,
    left_ref,
    out_ref,
    spread_ref,
    partial_ref,
    weight_cat,
    flip_hbm,
    left_flip,
    weight_rows,
    weight_flip,
    semaphore,
):
    fold = fold_of(blocks * cotangent_ref.shape[2])
    prepare_weight(weight_ref, weight_cat, fold)
    gradient_phase(blocks, cotangent_ref, out_ref, spread_ref, weight_cat)

    def store(step, found):
        partial_ref[step] = found

    right_phase(left_ref, out_ref, left_flip, store, 8)
    channels = ENTRY_CHANNELS
    wide = weight_rows.shape[1]
    for step in range(channels // fold):
        weight_rows[step * channels : (step + 1) * channels, :] = folded_weight(
            weight_ref, step, fold
        )
    flip_high, flip_low = halves(weight_rows[...].T)
    weight_flip[:wide, :] = flip_high
    weight_flip[wide:, :] = flip_low
    copy = pltpu.make_async_copy(weight_flip, flip_hbm, semaphore)
    copy.start()
    copy.wait()


def peer_kernel(blocks, weight_cat, cotangent_ref, out_ref, spread_ref):
    gradient_phase(blocks, cotangent_ref, out_ref, spread_ref, weight_cat)


def right_phase(left_ref, factor_ref, left_flip, store, unroll):
    sequences = left_ref.shape[1]
    lanes = factor_ref.shape[2] // 4
    flip_high, flip_low = halves((left_ref[...] * (1.0 / sequences)).T)
    left_flip[:sequences, :] = flip_high
    left_flip[sequences:, :] = flip_low

    def step_of(step, carry):
        high, low = (
            jnp.concatenate(
                [rows_of_step([factor_ref], 2 * step + part, half, lanes) for part in range(2)], 1
            )
            for half in range(2)
        )
        first = dot(left_flip[...], high)
        second = dot(left_flip[:sequences, :], low)
        store(step, first[:sequences] + first[sequences:] + second)
        return carry

    count = factor_ref.shape[1] // (2 * ENTRY_CHANNELS)
    lax.fori_loop(0, count, step_of, 0, unroll=unroll)


def rows_of_step(refs, step, half, lanes):
    channels = ENTRY_CHANNELS
    rows = pl.ds(pl.multiple_of(step * channels, channels), channels)
    start = 2 * half * lanes
    return jnp.concatenate(
        [
            ref[pair, rows, start + part * lanes : start + (part + 1) * lanes]
            for ref in refs
            for pair in range(ref.shape[0])
            for part in range(2)
        ],
        0,
    )


def both_left(left_refs):
    sequences = left_refs[0].shape[1]
    return jnp.concatenate([ref[...] for ref in left_refs], 0) * (1.0 / sequences)


def right_kernel(
    blocks, depth, peer_ref, left_ref, partial_ref, keep_ref, send_ref, left_flip
):
    fold = fold_of(blocks * depth)
    lanes = fold * blocks * depth

    def store(step, found):
        found = found + partial_ref[step]
        for part in range(2):
            turned = found[:, part * lanes : (part + 1) * lanes].T
            for place in range(fold):
                for slot in range(blocks):
                    start = (place * blocks + slot) * depth
                    row = pl.multiple_of(((2 * step + part) * fold + place) * depth, depth)
                    out_ref = keep_ref if slot < blocks // 2 else send_ref
                    out_ref[slot % (blocks // 2), pl.ds(row, depth), :] = turned[
                        start : start + depth
                    ]

    right_phase(left_ref, peer_ref, left_flip, store, 4)


def halve_kernel(keep_ref, found_ref, keep_out, send_out):
    half = keep_ref.shape[0] // 2
    for slot in range(half):
        keep_out[slot] = keep_ref[slot] + found_ref[slot]
        send_out[slot] = keep_ref[half + slot] + found_ref[half + slot]


def right_rows(right_refs, step, fold, depth):
    return jnp.concatenate(
        [
            ref[pl.ds(pl.multiple_of((step * fold + part) * depth, depth), depth), :]
            for part in range(fold)
            for ref in right_refs
        ],
        0,
    )


def weight_kernel(blocks, depth, own_left, peer_left, own_spread, peer_spread, *refs):
    right_refs = refs[:blocks]
    keep_ref, send_ref, own_out, peer_out, own_ref, peer_ref, total, semaphores = refs[blocks:]
    channels = ENTRY_CHANNELS
    fold = fold_of(blocks * depth)
    lanes = fold * blocks * depth
    pairs = total.shape[1] // fold
    high, low = halves(both_left([own_left, peer_left]))
    left_cat = jnp.concatenate([high, low, high], 1)

    def copies(step):
        size = 2 * channels
        rows = pl.ds(pl.multiple_of(step * size, size), size)
        return [
            pltpu.make_async_copy(ref.at[:, rows], out.at[:, rows], semaphores.at[step, side])
            for side, (ref, out) in enumerate(((own_ref, own_out), (peer_ref, peer_out)))
        ]

    def outer_step(step, carry):
        right = [right_rows(right_refs, 2 * step + part, fold, depth) for part in range(2)]
        high, low = halves(jnp.concatenate(right, 0))
        found = dot_rows(left_cat, jnp.concatenate([high, high, low], 1))
        both = halves(found)
        for part in range(2):
            start = pl.multiple_of((2 * step + part) * channels, channels)
            row = 0
            for ref in (own_ref, peer_ref):
                for index in range(2 * ref.shape[0]):
                    for half in range(2):
                        lane = (2 * half + index % 2) * lanes
                        ref[index // 2, pl.ds(start, channels), lane : lane + lanes] = both[half][
                            row : row + channels, part * lanes : (part + 1) * lanes
                        ]
                    row += channels
        for copy in copies(step):
            copy.start()
        return carry

    lax.fori_loop(0, channels // (2 * fold), outer_step, 0, unroll=4)
    total[...] = jnp.zeros_like(total)

    def weight_step(pair, carry):
        lefts, rights = [], []
        for ref, spread_ref in ((own_ref, own_spread), (peer_ref, peer_spread)):
            high = spread_ref[pair, 0]
            lefts += [ref[pair], ref[pair, :, : 2 * lanes]]
            rights += [high, high, spread_ref[pair, 1]]
        total[...] += dot(jnp.concatenate(lefts, 1), jnp.concatenate(rights, 0))
        return carry

    lax.fori_loop(0, own_ref.shape[0], weight_step, 0, unroll=4)
    core = lax.rem(lax.axis_index("inner"), 2)
    steps = channels // (2 * fold)
    for out_ref, half in ((keep_ref, core), (send_ref, 1 - core)):
        for step in range(steps):
            start = pl.multiple_of((half * steps + step) * channels, channels)
            found = total[pl.ds(start, channels), :]
            for part in range(fold):
                y = step * fold + part
                out_ref[y * channels : (y + 1) * channels, :] = found[
                    :, part * pairs : (part + 1) * pairs
                ]

    def finish(step, carry):
        for copy in copies(step):
            copy.wait()
        return carry

    lax.fori_loop(0, channels // (2 * fold), finish, 0)


def left_kernel(blocks, depth, own_ref, peer_ref, *refs):
    right_refs, out_refs, (total, flipped) = refs[:blocks], refs[blocks:-2], refs[-2:]
    lanes = own_ref.shape[2] // 4
    fold = lanes // (blocks * depth)
    sequences = right_refs[0].shape[1]
    group = 4
    total[...] = jnp.zeros_like(total)

    def step_of(step, carry):
        steps = [group * step + part for part in range(group)]
        right = [right_rows(right_refs, at, fold, depth) for at in steps]
        high, low = halves(jnp.concatenate(right, 0))
        grads = [
            jnp.concatenate([rows_of_step([own_ref, peer_ref], at, half, lanes) for at in steps], 1)
            for half in range(2)
        ]
        both = dot(grads[0], jnp.concatenate([high, low], 1))
        total[...] += both[:, :sequences] + both[:, sequences:] + dot(grads[1], high)
        return carry

    lax.fori_loop(0, ENTRY_CHANNELS // (fold * group), step_of, 0, unroll=4)
    flipped[...] = total[...].T * (1.0 / sequences)
    here = lax.axis_index("inner")
    size, width = out_refs[0].shape[1:]
    for slot, ref in enumerate(out_refs):
        start = pl.multiple_of(lax.bitwise_xor(here, slot) * size, size)
        for side in range(2):
            ref[side] = flipped[pl.ds(start, size), side * width : (side + 1) * width]


def left_add_kernel(*refs):
    parts, (own_out, send_out) = refs[:-2], refs[-2:]
    for side, ref in enumerate((own_out, send_out)):
        ref[...] = functools.reduce(jnp.add, [part[side] for part in parts])


def pair_kernel(blocks, outer_hbm, flip_hbm, out_ref, outer_ref, weight_flip, semaphores):
    depth, pairs = out_ref.shape[2:]
    count = outer_ref.shape[0]
    lanes = outer_ref.shape[2] // 4
    columns = blocks * depth
    fold = lanes // columns
    wide = fold * pairs

    def copy_of(pair):
        return pltpu.make_async_copy(outer_hbm.at[pair], outer_ref.at[pair], semaphores.at[pair])

    flip_copy = pltpu.make_async_copy(flip_hbm, weight_flip, semaphores.at[count])
    flip_copy.start()
    for pair in range(count):
        copy_of(pair).start()
    flip_copy.wait()
    slots = slots_of(blocks)

    def step_of(pair, carry):
        copy_of(pair).wait()
        first = dot(weight_flip[...], outer_ref[pair, :, : 2 * lanes])
        second = dot(weight_flip[:wide, :], outer_ref[pair, :, 2 * lanes :])
        found = first[:wide] + first[wide:] + second
        for part in range(2):
            turned = []
            for place in range(fold):
                start = part * lanes
                piece = found[place * pairs : (place + 1) * pairs, start : start + lanes].T
                turned.append(piece[place * columns : (place + 1) * columns])
            turned = functools.reduce(jnp.add, turned)
            row = 2 * pair + part
            for slot in range(blocks):
                out_ref[row, slots[slot]] = turned[slot * depth : (slot + 1) * depth]
        return carry

    lax.fori_loop(0, count, step_of, 0)


def finish_kernel(own_ref, other_ref, keep_ref, found_ref, *refs):
    left_refs, refs = refs[:-9], refs[-9:]
    pair_hbm, left_out, right_out = refs[:3]
    right_total, right_square, right_tiles, left_total, left_tiles, semaphores = refs[3:]
    parity = lax.rem(lax.axis_index("blk"), 2)
    copies = [
        pltpu.make_async_copy(ref, pair_hbm.at[:, :, side], semaphores.at[at])
        for at, (ref, side) in enumerate(((own_ref, parity), (other_ref, 1 - parity)))
    ]
    for copy in copies:
        copy.start()
    turn_right([keep_ref, found_ref], right_out, right_total, right_square, right_tiles)
    turn_left(left_refs, left_out, left_total, left_tiles)
    for copy in copies:
        copy.wait()


def spread_sum_kernel(in_ref, out_ref):
    found = in_ref[0]
    for part in range(1, in_ref.shape[0]):
        found = found + in_ref[part]
    for part in range(in_ref.shape[0]):
        out_ref[part] = found


def place_kernel(mine_ref, other_ref, out_ref):
    channels = ENTRY_CHANNELS
    core = lax.rem(lax.axis_index("inner"), 2)
    steps = mine_ref.shape[0] // channels
    for ref, half in ((mine_ref, core), (other_ref, 1 - core)):
        for step in range(steps):
            rows = ref[step * channels : (step + 1) * channels, :]
            out_ref[strided(half * steps + step, channels, channels), :] = rows


def shape(*sizes, kind=F32):
    return jax.ShapeDtypeStruct(sizes, kind)


def call(
    kernel,
    out_shape,
    scratch=(),
    name=None,
    limit=16 * MIB,
    far=(),
    after=(),
    out_specs=None,
    flops=1,
):
    def run(*operands):
        vmem = pl.BlockSpec(memory_space=pltpu.VMEM)
        hbm = pl.BlockSpec(memory_space=pltpu.HBM)
        in_specs = [pl.BlockSpec(memory_space=pl.ANY)] * len(after)
        in_specs += [hbm if at in far else vmem for at in range(len(operands))]
        operands = [
            pltpu.with_memory_space_constraint(operand, pltpu.HBM) if at in far else operand
            for at, operand in enumerate(operands)
        ]
        extra = {} if out_specs is None else {"out_specs": out_specs}
        return pl.pallas_call(
            lambda *refs: kernel(*refs[len(after) :]),
            out_shape=out_shape,
            in_specs=in_specs,
            scratch_shapes=list(scratch),
            compiler_params=pltpu.CompilerParams(vmem_limit_bytes=limit),
            cost_estimate=pl.CostEstimate(flops=flops, bytes_accessed=1, transcendentals=0),
            name=name,
            **extra,
        )(*after, *operands)

    return run


def local(alignment_left, alignment_right, projection_matrix, cotangent):
    rows, features = alignment_left.shape
    depth = alignment_right.shape[0]
    count = lax.axis_size("blk")
    inner = lax.axis_size("inner")
    channels = ENTRY_CHANNELS
    sequences = features // channels
    outer, pairs = projection_matrix.shape
    blocks = count // 2
    fold = fold_of(blocks * depth)
    lanes = fold * blocks * depth
    tall = outer // fold
    steps = channels // fold
    row_pairs = rows // 2
    everyone = ("blk", "inner")

    partner = [(here, here ^ 1) for here in range(count)]
    slot_moves = [[(here, here ^ (2 * slot)) for here in range(count)] for slot in range(blocks)]
    inner_moves = [[(here, here ^ slot) for here in range(inner)] for slot in range(inner)]
    cores = [(here, here ^ 1) for here in range(inner)]
    core_groups = [list(range(core, count * inner, 2)) for core in range(2)]

    limit = 20 * MIB * max(1, blocks * depth * fold // LANES * 2 // fold)
    large = functools.partial(call, limit=limit)
    work = 4 * 2 * rows * 2 * blocks * depth * outer * pairs * 3

    by_side = cotangent.reshape(rows, blocks, 2, depth, pairs)
    half_cotangent = shape(rows, blocks, depth, pairs)
    right, left, cotangent_send, cotangent_own, weight = call(
        prepare_kernel,
        [
            shape(channels * depth, sequences),
            shape(rows * channels, sequences),
            half_cotangent,
            half_cotangent,
            shape(outer, pairs),
        ],
        [
            pltpu.VMEM((2, rows, features), F32),
            pltpu.VMEM((2, rows * features // LANES, LANES), F32),
            pltpu.VMEM((2, rows // PACK, LANES, LANES), F32),
            pltpu.SemaphoreType.DMA((5,)),
        ],
        name="prepare",
        far=range(4),
    )(by_side, alignment_right, alignment_left, projection_matrix)
    cotangent_peer = lax.ppermute(cotangent_send, "blk", partner)
    left_peer = lax.ppermute(left, "blk", partner)

    vmem = pl.BlockSpec(memory_space=pltpu.VMEM)
    hbm = pl.BlockSpec(memory_space=pltpu.HBM)
    factor = shape(row_pairs, tall, 4 * lanes, kind=BF16)
    factor_scratch = pltpu.VMEM(factor.shape, BF16)
    weight_cat = shape(tall, 3 * fold * pairs, kind=BF16)
    flip_scratch = pltpu.VMEM((2 * sequences, rows * channels), BF16)
    flip_sizes = (2 * fold * pairs, tall)
    spread = shape(row_pairs, 2, 2 * lanes, fold * pairs, kind=BF16)
    grad_own, spread_own, partial, weight_cat, weight_flip = large(
        functools.partial(gradient_kernel, blocks),
        [
            factor,
            spread,
            shape(steps // 2, sequences, 2 * lanes),
            weight_cat,
            pltpu.HBM(flip_sizes, BF16),
        ],
        [
            flip_scratch,
            pltpu.VMEM((tall, fold * pairs), F32),
            pltpu.VMEM(flip_sizes, BF16),
            pltpu.SemaphoreType.DMA,
        ],
        "gradient_own",
        out_specs=[vmem, vmem, vmem, vmem, hbm],
    )(weight, cotangent_own, left)
    grad_peer, spread_peer = large(
        functools.partial(peer_kernel, blocks), [factor, spread], [], "gradient_peer"
    )(weight_cat, cotangent_peer)
    rights = {0: right}
    distance = blocks // 2
    while distance:
        for slot in list(rights):
            sent = rights[slot]
            if slot:
                sent, _ = lax.optimization_barrier((sent, grad_peer))
            rights[slot + distance] = lax.ppermute(sent, "blk", slot_moves[distance])
        distance = distance // 2
    rights = [rights[slot] for slot in range(blocks)]
    right_half = shape(blocks // 2, channels * depth, sequences)
    right_keep, right_send = large(
        functools.partial(right_kernel, blocks, depth),
        [right_half, right_half],
        [flip_scratch],
        "right_parts",
    )(grad_peer, left_peer, partial)
    right_send = lax.ppermute(right_send, "blk", slot_moves[blocks // 2])

    keep, send, outer_own, outer_peer = large(
        functools.partial(weight_kernel, blocks, depth),
        [shape(outer // 2, pairs)] * 2 + [pltpu.HBM(factor.shape, BF16)] * 2,
        [
            factor_scratch,
            factor_scratch,
            pltpu.VMEM((tall, fold * pairs), F32),
            pltpu.SemaphoreType.DMA((steps // 2, 2)),
        ],
        "weight",
        after=[right_keep],
        flops=2 * work,
        out_specs=[vmem, vmem, hbm, hbm],
    )(left, left_peer, spread_own, spread_peer, *rights)
    sent = lax.ppermute(send, "inner", cores)

    size = sequences // inner
    left_parts = large(
        functools.partial(left_kernel, blocks, depth),
        [shape(2, size, rows * channels)] * inner,
        [
            pltpu.VMEM((2 * rows * channels, sequences), F32),
            pltpu.VMEM((sequences, 2 * rows * channels), F32),
        ],
        "left_parts",
        after=[keep],
        flops=work,
    )(grad_own, grad_peer, *rights)
    keep, *left_parts = lax.optimization_barrier((keep, *left_parts))
    members = count * inner // 2
    pieces = (keep + sent).reshape(members, outer // 2 // members, pairs)

    def pair(values, after, name):
        return large(
            functools.partial(pair_kernel, blocks),
            shape(rows, blocks, depth, pairs),
            [
                factor_scratch,
                pltpu.VMEM(flip_sizes, BF16),
                pltpu.SemaphoreType.DMA((row_pairs + 1,)),
            ],
            name,
            far=[0, 1],
            after=after,
            flops=work,
        )(values, weight_flip)

    pair_other = pair(outer_peer, [pieces], "pair_peer")
    pair_found = lax.ppermute(pair_other, "blk", partner)
    _, *left_parts = lax.optimization_barrier((pair_other, *left_parts))
    left_parts = [
        lax.ppermute(part, "inner", inner_moves[slot]) if slot else part
        for slot, part in enumerate(left_parts)
    ]
    slot = blocks // 4
    while slot:
        part = shape(slot, channels * depth, sequences)
        right_keep, right_send = call(
            halve_kernel, [part, part], name="right_halve", after=[pair_other]
        )(right_keep, right_send)
        right_send = lax.ppermute(right_send, "blk", slot_moves[slot])
        slot = slot // 2

    pieces = lax.all_to_all(pieces, everyone, 0, 0, axis_index_groups=core_groups)
    pieces = call(
        spread_sum_kernel,
        shape(*pieces.shape),
        name="weight_sum",
        after=[pair_other, right_keep],
    )(pieces)
    pair_own = pair(outer_own, [pieces], "pair_own")
    left_own, left_send = call(
        left_add_kernel, [shape(size, rows * channels)] * 2, name="left_add", after=[pieces]
    )(*left_parts)
    pieces = lax.all_to_all(pieces, everyone, 0, 0, axis_index_groups=core_groups)

    left_found = [left_own, lax.ppermute(left_send, "blk", partner)]
    pair_update, grad_left, grad_right = call(
        finish_kernel,
        [
            pltpu.HBM(by_side.shape, F32),
            shape(rows, features // inner),
            shape(depth, features),
        ],
        [
            pltpu.VMEM((channels * depth, sequences), F32),
            pltpu.VMEM((depth // PACK, LANES, LANES), F32),
            pltpu.VMEM((depth * features // LANES, LANES), F32),
            pltpu.VMEM((size * rows * channels // LANES, LANES), F32),
            pltpu.VMEM((rows * features // inner // LANES, LANES), F32),
            pltpu.SemaphoreType.DMA((2,)),
        ],
        "finish",
        out_specs=[hbm, vmem, vmem],
    )(pair_own, pair_found, right_keep, right_send, *left_found)
    pair_update = pair_update.reshape(cotangent.shape)

    pieces, pair_update, grad_left, grad_right = lax.optimization_barrier(
        (pieces, pair_update, grad_left, grad_right)
    )
    mine = pieces.reshape(outer // 2, pairs)
    other = lax.ppermute(mine, "inner", cores)
    grad_weight = call(place_kernel, shape(outer, pairs), name="place")(mine, other)
    return (pair_update, grad_left, grad_right, grad_weight)


def solution(mesh):
    placed = (
        P(("groups", "blk"), None),
        P(("groups", "blk", "inner"), None),
        P(),
        P(("groups", "blk"), None, "inner", None),
    )
    return jax.shard_map(
        local,
        mesh=mesh,
        in_specs=placed,
        out_specs=(
            P(("groups", "blk"), None, "inner", None),
            P(("groups", "blk"), "inner"),
            P(("groups", "blk", "inner"), None),
            P("groups", None),
        ),
        check_vma=False,
    )
```

```python
import functools

import jax
import jax.numpy as jnp
from jax import lax
from jax.experimental import pallas as pl
from jax.experimental.pallas import tpu as pltpu
from jax.sharding import PartitionSpec as P

ENTRY_CHANNELS = 32
LANES = 128
PACK = LANES // ENTRY_CHANNELS
F32 = jnp.float32
BF16 = jnp.bfloat16
MIB = 1024 * 1024


def halves(values):
    high = values.astype(BF16)
    low = (values - high.astype(F32)).astype(BF16)
    return high, low


def dot(left, right):
    return jnp.dot(left, right, preferred_element_type=F32)


def dot_rows(left, right):
    return lax.dot_general(left, right, (((1,), (1,)), ((), ())), preferred_element_type=F32)


def fold_of(columns):
    return max(1, LANES // columns)


def strided(start, size, stride):
    return pl.ds(start, size, stride=stride)


def folded_weight(weight_ref, step, fold):
    channels = ENTRY_CHANNELS
    return jnp.concatenate(
        [weight_ref[strided(step * fold + part, channels, channels), :] for part in range(fold)], 1
    )


def slots_of(blocks):
    here = lax.axis_index("blk") // 2
    return [lax.bitwise_xor(here, slot) for slot in range(blocks)]


def spread_of(cotangent_ref, pair, slots, fold):
    columns = len(slots) * cotangent_ref.shape[2]
    empty = jnp.zeros((columns, cotangent_ref.shape[3]), BF16)
    spread = ([], [])
    for part in range(2):
        rows = jnp.concatenate([cotangent_ref[2 * pair + part, slot] for slot in slots], 0)
        for found, values in zip(spread, halves(rows)):
            for place in range(fold):
                found.append(
                    jnp.concatenate(
                        [values if place == other else empty for other in range(fold)], 1
                    )
                )
    return [jnp.concatenate(found, 0) for found in spread]


def turn_in(rows_minor, in_ref, out_ref, tiles, square):
    channels = ENTRY_CHANNELS
    rows, features = in_ref.shape
    count = features // LANES
    for tile in range(count):
        tiles[tile * rows : (tile + 1) * rows, :] = in_ref[:, tile * LANES : (tile + 1) * LANES]
    for group in range(rows // PACK):
        found = [tiles[strided(group * PACK + k, count, rows), :] for k in range(PACK)]
        for part in range(PACK):
            lanes = slice(part * channels, (part + 1) * channels)
            square[group, strided(part, count, PACK), :] = jnp.concatenate(
                [values[:, lanes] for values in found], 1
            )
        turned = square[group].T
        if rows_minor:
            for k in range(PACK):
                out_ref[strided(group * PACK + k, channels, rows), :] = turned[
                    k * channels : (k + 1) * channels
                ]
        else:
            out_ref[group * LANES : (group + 1) * LANES, :] = turned


def prepare_kernel(
    cotangent_hbm,
    right_hbm,
    left_hbm,
    weight_hbm,
    right_out,
    left_out,
    send_out,
    own_out,
    weight_out,
    inputs,
    tiles,
    square,
    semaphores,
):
    parity = lax.rem(lax.axis_index("blk"), 2)
    moves = (
        (right_hbm, inputs.at[0]),
        (left_hbm, inputs.at[1]),
        (cotangent_hbm.at[:, :, 1 - parity], send_out),
        (cotangent_hbm.at[:, :, parity], own_out),
        (weight_hbm, weight_out),
    )
    copies = [
        pltpu.make_async_copy(source, target, semaphores.at[at])
        for at, (source, target) in enumerate(moves)
    ]
    for copy in copies:
        copy.start()
    copies[0].wait()
    turn_in(True, inputs.at[0], right_out, tiles.at[0], square.at[0])
    copies[1].wait()
    turn_in(False, inputs.at[1], left_out, tiles.at[1], square.at[1])
    for copy in copies[2:]:
        copy.wait()


def turn_right(part_refs, out_ref, total, square, tiles):
    channels = ENTRY_CHANNELS
    rows, features = out_ref.shape
    count = features // LANES
    total[...] = functools.reduce(jnp.add, [ref[0] for ref in part_refs])
    for group in range(rows // PACK):
        stacked = [total[strided(group * PACK + k, channels, rows), :] for k in range(PACK)]
        square[group] = jnp.concatenate(stacked, 0).T
        pieces = [square[group, strided(part, count, PACK), :] for part in range(PACK)]
        for k in range(PACK):
            lanes = slice(k * channels, (k + 1) * channels)
            tiles[strided(group * PACK + k, count, rows), :] = jnp.concatenate(
                [piece[:, lanes] for piece in pieces], 1
            )
    for tile in range(count):
        out_ref[:, tile * LANES : (tile + 1) * LANES] = tiles[tile * rows : (tile + 1) * rows, :]


def turn_left(part_refs, out_ref, total, tiles):
    channels = ENTRY_CHANNELS
    size, width = part_refs[0].shape
    rows, features = out_ref.shape
    count = features // LANES
    found = functools.reduce(jnp.add, [ref[...] for ref in part_refs])
    for tile in range(width // LANES):
        total[tile * size : (tile + 1) * size, :] = found[:, tile * LANES : (tile + 1) * LANES]
    for tile in range(width // LANES):
        pieces = [total[strided(tile * size + part, count, PACK), :] for part in range(PACK)]
        for k in range(PACK):
            lanes = slice(k * channels, (k + 1) * channels)
            tiles[strided(tile * PACK + k, count, rows), :] = jnp.concatenate(
                [piece[:, lanes] for piece in pieces], 1
            )
    for tile in range(count):
        out_ref[:, tile * LANES : (tile + 1) * LANES] = tiles[tile * rows : (tile + 1) * rows, :]


def prepare_weight(weight_ref, weight_cat, fold):
    channels = ENTRY_CHANNELS
    for step in range(channels // fold):
        high, low = halves(folded_weight(weight_ref, step, fold))
        weight_cat[step * channels : (step + 1) * channels, :] = jnp.concatenate(
            [high, low, high], 1
        )


def gradient_phase(blocks, cotangent_ref, out_ref, spread_ref, weight_cat):
    fold = fold_of(blocks * cotangent_ref.shape[2])
    slots = slots_of(blocks)

    def step_of(pair, carry):
        high, low = spread_of(cotangent_ref, pair, slots, fold)
        spread_ref[pair, 0] = high
        spread_ref[pair, 1] = low
        found = dot_rows(weight_cat[...], jnp.concatenate([high, high, low], 1))
        out_ref[pair] = jnp.concatenate(halves(found), 1)
        return carry

    lax.fori_loop(0, out_ref.shape[0], step_of, 0, unroll=8)


def gradient_kernel(
    blocks,
    weight_ref,
    cotangent_ref,
    left_ref,
    out_ref,
    spread_ref,
    partial_ref,
    weight_cat,
    flip_hbm,
    left_flip,
    weight_rows,
    weight_flip,
    semaphore,
):
    fold = fold_of(blocks * cotangent_ref.shape[2])
    prepare_weight(weight_ref, weight_cat, fold)
    gradient_phase(blocks, cotangent_ref, out_ref, spread_ref, weight_cat)

    def store(step, found):
        partial_ref[step] = found

    right_phase(left_ref, out_ref, left_flip, store, 8)
    channels = ENTRY_CHANNELS
    wide = weight_rows.shape[1]
    for step in range(channels // fold):
        weight_rows[step * channels : (step + 1) * channels, :] = folded_weight(
            weight_ref, step, fold
        )
    flip_high, flip_low = halves(weight_rows[...].T)
    weight_flip[:wide, :] = flip_high
    weight_flip[wide:, :] = flip_low
    copy = pltpu.make_async_copy(weight_flip, flip_hbm, semaphore)
    copy.start()
    copy.wait()


def peer_kernel(blocks, weight_cat, cotangent_ref, out_ref, spread_ref):
    gradient_phase(blocks, cotangent_ref, out_ref, spread_ref, weight_cat)


def right_phase(left_ref, factor_ref, left_flip, store, unroll):
    sequences = left_ref.shape[1]
    lanes = factor_ref.shape[2] // 4
    flip_high, flip_low = halves((left_ref[...] * (1.0 / sequences)).T)
    left_flip[:sequences, :] = flip_high
    left_flip[sequences:, :] = flip_low

    def step_of(step, carry):
        high, low = (
            jnp.concatenate(
                [rows_of_step([factor_ref], 2 * step + part, half, lanes) for part in range(2)], 1
            )
            for half in range(2)
        )
        first = dot(left_flip[...], high)
        second = dot(left_flip[:sequences, :], low)
        store(step, first[:sequences] + first[sequences:] + second)
        return carry

    count = factor_ref.shape[1] // (2 * ENTRY_CHANNELS)
    lax.fori_loop(0, count, step_of, 0, unroll=unroll)


def rows_of_step(refs, step, half, lanes):
    channels = ENTRY_CHANNELS
    rows = pl.ds(pl.multiple_of(step * channels, channels), channels)
    start = 2 * half * lanes
    return jnp.concatenate(
        [
            ref[pair, rows, start + part * lanes : start + (part + 1) * lanes]
            for ref in refs
            for pair in range(ref.shape[0])
            for part in range(2)
        ],
        0,
    )


def both_left(left_refs):
    sequences = left_refs[0].shape[1]
    return jnp.concatenate([ref[...] for ref in left_refs], 0) * (1.0 / sequences)


def right_kernel(
    blocks, depth, peer_ref, left_ref, partial_ref, keep_ref, send_ref, left_flip
):
    fold = fold_of(blocks * depth)
    lanes = fold * blocks * depth

    def store(step, found):
        found = found + partial_ref[step]
        for part in range(2):
            turned = found[:, part * lanes : (part + 1) * lanes].T
            for place in range(fold):
                for slot in range(blocks):
                    start = (place * blocks + slot) * depth
                    row = pl.multiple_of(((2 * step + part) * fold + place) * depth, depth)
                    out_ref = send_ref if slot % 2 else keep_ref
                    out_ref[slot // 2, pl.ds(row, depth), :] = turned[start : start + depth]

    right_phase(left_ref, peer_ref, left_flip, store, 4)


def halve_kernel(keep_ref, found_ref, keep_out, send_out):
    for slot in range(keep_ref.shape[0]):
        out_ref = send_out if slot % 2 else keep_out
        out_ref[slot // 2] = keep_ref[slot] + found_ref[slot]


def right_rows(right_refs, step, fold, depth):
    return jnp.concatenate(
        [
            ref[pl.ds(pl.multiple_of((step * fold + part) * depth, depth), depth), :]
            for part in range(fold)
            for ref in right_refs
        ],
        0,
    )


def weight_kernel(blocks, depth, own_left, peer_left, own_spread, peer_spread, *refs):
    right_refs = refs[:blocks]
    keep_ref, send_ref, own_out, peer_out, own_ref, peer_ref, total, semaphores = refs[blocks:]
    channels = ENTRY_CHANNELS
    fold = fold_of(blocks * depth)
    lanes = fold * blocks * depth
    pairs = total.shape[1] // fold
    high, low = halves(both_left([own_left, peer_left]))
    left_cat = jnp.concatenate([high, low, high], 1)

    def copies(step):
        size = 2 * channels
        rows = pl.ds(pl.multiple_of(step * size, size), size)
        return [
            pltpu.make_async_copy(ref.at[:, rows], out.at[:, rows], semaphores.at[step, side])
            for side, (ref, out) in enumerate(((own_ref, own_out), (peer_ref, peer_out)))
        ]

    def outer_step(step, carry):
        right = [right_rows(right_refs, 2 * step + part, fold, depth) for part in range(2)]
        high, low = halves(jnp.concatenate(right, 0))
        found = dot_rows(left_cat, jnp.concatenate([high, high, low], 1))
        both = halves(found)
        for part in range(2):
            start = pl.multiple_of((2 * step + part) * channels, channels)
            row = 0
            for ref in (own_ref, peer_ref):
                for index in range(2 * ref.shape[0]):
                    for half in range(2):
                        lane = (2 * half + index % 2) * lanes
                        ref[index // 2, pl.ds(start, channels), lane : lane + lanes] = both[half][
                            row : row + channels, part * lanes : (part + 1) * lanes
                        ]
                    row += channels
        for copy in copies(step):
            copy.start()
        return carry

    lax.fori_loop(0, channels // (2 * fold), outer_step, 0, unroll=4)
    total[...] = jnp.zeros_like(total)

    def weight_step(pair, carry):
        lefts, rights = [], []
        for ref, spread_ref in ((own_ref, own_spread), (peer_ref, peer_spread)):
            high = spread_ref[pair, 0]
            lefts += [ref[pair], ref[pair, :, : 2 * lanes]]
            rights += [high, high, spread_ref[pair, 1]]
        total[...] += dot(jnp.concatenate(lefts, 1), jnp.concatenate(rights, 0))
        return carry

    lax.fori_loop(0, own_ref.shape[0], weight_step, 0, unroll=4)
    core = lax.rem(lax.axis_index("inner"), 2)
    steps = channels // (2 * fold)
    for out_ref, half in ((keep_ref, core), (send_ref, 1 - core)):
        for step in range(steps):
            start = pl.multiple_of((half * steps + step) * channels, channels)
            found = total[pl.ds(start, channels), :]
            for part in range(fold):
                y = step * fold + part
                out_ref[y * channels : (y + 1) * channels, :] = found[
                    :, part * pairs : (part + 1) * pairs
                ]

    def finish(step, carry):
        for copy in copies(step):
            copy.wait()
        return carry

    lax.fori_loop(0, channels // (2 * fold), finish, 0)


def left_kernel(blocks, depth, own_ref, peer_ref, *refs):
    right_refs, out_refs, (total, flipped) = refs[:blocks], refs[blocks:-2], refs[-2:]
    lanes = own_ref.shape[2] // 4
    fold = lanes // (blocks * depth)
    sequences = right_refs[0].shape[1]
    group = 4
    total[...] = jnp.zeros_like(total)

    def step_of(step, carry):
        steps = [group * step + part for part in range(group)]
        right = [right_rows(right_refs, at, fold, depth) for at in steps]
        high, low = halves(jnp.concatenate(right, 0))
        grads = [
            jnp.concatenate([rows_of_step([own_ref, peer_ref], at, half, lanes) for at in steps], 1)
            for half in range(2)
        ]
        both = dot(grads[0], jnp.concatenate([high, low], 1))
        total[...] += both[:, :sequences] + both[:, sequences:] + dot(grads[1], high)
        return carry

    lax.fori_loop(0, ENTRY_CHANNELS // (fold * group), step_of, 0, unroll=4)
    flipped[...] = total[...].T * (1.0 / sequences)
    here = lax.axis_index("inner")
    size, width = out_refs[0].shape[1:]
    for slot, ref in enumerate(out_refs):
        start = pl.multiple_of(lax.bitwise_xor(here, slot) * size, size)
        for side in range(2):
            ref[side] = flipped[pl.ds(start, size), side * width : (side + 1) * width]


def left_add_kernel(*refs):
    parts, (own_out, send_out) = refs[:-2], refs[-2:]
    for side, ref in enumerate((own_out, send_out)):
        ref[...] = functools.reduce(jnp.add, [part[side] for part in parts])


def pair_kernel(blocks, outer_hbm, flip_hbm, out_ref, outer_ref, weight_flip, semaphores):
    depth, pairs = out_ref.shape[2:]
    count = outer_ref.shape[0]
    lanes = outer_ref.shape[2] // 4
    columns = blocks * depth
    fold = lanes // columns
    wide = fold * pairs

    def copy_of(pair):
        return pltpu.make_async_copy(outer_hbm.at[pair], outer_ref.at[pair], semaphores.at[pair])

    flip_copy = pltpu.make_async_copy(flip_hbm, weight_flip, semaphores.at[count])
    flip_copy.start()
    for pair in range(count):
        copy_of(pair).start()
    flip_copy.wait()
    slots = slots_of(blocks)

    def step_of(pair, carry):
        copy_of(pair).wait()
        first = dot(weight_flip[...], outer_ref[pair, :, : 2 * lanes])
        second = dot(weight_flip[:wide, :], outer_ref[pair, :, 2 * lanes :])
        found = first[:wide] + first[wide:] + second
        for part in range(2):
            turned = []
            for place in range(fold):
                start = part * lanes
                piece = found[place * pairs : (place + 1) * pairs, start : start + lanes].T
                turned.append(piece[place * columns : (place + 1) * columns])
            turned = functools.reduce(jnp.add, turned)
            row = 2 * pair + part
            for slot in range(blocks):
                out_ref[row, slots[slot]] = turned[slot * depth : (slot + 1) * depth]
        return carry

    lax.fori_loop(0, count, step_of, 0)


def finish_kernel(own_ref, other_ref, keep_ref, found_ref, *refs):
    left_refs, refs = refs[:-9], refs[-9:]
    pair_hbm, left_out, right_out = refs[:3]
    right_total, right_square, right_tiles, left_total, left_tiles, semaphores = refs[3:]
    parity = lax.rem(lax.axis_index("blk"), 2)
    copies = [
        pltpu.make_async_copy(ref, pair_hbm.at[:, :, side], semaphores.at[at])
        for at, (ref, side) in enumerate(((own_ref, parity), (other_ref, 1 - parity)))
    ]
    for copy in copies:
        copy.start()
    turn_right([keep_ref, found_ref], right_out, right_total, right_square, right_tiles)
    turn_left(left_refs, left_out, left_total, left_tiles)
    for copy in copies:
        copy.wait()


def spread_sum_kernel(in_ref, out_ref):
    found = in_ref[0]
    for part in range(1, in_ref.shape[0]):
        found = found + in_ref[part]
    for part in range(in_ref.shape[0]):
        out_ref[part] = found


def place_kernel(mine_ref, other_ref, out_ref):
    channels = ENTRY_CHANNELS
    core = lax.rem(lax.axis_index("inner"), 2)
    steps = mine_ref.shape[0] // channels
    for ref, half in ((mine_ref, core), (other_ref, 1 - core)):
        for step in range(steps):
            rows = ref[step * channels : (step + 1) * channels, :]
            out_ref[strided(half * steps + step, channels, channels), :] = rows


def shape(*sizes, kind=F32):
    return jax.ShapeDtypeStruct(sizes, kind)


def call(
    kernel,
    out_shape,
    scratch=(),
    name=None,
    limit=16 * MIB,
    far=(),
    after=(),
    out_specs=None,
    flops=1,
):
    def run(*operands):
        vmem = pl.BlockSpec(memory_space=pltpu.VMEM)
        hbm = pl.BlockSpec(memory_space=pltpu.HBM)
        in_specs = [pl.BlockSpec(memory_space=pl.ANY)] * len(after)
        in_specs += [hbm if at in far else vmem for at in range(len(operands))]
        operands = [
            pltpu.with_memory_space_constraint(operand, pltpu.HBM) if at in far else operand
            for at, operand in enumerate(operands)
        ]
        extra = {} if out_specs is None else {"out_specs": out_specs}
        return pl.pallas_call(
            lambda *refs: kernel(*refs[len(after) :]),
            out_shape=out_shape,
            in_specs=in_specs,
            scratch_shapes=list(scratch),
            compiler_params=pltpu.CompilerParams(vmem_limit_bytes=limit),
            cost_estimate=pl.CostEstimate(flops=flops, bytes_accessed=1, transcendentals=0),
            name=name,
            **extra,
        )(*after, *operands)

    return run


def local(alignment_left, alignment_right, projection_matrix, cotangent):
    rows, features = alignment_left.shape
    depth = alignment_right.shape[0]
    count = lax.axis_size("blk")
    inner = lax.axis_size("inner")
    channels = ENTRY_CHANNELS
    sequences = features // channels
    outer, pairs = projection_matrix.shape
    blocks = count // 2
    fold = fold_of(blocks * depth)
    lanes = fold * blocks * depth
    tall = outer // fold
    steps = channels // fold
    row_pairs = rows // 2
    everyone = ("blk", "inner")

    partner = [(here, here ^ 1) for here in range(count)]
    slot_moves = [[(here, here ^ (2 * slot)) for here in range(count)] for slot in range(blocks)]
    inner_moves = [[(here, here ^ slot) for here in range(inner)] for slot in range(inner)]
    cores = [(here, here ^ 1) for here in range(inner)]
    core_groups = [list(range(core, count * inner, 2)) for core in range(2)]

    limit = 20 * MIB * max(1, blocks * depth * fold // LANES * 2 // fold)
    large = functools.partial(call, limit=limit)
    work = 4 * 2 * rows * 2 * blocks * depth * outer * pairs * 3

    by_side = cotangent.reshape(rows, blocks, 2, depth, pairs)
    half_cotangent = shape(rows, blocks, depth, pairs)
    right, left, cotangent_send, cotangent_own, weight = call(
        prepare_kernel,
        [
            shape(channels * depth, sequences),
            shape(rows * channels, sequences),
            half_cotangent,
            half_cotangent,
            shape(outer, pairs),
        ],
        [
            pltpu.VMEM((2, rows, features), F32),
            pltpu.VMEM((2, rows * features // LANES, LANES), F32),
            pltpu.VMEM((2, rows // PACK, LANES, LANES), F32),
            pltpu.SemaphoreType.DMA((5,)),
        ],
        name="prepare",
        far=range(4),
    )(by_side, alignment_right, alignment_left, projection_matrix)
    cotangent_peer = lax.ppermute(cotangent_send, "blk", partner)
    left_peer = lax.ppermute(left, "blk", partner)

    vmem = pl.BlockSpec(memory_space=pltpu.VMEM)
    hbm = pl.BlockSpec(memory_space=pltpu.HBM)
    factor = shape(row_pairs, tall, 4 * lanes, kind=BF16)
    factor_scratch = pltpu.VMEM(factor.shape, BF16)
    weight_cat = shape(tall, 3 * fold * pairs, kind=BF16)
    flip_scratch = pltpu.VMEM((2 * sequences, rows * channels), BF16)
    flip_sizes = (2 * fold * pairs, tall)
    spread = shape(row_pairs, 2, 2 * lanes, fold * pairs, kind=BF16)
    grad_own, spread_own, partial, weight_cat, weight_flip = large(
        functools.partial(gradient_kernel, blocks),
        [
            factor,
            spread,
            shape(steps // 2, sequences, 2 * lanes),
            weight_cat,
            pltpu.HBM(flip_sizes, BF16),
        ],
        [
            flip_scratch,
            pltpu.VMEM((tall, fold * pairs), F32),
            pltpu.VMEM(flip_sizes, BF16),
            pltpu.SemaphoreType.DMA,
        ],
        "gradient_own",
        out_specs=[vmem, vmem, vmem, vmem, hbm],
    )(weight, cotangent_own, left)
    grad_peer, spread_peer = large(
        functools.partial(peer_kernel, blocks), [factor, spread], [], "gradient_peer"
    )(weight_cat, cotangent_peer)
    rights = {0: right}
    distance = blocks // 2
    while distance:
        for slot in list(rights):
            sent = rights[slot]
            if slot:
                sent, _ = lax.optimization_barrier((sent, grad_peer))
            rights[slot + distance] = lax.ppermute(sent, "blk", slot_moves[distance])
        distance = distance // 2
    rights = [rights[slot] for slot in range(blocks)]
    right_half = shape(blocks // 2, channels * depth, sequences)
    right_keep, right_send = large(
        functools.partial(right_kernel, blocks, depth),
        [right_half, right_half],
        [flip_scratch],
        "right_parts",
    )(grad_peer, left_peer, partial)
    right_send = lax.ppermute(right_send, "blk", slot_moves[1])

    keep, send, outer_own, outer_peer = large(
        functools.partial(weight_kernel, blocks, depth),
        [shape(outer // 2, pairs)] * 2 + [pltpu.HBM(factor.shape, BF16)] * 2,
        [
            factor_scratch,
            factor_scratch,
            pltpu.VMEM((tall, fold * pairs), F32),
            pltpu.SemaphoreType.DMA((steps // 2, 2)),
        ],
        "weight",
        after=[right_keep],
        flops=2 * work,
        out_specs=[vmem, vmem, hbm, hbm],
    )(left, left_peer, spread_own, spread_peer, *rights)
    sent = lax.ppermute(send, "inner", cores)

    size = sequences // inner
    left_parts = large(
        functools.partial(left_kernel, blocks, depth),
        [shape(2, size, rows * channels)] * inner,
        [
            pltpu.VMEM((2 * rows * channels, sequences), F32),
            pltpu.VMEM((sequences, 2 * rows * channels), F32),
        ],
        "left_parts",
        after=[keep],
        flops=work,
    )(grad_own, grad_peer, *rights)
    slot = 2
    while slot < blocks:
        part = shape(blocks // (2 * slot), channels * depth, sequences)
        right_keep, right_send = call(
            halve_kernel, [part, part], name="right_halve", after=[left_parts[0]]
        )(right_keep, right_send)
        right_send = lax.ppermute(right_send, "blk", slot_moves[slot])
        slot = 2 * slot
    keep, right_keep, *left_parts = lax.optimization_barrier((keep, right_keep, *left_parts))
    members = count * inner // 2
    pieces = (keep + sent).reshape(members, outer // 2 // members, pairs)

    def pair(values, after, name):
        return large(
            functools.partial(pair_kernel, blocks),
            shape(rows, blocks, depth, pairs),
            [
                factor_scratch,
                pltpu.VMEM(flip_sizes, BF16),
                pltpu.SemaphoreType.DMA((row_pairs + 1,)),
            ],
            name,
            far=[0, 1],
            after=after,
            flops=work,
        )(values, weight_flip)

    pair_other = pair(outer_peer, [pieces], "pair_peer")
    pair_found = lax.ppermute(pair_other, "blk", partner)
    _, *left_parts = lax.optimization_barrier((pair_other, *left_parts))
    left_parts = [
        lax.ppermute(part, "inner", inner_moves[slot]) if slot else part
        for slot, part in enumerate(left_parts)
    ]
    pieces = lax.all_to_all(pieces, everyone, 0, 0, axis_index_groups=core_groups)
    pieces = call(
        spread_sum_kernel,
        shape(*pieces.shape),
        name="weight_sum",
        after=[pair_other],
    )(pieces)
    pair_own = pair(outer_own, [pieces], "pair_own")
    left_own, left_send = call(
        left_add_kernel, [shape(size, rows * channels)] * 2, name="left_add", after=[pieces]
    )(*left_parts)
    pieces = lax.all_to_all(pieces, everyone, 0, 0, axis_index_groups=core_groups)

    left_found = [left_own, lax.ppermute(left_send, "blk", partner)]
    pair_update, grad_left, grad_right = call(
        finish_kernel,
        [
            pltpu.HBM(by_side.shape, F32),
            shape(rows, features // inner),
            shape(depth, features),
        ],
        [
            pltpu.VMEM((channels * depth, sequences), F32),
            pltpu.VMEM((depth // PACK, LANES, LANES), F32),
            pltpu.VMEM((depth * features // LANES, LANES), F32),
            pltpu.VMEM((size * rows * channels // LANES, LANES), F32),
            pltpu.VMEM((rows * features // inner // LANES, LANES), F32),
            pltpu.SemaphoreType.DMA((2,)),
        ],
        "finish",
        out_specs=[hbm, vmem, vmem],
    )(pair_own, pair_found, right_keep, right_send, *left_found)
    pair_update = pair_update.reshape(cotangent.shape)

    pieces, pair_update, grad_left, grad_right = lax.optimization_barrier(
        (pieces, pair_update, grad_left, grad_right)
    )
    mine = pieces.reshape(outer // 2, pairs)
    other = lax.ppermute(mine, "inner", cores)
    grad_weight = call(place_kernel, shape(outer, pairs), name="place")(mine, other)
    return (pair_update, grad_left, grad_right, grad_weight)


def solution(mesh):
    placed = (
        P(("groups", "blk"), None),
        P(("groups", "blk", "inner"), None),
        P(),
        P(("groups", "blk"), None, "inner", None),
    )
    return jax.shard_map(
        local,
        mesh=mesh,
        in_specs=placed,
        out_specs=(
            P(("groups", "blk"), None, "inner", None),
            P(("groups", "blk"), "inner"),
            P(("groups", "blk", "inner"), None),
            P("groups", None),
        ),
        check_vma=False,
    )
```

```python
import functools

import jax
import jax.numpy as jnp
from jax import lax
from jax.experimental import pallas as pl
from jax.experimental.pallas import tpu as pltpu
from jax.sharding import PartitionSpec as P

ENTRY_CHANNELS = 32
LANES = 128
PACK = LANES // ENTRY_CHANNELS
F32 = jnp.float32
BF16 = jnp.bfloat16
MIB = 1024 * 1024


def halves(values):
    high = values.astype(BF16)
    low = (values - high.astype(F32)).astype(BF16)
    return high, low


def dot(left, right):
    return jnp.dot(left, right, preferred_element_type=F32)


def dot_rows(left, right):
    return lax.dot_general(left, right, (((1,), (1,)), ((), ())), preferred_element_type=F32)


def fold_of(columns):
    return max(1, LANES // columns)


def strided(start, size, stride):
    return pl.ds(start, size, stride=stride)


def folded_weight(weight_ref, step, fold):
    channels = ENTRY_CHANNELS
    return jnp.concatenate(
        [weight_ref[strided(step * fold + part, channels, channels), :] for part in range(fold)], 1
    )


def slots_of(blocks):
    here = lax.axis_index("blk") // 2
    return [lax.bitwise_xor(here, slot) for slot in range(blocks)]


def spread_of(cotangent_ref, pair, slots, fold):
    columns = len(slots) * cotangent_ref.shape[2]
    empty = jnp.zeros((columns, cotangent_ref.shape[3]), BF16)
    spread = ([], [])
    for part in range(2):
        rows = jnp.concatenate([cotangent_ref[2 * pair + part, slot] for slot in slots], 0)
        for found, values in zip(spread, halves(rows)):
            for place in range(fold):
                found.append(
                    jnp.concatenate(
                        [values if place == other else empty for other in range(fold)], 1
                    )
                )
    return [jnp.concatenate(found, 0) for found in spread]


def turn_in(rows_minor, in_ref, out_ref, tiles, square):
    channels = ENTRY_CHANNELS
    rows, features = in_ref.shape
    count = features // LANES
    for tile in range(count):
        tiles[tile * rows : (tile + 1) * rows, :] = in_ref[:, tile * LANES : (tile + 1) * LANES]
    for group in range(rows // PACK):
        found = [tiles[strided(group * PACK + k, count, rows), :] for k in range(PACK)]
        for part in range(PACK):
            lanes = slice(part * channels, (part + 1) * channels)
            square[group, strided(part, count, PACK), :] = jnp.concatenate(
                [values[:, lanes] for values in found], 1
            )
        turned = square[group].T
        if rows_minor:
            for k in range(PACK):
                out_ref[strided(group * PACK + k, channels, rows), :] = turned[
                    k * channels : (k + 1) * channels
                ]
        else:
            out_ref[group * LANES : (group + 1) * LANES, :] = turned


def prepare_kernel(
    cotangent_hbm,
    right_hbm,
    left_hbm,
    weight_hbm,
    right_out,
    left_out,
    send_out,
    own_out,
    weight_out,
    inputs,
    tiles,
    square,
    semaphores,
):
    parity = lax.rem(lax.axis_index("blk"), 2)
    moves = (
        (right_hbm, inputs.at[0]),
        (left_hbm, inputs.at[1]),
        (cotangent_hbm.at[:, :, 1 - parity], send_out),
        (cotangent_hbm.at[:, :, parity], own_out),
        (weight_hbm, weight_out),
    )
    copies = [
        pltpu.make_async_copy(source, target, semaphores.at[at])
        for at, (source, target) in enumerate(moves)
    ]
    for copy in copies:
        copy.start()
    copies[0].wait()
    turn_in(True, inputs.at[0], right_out, tiles.at[0], square.at[0])
    copies[1].wait()
    turn_in(False, inputs.at[1], left_out, tiles.at[1], square.at[1])
    for copy in copies[2:]:
        copy.wait()


def turn_right(part_refs, out_ref, total, square, tiles):
    channels = ENTRY_CHANNELS
    rows, features = out_ref.shape
    count = features // LANES
    size = part_refs[0].shape[1]
    total[:size, :] = part_refs[0][0] + part_refs[1][0]
    total[size:, :] = part_refs[2][0] + part_refs[3][0]
    for group in range(rows // PACK):
        stacked = [total[strided(group * PACK + k, channels, rows), :] for k in range(PACK)]
        square[group] = jnp.concatenate(stacked, 0).T
        pieces = [square[group, strided(part, count, PACK), :] for part in range(PACK)]
        for k in range(PACK):
            lanes = slice(k * channels, (k + 1) * channels)
            tiles[strided(group * PACK + k, count, rows), :] = jnp.concatenate(
                [piece[:, lanes] for piece in pieces], 1
            )
    for tile in range(count):
        out_ref[:, tile * LANES : (tile + 1) * LANES] = tiles[tile * rows : (tile + 1) * rows, :]


def turn_left(part_refs, out_ref, total, tiles):
    channels = ENTRY_CHANNELS
    size, width = part_refs[0].shape
    rows, features = out_ref.shape
    count = features // LANES
    found = functools.reduce(jnp.add, [ref[...] for ref in part_refs])
    for tile in range(width // LANES):
        total[tile * size : (tile + 1) * size, :] = found[:, tile * LANES : (tile + 1) * LANES]
    for tile in range(width // LANES):
        pieces = [total[strided(tile * size + part, count, PACK), :] for part in range(PACK)]
        for k in range(PACK):
            lanes = slice(k * channels, (k + 1) * channels)
            tiles[strided(tile * PACK + k, count, rows), :] = jnp.concatenate(
                [piece[:, lanes] for piece in pieces], 1
            )
    for tile in range(count):
        out_ref[:, tile * LANES : (tile + 1) * LANES] = tiles[tile * rows : (tile + 1) * rows, :]


def prepare_weight(weight_ref, weight_cat, fold):
    channels = ENTRY_CHANNELS
    for step in range(channels // fold):
        high, low = halves(folded_weight(weight_ref, step, fold))
        weight_cat[step * channels : (step + 1) * channels, :] = jnp.concatenate(
            [high, low, high], 1
        )


def gradient_phase(blocks, cotangent_ref, out_ref, spread_ref, weight_cat):
    fold = fold_of(blocks * cotangent_ref.shape[2])
    slots = slots_of(blocks)

    def step_of(pair, carry):
        high, low = spread_of(cotangent_ref, pair, slots, fold)
        spread_ref[pair, 0] = high
        spread_ref[pair, 1] = low
        found = dot_rows(weight_cat[...], jnp.concatenate([high, high, low], 1))
        out_ref[pair] = jnp.concatenate(halves(found), 1)
        return carry

    lax.fori_loop(0, out_ref.shape[0], step_of, 0, unroll=8)


def gradient_kernel(
    blocks,
    weight_ref,
    cotangent_ref,
    left_ref,
    out_ref,
    spread_ref,
    partial_ref,
    weight_cat,
    flip_hbm,
    left_flip,
    weight_rows,
    weight_flip,
    semaphore,
):
    fold = fold_of(blocks * cotangent_ref.shape[2])
    prepare_weight(weight_ref, weight_cat, fold)
    gradient_phase(blocks, cotangent_ref, out_ref, spread_ref, weight_cat)

    def store(step, found):
        partial_ref[step] = found

    right_phase(left_ref, out_ref, left_flip, [store])
    channels = ENTRY_CHANNELS
    wide = weight_rows.shape[1]
    for step in range(channels // fold):
        weight_rows[step * channels : (step + 1) * channels, :] = folded_weight(
            weight_ref, step, fold
        )
    flip_high, flip_low = halves(weight_rows[...].T)
    weight_flip[:wide, :] = flip_high
    weight_flip[wide:, :] = flip_low
    copy = pltpu.make_async_copy(weight_flip, flip_hbm, semaphore)
    copy.start()
    copy.wait()


def peer_kernel(blocks, weight_cat, cotangent_ref, out_ref, spread_ref):
    gradient_phase(blocks, cotangent_ref, out_ref, spread_ref, weight_cat)


def right_phase(left_ref, factor_ref, left_flip, stores):
    sequences = left_ref.shape[1]
    lanes = factor_ref.shape[2] // 4
    flip_high, flip_low = halves((left_ref[...] * (1.0 / sequences)).T)
    left_flip[:sequences, :] = flip_high
    left_flip[sequences:, :] = flip_low

    def compute(step, store):
        high, low = (
            jnp.concatenate(
                [rows_of_step([factor_ref], 2 * step + part, half, lanes) for part in range(2)], 1
            )
            for half in range(2)
        )
        first = dot(left_flip[...], high)
        second = dot(left_flip[:sequences, :], low)
        store(step, first[:sequences] + first[sequences:] + second)

    count = factor_ref.shape[1] // (2 * ENTRY_CHANNELS)
    size = count // len(stores)
    for at, store in enumerate(stores):

        def step_of(step, carry):
            compute(step, store)
            return carry

        lax.fori_loop(at * size, (at + 1) * size, step_of, 0, unroll=min(size, 8))


def rows_of_step(refs, step, half, lanes):
    channels = ENTRY_CHANNELS
    rows = pl.ds(pl.multiple_of(step * channels, channels), channels)
    start = 2 * half * lanes
    return jnp.concatenate(
        [
            ref[pair, rows, start + part * lanes : start + (part + 1) * lanes]
            for ref in refs
            for pair in range(ref.shape[0])
            for part in range(2)
        ],
        0,
    )


def both_left(left_refs):
    sequences = left_refs[0].shape[1]
    return jnp.concatenate([ref[...] for ref in left_refs], 0) * (1.0 / sequences)


def right_kernel(
    blocks,
    depth,
    peer_ref,
    left_ref,
    partial_ref,
    near_keep,
    near_send,
    far_keep,
    far_send,
    left_flip,
):
    fold = fold_of(blocks * depth)
    lanes = fold * blocks * depth
    size = near_keep.shape[1]

    def store_to(outs, first_row):
        def store(step, found):
            found = found + partial_ref[step]
            for part in range(2):
                turned = found[:, part * lanes : (part + 1) * lanes].T
                for place in range(fold):
                    for slot in range(blocks):
                        start = (place * blocks + slot) * depth
                        row = ((2 * step + part) * fold + place) * depth - first_row
                        row = pl.multiple_of(row, depth)
                        ref, at = outs[slot]
                        ref[at, pl.ds(row, depth), :] = turned[start : start + depth]

        return store

    half = blocks // 2
    near = [(near_send if slot % 2 else near_keep, slot // 2) for slot in range(blocks)]
    far = [(far_send if slot >= half else far_keep, slot % half) for slot in range(blocks)]
    right_phase(left_ref, peer_ref, left_flip, [store_to(near, 0), store_to(far, size)])


def halve_kernel(
    near_keep,
    near_found,
    far_keep,
    far_found,
    near_keep_out,
    near_send_out,
    far_keep_out,
    far_send_out,
):
    half = near_keep.shape[0] // 2
    for slot in range(2 * half):
        out_ref = near_send_out if slot % 2 else near_keep_out
        out_ref[slot // 2] = near_keep[slot] + near_found[slot]
        out_ref = far_send_out if slot >= half else far_keep_out
        out_ref[slot % half] = far_keep[slot] + far_found[slot]


def right_rows(right_refs, step, fold, depth):
    return jnp.concatenate(
        [
            ref[pl.ds(pl.multiple_of((step * fold + part) * depth, depth), depth), :]
            for part in range(fold)
            for ref in right_refs
        ],
        0,
    )


def weight_kernel(blocks, depth, own_left, peer_left, own_spread, peer_spread, *refs):
    right_refs = refs[:blocks]
    keep_ref, send_ref, own_out, peer_out, own_ref, peer_ref, total, semaphores = refs[blocks:]
    channels = ENTRY_CHANNELS
    fold = fold_of(blocks * depth)
    lanes = fold * blocks * depth
    pairs = total.shape[1] // fold
    high, low = halves(both_left([own_left, peer_left]))
    left_cat = jnp.concatenate([high, low, high], 1)

    def copies(step):
        size = 2 * channels
        rows = pl.ds(pl.multiple_of(step * size, size), size)
        return [
            pltpu.make_async_copy(ref.at[:, rows], out.at[:, rows], semaphores.at[step, side])
            for side, (ref, out) in enumerate(((own_ref, own_out), (peer_ref, peer_out)))
        ]

    def outer_step(step, carry):
        right = [right_rows(right_refs, 2 * step + part, fold, depth) for part in range(2)]
        high, low = halves(jnp.concatenate(right, 0))
        found = dot_rows(left_cat, jnp.concatenate([high, high, low], 1))
        both = halves(found)
        for part in range(2):
            start = pl.multiple_of((2 * step + part) * channels, channels)
            row = 0
            for ref in (own_ref, peer_ref):
                for index in range(2 * ref.shape[0]):
                    for half in range(2):
                        lane = (2 * half + index % 2) * lanes
                        ref[index // 2, pl.ds(start, channels), lane : lane + lanes] = both[half][
                            row : row + channels, part * lanes : (part + 1) * lanes
                        ]
                    row += channels
        for copy in copies(step):
            copy.start()
        return carry

    lax.fori_loop(0, channels // (2 * fold), outer_step, 0, unroll=4)
    total[...] = jnp.zeros_like(total)

    def weight_step(pair, carry):
        lefts, rights = [], []
        for ref, spread_ref in ((own_ref, own_spread), (peer_ref, peer_spread)):
            high = spread_ref[pair, 0]
            lefts += [ref[pair], ref[pair, :, : 2 * lanes]]
            rights += [high, high, spread_ref[pair, 1]]
        total[...] += dot(jnp.concatenate(lefts, 1), jnp.concatenate(rights, 0))
        return carry

    lax.fori_loop(0, own_ref.shape[0], weight_step, 0, unroll=4)
    core = lax.rem(lax.axis_index("inner"), 2)
    steps = channels // (2 * fold)
    for out_ref, half in ((keep_ref, core), (send_ref, 1 - core)):
        for step in range(steps):
            start = pl.multiple_of((half * steps + step) * channels, channels)
            found = total[pl.ds(start, channels), :]
            for part in range(fold):
                y = step * fold + part
                out_ref[y * channels : (y + 1) * channels, :] = found[
                    :, part * pairs : (part + 1) * pairs
                ]

    def finish(step, carry):
        for copy in copies(step):
            copy.wait()
        return carry

    lax.fori_loop(0, channels // (2 * fold), finish, 0)


def left_kernel(blocks, depth, own_ref, peer_ref, *refs):
    right_refs, out_refs, (total, flipped) = refs[:blocks], refs[blocks:-2], refs[-2:]
    lanes = own_ref.shape[2] // 4
    fold = lanes // (blocks * depth)
    sequences = right_refs[0].shape[1]
    group = 4
    total[...] = jnp.zeros_like(total)

    def step_of(step, carry):
        steps = [group * step + part for part in range(group)]
        right = [right_rows(right_refs, at, fold, depth) for at in steps]
        high, low = halves(jnp.concatenate(right, 0))
        grads = [
            jnp.concatenate([rows_of_step([own_ref, peer_ref], at, half, lanes) for at in steps], 1)
            for half in range(2)
        ]
        both = dot(grads[0], jnp.concatenate([high, low], 1))
        total[...] += both[:, :sequences] + both[:, sequences:] + dot(grads[1], high)
        return carry

    lax.fori_loop(0, ENTRY_CHANNELS // (fold * group), step_of, 0, unroll=4)
    flipped[...] = total[...].T * (1.0 / sequences)
    here = lax.axis_index("inner")
    size, width = out_refs[0].shape[1:]
    for slot, ref in enumerate(out_refs):
        start = pl.multiple_of(lax.bitwise_xor(here, slot) * size, size)
        for side in range(2):
            ref[side] = flipped[pl.ds(start, size), side * width : (side + 1) * width]


def left_add_kernel(*refs):
    parts, (own_out, send_out) = refs[:-2], refs[-2:]
    for side, ref in enumerate((own_out, send_out)):
        ref[...] = functools.reduce(jnp.add, [part[side] for part in parts])


def pair_kernel(blocks, outer_hbm, flip_hbm, out_ref, outer_ref, weight_flip, semaphores):
    depth, pairs = out_ref.shape[2:]
    count = outer_ref.shape[0]
    lanes = outer_ref.shape[2] // 4
    columns = blocks * depth
    fold = lanes // columns
    wide = fold * pairs

    def copy_of(pair):
        return pltpu.make_async_copy(outer_hbm.at[pair], outer_ref.at[pair], semaphores.at[pair])

    flip_copy = pltpu.make_async_copy(flip_hbm, weight_flip, semaphores.at[count])
    flip_copy.start()
    for pair in range(count):
        copy_of(pair).start()
    flip_copy.wait()
    slots = slots_of(blocks)

    def step_of(pair, carry):
        copy_of(pair).wait()
        first = dot(weight_flip[...], outer_ref[pair, :, : 2 * lanes])
        second = dot(weight_flip[:wide, :], outer_ref[pair, :, 2 * lanes :])
        found = first[:wide] + first[wide:] + second
        for part in range(2):
            turned = []
            for place in range(fold):
                start = part * lanes
                piece = found[place * pairs : (place + 1) * pairs, start : start + lanes].T
                turned.append(piece[place * columns : (place + 1) * columns])
            turned = functools.reduce(jnp.add, turned)
            row = 2 * pair + part
            for slot in range(blocks):
                out_ref[row, slots[slot]] = turned[slot * depth : (slot + 1) * depth]
        return carry

    lax.fori_loop(0, count, step_of, 0)


def finish_kernel(own_ref, other_ref, *refs):
    right_refs, left_refs, refs = refs[:4], refs[4:-9], refs[-9:]
    pair_hbm, left_out, right_out = refs[:3]
    right_total, right_square, right_tiles, left_total, left_tiles, semaphores = refs[3:]
    parity = lax.rem(lax.axis_index("blk"), 2)
    copies = [
        pltpu.make_async_copy(ref, pair_hbm.at[:, :, side], semaphores.at[at])
        for at, (ref, side) in enumerate(((own_ref, parity), (other_ref, 1 - parity)))
    ]
    for copy in copies:
        copy.start()
    turn_right(right_refs, right_out, right_total, right_square, right_tiles)
    turn_left(left_refs, left_out, left_total, left_tiles)
    for copy in copies:
        copy.wait()


def spread_sum_kernel(in_ref, out_ref):
    found = in_ref[0]
    for part in range(1, in_ref.shape[0]):
        found = found + in_ref[part]
    for part in range(in_ref.shape[0]):
        out_ref[part] = found


def place_kernel(mine_ref, other_ref, out_ref):
    channels = ENTRY_CHANNELS
    core = lax.rem(lax.axis_index("inner"), 2)
    steps = mine_ref.shape[0] // channels
    for ref, half in ((mine_ref, core), (other_ref, 1 - core)):
        for step in range(steps):
            rows = ref[step * channels : (step + 1) * channels, :]
            out_ref[strided(half * steps + step, channels, channels), :] = rows


def shape(*sizes, kind=F32):
    return jax.ShapeDtypeStruct(sizes, kind)


def call(
    kernel,
    out_shape,
    scratch=(),
    name=None,
    limit=16 * MIB,
    far=(),
    after=(),
    out_specs=None,
    flops=1,
):
    def run(*operands):
        vmem = pl.BlockSpec(memory_space=pltpu.VMEM)
        hbm = pl.BlockSpec(memory_space=pltpu.HBM)
        in_specs = [pl.BlockSpec(memory_space=pl.ANY)] * len(after)
        in_specs += [hbm if at in far else vmem for at in range(len(operands))]
        operands = [
            pltpu.with_memory_space_constraint(operand, pltpu.HBM) if at in far else operand
            for at, operand in enumerate(operands)
        ]
        extra = {} if out_specs is None else {"out_specs": out_specs}
        return pl.pallas_call(
            lambda *refs: kernel(*refs[len(after) :]),
            out_shape=out_shape,
            in_specs=in_specs,
            scratch_shapes=list(scratch),
            compiler_params=pltpu.CompilerParams(vmem_limit_bytes=limit),
            cost_estimate=pl.CostEstimate(flops=flops, bytes_accessed=1, transcendentals=0),
            name=name,
            **extra,
        )(*after, *operands)

    return run


def local(alignment_left, alignment_right, projection_matrix, cotangent):
    rows, features = alignment_left.shape
    depth = alignment_right.shape[0]
    count = lax.axis_size("blk")
    inner = lax.axis_size("inner")
    channels = ENTRY_CHANNELS
    sequences = features // channels
    outer, pairs = projection_matrix.shape
    blocks = count // 2
    fold = fold_of(blocks * depth)
    lanes = fold * blocks * depth
    tall = outer // fold
    steps = channels // fold
    row_pairs = rows // 2
    everyone = ("blk", "inner")

    partner = [(here, here ^ 1) for here in range(count)]
    slot_moves = [[(here, here ^ (2 * slot)) for here in range(count)] for slot in range(blocks)]
    inner_moves = [[(here, here ^ slot) for here in range(inner)] for slot in range(inner)]
    cores = [(here, here ^ 1) for here in range(inner)]
    core_groups = [list(range(core, count * inner, 2)) for core in range(2)]

    limit = 20 * MIB * max(1, blocks * depth * fold // LANES * 2 // fold)
    large = functools.partial(call, limit=limit)
    work = 4 * 2 * rows * 2 * blocks * depth * outer * pairs * 3

    by_side = cotangent.reshape(rows, blocks, 2, depth, pairs)
    half_cotangent = shape(rows, blocks, depth, pairs)
    right, left, cotangent_send, cotangent_own, weight = call(
        prepare_kernel,
        [
            shape(channels * depth, sequences),
            shape(rows * channels, sequences),
            half_cotangent,
            half_cotangent,
            shape(outer, pairs),
        ],
        [
            pltpu.VMEM((2, rows, features), F32),
            pltpu.VMEM((2, rows * features // LANES, LANES), F32),
            pltpu.VMEM((2, rows // PACK, LANES, LANES), F32),
            pltpu.SemaphoreType.DMA((5,)),
        ],
        name="prepare",
        far=range(4),
    )(by_side, alignment_right, alignment_left, projection_matrix)
    cotangent_peer = lax.ppermute(cotangent_send, "blk", partner)
    left_peer = lax.ppermute(left, "blk", partner)

    vmem = pl.BlockSpec(memory_space=pltpu.VMEM)
    hbm = pl.BlockSpec(memory_space=pltpu.HBM)
    factor = shape(row_pairs, tall, 4 * lanes, kind=BF16)
    factor_scratch = pltpu.VMEM(factor.shape, BF16)
    weight_cat = shape(tall, 3 * fold * pairs, kind=BF16)
    flip_scratch = pltpu.VMEM((2 * sequences, rows * channels), BF16)
    flip_sizes = (2 * fold * pairs, tall)
    spread = shape(row_pairs, 2, 2 * lanes, fold * pairs, kind=BF16)
    grad_own, spread_own, partial, weight_cat, weight_flip = large(
        functools.partial(gradient_kernel, blocks),
        [
            factor,
            spread,
            shape(steps // 2, sequences, 2 * lanes),
            weight_cat,
            pltpu.HBM(flip_sizes, BF16),
        ],
        [
            flip_scratch,
            pltpu.VMEM((tall, fold * pairs), F32),
            pltpu.VMEM(flip_sizes, BF16),
            pltpu.SemaphoreType.DMA,
        ],
        "gradient_own",
        out_specs=[vmem, vmem, vmem, vmem, hbm],
    )(weight, cotangent_own, left)
    grad_peer, spread_peer = large(
        functools.partial(peer_kernel, blocks), [factor, spread], [], "gradient_peer"
    )(weight_cat, cotangent_peer)
    rights = {0: right}
    distance = blocks // 2
    while distance:
        for slot in list(rights):
            sent = rights[slot]
            if slot:
                sent, _ = lax.optimization_barrier((sent, grad_peer))
            rights[slot + distance] = lax.ppermute(sent, "blk", slot_moves[distance])
        distance = distance // 2
    rights = [rights[slot] for slot in range(blocks)]
    right_half = shape(blocks // 2, channels * depth // 2, sequences)
    near_keep, near_send, far_keep, far_send = large(
        functools.partial(right_kernel, blocks, depth),
        [right_half] * 4,
        [flip_scratch],
        "right_parts",
    )(grad_peer, left_peer, partial)
    near_send = lax.ppermute(near_send, "blk", slot_moves[1])
    far_send = lax.ppermute(far_send, "blk", slot_moves[blocks // 2])

    keep, send, outer_own, outer_peer = large(
        functools.partial(weight_kernel, blocks, depth),
        [shape(outer // 2, pairs)] * 2 + [pltpu.HBM(factor.shape, BF16)] * 2,
        [
            factor_scratch,
            factor_scratch,
            pltpu.VMEM((tall, fold * pairs), F32),
            pltpu.SemaphoreType.DMA((steps // 2, 2)),
        ],
        "weight",
        after=[near_keep],
        flops=2 * work,
        out_specs=[vmem, vmem, hbm, hbm],
    )(left, left_peer, spread_own, spread_peer, *rights)
    sent = lax.ppermute(send, "inner", cores)

    size = sequences // inner
    left_parts = large(
        functools.partial(left_kernel, blocks, depth),
        [shape(2, size, rows * channels)] * inner,
        [
            pltpu.VMEM((2 * rows * channels, sequences), F32),
            pltpu.VMEM((sequences, 2 * rows * channels), F32),
        ],
        "left_parts",
        after=[keep],
        flops=work,
    )(grad_own, grad_peer, *rights)
    keep, *left_parts = lax.optimization_barrier((keep, *left_parts))
    members = count * inner // 2
    pieces = (keep + sent).reshape(members, outer // 2 // members, pairs)

    def pair(values, after, name):
        return large(
            functools.partial(pair_kernel, blocks),
            shape(rows, blocks, depth, pairs),
            [
                factor_scratch,
                pltpu.VMEM(flip_sizes, BF16),
                pltpu.SemaphoreType.DMA((row_pairs + 1,)),
            ],
            name,
            far=[0, 1],
            after=after,
            flops=work,
        )(values, weight_flip)

    pair_other = pair(outer_peer, [pieces], "pair_peer")
    pair_found = lax.ppermute(pair_other, "blk", partner)
    _, *left_parts = lax.optimization_barrier((pair_other, *left_parts))
    left_parts = [
        lax.ppermute(part, "inner", inner_moves[slot]) if slot else part
        for slot, part in enumerate(left_parts)
    ]
    slot = 2
    while slot < blocks:
        part = shape(blocks // (2 * slot), channels * depth // 2, sequences)
        near_keep, near_send, far_keep, far_send = call(
            halve_kernel, [part] * 4, name="right_halve", after=[pair_other]
        )(near_keep, near_send, far_keep, far_send)
        near_send = lax.ppermute(near_send, "blk", slot_moves[slot])
        far_send = lax.ppermute(far_send, "blk", slot_moves[blocks // (2 * slot)])
        slot = 2 * slot

    pieces = lax.all_to_all(pieces, everyone, 0, 0, axis_index_groups=core_groups)
    pieces = call(
        spread_sum_kernel,
        shape(*pieces.shape),
        name="weight_sum",
        after=[pair_other, near_keep],
    )(pieces)
    pair_own = pair(outer_own, [pieces], "pair_own")
    left_own, left_send = call(
        left_add_kernel, [shape(size, rows * channels)] * 2, name="left_add", after=[pieces]
    )(*left_parts)
    pieces = lax.all_to_all(pieces, everyone, 0, 0, axis_index_groups=core_groups)

    left_found = [left_own, lax.ppermute(left_send, "blk", partner)]
    pair_update, grad_left, grad_right = call(
        finish_kernel,
        [
            pltpu.HBM(by_side.shape, F32),
            shape(rows, features // inner),
            shape(depth, features),
        ],
        [
            pltpu.VMEM((channels * depth, sequences), F32),
            pltpu.VMEM((depth // PACK, LANES, LANES), F32),
            pltpu.VMEM((depth * features // LANES, LANES), F32),
            pltpu.VMEM((size * rows * channels // LANES, LANES), F32),
            pltpu.VMEM((rows * features // inner // LANES, LANES), F32),
            pltpu.SemaphoreType.DMA((2,)),
        ],
        "finish",
        out_specs=[hbm, vmem, vmem],
    )(pair_own, pair_found, near_keep, near_send, far_keep, far_send, *left_found)
    pair_update = pair_update.reshape(cotangent.shape)

    pieces, pair_update, grad_left, grad_right = lax.optimization_barrier(
        (pieces, pair_update, grad_left, grad_right)
    )
    mine = pieces.reshape(outer // 2, pairs)
    other = lax.ppermute(mine, "inner", cores)
    grad_weight = call(place_kernel, shape(outer, pairs), name="place")(mine, other)
    return (pair_update, grad_left, grad_right, grad_weight)


def solution(mesh):
    placed = (
        P(("groups", "blk"), None),
        P(("groups", "blk", "inner"), None),
        P(),
        P(("groups", "blk"), None, "inner", None),
    )
    return jax.shard_map(
        local,
        mesh=mesh,
        in_specs=placed,
        out_specs=(
            P(("groups", "blk"), None, "inner", None),
            P(("groups", "blk"), "inner"),
            P(("groups", "blk", "inner"), None),
            P("groups", None),
        ),
        check_vma=False,
    )
```

```python
import functools

import jax
import jax.numpy as jnp
from jax import lax
from jax.experimental import pallas as pl
from jax.experimental.pallas import tpu as pltpu
from jax.sharding import PartitionSpec as P

ENTRY_CHANNELS = 32
LANES = 128
PACK = LANES // ENTRY_CHANNELS
F32 = jnp.float32
BF16 = jnp.bfloat16
MIB = 1024 * 1024


def halves(values):
    high = values.astype(BF16)
    low = (values - high.astype(F32)).astype(BF16)
    return high, low


def dot(left, right):
    return jnp.dot(left, right, preferred_element_type=F32)


def dot_rows(left, right):
    return lax.dot_general(left, right, (((1,), (1,)), ((), ())), preferred_element_type=F32)


def fold_of(columns):
    return max(1, LANES // columns)


def strided(start, size, stride):
    return pl.ds(start, size, stride=stride)


def folded_weight(weight_ref, step, fold):
    channels = ENTRY_CHANNELS
    return jnp.concatenate(
        [weight_ref[strided(step * fold + part, channels, channels), :] for part in range(fold)], 1
    )


def slots_of(blocks):
    here = lax.axis_index("blk") // 2
    return [lax.bitwise_xor(here, slot) for slot in range(blocks)]


def spread_of(cotangent_ref, pair, slots, fold):
    columns = len(slots) * cotangent_ref.shape[2]
    empty = jnp.zeros((columns, cotangent_ref.shape[3]), BF16)
    spread = ([], [])
    for part in range(2):
        rows = jnp.concatenate([cotangent_ref[2 * pair + part, slot] for slot in slots], 0)
        for found, values in zip(spread, halves(rows)):
            for place in range(fold):
                found.append(
                    jnp.concatenate(
                        [values if place == other else empty for other in range(fold)], 1
                    )
                )
    return [jnp.concatenate(found, 0) for found in spread]


def turn_in(rows_minor, in_ref, out_ref, tiles, square):
    channels = ENTRY_CHANNELS
    rows, features = in_ref.shape
    count = features // LANES
    for tile in range(count):
        tiles[tile * rows : (tile + 1) * rows, :] = in_ref[:, tile * LANES : (tile + 1) * LANES]
    for group in range(rows // PACK):
        found = [tiles[strided(group * PACK + k, count, rows), :] for k in range(PACK)]
        for part in range(PACK):
            lanes = slice(part * channels, (part + 1) * channels)
            square[group, strided(part, count, PACK), :] = jnp.concatenate(
                [values[:, lanes] for values in found], 1
            )
        turned = square[group].T
        if rows_minor:
            for k in range(PACK):
                out_ref[strided(group * PACK + k, channels, rows), :] = turned[
                    k * channels : (k + 1) * channels
                ]
        else:
            out_ref[group * LANES : (group + 1) * LANES, :] = turned


def prepare_kernel(
    cotangent_hbm,
    right_hbm,
    left_hbm,
    weight_hbm,
    right_out,
    left_out,
    send_out,
    own_out,
    weight_out,
    inputs,
    tiles,
    square,
    semaphores,
):
    parity = lax.rem(lax.axis_index("blk"), 2)
    moves = (
        (right_hbm, inputs.at[0]),
        (left_hbm, inputs.at[1]),
        (cotangent_hbm.at[:, :, 1 - parity], send_out),
        (cotangent_hbm.at[:, :, parity], own_out),
        (weight_hbm, weight_out),
    )
    copies = [
        pltpu.make_async_copy(source, target, semaphores.at[at])
        for at, (source, target) in enumerate(moves)
    ]
    for copy in copies:
        copy.start()
    copies[0].wait()
    turn_in(True, inputs.at[0], right_out, tiles.at[0], square.at[0])
    copies[1].wait()
    turn_in(False, inputs.at[1], left_out, tiles.at[1], square.at[1])
    for copy in copies[2:]:
        copy.wait()


def turn_right(part_refs, out_ref, total, square, tiles):
    channels = ENTRY_CHANNELS
    rows, features = out_ref.shape
    count = features // LANES
    total[...] = functools.reduce(jnp.add, [ref[0] for ref in part_refs])
    for group in range(rows // PACK):
        stacked = [total[strided(group * PACK + k, channels, rows), :] for k in range(PACK)]
        square[group] = jnp.concatenate(stacked, 0).T
        pieces = [square[group, strided(part, count, PACK), :] for part in range(PACK)]
        for k in range(PACK):
            lanes = slice(k * channels, (k + 1) * channels)
            tiles[strided(group * PACK + k, count, rows), :] = jnp.concatenate(
                [piece[:, lanes] for piece in pieces], 1
            )
    for tile in range(count):
        out_ref[:, tile * LANES : (tile + 1) * LANES] = tiles[tile * rows : (tile + 1) * rows, :]


def turn_left(part_refs, out_ref, total, tiles):
    channels = ENTRY_CHANNELS
    size, width = part_refs[0].shape
    rows, features = out_ref.shape
    count = features // LANES
    found = functools.reduce(jnp.add, [ref[...] for ref in part_refs])
    for tile in range(width // LANES):
        total[tile * size : (tile + 1) * size, :] = found[:, tile * LANES : (tile + 1) * LANES]
    for tile in range(width // LANES):
        pieces = [total[strided(tile * size + part, count, PACK), :] for part in range(PACK)]
        for k in range(PACK):
            lanes = slice(k * channels, (k + 1) * channels)
            tiles[strided(tile * PACK + k, count, rows), :] = jnp.concatenate(
                [piece[:, lanes] for piece in pieces], 1
            )
    for tile in range(count):
        out_ref[:, tile * LANES : (tile + 1) * LANES] = tiles[tile * rows : (tile + 1) * rows, :]


def prepare_weight(weight_ref, weight_cat, fold):
    channels = ENTRY_CHANNELS
    for step in range(channels // fold):
        high, low = halves(folded_weight(weight_ref, step, fold))
        weight_cat[step * channels : (step + 1) * channels, :] = jnp.concatenate(
            [high, low, high], 1
        )


def gradient_phase(blocks, cotangent_ref, out_ref, spread_ref, weight_cat):
    fold = fold_of(blocks * cotangent_ref.shape[2])
    slots = slots_of(blocks)

    def step_of(pair, carry):
        high, low = spread_of(cotangent_ref, pair, slots, fold)
        spread_ref[pair, 0] = high
        spread_ref[pair, 1] = low
        found = dot_rows(weight_cat[...], jnp.concatenate([high, high, low], 1))
        out_ref[pair] = jnp.concatenate(halves(found), 1)
        return carry

    lax.fori_loop(0, out_ref.shape[0], step_of, 0, unroll=8)


def gradient_kernel(
    blocks,
    weight_ref,
    cotangent_ref,
    left_ref,
    out_ref,
    spread_ref,
    partial_ref,
    weight_cat,
    flip_hbm,
    left_flip,
    weight_rows,
    weight_flip,
    semaphore,
):
    fold = fold_of(blocks * cotangent_ref.shape[2])
    prepare_weight(weight_ref, weight_cat, fold)
    gradient_phase(blocks, cotangent_ref, out_ref, spread_ref, weight_cat)

    def store(step, found):
        partial_ref[step] = found

    right_phase(left_ref, out_ref, left_flip, store, 1)
    channels = ENTRY_CHANNELS
    wide = weight_rows.shape[1]
    for step in range(channels // fold):
        weight_rows[step * channels : (step + 1) * channels, :] = folded_weight(
            weight_ref, step, fold
        )
    flip_high, flip_low = halves(weight_rows[...].T)
    weight_flip[:wide, :] = flip_high
    weight_flip[wide:, :] = flip_low
    copy = pltpu.make_async_copy(weight_flip, flip_hbm, semaphore)
    copy.start()
    copy.wait()


def peer_kernel(blocks, weight_cat, cotangent_ref, out_ref, spread_ref):
    gradient_phase(blocks, cotangent_ref, out_ref, spread_ref, weight_cat)


def right_phase(left_ref, factor_ref, left_flip, store, loops):
    sequences = left_ref.shape[1]
    lanes = factor_ref.shape[2] // 4
    flip_high, flip_low = halves((left_ref[...] * (1.0 / sequences)).T)
    left_flip[:sequences, :] = flip_high
    left_flip[sequences:, :] = flip_low

    def step_of(step, carry):
        high, low = (
            jnp.concatenate(
                [rows_of_step([factor_ref], 2 * step + part, half, lanes) for part in range(2)], 1
            )
            for half in range(2)
        )
        first = dot(left_flip[...], high)
        second = dot(left_flip[:sequences, :], low)
        store(step, first[:sequences] + first[sequences:] + second)
        return carry

    count = factor_ref.shape[1] // (2 * ENTRY_CHANNELS)
    size = count // loops
    for at in range(loops):
        lax.fori_loop(at * size, (at + 1) * size, step_of, 0, unroll=min(size, 8))


def rows_of_step(refs, step, half, lanes):
    channels = ENTRY_CHANNELS
    rows = pl.ds(pl.multiple_of(step * channels, channels), channels)
    start = 2 * half * lanes
    return jnp.concatenate(
        [
            ref[pair, rows, start + part * lanes : start + (part + 1) * lanes]
            for ref in refs
            for pair in range(ref.shape[0])
            for part in range(2)
        ],
        0,
    )


def both_left(left_refs):
    sequences = left_refs[0].shape[1]
    return jnp.concatenate([ref[...] for ref in left_refs], 0) * (1.0 / sequences)


def right_kernel(
    blocks, depth, peer_ref, left_ref, partial_ref, keep_ref, send_ref, left_flip
):
    fold = fold_of(blocks * depth)
    lanes = fold * blocks * depth

    def store(step, found):
        found = found + partial_ref[step]
        for part in range(2):
            turned = found[:, part * lanes : (part + 1) * lanes].T
            for place in range(fold):
                for slot in range(blocks):
                    start = (place * blocks + slot) * depth
                    row = pl.multiple_of(((2 * step + part) * fold + place) * depth, depth)
                    out_ref = keep_ref if slot < blocks // 2 else send_ref
                    out_ref[slot % (blocks // 2), pl.ds(row, depth), :] = turned[
                        start : start + depth
                    ]

    right_phase(left_ref, peer_ref, left_flip, store, 2)


def halve_kernel(keep_ref, found_ref, keep_out, send_out):
    half = keep_ref.shape[0] // 2
    for slot in range(half):
        keep_out[slot] = keep_ref[slot] + found_ref[slot]
        send_out[slot] = keep_ref[half + slot] + found_ref[half + slot]


def right_rows(right_refs, step, fold, depth):
    return jnp.concatenate(
        [
            ref[pl.ds(pl.multiple_of((step * fold + part) * depth, depth), depth), :]
            for part in range(fold)
            for ref in right_refs
        ],
        0,
    )


def weight_kernel(blocks, depth, own_left, peer_left, own_spread, peer_spread, *refs):
    right_refs = refs[:blocks]
    keep_ref, send_ref, own_out, peer_out, own_ref, peer_ref, total, semaphores = refs[blocks:]
    channels = ENTRY_CHANNELS
    fold = fold_of(blocks * depth)
    lanes = fold * blocks * depth
    pairs = total.shape[1] // fold
    high, low = halves(both_left([own_left, peer_left]))
    left_cat = jnp.concatenate([high, low, high], 1)

    def copies(step):
        size = 2 * channels
        rows = pl.ds(pl.multiple_of(step * size, size), size)
        return [
            pltpu.make_async_copy(ref.at[:, rows], out.at[:, rows], semaphores.at[step, side])
            for side, (ref, out) in enumerate(((own_ref, own_out), (peer_ref, peer_out)))
        ]

    def outer_step(step, carry):
        right = [right_rows(right_refs, 2 * step + part, fold, depth) for part in range(2)]
        high, low = halves(jnp.concatenate(right, 0))
        found = dot_rows(left_cat, jnp.concatenate([high, high, low], 1))
        both = halves(found)
        for part in range(2):
            start = pl.multiple_of((2 * step + part) * channels, channels)
            row = 0
            for ref in (own_ref, peer_ref):
                for index in range(2 * ref.shape[0]):
                    for half in range(2):
                        lane = (2 * half + index % 2) * lanes
                        ref[index // 2, pl.ds(start, channels), lane : lane + lanes] = both[half][
                            row : row + channels, part * lanes : (part + 1) * lanes
                        ]
                    row += channels
        for copy in copies(step):
            copy.start()
        return carry

    lax.fori_loop(0, channels // (2 * fold), outer_step, 0, unroll=4)
    total[...] = jnp.zeros_like(total)

    def weight_step(pair, carry):
        lefts, rights = [], []
        for ref, spread_ref in ((own_ref, own_spread), (peer_ref, peer_spread)):
            high = spread_ref[pair, 0]
            lefts += [ref[pair], ref[pair, :, : 2 * lanes]]
            rights += [high, high, spread_ref[pair, 1]]
        total[...] += dot(jnp.concatenate(lefts, 1), jnp.concatenate(rights, 0))
        return carry

    lax.fori_loop(0, own_ref.shape[0], weight_step, 0, unroll=4)
    core = lax.rem(lax.axis_index("inner"), 2)
    steps = channels // (2 * fold)
    for out_ref, half in ((keep_ref, core), (send_ref, 1 - core)):
        for step in range(steps):
            start = pl.multiple_of((half * steps + step) * channels, channels)
            found = total[pl.ds(start, channels), :]
            for part in range(fold):
                y = step * fold + part
                out_ref[y * channels : (y + 1) * channels, :] = found[
                    :, part * pairs : (part + 1) * pairs
                ]

    def finish(step, carry):
        for copy in copies(step):
            copy.wait()
        return carry

    lax.fori_loop(0, channels // (2 * fold), finish, 0)


def left_kernel(blocks, depth, own_ref, peer_ref, *refs):
    right_refs, out_refs, (total, flipped) = refs[:blocks], refs[blocks:-2], refs[-2:]
    lanes = own_ref.shape[2] // 4
    fold = lanes // (blocks * depth)
    sequences = right_refs[0].shape[1]
    group = 4
    total[...] = jnp.zeros_like(total)

    def step_of(step, carry):
        steps = [group * step + part for part in range(group)]
        right = [right_rows(right_refs, at, fold, depth) for at in steps]
        high, low = halves(jnp.concatenate(right, 0))
        grads = [
            jnp.concatenate([rows_of_step([own_ref, peer_ref], at, half, lanes) for at in steps], 1)
            for half in range(2)
        ]
        both = dot(grads[0], jnp.concatenate([high, low], 1))
        total[...] += both[:, :sequences] + both[:, sequences:] + dot(grads[1], high)
        return carry

    lax.fori_loop(0, ENTRY_CHANNELS // (fold * group), step_of, 0, unroll=4)
    flipped[...] = total[...].T * (1.0 / sequences)
    here = lax.axis_index("inner")
    size, width = out_refs[0].shape[1:]
    for slot, ref in enumerate(out_refs):
        start = pl.multiple_of(lax.bitwise_xor(here, slot) * size, size)
        for side in range(2):
            ref[side] = flipped[pl.ds(start, size), side * width : (side + 1) * width]


def left_add_kernel(*refs):
    parts, (own_out, send_out) = refs[:-2], refs[-2:]
    for side, ref in enumerate((own_out, send_out)):
        ref[...] = functools.reduce(jnp.add, [part[side] for part in parts])


def pair_kernel(blocks, outer_hbm, flip_hbm, out_ref, outer_ref, weight_flip, semaphores):
    depth, pairs = out_ref.shape[2:]
    count = outer_ref.shape[0]
    lanes = outer_ref.shape[2] // 4
    columns = blocks * depth
    fold = lanes // columns
    wide = fold * pairs

    def copy_of(pair):
        return pltpu.make_async_copy(outer_hbm.at[pair], outer_ref.at[pair], semaphores.at[pair])

    flip_copy = pltpu.make_async_copy(flip_hbm, weight_flip, semaphores.at[count])
    flip_copy.start()
    for pair in range(count):
        copy_of(pair).start()
    flip_copy.wait()
    slots = slots_of(blocks)

    def step_of(pair, carry):
        copy_of(pair).wait()
        first = dot(weight_flip[...], outer_ref[pair, :, : 2 * lanes])
        second = dot(weight_flip[:wide, :], outer_ref[pair, :, 2 * lanes :])
        found = first[:wide] + first[wide:] + second
        for part in range(2):
            turned = []
            for place in range(fold):
                start = part * lanes
                piece = found[place * pairs : (place + 1) * pairs, start : start + lanes].T
                turned.append(piece[place * columns : (place + 1) * columns])
            turned = functools.reduce(jnp.add, turned)
            row = 2 * pair + part
            for slot in range(blocks):
                out_ref[row, slots[slot]] = turned[slot * depth : (slot + 1) * depth]
        return carry

    lax.fori_loop(0, count, step_of, 0)


def finish_kernel(own_ref, other_ref, keep_ref, found_ref, *refs):
    left_refs, refs = refs[:-9], refs[-9:]
    pair_hbm, left_out, right_out = refs[:3]
    right_total, right_square, right_tiles, left_total, left_tiles, semaphores = refs[3:]
    parity = lax.rem(lax.axis_index("blk"), 2)
    copies = [
        pltpu.make_async_copy(ref, pair_hbm.at[:, :, side], semaphores.at[at])
        for at, (ref, side) in enumerate(((own_ref, parity), (other_ref, 1 - parity)))
    ]
    for copy in copies:
        copy.start()
    turn_right([keep_ref, found_ref], right_out, right_total, right_square, right_tiles)
    turn_left(left_refs, left_out, left_total, left_tiles)
    for copy in copies:
        copy.wait()


def spread_sum_kernel(in_ref, out_ref):
    found = in_ref[0]
    for part in range(1, in_ref.shape[0]):
        found = found + in_ref[part]
    for part in range(in_ref.shape[0]):
        out_ref[part] = found


def place_kernel(mine_ref, other_ref, out_ref):
    channels = ENTRY_CHANNELS
    core = lax.rem(lax.axis_index("inner"), 2)
    steps = mine_ref.shape[0] // channels
    for ref, half in ((mine_ref, core), (other_ref, 1 - core)):
        for step in range(steps):
            rows = ref[step * channels : (step + 1) * channels, :]
            out_ref[strided(half * steps + step, channels, channels), :] = rows


def shape(*sizes, kind=F32):
    return jax.ShapeDtypeStruct(sizes, kind)


def call(
    kernel,
    out_shape,
    scratch=(),
    name=None,
    limit=16 * MIB,
    far=(),
    after=(),
    out_specs=None,
    flops=1,
):
    def run(*operands):
        vmem = pl.BlockSpec(memory_space=pltpu.VMEM)
        hbm = pl.BlockSpec(memory_space=pltpu.HBM)
        in_specs = [pl.BlockSpec(memory_space=pl.ANY)] * len(after)
        in_specs += [hbm if at in far else vmem for at in range(len(operands))]
        operands = [
            pltpu.with_memory_space_constraint(operand, pltpu.HBM) if at in far else operand
            for at, operand in enumerate(operands)
        ]
        extra = {} if out_specs is None else {"out_specs": out_specs}
        return pl.pallas_call(
            lambda *refs: kernel(*refs[len(after) :]),
            out_shape=out_shape,
            in_specs=in_specs,
            scratch_shapes=list(scratch),
            compiler_params=pltpu.CompilerParams(vmem_limit_bytes=limit),
            cost_estimate=pl.CostEstimate(flops=flops, bytes_accessed=1, transcendentals=0),
            name=name,
            **extra,
        )(*after, *operands)

    return run


def local(alignment_left, alignment_right, projection_matrix, cotangent):
    rows, features = alignment_left.shape
    depth = alignment_right.shape[0]
    count = lax.axis_size("blk")
    inner = lax.axis_size("inner")
    channels = ENTRY_CHANNELS
    sequences = features // channels
    outer, pairs = projection_matrix.shape
    blocks = count // 2
    fold = fold_of(blocks * depth)
    lanes = fold * blocks * depth
    tall = outer // fold
    steps = channels // fold
    row_pairs = rows // 2
    everyone = ("blk", "inner")

    partner = [(here, here ^ 1) for here in range(count)]
    slot_moves = [[(here, here ^ (2 * slot)) for here in range(count)] for slot in range(blocks)]
    inner_moves = [[(here, here ^ slot) for here in range(inner)] for slot in range(inner)]
    cores = [(here, here ^ 1) for here in range(inner)]
    core_groups = [list(range(core, count * inner, 2)) for core in range(2)]

    limit = 20 * MIB * max(1, blocks * depth * fold // LANES * 2 // fold)
    large = functools.partial(call, limit=limit)
    work = 4 * 2 * rows * 2 * blocks * depth * outer * pairs * 3

    by_side = cotangent.reshape(rows, blocks, 2, depth, pairs)
    half_cotangent = shape(rows, blocks, depth, pairs)
    right, left, cotangent_send, cotangent_own, weight = call(
        prepare_kernel,
        [
            shape(channels * depth, sequences),
            shape(rows * channels, sequences),
            half_cotangent,
            half_cotangent,
            shape(outer, pairs),
        ],
        [
            pltpu.VMEM((2, rows, features), F32),
            pltpu.VMEM((2, rows * features // LANES, LANES), F32),
            pltpu.VMEM((2, rows // PACK, LANES, LANES), F32),
            pltpu.SemaphoreType.DMA((5,)),
        ],
        name="prepare",
        far=range(4),
    )(by_side, alignment_right, alignment_left, projection_matrix)
    cotangent_peer = lax.ppermute(cotangent_send, "blk", partner)
    left_peer = lax.ppermute(left, "blk", partner)

    vmem = pl.BlockSpec(memory_space=pltpu.VMEM)
    hbm = pl.BlockSpec(memory_space=pltpu.HBM)
    factor = shape(row_pairs, tall, 4 * lanes, kind=BF16)
    factor_scratch = pltpu.VMEM(factor.shape, BF16)
    weight_cat = shape(tall, 3 * fold * pairs, kind=BF16)
    flip_scratch = pltpu.VMEM((2 * sequences, rows * channels), BF16)
    flip_sizes = (2 * fold * pairs, tall)
    spread = shape(row_pairs, 2, 2 * lanes, fold * pairs, kind=BF16)
    grad_own, spread_own, partial, weight_cat, weight_flip = large(
        functools.partial(gradient_kernel, blocks),
        [
            factor,
            spread,
            shape(steps // 2, sequences, 2 * lanes),
            weight_cat,
            pltpu.HBM(flip_sizes, BF16),
        ],
        [
            flip_scratch,
            pltpu.VMEM((tall, fold * pairs), F32),
            pltpu.VMEM(flip_sizes, BF16),
            pltpu.SemaphoreType.DMA,
        ],
        "gradient_own",
        out_specs=[vmem, vmem, vmem, vmem, hbm],
    )(weight, cotangent_own, left)
    grad_peer, spread_peer = large(
        functools.partial(peer_kernel, blocks), [factor, spread], [], "gradient_peer"
    )(weight_cat, cotangent_peer)
    rights = {0: right}
    distance = blocks // 2
    while distance:
        for slot in list(rights):
            sent = rights[slot]
            if slot:
                sent, _ = lax.optimization_barrier((sent, grad_peer))
            rights[slot + distance] = lax.ppermute(sent, "blk", slot_moves[distance])
        distance = distance // 2
    rights = [rights[slot] for slot in range(blocks)]
    right_half = shape(blocks // 2, channels * depth, sequences)
    right_keep, right_send = large(
        functools.partial(right_kernel, blocks, depth),
        [right_half, right_half],
        [flip_scratch],
        "right_parts",
    )(grad_peer, left_peer, partial)
    right_send = lax.ppermute(right_send, "blk", slot_moves[blocks // 2])

    keep, send, outer_own, outer_peer = large(
        functools.partial(weight_kernel, blocks, depth),
        [shape(outer // 2, pairs)] * 2 + [pltpu.HBM(factor.shape, BF16)] * 2,
        [
            factor_scratch,
            factor_scratch,
            pltpu.VMEM((tall, fold * pairs), F32),
            pltpu.SemaphoreType.DMA((steps // 2, 2)),
        ],
        "weight",
        after=[right_keep],
        flops=2 * work,
        out_specs=[vmem, vmem, hbm, hbm],
    )(left, left_peer, spread_own, spread_peer, *rights)
    sent = lax.ppermute(send, "inner", cores)

    size = sequences // inner
    left_parts = large(
        functools.partial(left_kernel, blocks, depth),
        [shape(2, size, rows * channels)] * inner,
        [
            pltpu.VMEM((2 * rows * channels, sequences), F32),
            pltpu.VMEM((sequences, 2 * rows * channels), F32),
        ],
        "left_parts",
        after=[keep],
        flops=work,
    )(grad_own, grad_peer, *rights)
    keep, *left_parts = lax.optimization_barrier((keep, *left_parts))
    members = count * inner // 2
    pieces = (keep + sent).reshape(members, outer // 2 // members, pairs)

    def pair(values, after, name):
        return large(
            functools.partial(pair_kernel, blocks),
            shape(rows, blocks, depth, pairs),
            [
                factor_scratch,
                pltpu.VMEM(flip_sizes, BF16),
                pltpu.SemaphoreType.DMA((row_pairs + 1,)),
            ],
            name,
            far=[0, 1],
            after=after,
            flops=work,
        )(values, weight_flip)

    pair_other = pair(outer_peer, [pieces], "pair_peer")
    pair_found = lax.ppermute(pair_other, "blk", partner)
    slot = blocks // 4
    while slot:
        part = shape(slot, channels * depth, sequences)
        right_keep, right_send = call(
            halve_kernel, [part, part], name="right_halve", after=[pair_other]
        )(right_keep, right_send)
        right_send = lax.ppermute(right_send, "blk", slot_moves[slot])
        slot = slot // 2

    _, *left_parts = lax.optimization_barrier((right_keep, *left_parts))
    left_parts = [
        lax.ppermute(part, "inner", inner_moves[slot]) if slot else part
        for slot, part in enumerate(left_parts)
    ]
    pieces = lax.all_to_all(pieces, everyone, 0, 0, axis_index_groups=core_groups)
    pieces = call(
        spread_sum_kernel,
        shape(*pieces.shape),
        name="weight_sum",
        after=[pair_other, right_keep],
    )(pieces)
    pair_own = pair(outer_own, [pieces], "pair_own")
    left_own, left_send = call(
        left_add_kernel, [shape(size, rows * channels)] * 2, name="left_add", after=[pieces]
    )(*left_parts)
    pieces = lax.all_to_all(pieces, everyone, 0, 0, axis_index_groups=core_groups)

    left_found = [left_own, lax.ppermute(left_send, "blk", partner)]
    pair_update, grad_left, grad_right = call(
        finish_kernel,
        [
            pltpu.HBM(by_side.shape, F32),
            shape(rows, features // inner),
            shape(depth, features),
        ],
        [
            pltpu.VMEM((channels * depth, sequences), F32),
            pltpu.VMEM((depth // PACK, LANES, LANES), F32),
            pltpu.VMEM((depth * features // LANES, LANES), F32),
            pltpu.VMEM((size * rows * channels // LANES, LANES), F32),
            pltpu.VMEM((rows * features // inner // LANES, LANES), F32),
            pltpu.SemaphoreType.DMA((2,)),
        ],
        "finish",
        out_specs=[hbm, vmem, vmem],
    )(pair_own, pair_found, right_keep, right_send, *left_found)
    pair_update = pair_update.reshape(cotangent.shape)

    pieces, pair_update, grad_left, grad_right = lax.optimization_barrier(
        (pieces, pair_update, grad_left, grad_right)
    )
    mine = pieces.reshape(outer // 2, pairs)
    other = lax.ppermute(mine, "inner", cores)
    grad_weight = call(place_kernel, shape(outer, pairs), name="place")(mine, other)
    return (pair_update, grad_left, grad_right, grad_weight)


def solution(mesh):
    placed = (
        P(("groups", "blk"), None),
        P(("groups", "blk", "inner"), None),
        P(),
        P(("groups", "blk"), None, "inner", None),
    )
    return jax.shard_map(
        local,
        mesh=mesh,
        in_specs=placed,
        out_specs=(
            P(("groups", "blk"), None, "inner", None),
            P(("groups", "blk"), "inner"),
            P(("groups", "blk", "inner"), None),
            P("groups", None),
        ),
        check_vma=False,
    )
```

```python
import functools

import jax
import jax.numpy as jnp
from jax import lax
from jax.experimental import pallas as pl
from jax.experimental.pallas import tpu as pltpu
from jax.sharding import PartitionSpec as P

ENTRY_CHANNELS = 32
LANES = 128
PACK = LANES // ENTRY_CHANNELS
F32 = jnp.float32
BF16 = jnp.bfloat16
MIB = 1024 * 1024


def halves(values):
    high = values.astype(BF16)
    low = (values - high.astype(F32)).astype(BF16)
    return high, low


def dot(left, right):
    return jnp.dot(left, right, preferred_element_type=F32)


def dot_rows(left, right):
    return lax.dot_general(left, right, (((1,), (1,)), ((), ())), preferred_element_type=F32)


def fold_of(columns):
    return max(1, LANES // columns)


def strided(start, size, stride):
    return pl.ds(start, size, stride=stride)


def folded_weight(weight_ref, step, fold):
    channels = ENTRY_CHANNELS
    return jnp.concatenate(
        [weight_ref[strided(step * fold + part, channels, channels), :] for part in range(fold)], 1
    )


def slots_of(blocks):
    here = lax.axis_index("blk") // 2
    return [lax.bitwise_xor(here, slot) for slot in range(blocks)]


def spread_of(cotangent_ref, pair, slots, fold):
    columns = len(slots) * cotangent_ref.shape[2]
    empty = jnp.zeros((columns, cotangent_ref.shape[3]), BF16)
    spread = ([], [])
    for part in range(2):
        rows = jnp.concatenate([cotangent_ref[2 * pair + part, slot] for slot in slots], 0)
        for found, values in zip(spread, halves(rows)):
            for place in range(fold):
                found.append(
                    jnp.concatenate(
                        [values if place == other else empty for other in range(fold)], 1
                    )
                )
    return [jnp.concatenate(found, 0) for found in spread]


def turn_in(rows_minor, in_ref, out_ref, tiles, square):
    channels = ENTRY_CHANNELS
    rows, features = in_ref.shape
    count = features // LANES
    for tile in range(count):
        tiles[tile * rows : (tile + 1) * rows, :] = in_ref[:, tile * LANES : (tile + 1) * LANES]
    for group in range(rows // PACK):
        found = [tiles[strided(group * PACK + k, count, rows), :] for k in range(PACK)]
        for part in range(PACK):
            lanes = slice(part * channels, (part + 1) * channels)
            square[group, strided(part, count, PACK), :] = jnp.concatenate(
                [values[:, lanes] for values in found], 1
            )
        turned = square[group].T
        if rows_minor:
            for k in range(PACK):
                out_ref[strided(group * PACK + k, channels, rows), :] = turned[
                    k * channels : (k + 1) * channels
                ]
        else:
            out_ref[group * LANES : (group + 1) * LANES, :] = turned


def prepare_kernel(
    cotangent_hbm,
    right_hbm,
    left_hbm,
    weight_hbm,
    right_out,
    left_out,
    send_out,
    own_out,
    weight_out,
    inputs,
    tiles,
    square,
    semaphores,
):
    parity = lax.rem(lax.axis_index("blk"), 2)
    moves = (
        (right_hbm, inputs.at[0]),
        (left_hbm, inputs.at[1]),
        (cotangent_hbm.at[:, :, 1 - parity], send_out),
        (cotangent_hbm.at[:, :, parity], own_out),
        (weight_hbm, weight_out),
    )
    copies = [
        pltpu.make_async_copy(source, target, semaphores.at[at])
        for at, (source, target) in enumerate(moves)
    ]
    for copy in copies:
        copy.start()
    copies[0].wait()
    turn_in(True, inputs.at[0], right_out, tiles.at[0], square.at[0])
    copies[1].wait()
    turn_in(False, inputs.at[1], left_out, tiles.at[1], square.at[1])
    for copy in copies[2:]:
        copy.wait()


def turn_right(part_refs, out_ref, total, square, tiles):
    channels = ENTRY_CHANNELS
    rows, features = out_ref.shape
    count = features // LANES
    total[...] = functools.reduce(jnp.add, [ref[0] for ref in part_refs])
    for group in range(rows // PACK):
        stacked = [total[strided(group * PACK + k, channels, rows), :] for k in range(PACK)]
        square[group] = jnp.concatenate(stacked, 0).T
        pieces = [square[group, strided(part, count, PACK), :] for part in range(PACK)]
        for k in range(PACK):
            lanes = slice(k * channels, (k + 1) * channels)
            tiles[strided(group * PACK + k, count, rows), :] = jnp.concatenate(
                [piece[:, lanes] for piece in pieces], 1
            )
    for tile in range(count):
        out_ref[:, tile * LANES : (tile + 1) * LANES] = tiles[tile * rows : (tile + 1) * rows, :]


def turn_left(part_refs, out_ref, total, tiles):
    channels = ENTRY_CHANNELS
    size, width = part_refs[0].shape
    rows, features = out_ref.shape
    count = features // LANES
    found = functools.reduce(jnp.add, [ref[...] for ref in part_refs])
    for tile in range(width // LANES):
        total[tile * size : (tile + 1) * size, :] = found[:, tile * LANES : (tile + 1) * LANES]
    for tile in range(width // LANES):
        pieces = [total[strided(tile * size + part, count, PACK), :] for part in range(PACK)]
        for k in range(PACK):
            lanes = slice(k * channels, (k + 1) * channels)
            tiles[strided(tile * PACK + k, count, rows), :] = jnp.concatenate(
                [piece[:, lanes] for piece in pieces], 1
            )
    for tile in range(count):
        out_ref[:, tile * LANES : (tile + 1) * LANES] = tiles[tile * rows : (tile + 1) * rows, :]


def prepare_weight(weight_ref, weight_cat, fold):
    channels = ENTRY_CHANNELS
    for step in range(channels // fold):
        high, low = halves(folded_weight(weight_ref, step, fold))
        weight_cat[step * channels : (step + 1) * channels, :] = jnp.concatenate(
            [high, low, high], 1
        )


def gradient_phase(blocks, cotangent_ref, out_ref, spread_ref, weight_cat):
    fold = fold_of(blocks * cotangent_ref.shape[2])
    slots = slots_of(blocks)

    def step_of(pair, carry):
        high, low = spread_of(cotangent_ref, pair, slots, fold)
        spread_ref[pair, 0] = high
        spread_ref[pair, 1] = low
        found = dot_rows(weight_cat[...], jnp.concatenate([high, high, low], 1))
        out_ref[pair] = jnp.concatenate(halves(found), 1)
        return carry

    lax.fori_loop(0, out_ref.shape[0], step_of, 0, unroll=8)


def gradient_kernel(
    blocks,
    weight_ref,
    cotangent_ref,
    left_ref,
    out_ref,
    spread_ref,
    partial_ref,
    weight_cat,
    flip_hbm,
    left_flip,
    weight_rows,
    weight_flip,
    semaphore,
):
    fold = fold_of(blocks * cotangent_ref.shape[2])
    prepare_weight(weight_ref, weight_cat, fold)
    gradient_phase(blocks, cotangent_ref, out_ref, spread_ref, weight_cat)

    def store(step, found):
        partial_ref[step] = found

    right_phase(left_ref, out_ref, left_flip, store, 1)
    channels = ENTRY_CHANNELS
    wide = weight_rows.shape[1]
    for step in range(channels // fold):
        weight_rows[step * channels : (step + 1) * channels, :] = folded_weight(
            weight_ref, step, fold
        )
    flip_high, flip_low = halves(weight_rows[...].T)
    weight_flip[:wide, :] = flip_high
    weight_flip[wide:, :] = flip_low
    copy = pltpu.make_async_copy(weight_flip, flip_hbm, semaphore)
    copy.start()
    copy.wait()


def peer_kernel(blocks, weight_cat, cotangent_ref, out_ref, spread_ref):
    gradient_phase(blocks, cotangent_ref, out_ref, spread_ref, weight_cat)


def right_phase(left_ref, factor_ref, left_flip, store, loops):
    sequences = left_ref.shape[1]
    lanes = factor_ref.shape[2] // 4
    flip_high, flip_low = halves((left_ref[...] * (1.0 / sequences)).T)
    left_flip[:sequences, :] = flip_high
    left_flip[sequences:, :] = flip_low

    def step_of(step, carry):
        high, low = (
            jnp.concatenate(
                [rows_of_step([factor_ref], 2 * step + part, half, lanes) for part in range(2)], 1
            )
            for half in range(2)
        )
        first = dot(left_flip[...], high)
        second = dot(left_flip[:sequences, :], low)
        store(step, first[:sequences] + first[sequences:] + second)
        return carry

    count = factor_ref.shape[1] // (2 * ENTRY_CHANNELS)
    size = count // loops
    for at in range(loops):
        lax.fori_loop(at * size, (at + 1) * size, step_of, 0, unroll=min(size, 8))


def rows_of_step(refs, step, half, lanes):
    channels = ENTRY_CHANNELS
    rows = pl.ds(pl.multiple_of(step * channels, channels), channels)
    start = 2 * half * lanes
    return jnp.concatenate(
        [
            ref[pair, rows, start + part * lanes : start + (part + 1) * lanes]
            for ref in refs
            for pair in range(ref.shape[0])
            for part in range(2)
        ],
        0,
    )


def both_left(left_refs):
    sequences = left_refs[0].shape[1]
    return jnp.concatenate([ref[...] for ref in left_refs], 0) * (1.0 / sequences)


def right_kernel(
    blocks, depth, peer_ref, left_ref, partial_ref, keep_ref, send_ref, left_flip
):
    fold = fold_of(blocks * depth)
    lanes = fold * blocks * depth

    def store(step, found):
        found = found + partial_ref[step]
        for part in range(2):
            turned = found[:, part * lanes : (part + 1) * lanes].T
            for place in range(fold):
                for slot in range(blocks):
                    start = (place * blocks + slot) * depth
                    row = pl.multiple_of(((2 * step + part) * fold + place) * depth, depth)
                    out_ref = keep_ref if slot < blocks // 2 else send_ref
                    out_ref[slot % (blocks // 2), pl.ds(row, depth), :] = turned[
                        start : start + depth
                    ]

    right_phase(left_ref, peer_ref, left_flip, store, 2)


def halve_kernel(keep_ref, found_ref, keep_out, send_out):
    half = keep_ref.shape[0] // 2
    for slot in range(half):
        keep_out[slot] = keep_ref[slot] + found_ref[slot]
        send_out[slot] = keep_ref[half + slot] + found_ref[half + slot]


def right_rows(right_refs, step, fold, depth):
    return jnp.concatenate(
        [
            ref[pl.ds(pl.multiple_of((step * fold + part) * depth, depth), depth), :]
            for part in range(fold)
            for ref in right_refs
        ],
        0,
    )


def weight_kernel(blocks, depth, own_left, peer_left, own_spread, peer_spread, *refs):
    right_refs = refs[:blocks]
    keep_ref, send_ref, own_out, peer_out, own_ref, peer_ref, total, semaphores = refs[blocks:]
    channels = ENTRY_CHANNELS
    fold = fold_of(blocks * depth)
    lanes = fold * blocks * depth
    pairs = total.shape[1] // fold
    high, low = halves(both_left([own_left, peer_left]))
    left_cat = jnp.concatenate([high, low, high], 1)

    def copies(step):
        size = 2 * channels
        rows = pl.ds(pl.multiple_of(step * size, size), size)
        return [
            pltpu.make_async_copy(ref.at[:, rows], out.at[:, rows], semaphores.at[step, side])
            for side, (ref, out) in enumerate(((own_ref, own_out), (peer_ref, peer_out)))
        ]

    def outer_step(step, carry):
        right = [right_rows(right_refs, 2 * step + part, fold, depth) for part in range(2)]
        high, low = halves(jnp.concatenate(right, 0))
        found = dot_rows(left_cat, jnp.concatenate([high, high, low], 1))
        both = halves(found)
        for part in range(2):
            start = pl.multiple_of((2 * step + part) * channels, channels)
            row = 0
            for ref in (own_ref, peer_ref):
                for index in range(2 * ref.shape[0]):
                    for half in range(2):
                        lane = (2 * half + index % 2) * lanes
                        ref[index // 2, pl.ds(start, channels), lane : lane + lanes] = both[half][
                            row : row + channels, part * lanes : (part + 1) * lanes
                        ]
                    row += channels
        for copy in copies(step):
            copy.start()
        return carry

    lax.fori_loop(0, channels // (2 * fold), outer_step, 0, unroll=4)
    total[...] = jnp.zeros_like(total)

    def weight_step(pair, carry):
        lefts, rights = [], []
        for ref, spread_ref in ((own_ref, own_spread), (peer_ref, peer_spread)):
            high = spread_ref[pair, 0]
            lefts += [ref[pair], ref[pair, :, : 2 * lanes]]
            rights += [high, high, spread_ref[pair, 1]]
        total[...] += dot(jnp.concatenate(lefts, 1), jnp.concatenate(rights, 0))
        return carry

    lax.fori_loop(0, own_ref.shape[0], weight_step, 0, unroll=4)
    core = lax.rem(lax.axis_index("inner"), 2)
    steps = channels // (2 * fold)
    for out_ref, half in ((keep_ref, core), (send_ref, 1 - core)):
        for step in range(steps):
            start = pl.multiple_of((half * steps + step) * channels, channels)
            found = total[pl.ds(start, channels), :]
            for part in range(fold):
                y = step * fold + part
                out_ref[y * channels : (y + 1) * channels, :] = found[
                    :, part * pairs : (part + 1) * pairs
                ]

    def finish(step, carry):
        for copy in copies(step):
            copy.wait()
        return carry

    lax.fori_loop(0, channels // (2 * fold), finish, 0)


def left_kernel(blocks, depth, own_ref, peer_ref, *refs):
    right_refs, out_refs, (total, flipped) = refs[:blocks], refs[blocks:-2], refs[-2:]
    lanes = own_ref.shape[2] // 4
    fold = lanes // (blocks * depth)
    sequences = right_refs[0].shape[1]
    group = 4
    total[...] = jnp.zeros_like(total)

    def step_of(step, carry):
        steps = [group * step + part for part in range(group)]
        right = [right_rows(right_refs, at, fold, depth) for at in steps]
        high, low = halves(jnp.concatenate(right, 0))
        grads = [
            jnp.concatenate([rows_of_step([own_ref, peer_ref], at, half, lanes) for at in steps], 1)
            for half in range(2)
        ]
        both = dot(grads[0], jnp.concatenate([high, low], 1))
        total[...] += both[:, :sequences] + both[:, sequences:] + dot(grads[1], high)
        return carry

    lax.fori_loop(0, ENTRY_CHANNELS // (fold * group), step_of, 0, unroll=4)
    flipped[...] = total[...].T * (1.0 / sequences)
    here = lax.axis_index("inner")
    size, width = out_refs[0].shape[1:]
    for slot, ref in enumerate(out_refs):
        start = pl.multiple_of(lax.bitwise_xor(here, slot) * size, size)
        for side in range(2):
            ref[side] = flipped[pl.ds(start, size), side * width : (side + 1) * width]


def left_add_kernel(*refs):
    parts, (own_out, send_out) = refs[:-2], refs[-2:]
    for side, ref in enumerate((own_out, send_out)):
        ref[...] = functools.reduce(jnp.add, [part[side] for part in parts])


def pair_kernel(blocks, outer_hbm, flip_hbm, out_ref, outer_ref, weight_flip, semaphores):
    depth, pairs = out_ref.shape[2:]
    count = outer_ref.shape[0]
    lanes = outer_ref.shape[2] // 4
    columns = blocks * depth
    fold = lanes // columns
    wide = fold * pairs

    def copy_of(pair):
        return pltpu.make_async_copy(outer_hbm.at[pair], outer_ref.at[pair], semaphores.at[pair])

    flip_copy = pltpu.make_async_copy(flip_hbm, weight_flip, semaphores.at[count])
    flip_copy.start()
    for pair in range(count):
        copy_of(pair).start()
    flip_copy.wait()
    slots = slots_of(blocks)

    def step_of(pair, carry):
        copy_of(pair).wait()
        first = dot(weight_flip[...], outer_ref[pair, :, : 2 * lanes])
        second = dot(weight_flip[:wide, :], outer_ref[pair, :, 2 * lanes :])
        found = first[:wide] + first[wide:] + second
        for part in range(2):
            turned = []
            for place in range(fold):
                start = part * lanes
                piece = found[place * pairs : (place + 1) * pairs, start : start + lanes].T
                turned.append(piece[place * columns : (place + 1) * columns])
            turned = functools.reduce(jnp.add, turned)
            row = 2 * pair + part
            for slot in range(blocks):
                out_ref[row, slots[slot]] = turned[slot * depth : (slot + 1) * depth]
        return carry

    lax.fori_loop(0, count, step_of, 0)


def finish_kernel(own_ref, other_ref, keep_ref, found_ref, *refs):
    left_refs, refs = refs[:-9], refs[-9:]
    pair_hbm, left_out, right_out = refs[:3]
    right_total, right_square, right_tiles, left_total, left_tiles, semaphores = refs[3:]
    parity = lax.rem(lax.axis_index("blk"), 2)
    copies = [
        pltpu.make_async_copy(ref, pair_hbm.at[:, :, side], semaphores.at[at])
        for at, (ref, side) in enumerate(((own_ref, parity), (other_ref, 1 - parity)))
    ]
    for copy in copies:
        copy.start()
    turn_right([keep_ref, found_ref], right_out, right_total, right_square, right_tiles)
    turn_left(left_refs, left_out, left_total, left_tiles)
    for copy in copies:
        copy.wait()


def spread_sum_kernel(in_ref, out_ref):
    found = in_ref[0]
    for part in range(1, in_ref.shape[0]):
        found = found + in_ref[part]
    for part in range(in_ref.shape[0]):
        out_ref[part] = found


def place_kernel(mine_ref, other_ref, out_ref):
    channels = ENTRY_CHANNELS
    core = lax.rem(lax.axis_index("inner"), 2)
    steps = mine_ref.shape[0] // channels
    for ref, half in ((mine_ref, core), (other_ref, 1 - core)):
        for step in range(steps):
            rows = ref[step * channels : (step + 1) * channels, :]
            out_ref[strided(half * steps + step, channels, channels), :] = rows


def shape(*sizes, kind=F32):
    return jax.ShapeDtypeStruct(sizes, kind)


def call(
    kernel,
    out_shape,
    scratch=(),
    name=None,
    limit=16 * MIB,
    far=(),
    after=(),
    out_specs=None,
    flops=1,
):
    def run(*operands):
        vmem = pl.BlockSpec(memory_space=pltpu.VMEM)
        hbm = pl.BlockSpec(memory_space=pltpu.HBM)
        in_specs = [pl.BlockSpec(memory_space=pl.ANY)] * len(after)
        in_specs += [hbm if at in far else vmem for at in range(len(operands))]
        operands = [
            pltpu.with_memory_space_constraint(operand, pltpu.HBM) if at in far else operand
            for at, operand in enumerate(operands)
        ]
        extra = {} if out_specs is None else {"out_specs": out_specs}
        return pl.pallas_call(
            lambda *refs: kernel(*refs[len(after) :]),
            out_shape=out_shape,
            in_specs=in_specs,
            scratch_shapes=list(scratch),
            compiler_params=pltpu.CompilerParams(vmem_limit_bytes=limit),
            cost_estimate=pl.CostEstimate(flops=flops, bytes_accessed=1, transcendentals=0),
            name=name,
            **extra,
        )(*after, *operands)

    return run


def local(alignment_left, alignment_right, projection_matrix, cotangent):
    rows, features = alignment_left.shape
    depth = alignment_right.shape[0]
    count = lax.axis_size("blk")
    inner = lax.axis_size("inner")
    channels = ENTRY_CHANNELS
    sequences = features // channels
    outer, pairs = projection_matrix.shape
    blocks = count // 2
    fold = fold_of(blocks * depth)
    lanes = fold * blocks * depth
    tall = outer // fold
    steps = channels // fold
    row_pairs = rows // 2
    everyone = ("blk", "inner")

    partner = [(here, here ^ 1) for here in range(count)]
    slot_moves = [[(here, here ^ (2 * slot)) for here in range(count)] for slot in range(blocks)]
    inner_moves = [[(here, here ^ slot) for here in range(inner)] for slot in range(inner)]
    cores = [(here, here ^ 1) for here in range(inner)]
    core_groups = [list(range(core, count * inner, 2)) for core in range(2)]

    limit = 20 * MIB * max(1, blocks * depth * fold // LANES * 2 // fold)
    large = functools.partial(call, limit=limit)
    work = 4 * 2 * rows * 2 * blocks * depth * outer * pairs * 3

    by_side = cotangent.reshape(rows, blocks, 2, depth, pairs)
    half_cotangent = shape(rows, blocks, depth, pairs)
    right, left, cotangent_send, cotangent_own, weight = call(
        prepare_kernel,
        [
            shape(channels * depth, sequences),
            shape(rows * channels, sequences),
            half_cotangent,
            half_cotangent,
            shape(outer, pairs),
        ],
        [
            pltpu.VMEM((2, rows, features), F32),
            pltpu.VMEM((2, rows * features // LANES, LANES), F32),
            pltpu.VMEM((2, rows // PACK, LANES, LANES), F32),
            pltpu.SemaphoreType.DMA((5,)),
        ],
        name="prepare",
        far=range(4),
    )(by_side, alignment_right, alignment_left, projection_matrix)
    cotangent_peer = lax.ppermute(cotangent_send, "blk", partner)
    left_peer = lax.ppermute(left, "blk", partner)

    vmem = pl.BlockSpec(memory_space=pltpu.VMEM)
    hbm = pl.BlockSpec(memory_space=pltpu.HBM)
    factor = shape(row_pairs, tall, 4 * lanes, kind=BF16)
    factor_scratch = pltpu.VMEM(factor.shape, BF16)
    weight_cat = shape(tall, 3 * fold * pairs, kind=BF16)
    flip_scratch = pltpu.VMEM((2 * sequences, rows * channels), BF16)
    flip_sizes = (2 * fold * pairs, tall)
    spread = shape(row_pairs, 2, 2 * lanes, fold * pairs, kind=BF16)
    grad_own, spread_own, partial, weight_cat, weight_flip = large(
        functools.partial(gradient_kernel, blocks),
        [
            factor,
            spread,
            shape(steps // 2, sequences, 2 * lanes),
            weight_cat,
            pltpu.HBM(flip_sizes, BF16),
        ],
        [
            flip_scratch,
            pltpu.VMEM((tall, fold * pairs), F32),
            pltpu.VMEM(flip_sizes, BF16),
            pltpu.SemaphoreType.DMA,
        ],
        "gradient_own",
        out_specs=[vmem, vmem, vmem, vmem, hbm],
    )(weight, cotangent_own, left)
    grad_peer, spread_peer = large(
        functools.partial(peer_kernel, blocks), [factor, spread], [], "gradient_peer"
    )(weight_cat, cotangent_peer)
    rights = {0: right}
    distance = blocks // 2
    while distance:
        for slot in list(rights):
            sent = rights[slot]
            if slot:
                sent, _ = lax.optimization_barrier((sent, grad_own))
            rights[slot + distance] = lax.ppermute(sent, "blk", slot_moves[distance])
        distance = distance // 2
    rights = [rights[slot] for slot in range(blocks)]
    right_half = shape(blocks // 2, channels * depth, sequences)
    right_keep, right_send = large(
        functools.partial(right_kernel, blocks, depth),
        [right_half, right_half],
        [flip_scratch],
        "right_parts",
    )(grad_peer, left_peer, partial)
    right_send = lax.ppermute(right_send, "blk", slot_moves[blocks // 2])

    keep, send, outer_own, outer_peer = large(
        functools.partial(weight_kernel, blocks, depth),
        [shape(outer // 2, pairs)] * 2 + [pltpu.HBM(factor.shape, BF16)] * 2,
        [
            factor_scratch,
            factor_scratch,
            pltpu.VMEM((tall, fold * pairs), F32),
            pltpu.SemaphoreType.DMA((steps // 2, 2)),
        ],
        "weight",
        after=[right_keep],
        flops=2 * work,
        out_specs=[vmem, vmem, hbm, hbm],
    )(left, left_peer, spread_own, spread_peer, *rights)
    sent = lax.ppermute(send, "inner", cores)

    size = sequences // inner
    left_parts = large(
        functools.partial(left_kernel, blocks, depth),
        [shape(2, size, rows * channels)] * inner,
        [
            pltpu.VMEM((2 * rows * channels, sequences), F32),
            pltpu.VMEM((sequences, 2 * rows * channels), F32),
        ],
        "left_parts",
        after=[keep],
        flops=work,
    )(grad_own, grad_peer, *rights)
    keep, *left_parts = lax.optimization_barrier((keep, *left_parts))
    members = count * inner // 2
    pieces = (keep + sent).reshape(members, outer // 2 // members, pairs)

    def pair(values, after, name):
        return large(
            functools.partial(pair_kernel, blocks),
            shape(rows, blocks, depth, pairs),
            [
                factor_scratch,
                pltpu.VMEM(flip_sizes, BF16),
                pltpu.SemaphoreType.DMA((row_pairs + 1,)),
            ],
            name,
            far=[0, 1],
            after=after,
            flops=work,
        )(values, weight_flip)

    pair_other = pair(outer_peer, [pieces], "pair_peer")
    pair_found = lax.ppermute(pair_other, "blk", partner)
    slot = blocks // 4
    while slot:
        part = shape(slot, channels * depth, sequences)
        right_keep, right_send = call(
            halve_kernel, [part, part], name="right_halve", after=[pair_other]
        )(right_keep, right_send)
        right_send = lax.ppermute(right_send, "blk", slot_moves[slot])
        slot = slot // 2

    _, *left_parts = lax.optimization_barrier((right_keep, *left_parts))
    left_parts = [
        lax.ppermute(part, "inner", inner_moves[slot]) if slot else part
        for slot, part in enumerate(left_parts)
    ]
    pieces = lax.all_to_all(pieces, everyone, 0, 0, axis_index_groups=core_groups)
    pieces = call(
        spread_sum_kernel,
        shape(*pieces.shape),
        name="weight_sum",
        after=[pair_other, right_keep],
    )(pieces)
    pair_own = pair(outer_own, [pieces], "pair_own")
    left_own, left_send = call(
        left_add_kernel, [shape(size, rows * channels)] * 2, name="left_add", after=[pieces]
    )(*left_parts)
    pieces = lax.all_to_all(pieces, everyone, 0, 0, axis_index_groups=core_groups)

    left_found = [left_own, lax.ppermute(left_send, "blk", partner)]
    pair_update, grad_left, grad_right = call(
        finish_kernel,
        [
            pltpu.HBM(by_side.shape, F32),
            shape(rows, features // inner),
            shape(depth, features),
        ],
        [
            pltpu.VMEM((channels * depth, sequences), F32),
            pltpu.VMEM((depth // PACK, LANES, LANES), F32),
            pltpu.VMEM((depth * features // LANES, LANES), F32),
            pltpu.VMEM((size * rows * channels // LANES, LANES), F32),
            pltpu.VMEM((rows * features // inner // LANES, LANES), F32),
            pltpu.SemaphoreType.DMA((2,)),
        ],
        "finish",
        out_specs=[hbm, vmem, vmem],
    )(pair_own, pair_found, right_keep, right_send, *left_found)
    pair_update = pair_update.reshape(cotangent.shape)

    pieces, pair_update, grad_left, grad_right = lax.optimization_barrier(
        (pieces, pair_update, grad_left, grad_right)
    )
    mine = pieces.reshape(outer // 2, pairs)
    other = lax.ppermute(mine, "inner", cores)
    grad_weight = call(place_kernel, shape(outer, pairs), name="place")(mine, other)
    return (pair_update, grad_left, grad_right, grad_weight)


def solution(mesh):
    placed = (
        P(("groups", "blk"), None),
        P(("groups", "blk", "inner"), None),
        P(),
        P(("groups", "blk"), None, "inner", None),
    )
    return jax.shard_map(
        local,
        mesh=mesh,
        in_specs=placed,
        out_specs=(
            P(("groups", "blk"), None, "inner", None),
            P(("groups", "blk"), "inner"),
            P(("groups", "blk", "inner"), None),
            P("groups", None),
        ),
        check_vma=False,
    )
```
